32 devices in a mesh: ctx: 8 (over y, x, core), fsdp: 4 (over z).
Axes of the slice: x: 2, y: 2, z: 4, core: 2. Of those that a mesh axis runs over, the one named last changes fastest.
Arguments:
- tokens: bfloat16 [4, 3072, 1536], P('fsdp', 'ctx'), may hold values from -6 to 6
- order: int32 [4, 3072], P('fsdp'), may hold values from 0 to 3071, as said below
- lengths: int32 [4, 4], P('fsdp'), may hold values from 1 to 2688, 3072 in all within a row
- norm_attn: bfloat16 [1536], P('fsdp'), may hold values from 0.099609375 to 1.8984375
- w_attn_in: bfloat16 [1536, 1792], P('fsdp'), may hold values from -0.15625 to 0.15625
- w_attn_out: bfloat16 [1536, 1536], P('fsdp'), may hold values from -2.5 to 2.5
- norm_mlp: bfloat16 [1536], P('fsdp'), may hold values from 0.099609375 to 1.8984375
- w_mlp_in: bfloat16 [1536, 9216], P('fsdp'), may hold values from -0.15625 to 0.15625
- w_mlp_out: bfloat16 [4608, 1536], P('fsdp'), may hold values from -0.09375 to 0.09375
- cotangent: bfloat16 [4, 3072, 1536], P('fsdp', 'ctx'), may hold values from -6 to 6
Outputs:
- output: bfloat16 [4, 3072, 1536], P('fsdp', 'ctx')
- input_grad: float32 [4, 3072, 1536], P('fsdp', 'ctx')
- grad_norm_attn: float32 [1536], P('fsdp')
- grad_w_attn_in: float32 [1536, 1792], P('fsdp')
- grad_w_attn_out: float32 [1536, 1536], P('fsdp')
- grad_norm_mlp: float32 [1536], P('fsdp')
- grad_w_mlp_in: float32 [1536, 9216], P('fsdp')
- grad_w_mlp_out: float32 [4608, 1536], P('fsdp')
The draws below stay inside these ranges and needn't reach their ends.
Inputs may be any that keep to these rules, and one draw needn't show every extreme that they name: Each group's rows hold every place of its pack once; the rows of one ctx device take one block of 96 consecutive places from each of 4 rounds of 768 places, rounds in order. A group's lengths sum to 3072.
All inputs are finite; a program needn't handle non-finite values.
Results may differ from the reference program's by a relative error of at most 0.024.
Values may be sent and summed in bfloat16 or wider, within the bound.
A program may use at most 384 MiB of HBM per device.

```python
import math
import jax
import jax.numpy as jnp
import numpy as np
from jax import lax

D = 1536
H = 12
HD = 128
FF = 4608
WINDOW = 1024
TOK_DEV = 384
NSEQ = 4
ROUNDS = 4
GROUPS = 4
GROUP_TOK = 3072
BLOCK = 96
LONGEST = 2688


def draw_order(key, part):
    key = jax.random.fold_in(key, 11)
    ctx_count = GROUP_TOK // TOK_DEV
    round_keys = jax.random.split(key, GROUPS * ROUNDS)
    shuffles = jax.vmap(lambda one_key: jax.random.permutation(one_key, ctx_count))(round_keys)
    shuffles = shuffles.reshape(GROUPS, ROUNDS, ctx_count)
    row_index = jnp.arange(GROUP_TOK, dtype=jnp.int32)
    device_index = row_index // TOK_DEV
    local_index = row_index % TOK_DEV
    round_index = local_index // BLOCK
    offset_index = local_index % BLOCK
    chosen = shuffles[:, round_index, device_index]
    block_index = round_index[None, :] * ctx_count + chosen
    return (block_index * BLOCK + offset_index[None, :]).astype(jnp.int32)


def shard_levels(own_key, shape, cuts, least, high):
    factor_of, own = 1.0, jax.random.fold_in(own_key, 6)
    for dim, parts in cuts:
        heights = jnp.exp(jax.random.uniform(jax.random.fold_in(own, dim), (parts,), jnp.float32, least / len(cuts), high / len(cuts)))
        factor_of = factor_of * jnp.repeat(heights, shape[dim] // parts).reshape([-1 if axis == dim else 1 for axis in range(len(shape))])
    return factor_of


def split_up(number_of, total, limit, slope):
    portions = [(1 << 20) // math.isqrt(standing ** slope) + 1 for standing in range(2, number_of + 1)]
    rest, holding = total - limit - (number_of - 1), [1] * (number_of - 1)
    while rest > 0:
        free = [i for i in range(number_of - 1) if holding[i] < limit]
        pool, remaining = sum([portions[i] for i in free]), rest
        for i in free:
            addition = min(limit - holding[i], max(1, remaining * portions[i] // pool), rest)
            holding[i] = holding[i] + addition
            rest = rest - addition
    return np.array([limit] + holding)


def ragged_sizes(stream_key, number_of, total, reach, slope):
    if number_of == 2:
        one = jax.random.randint(stream_key, (), max(1, total - reach), min(reach, total - 1) + 1)
        return jnp.stack([one, total - one])
    sizes = jnp.asarray(split_up(number_of, total, reach, slope), jnp.int32)
    pairs = (number_of - 1) // 2
    giver, receiver = sizes[1:1 + 2 * pairs:2], sizes[2:2 + 2 * pairs:2]
    slack = jnp.minimum(giver - 1, reach - receiver)
    moved = jax.random.randint(jax.random.fold_in(stream_key, 1), (pairs,), 0, 1 << 20) % (slack + 1)
    sizes = sizes.at[1:1 + 2 * pairs:2].set(giver - moved).at[2:2 + 2 * pairs:2].set(receiver + moved)
    return sizes[jax.random.permutation(jax.random.fold_in(stream_key, 2), number_of)]


def gaussian(key, dims, spread, limit, shards=(), kind=jnp.bfloat16):
    drawn = spread * jax.random.normal(key, dims, jnp.float32)
    if shards:
        drawn = drawn * shard_levels(key, dims, shards, -0.22, 0.18)
    return jnp.clip(drawn, -limit, limit).astype(kind)


def setup_inputs(seed: int = 0) -> dict:
    key_list = jax.random.split(jax.random.key(seed), 11)
    tokens = gaussian(key_list[0], (GROUPS, GROUP_TOK, D), 1.0, 6.0, ((0, 4), (1, 8)))
    order = draw_order(jax.random.fold_in(key_list[10], 71), 0)
    lengths = jax.vmap(lambda own: ragged_sizes(own, NSEQ, GROUP_TOK, LONGEST, 2))(jax.random.split(key_list[2], GROUPS)).reshape((GROUPS, NSEQ)).astype(jnp.int32)
    norm_attn = jnp.clip(1.0 + 0.18 * jax.random.normal(key_list[3], (D,), jnp.float32), 0.099609375, 1.8984375).astype(jnp.bfloat16)
    w_attn_in = gaussian(key_list[4], (D, H * HD + 2 * HD), D ** -0.5, 0.15625, ((0, 4),))
    w_attn_out = gaussian(key_list[5], (H * HD, D), (max(H * HD // 256, 1)) ** -0.5, 2.5, ((0, 4),))
    norm_mlp = jnp.clip(1.0 + 0.18 * jax.random.normal(key_list[6], (D,), jnp.float32), 0.099609375, 1.8984375).astype(jnp.bfloat16)
    w_mlp_in = gaussian(key_list[7], (D, 2 * FF), D ** -0.5, 0.15625, ((0, 4),))
    w_mlp_out = gaussian(key_list[8], (FF, D), FF ** -0.5, 0.09375, ((0, 4),))
    cotangent = gaussian(key_list[9], (GROUPS, GROUP_TOK, D), 1.0, 6.0, ((0, 4), (1, 8)))
    return dict(tokens=tokens, order=order, lengths=lengths, norm_attn=norm_attn, w_attn_in=w_attn_in, w_attn_out=w_attn_out, norm_mlp=norm_mlp, w_mlp_in=w_mlp_in, w_mlp_out=w_mlp_out, cotangent=cotangent)


@jax.custom_vjp
def low(v):
    return lax.optimization_barrier(v.astype(jnp.bfloat16)).astype(jnp.float32)

@jax.custom_vjp
def low_back(v):
    return v

def low_keep(v):
    return (low(v), None)

def low_pass(kept, grad):
    return (grad,)

def back_keep(v):
    return (v, None)

def back_low(kept, grad):
    return (low(grad),)
low.defvjp(low_keep, low_pass)
low_back.defvjp(back_keep, back_low)
EPS = 1e-06
HIGHEST = lax.Precision.HIGHEST

def rms_norm(values, gain):
    return values * lax.rsqrt(lax.optimization_barrier(jnp.mean(values * values, axis=-1, keepdims=True)) + EPS) * gain

def rotate(values, places):
    half_dim = values.shape[-1] // 2
    frequency = 10000.0 ** (-jnp.arange(half_dim, dtype=jnp.float32) / half_dim)
    angles = places[:, None] * frequency[None, :]
    cosine = jnp.cos(angles)[:, None, :]
    sine_part = jnp.sin(angles)[:, None, :]
    first_half = values[..., :half_dim]
    second_half = values[..., half_dim:]
    return jnp.concatenate([first_half * cosine - second_half * sine_part, second_half * cosine + first_half * sine_part], axis=-1)

def attend(queries, keys_rot, values, places, segment):
    count_rows = queries.shape[0]
    block_rows = min(512, count_rows)
    blocks = count_rows // block_rows

    def one_block(items):
        query_block, place_block, segment_block = items
        scores = jnp.einsum('qhd,kd->qhk', query_block, keys_rot, precision=HIGHEST)
        scores = low_back(scores)
        distance = place_block[:, None] - places[None, :]
        allowed_mask = (segment_block[:, None] == segment[None, :]) & (distance >= 0) & (distance < WINDOW)
        allowed_mask = allowed_mask[:, None, :]
        masked = jnp.where(allowed_mask, scores, -1e+30)
        row_peak = lax.optimization_barrier(jnp.max(masked, axis=-1, keepdims=True))
        weights_exp = jnp.where(allowed_mask, jnp.exp(masked - row_peak), 0.0)
        probs_low = low(weights_exp / lax.optimization_barrier(jnp.sum(weights_exp, axis=-1, keepdims=True)))
        return jnp.einsum('qhk,kd->qhd', probs_low, values, precision=HIGHEST)
    mixed = lax.map(jax.checkpoint(one_block), (queries.reshape(blocks, block_rows, H, HD), places.reshape(blocks, block_rows), segment.reshape(blocks, block_rows)))
    return mixed.reshape(count_rows, H * HD)

def forward(inputs, gain_attn, in_attn, out_attn, gain_mlp, in_mlp, out_mlp, places, segment):
    place_float = places.astype(jnp.float32)
    count_rows = inputs.shape[0]
    query_dim = H * HD
    normed_one = low(rms_norm(inputs, gain_attn))
    projected = low_back(jnp.dot(normed_one, in_attn, precision=HIGHEST))
    queries = low(rotate(projected[:, :query_dim].reshape(count_rows, H, HD), place_float) * HD ** (-0.5))
    keys_rot = low(rotate(projected[:, query_dim:query_dim + HD][:, None, :], place_float)[:, 0, :])
    values = low(projected[:, query_dim + HD:])
    mixed = low(low_back(attend(queries, keys_rot, values, places, segment)))
    middle = inputs + low_back(jnp.dot(mixed, out_attn, precision=HIGHEST))
    normed_two = low(rms_norm(middle, gain_mlp))
    joined = low_back(jnp.dot(normed_two, in_mlp, precision=HIGHEST))
    hidden = low(jax.nn.gelu(joined[:, :FF], approximate=True) * joined[:, FF:])
    return middle + jnp.dot(hidden, out_mlp, precision=HIGHEST)

def reference(tokens, order, lengths, norm_attn, w_attn_in, w_attn_out, norm_mlp, w_mlp_in, w_mlp_out, cotangent):
    params = tuple((w.astype(jnp.float32) for w in (norm_attn, w_attn_in, w_attn_out, norm_mlp, w_mlp_in, w_mlp_out)))

    def one_group(carry, items):
        group_tokens, places, group_lengths, group_cot = items
        seq_ends = jnp.cumsum(group_lengths)
        segment = lax.optimization_barrier(jnp.sum((seq_ends[None, :] <= places[:, None]).astype(jnp.int32), axis=1))

        def apply(inputs, *weights):
            return forward(inputs, *weights, places, segment)
        result, pullback = jax.vjp(apply, group_tokens.astype(jnp.float32), *params)
        grads = pullback(group_cot.astype(jnp.float32))
        carry = tuple((total + grad for total, grad in zip(carry, grads[1:])))
        return (carry, (result.astype(jnp.bfloat16), grads[0]))
    start_sums = tuple((jnp.zeros(w.shape, jnp.float32) for w in params))
    sums, (results, input_grads) = lax.scan(one_group, start_sums, (tokens, order, lengths, cotangent))
    return (results, input_grads, sums[0], sums[1], sums[2], sums[3], sums[4], sums[5])
```

```python
import jax
import jax.numpy as jnp
from jax import lax
from jax.sharding import PartitionSpec as P

H = 12
HD = 128
FF = 4608
WINDOW = 1024
LANES = 128


EPS = 1e-06


def rms_norm(values, gain):
    return values * lax.rsqrt(jnp.mean(values * values, axis=-1, keepdims=True) + EPS) * gain


def rotate(values, places):
    half_dim = values.shape[-1] // 2
    frequency = 10000.0 ** (-jnp.arange(half_dim, dtype=jnp.float32) / half_dim)
    angles = places[:, None] * frequency[None, :]
    cosine = jnp.cos(angles)[:, None, :]
    sine_part = jnp.sin(angles)[:, None, :]
    first_half = values[..., :half_dim]
    second_half = values[..., half_dim:]
    return jnp.concatenate(
        [
            first_half * cosine - second_half * sine_part,
            second_half * cosine + first_half * sine_part,
        ],
        axis=-1,
    )


def geglu(gate, up):
    return jax.nn.gelu(gate, approximate=True) * up


def dot(left, right):
    return jnp.dot(left, right, preferred_element_type=jnp.float32)


def dot_nt(left, right):
    return jnp.einsum("ab,cb->ac", left, right, preferred_element_type=jnp.float32)


def dot_tn(left, right):
    return jnp.einsum("ab,ac->bc", left, right, preferred_element_type=jnp.float32)


def low(values):
    return values.astype(jnp.bfloat16)


class Layout:
    def __init__(self, ctx_size, fsdp_size):
        self.ctx_size = ctx_size
        self.shards = fsdp_size
        self.chips = ctx_size // 2
        self.index = lax.axis_index("ctx")
        self.chip = self.index // 2
        self.core = self.index % 2
        units = FF // (self.shards * self.chips)
        self.main = units // LANES * LANES
        self.rest = units - self.main
        self.per_shard = FF // self.shards
        self.rest_start = self.chips * self.main

    def xor(self, values, mask):
        pairs = [(i, i ^ mask) for i in range(self.ctx_size)]
        return lax.ppermute(values, "ctx", pairs)

    def same_core_groups(self):
        return [[chip * 2 + core for chip in range(self.chips)] for core in range(2)]

    def gather_chips(self, values):
        if self.chips != 4:
            return lax.all_gather(
                values, "ctx", axis=0, tiled=True, axis_index_groups=self.same_core_groups()
            )
        half = values.shape[1] // 2
        from_x = self.xor(values, 2)
        from_y = self.xor(values, 4)
        corner_left = self.xor(from_x[:, :half], 4)
        corner_right = self.xor(from_y[:, half:], 2)
        corner = jnp.concatenate([corner_left, corner_right], axis=1)
        return jnp.concatenate([values, from_x, from_y, corner], axis=0)

    def scatter_chips(self, partial):
        if self.chips != 4:
            return lax.psum_scatter(
                low(partial),
                "ctx",
                scatter_dimension=0,
                tiled=True,
                axis_index_groups=self.same_core_groups(),
            ).astype(jnp.float32)
        own, to_x, to_y, corner = jnp.split(partial, 4, axis=0)
        half = own.shape[1] // 2
        corner = low(corner)
        left = self.xor(corner[:, :half], 2).astype(jnp.float32)
        right = self.xor(corner[:, half:], 4).astype(jnp.float32)
        to_y = jnp.concatenate([to_y[:, :half] + left, to_y[:, half:]], axis=1)
        to_x = jnp.concatenate([to_x[:, :half], to_x[:, half:] + right], axis=1)
        from_y = self.xor(low(to_y), 4).astype(jnp.float32)
        from_x = self.xor(low(to_x), 2).astype(jnp.float32)
        return own + from_y + from_x

    def columns_of_chip(self, weights, start):
        parts = []
        if self.main:
            for shard in range(self.shards):
                at = start + shard * self.per_shard + self.chip * self.main
                parts.append(lax.dynamic_slice_in_dim(weights, at, self.main, 1))
        if self.rest:
            for shard in range(self.shards):
                at = start + shard * self.per_shard + self.rest_start + self.chip * self.rest
                parts.append(lax.dynamic_slice_in_dim(weights, at, self.rest, 1))
        return jnp.concatenate(parts, axis=1)

    def rows_of_chip(self, weights):
        parts = []
        if self.main:
            parts.append(lax.dynamic_slice_in_dim(weights, self.chip * self.main, self.main, 0))
        if self.rest:
            at = self.rest_start + self.chip * self.rest
            parts.append(lax.dynamic_slice_in_dim(weights, at, self.rest, 0))
        return jnp.concatenate(parts, axis=0)

    def by_core(self, mine, other):
        first = jnp.where(self.core == 0, mine, other)
        second = jnp.where(self.core == 0, other, mine)
        return first, second

    def gather_mlp_in(self, shard):
        mine = self.columns_of_chip(shard, self.core * FF)
        mine = lax.all_gather(mine, "fsdp", axis=0, tiled=True)
        return self.by_core(mine, self.xor(mine, 1))

    def gather_mlp_out(self, shard):
        width = shard.shape[1]
        half = lax.dynamic_slice_in_dim(shard, self.core * (width // 2), width // 2, 1)
        mine = lax.all_gather(self.rows_of_chip(half), "fsdp", axis=0)
        mine = jnp.concatenate(
            [
                mine[:, : self.main].reshape(self.shards * self.main, width // 2),
                mine[:, self.main :].reshape(self.shards * self.rest, width // 2),
            ],
            axis=0,
        )
        return jnp.concatenate(self.by_core(mine, self.xor(mine, 1)), axis=1)

    def sum_pair(self, first, second):
        keep = jnp.where(self.core == 0, first, second)
        send = jnp.where(self.core == 0, second, first)
        return keep + self.xor(low(send), 1).astype(jnp.float32)

    def reduce_mlp_in(self, gate, up):
        total = low(self.sum_pair(gate, up))
        total = lax.psum_scatter(total, "fsdp", scatter_dimension=0, tiled=True)
        rows = total.shape[0]
        every = lax.all_gather(total, "ctx", axis=0)
        every = every.reshape(self.chips, 2, rows, total.shape[1])
        split = self.shards * self.main
        main = every[..., :split].reshape(self.chips, 2, rows, self.shards, self.main)
        rest = every[..., split:].reshape(self.chips, 2, rows, self.shards, self.rest)
        main = main.transpose(2, 1, 3, 0, 4).reshape(rows, 2, self.shards, -1)
        rest = rest.transpose(2, 1, 3, 0, 4).reshape(rows, 2, self.shards, -1)
        return jnp.concatenate([main, rest], axis=3).reshape(rows, 2 * FF).astype(jnp.float32)

    def reduce_mlp_out(self, grad):
        width = grad.shape[1]
        total = low(self.sum_pair(grad[:, : width // 2], grad[:, width // 2 :]))
        split = self.shards * self.main
        main = total[:split].reshape(self.shards, self.main, width // 2)
        rest = total[split:].reshape(self.shards, self.rest, width // 2)
        total = jnp.concatenate([main, rest], axis=1)
        total = lax.psum_scatter(total, "fsdp", scatter_dimension=0, tiled=True)[0]
        every = lax.all_gather(total, "ctx", axis=0)
        every = every.reshape(self.chips, 2, self.main + self.rest, width // 2)
        main = every[:, :, : self.main].transpose(0, 2, 1, 3).reshape(-1, width)
        rest = every[:, :, self.main :].transpose(0, 2, 1, 3).reshape(-1, width)
        return jnp.concatenate([main, rest], axis=0).astype(jnp.float32)

    def gather_whole(self, shard):
        rows = shard.shape[0] // self.ctx_size
        piece = lax.dynamic_slice_in_dim(shard, self.index * rows, rows, 0)
        piece = lax.all_gather(piece, "fsdp", axis=0)
        piece = lax.all_gather(piece, "ctx", axis=1, tiled=True)
        return piece.reshape(-1, shard.shape[1])

    def reduce_whole(self, grad):
        rows = grad.shape[0] // self.shards
        total = low(grad).reshape(self.shards, rows, grad.shape[1])
        total = lax.psum_scatter(total, "ctx", scatter_dimension=1, tiled=True)
        total = lax.psum_scatter(total, "fsdp", scatter_dimension=0, tiled=True)[0]
        return lax.all_gather(total, "ctx", axis=0, tiled=True).astype(jnp.float32)

    def reduce_gain(self, grad):
        total = jnp.sum(lax.all_gather(grad, ("ctx", "fsdp"), axis=0), axis=0)
        rows = grad.shape[0] // self.shards
        return lax.dynamic_slice_in_dim(total, lax.axis_index("fsdp") * rows, rows)


def attend(queries, key_value, row_places, row_segment, places_all, segment_all):
    distance = row_places[:, None] - places_all[None, :]
    allowed = (row_segment[:, None] == segment_all[None, :]) & (distance >= 0) & (distance < WINDOW)
    scores = dot_nt(queries, key_value[:, :HD])
    peak = jnp.max(jnp.where(allowed, scores, -1e30), axis=1)
    weights_exp = jnp.where(allowed, jnp.exp(scores - peak[:, None]), 0.0)
    row_total = jnp.sum(weights_exp, axis=1)
    attended = dot(low(weights_exp), key_value[:, HD:]) / row_total[:, None]
    return attended, peak + jnp.log(row_total)


def attend_back(
    queries, key_value, grad_mixed, row_delta, log_total, row_places, row_segment, places_all, segment_all
):
    distance = row_places[:, None] - places_all[None, :]
    allowed = (row_segment[:, None] == segment_all[None, :]) & (distance >= 0) & (distance < WINDOW)
    key_part = key_value[:, :HD]
    scores = dot_nt(queries, key_part)
    probs = jnp.where(allowed, jnp.exp(scores - log_total[:, None]), 0.0)
    grad_probs = dot_nt(grad_mixed, key_value[:, HD:])
    grad_scores = low(probs * (grad_probs - row_delta[:, None]))
    grad_query = dot(grad_scores, key_part)
    grad_key = dot_tn(grad_scores, queries)
    grad_value = dot_tn(low(probs), grad_mixed)
    return grad_query, jnp.concatenate([grad_key, grad_value], axis=1)


def per_device(
    ctx_size,
    fsdp_size,
    tokens,
    order,
    lengths,
    norm_attn,
    w_attn_in,
    w_attn_out,
    norm_mlp,
    w_mlp_in,
    w_mlp_out,
    cotangent,
):
    lay = Layout(ctx_size, fsdp_size)
    own_rows = tokens.shape[1]
    query_dim = H * HD
    places_all = order[0]
    seq_ends = jnp.cumsum(lengths[0])
    segment_all = jnp.sum((seq_ends[None, :] <= places_all[:, None]).astype(jnp.int32), axis=1)
    own_places = lax.dynamic_slice_in_dim(places_all, lay.index * own_rows, own_rows)
    own_segment = lax.dynamic_slice_in_dim(segment_all, lay.index * own_rows, own_rows)
    row_places = jnp.repeat(own_places, H)
    row_segment = jnp.repeat(own_segment, H)

    in_attn = lay.gather_whole(w_attn_in)
    out_attn = lay.gather_whole(w_attn_out)
    gains = lax.all_gather(jnp.stack([norm_attn, norm_mlp]), "fsdp", axis=1, tiled=True)
    gain_attn = gains[0].astype(jnp.float32)
    gain_mlp = gains[1].astype(jnp.float32)
    gate_in, up_in = lay.gather_mlp_in(w_mlp_in)
    out_mlp = lay.gather_mlp_out(w_mlp_out)
    upstream = cotangent[0]
    upstream_all = lay.gather_chips(upstream)

    inputs = tokens[0].astype(jnp.float32)
    normed_one, norm_one_back = jax.vjp(rms_norm, inputs, gain_attn)
    normed_one = low(normed_one)
    projected = dot(normed_one, in_attn)
    place_float = own_places.astype(jnp.float32)

    def query_map(part):
        return rotate(part, place_float) * HD ** (-0.5)

    def key_map(part):
        return rotate(part[:, None, :], place_float)[:, 0, :]

    query_rot, query_back = jax.vjp(query_map, projected[:, :query_dim].reshape(own_rows, H, HD))
    key_rot, key_back = jax.vjp(key_map, projected[:, query_dim : query_dim + HD])
    queries = low(query_rot).reshape(own_rows * H, HD)
    key_value = jnp.concatenate([low(key_rot), low(projected[:, query_dim + HD :])], axis=1)
    key_value = lax.all_gather(key_value, "ctx", axis=0, tiled=True)
    attended, log_total = attend(
        queries, key_value, row_places, row_segment, places_all, segment_all
    )
    mixed = low(attended.reshape(own_rows, query_dim))
    middle = inputs + dot(mixed, out_attn)
    normed_two, norm_two_back = jax.vjp(rms_norm, middle, gain_mlp)
    normed_all = lay.gather_chips(low(normed_two))

    gate = dot(normed_all, gate_in)
    up = dot(normed_all, up_in)
    hidden, hidden_back = jax.vjp(geglu, gate, up)
    hidden = low(hidden)
    grad_hidden = dot_nt(upstream_all, out_mlp)
    grad_gate, grad_up = hidden_back(grad_hidden)
    grad_gate = low(grad_gate)
    grad_up = low(grad_up)
    grad_normed_two = lay.scatter_chips(dot_nt(grad_gate, gate_in) + dot_nt(grad_up, up_in))
    result = middle + lay.scatter_chips(dot(hidden, out_mlp))
    grad_out_mlp = lay.reduce_mlp_out(dot_tn(hidden, upstream_all))
    grad_in_mlp = lay.reduce_mlp_in(dot_tn(normed_all, grad_gate), dot_tn(normed_all, grad_up))

    grad_middle_norm, grad_gain_mlp = norm_two_back(grad_normed_two)
    grad_middle = upstream.astype(jnp.float32) + grad_middle_norm
    grad_branch = low(grad_middle)
    grad_out_attn = lay.reduce_whole(dot_tn(mixed, grad_branch))
    grad_mixed = low(dot_nt(grad_branch, out_attn)).reshape(own_rows * H, HD)
    row_delta = jnp.sum(grad_mixed.astype(jnp.float32) * attended, axis=1)
    grad_query, grad_keys = attend_back(
        queries,
        key_value,
        grad_mixed,
        row_delta,
        log_total,
        row_places,
        row_segment,
        places_all,
        segment_all,
    )
    grad_kv = lax.psum_scatter(low(grad_keys), "ctx", scatter_dimension=0, tiled=True)
    grad_kv = grad_kv.astype(jnp.float32)
    grad_query_raw = query_back(grad_query.reshape(own_rows, H, HD))[0].reshape(own_rows, query_dim)
    grad_key_raw = key_back(grad_kv[:, :HD])[0]
    grad_projected = low(
        jnp.concatenate([grad_query_raw, grad_key_raw, grad_kv[:, HD:]], axis=1)
    )
    grad_in_attn = lay.reduce_whole(dot_tn(normed_one, grad_projected))
    grad_inputs_norm, grad_gain_attn = norm_one_back(dot_nt(grad_projected, in_attn))
    grad_inputs = grad_middle + grad_inputs_norm
    return (
        low(result)[None],
        grad_inputs[None],
        lay.reduce_gain(grad_gain_attn),
        grad_in_attn,
        grad_out_attn,
        lay.reduce_gain(grad_gain_mlp),
        grad_in_mlp,
        grad_out_mlp,
    )


def solution(mesh):
    in_specs = (
        P("fsdp", "ctx", None),
        P("fsdp", None),
        P("fsdp", None),
        P("fsdp"),
        P("fsdp", None),
        P("fsdp", None),
        P("fsdp"),
        P("fsdp", None),
        P("fsdp", None),
        P("fsdp", "ctx", None),
    )
    out_specs = (
        P("fsdp", "ctx", None),
        P("fsdp", "ctx", None),
        P("fsdp"),
        P("fsdp", None),
        P("fsdp", None),
        P("fsdp"),
        P("fsdp", None),
        P("fsdp", None),
    )

    def run(*arrays):
        return per_device(mesh.shape["ctx"], mesh.shape["fsdp"], *arrays)

    return jax.shard_map(run, mesh=mesh, in_specs=in_specs, out_specs=out_specs, check_vma=False)
```

```python
import functools

import jax
import jax.numpy as jnp
from jax import lax
from jax.experimental import pallas as pl
from jax.experimental.pallas import tpu as pltpu
from jax.sharding import PartitionSpec as P

H = 12
HD = 128
FF = 4608
WINDOW = 1024
ROUNDS = 4
LANES = 128


EPS = 1e-06


def rms_norm(values, gain):
    return values * lax.rsqrt(jnp.mean(values * values, axis=-1, keepdims=True) + EPS) * gain


def geglu(gate, up):
    return jax.nn.gelu(gate, approximate=True) * up


def dot(left, right):
    return jnp.dot(left, right, preferred_element_type=jnp.float32)


def dot_nt(left, right):
    return jnp.einsum("ab,cb->ac", left, right, preferred_element_type=jnp.float32)


def dot_tn(left, right):
    return jnp.einsum("ab,ac->bc", left, right, preferred_element_type=jnp.float32)


def low(values):
    return values.astype(jnp.bfloat16)


VMEM_LIMIT = 56 * 1024 * 1024

def project_kernel(heads, x_ref, gain_ref, w_ref, cos_ref, sin_ref, normed_ref, q_ref, kv_ref):
    step = pl.program_id(0)

    @pl.when(step == 0)
    def _():
        x = x_ref[...].astype(jnp.float32)
        scale = lax.rsqrt(jnp.mean(x * x, axis=-1, keepdims=True) + EPS)
        normed_ref[...] = (x * scale * gain_ref[...]).astype(jnp.bfloat16)

    part = jnp.dot(normed_ref[...], w_ref[...], preferred_element_type=jnp.float32)
    cosine, sine_part = cos_ref[...], sin_ref[...]

    def turn(value):
        return value * cosine + pltpu.roll(value, HD // 2, 1) * sine_part

    @pl.when(step < heads // 2)
    def _():
        for j in range(2):
            q_ref[j] = (turn(part[:, j * HD : (j + 1) * HD]) * HD ** (-0.5)).astype(jnp.bfloat16)

    @pl.when(step == heads // 2)
    def _():
        kv_ref[:, :HD] = turn(part[:, :HD]).astype(jnp.bfloat16)
        kv_ref[:, HD:] = part[:, HD:].astype(jnp.bfloat16)


def project(x, gain, w, cosine, sine_part):
    rows, width = x.shape
    steps = H // 2 + 1
    whole = lambda *shape: pl.BlockSpec(shape, lambda i: (0,) * len(shape))
    return pl.pallas_call(
        functools.partial(project_kernel, H),
        grid=(steps,),
        name="project",
        in_specs=[
            whole(rows, width),
            whole(1, width),
            pl.BlockSpec((width, 2 * HD), lambda i: (0, i)),
            whole(rows, HD),
            whole(rows, HD),
        ],
        out_specs=[
            whole(rows, width),
            pl.BlockSpec((2, rows, HD), lambda i: (jnp.minimum(i, H // 2 - 1), 0, 0)),
            whole(rows, 2 * HD),
        ],
        out_shape=[
            jax.ShapeDtypeStruct((rows, width), jnp.bfloat16),
            jax.ShapeDtypeStruct((H, rows, HD), jnp.bfloat16),
            jax.ShapeDtypeStruct((rows, 2 * HD), jnp.bfloat16),
        ],
        compiler_params=pltpu.CompilerParams(vmem_limit_bytes=VMEM_LIMIT),
    )(x, gain, w, cosine, sine_part)


HEADS_STEP = 4


def attend_kernel(blocks, block, where_ref, q_ref, kv_ref, key_place_ref, place_ref, least_ref, out_ref, window, bias):
    r = pl.program_id(0)

    @pl.when(pl.program_id(1) == 0)
    def _():
        for j in range(blocks):
            window[j * block : (j + 1) * block, :] = kv_ref[where_ref[r, j]]
        key_place = key_place_ref[0]
        allowed = (key_place <= place_ref[...]) & (key_place >= least_ref[...])
        bias[...] = jnp.where(allowed, 0.0, -1e30)

    queries = q_ref[...].reshape(HEADS_STEP * block, HD)
    scores = lax.dot_general(
        queries, window[:, :HD], (((1,), (1,)), ((), ())), preferred_element_type=jnp.float32
    )
    scores = scores.reshape(HEADS_STEP, block, blocks * block) + bias[...][None]
    peak = jnp.max(scores, axis=-1, keepdims=True)
    weights = jnp.exp(scores - peak)
    total = jnp.sum(weights, axis=-1, keepdims=True).reshape(HEADS_STEP * block, 1)
    weights = weights.astype(jnp.bfloat16).reshape(HEADS_STEP * block, blocks * block)
    mixed = jnp.dot(weights, window[:, HD:], preferred_element_type=jnp.float32) / total
    mixed = mixed.astype(jnp.bfloat16)
    for j in range(HEADS_STEP):
        out_ref[:, j * HD : (j + 1) * HD] = mixed[j * block : (j + 1) * block]


def attend(where, queries, kv_blocks, key_place, place, least):
    rounds, blocks = where.shape
    heads, rows, _ = queries.shape
    block = rows // rounds
    span = blocks * block
    grid_spec = pltpu.PrefetchScalarGridSpec(
        num_scalar_prefetch=1,
        grid=(rounds, heads // HEADS_STEP),
        in_specs=[
            pl.BlockSpec((HEADS_STEP, block, HD), lambda r, h, *_: (h, r, 0)),
            pl.BlockSpec(kv_blocks.shape, lambda r, h, *_: (0, 0, 0)),
            pl.BlockSpec((1, 1, span), lambda r, h, *_: (r, 0, 0)),
            pl.BlockSpec((block, 1), lambda r, h, *_: (r, 0)),
            pl.BlockSpec((block, 1), lambda r, h, *_: (r, 0)),
        ],
        out_specs=pl.BlockSpec((block, HEADS_STEP * HD), lambda r, h, *_: (r, h)),
        scratch_shapes=[
            pltpu.VMEM((span, 2 * HD), jnp.bfloat16),
            pltpu.VMEM((block, span), jnp.float32),
        ],
    )
    return pl.pallas_call(
        functools.partial(attend_kernel, blocks, block),
        name="attend",
        grid_spec=grid_spec,
        out_shape=jax.ShapeDtypeStruct((rows, heads * HD), jnp.bfloat16),
        compiler_params=pltpu.CompilerParams(vmem_limit_bytes=VMEM_LIMIT),
    )(where, queries, kv_blocks, key_place, place, least)


def attend_back_kernel(
    blocks, block, where_ref, q_ref, kv_ref, grad_ref, key_place_ref, place_ref, least_ref, cos_ref, sin_ref,
    grad_q_ref, grad_kv_ref, window, bias, window_grad, total_grad,
):
    r, h = pl.program_id(0), pl.program_id(1)
    last = pl.num_programs(1) - 1

    @pl.when((r == 0) & (h == 0))
    def _():
        total_grad[...] = jnp.zeros_like(total_grad)

    @pl.when(h == 0)
    def _():
        for j in range(blocks):
            window[j * block : (j + 1) * block, :] = kv_ref[where_ref[r, j]]
        key_place = key_place_ref[0]
        allowed = (key_place <= place_ref[0]) & (key_place >= least_ref[0])
        bias[...] = jnp.where(allowed, 0.0, -1e30)
        window_grad[...] = jnp.zeros_like(window_grad)

    queries = q_ref[...].reshape(HEADS_STEP * block, HD)
    grads = jnp.concatenate([grad_ref[:, j * HD : (j + 1) * HD] for j in range(HEADS_STEP)], axis=0)
    keys, values = window[:, :HD], window[:, HD:]
    nt = (((1,), (1,)), ((), ()))
    tn = (((0,), (0,)), ((), ()))
    scores = lax.dot_general(keys, queries, nt, preferred_element_type=jnp.float32) + bias[...]
    peak = jnp.max(scores, axis=0, keepdims=True)
    weights = jnp.exp(scores - peak)
    probs = weights * (1.0 / jnp.sum(weights, axis=0, keepdims=True))
    grad_probs = lax.dot_general(values, grads, nt, preferred_element_type=jnp.float32)
    delta = jnp.sum(probs * grad_probs, axis=0, keepdims=True)
    grad_scores = (probs * (grad_probs - delta)).astype(jnp.bfloat16)
    window_grad[:, :HD] += jnp.dot(grad_scores, queries, preferred_element_type=jnp.float32)
    window_grad[:, HD:] += jnp.dot(
        probs.astype(jnp.bfloat16), grads, preferred_element_type=jnp.float32
    )
    grad_q = lax.dot_general(grad_scores, keys, tn, preferred_element_type=jnp.float32)
    cosine, sine_part = cos_ref[...], sin_ref[...]
    for j in range(HEADS_STEP):
        one = grad_q[j * block : (j + 1) * block]
        one = (one * cosine - pltpu.roll(one, HD // 2, 1) * sine_part) * HD ** (-0.5)
        grad_q_ref[:, j * HD : (j + 1) * HD] = one.astype(jnp.bfloat16)

    @pl.when(h == last)
    def _():
        for j in range(blocks):
            total_grad[where_ref[r, blocks + j]] += window_grad[j * block : (j + 1) * block, :]

    @pl.when((h == last) & (r == pl.num_programs(0) - 1))
    def _():
        grad_kv_ref[...] = total_grad[...].astype(jnp.bfloat16)


def attend_back(where, queries, kv_blocks, grads, key_place, place, least, cosine, sine_part):
    rounds, blocks = where.shape[0], where.shape[1] // 2
    heads, rows, _ = queries.shape
    block = rows // rounds
    span = blocks * block
    width = HEADS_STEP * block
    grid_spec = pltpu.PrefetchScalarGridSpec(
        num_scalar_prefetch=1,
        grid=(rounds, heads // HEADS_STEP),
        in_specs=[
            pl.BlockSpec((HEADS_STEP, block, HD), lambda r, h, *_: (h, r, 0)),
            pl.BlockSpec(kv_blocks.shape, lambda r, h, *_: (0, 0, 0)),
            pl.BlockSpec((block, HEADS_STEP * HD), lambda r, h, *_: (r, h)),
            pl.BlockSpec((1, span, 1), lambda r, h, *_: (r, 0, 0)),
            pl.BlockSpec((1, 1, width), lambda r, h, *_: (r, 0, 0)),
            pl.BlockSpec((1, 1, width), lambda r, h, *_: (r, 0, 0)),
            pl.BlockSpec((block, HD), lambda r, h, *_: (r, 0)),
            pl.BlockSpec((block, HD), lambda r, h, *_: (r, 0)),
        ],
        out_specs=[
            pl.BlockSpec((block, HEADS_STEP * HD), lambda r, h, *_: (r, h)),
            pl.BlockSpec(kv_blocks.shape, lambda r, h, *_: (0, 0, 0)),
        ],
        scratch_shapes=[
            pltpu.VMEM((span, 2 * HD), jnp.bfloat16),
            pltpu.VMEM((span, width), jnp.float32),
            pltpu.VMEM((span, 2 * HD), jnp.float32),
            pltpu.VMEM(kv_blocks.shape, jnp.float32),
        ],
    )
    return pl.pallas_call(
        functools.partial(attend_back_kernel, blocks, block),
        name="attend_back",
        grid_spec=grid_spec,
        out_shape=[
            jax.ShapeDtypeStruct((rows, heads * HD), jnp.bfloat16),
            jax.ShapeDtypeStruct(kv_blocks.shape, jnp.bfloat16),
        ],
        compiler_params=pltpu.CompilerParams(vmem_limit_bytes=VMEM_LIMIT),
    )(where, queries, kv_blocks, grads, key_place, place, least, cosine, sine_part)


MESH_ID = pl.DeviceIdType.MESH


class Wire:
    def __init__(self, send_sems, recv_sems):
        self.send_sems = send_sems
        self.recv_sems = recv_sems
        self.count = 0
        self.open = []
        self.ctx = lax.axis_index("ctx")
        self.shard = lax.axis_index("fsdp")

    def other(self, mask):
        at = self.ctx
        for bit in (1, 2, 4):
            if mask & bit:
                at = at + bit - 2 * bit * lax.rem(at // bit, 2)
        return at

    def plane(self, mask):
        return (self.other(mask), self.shard)

    def line(self, step, shards):
        return (self.ctx, lax.rem(self.shard + step, shards))

    def meet(self, peers):
        barrier = pltpu.get_barrier_semaphore()
        for peer in peers:
            pl.semaphore_signal(barrier, inc=1, device_id=peer, device_id_type=MESH_ID)
        pl.semaphore_wait(barrier, len(peers))

    def send(self, source, target, peer):
        at = self.count
        self.count += 1
        copy = pltpu.make_async_remote_copy(
            src_ref=source,
            dst_ref=target,
            send_sem=self.send_sems.at[at],
            recv_sem=self.recv_sems.at[at],
            device_id=peer,
            device_id_type=MESH_ID,
        )
        copy.start()
        self.open.append(copy)
        return copy

    def sent(self, copy):
        copy.wait_send()
        self.open = [one for one in self.open if one is not copy]

    def finish(self):
        for copy in self.open:
            copy.wait_send()


class PlaneGather:
    COPIES = 9

    def __init__(self, wire, source, out_at, rows, split):
        self.wire, self.out_at, self.rows, self.split = wire, out_at, rows, split
        ctx = wire.ctx
        self.core = wire.send(source, out_at(ctx), wire.plane(1))
        self.x = wire.send(source, out_at(ctx), wire.plane(2))
        self.y = wire.send(source, out_at(ctx), wire.plane(4))

    def forward(self):
        wire, split = self.wire, self.split
        rest = self.rows - split
        self.x.wait_recv()
        block = self.out_at(wire.other(2))
        part = block.at[pl.ds(0, split)]
        self.corner_y = wire.send(part, part, wire.plane(4))
        self.core_x = wire.send(block, block, wire.plane(1))
        self.y.wait_recv()
        block = self.out_at(wire.other(4))
        part = block.at[pl.ds(split, rest)]
        self.corner_x = wire.send(part, part, wire.plane(2))
        self.core_y = wire.send(block, block, wire.plane(1))

    def corner(self):
        self.corner_y.wait_recv()
        self.corner_x.wait_recv()
        block = self.out_at(self.wire.other(6))
        self.core_corner = self.wire.send(block, block, self.wire.plane(1))

    def settle(self):
        self.core.wait_recv()
        self.core_x.wait_recv()
        self.core_y.wait_recv()
        self.core_corner.wait_recv()


def half_rows(rows, turn):
    low_half = rows // 32 * 16
    return low_half if turn % 2 else rows - low_half


def add_low(first, second):
    return (first.astype(jnp.float32) + second.astype(jnp.float32)).astype(jnp.bfloat16)


class PlaneSum:
    COPIES = 7

    def __init__(self, wire, source, own, pair, first, second, local_sem):
        self.wire, self.own, self.pair, self.first, self.second = wire, own, pair, first, second
        core = lax.rem(wire.ctx, 2)
        self.chips = {mask: wire.other(2 * mask) // 2 for mask in range(4)}
        self.swap = wire.send(source.at[:, :, 1 - core], pair, wire.plane(1))
        self.local = pltpu.make_async_copy(source.at[:, :, core], own, local_sem)
        self.local.start()

    def step_one(self):
        wire, own, pair, first, chips = self.wire, self.own, self.pair, self.first, self.chips
        self.local.wait()
        self.swap.wait_recv()

        def add_pair(index, carry):
            part, other = index // 4, lax.rem(index, 4)
            own[part, other] = add_low(own[part, other], pair[part, other])
            return carry

        lax.fori_loop(0, 16, add_pair, 0)
        low, high = pl.ds(0, 2), pl.ds(2, 2)
        self.one = [
            wire.send(own.at[low, chips[3]], first.at[0, 1], wire.plane(2)),
            wire.send(own.at[high, chips[3]], first.at[1, 1], wire.plane(4)),
            wire.send(own.at[low, chips[1]], first.at[0, 0], wire.plane(2)),
            wire.send(own.at[high, chips[2]], first.at[1, 0], wire.plane(4)),
        ]

    def step_two(self):
        wire, own, first, second, chips = self.wire, self.own, self.first, self.second, self.chips
        self.one[0].wait_recv()
        for part in range(2):
            own[part, chips[2]] = add_low(own[part, chips[2]], first[0, 1, part])
        self.two = [wire.send(own.at[pl.ds(0, 2), chips[2]], second.at[pl.ds(0, 2)], wire.plane(4))]
        self.one[1].wait_recv()
        for part in range(2):
            own[part + 2, chips[1]] = add_low(own[part + 2, chips[1]], first[1, 1, part])
        self.two.append(
            wire.send(own.at[pl.ds(2, 2), chips[1]], second.at[pl.ds(2, 2)], wire.plane(2))
        )

    def result(self, store):
        own, first, second, chips = self.own, self.first, self.second, self.chips
        for copy in self.one[2:] + self.two:
            copy.wait_recv()
        for part in range(4):
            total = own[part, chips[0]].astype(jnp.float32)
            total += first[part // 2, 0, part % 2].astype(jnp.float32)
            total += second[part].astype(jnp.float32)
            store(part, total)


def plane_sum_scratch(rows, columns):
    shape = lambda *lead: pltpu.VMEM(lead + (rows, columns), jnp.bfloat16)
    return [shape(4, 4), shape(4, 4), shape(2, 2, 2), shape(4)]


def dma_sems(count):
    return pltpu.SemaphoreType.DMA((count,))


ANY = pl.BlockSpec(memory_space=pl.ANY)
PLANE_PEERS = (1, 2, 4)


def comm_params(number):
    return pltpu.CompilerParams(
        collective_id=number, has_side_effects=True, vmem_limit_bytes=VMEM_LIMIT
    )


def gather_weights_kernel(shards, in_ref, out_ref, gain_ref, in_all, out_all, gain_all, local_sems, send_sems, recv_sems):
    wire = Wire(send_sems, recv_sems)
    ctx, shard = wire.ctx, wire.shard
    wire.meet(
        [wire.plane(mask) for mask in PLANE_PEERS] + [wire.line(s, shards) for s in range(1, shards)]
    )
    pairs = ((in_ref, in_all), (out_ref, out_all))
    arrivals = []
    for source, target in pairs:
        for step in range(1, shards):
            arrivals.append(
                wire.send(source.at[ctx], target.at[shard, ctx], wire.line(step, shards))
            )
    gains = [
        wire.send(gain_ref, gain_all.at[shard], wire.line(step, shards))
        for step in range(1, shards)
    ]
    locals_ = []
    for i, (source, target) in enumerate(((in_ref, in_all), (out_ref, out_all), (gain_ref, gain_all))):
        copy = pltpu.make_async_copy(source, target.at[shard], local_sems.at[i])
        copy.start()
        locals_.append(copy)
    gathers = []
    rows = in_ref.shape[1]
    for source, target in pairs:
        for step in range(1, shards):
            arrivals[len(gathers)].wait_recv()
            origin = lax.rem(shard + shards - step, shards)
            place = lambda who, target=target, origin=origin: target.at[origin, who]
            gathers.append(
                PlaneGather(wire, place(ctx), place, rows, half_rows(rows, len(gathers)))
            )
    for gather in gathers:
        gather.forward()
    for gather in gathers:
        gather.corner()
    for gather in gathers:
        gather.settle()
    for copy in gains:
        copy.wait_recv()
    for copy in locals_:
        copy.wait()
    wire.finish()


def gather_weights(w_in, w_out, gains, ctx_size, shards):
    rows = w_in.shape[0] // ctx_size
    w_in = w_in.reshape(ctx_size, rows, -1)
    w_out = w_out.reshape(ctx_size, rows, -1)
    copies = 2 * (shards - 1) * (1 + PlaneGather.COPIES) + shards - 1
    w_in, w_out, gains = pl.pallas_call(
        functools.partial(gather_weights_kernel, shards),
        name="gather_weights",
        in_specs=[ANY] * 3,
        out_specs=[ANY] * 3,
        out_shape=[
            jax.ShapeDtypeStruct((shards,) + w_in.shape, w_in.dtype),
            jax.ShapeDtypeStruct((shards,) + w_out.shape, w_out.dtype),
            jax.ShapeDtypeStruct((shards,) + gains.shape, gains.dtype),
        ],
        scratch_shapes=[dma_sems(3), dma_sems(copies), dma_sems(copies)],
        compiler_params=comm_params(1),
    )(w_in, w_out, gains)
    width = shards * ctx_size * rows
    return w_in.reshape(width, -1), w_out.reshape(width, -1), gains


def gather_plane_kernel(in_ref, all_ref, local_sem, send_sems, recv_sems):
    wire = Wire(send_sems, recv_sems)
    wire.meet([wire.plane(mask) for mask in PLANE_PEERS])
    place = lambda who: all_ref.at[who]
    rows = in_ref.shape[0]
    gather = PlaneGather(wire, in_ref, place, rows, rows // 2)
    copy = pltpu.make_async_copy(in_ref, place(wire.ctx), local_sem)
    copy.start()
    gather.forward()
    gather.corner()
    gather.settle()
    copy.wait()
    wire.finish()


def gather_plane(values, ctx_size):
    return pl.pallas_call(
        gather_plane_kernel,
        name="gather_plane",
        in_specs=[ANY],
        out_specs=ANY,
        out_shape=jax.ShapeDtypeStruct((ctx_size,) + values.shape, values.dtype),
        scratch_shapes=[
            pltpu.SemaphoreType.DMA,
            dma_sems(PlaneGather.COPIES),
            dma_sems(PlaneGather.COPIES),
        ],
        compiler_params=comm_params(2),
    )(values)


def sum_plane_kernel(in_ref, out_ref, own, pair, first, second, local_sem, send_sems, recv_sems):
    wire = Wire(send_sems, recv_sems)
    wire.meet([wire.plane(mask) for mask in PLANE_PEERS])
    total = PlaneSum(wire, in_ref, own, pair, first, second, local_sem)
    total.step_one()
    total.step_two()

    def store(part, value):
        out_ref[part] = value

    total.result(store)
    wire.finish()


def sum_plane(values):
    rows, columns = values.shape[3:]
    return pl.pallas_call(
        sum_plane_kernel,
        name="sum_plane",
        in_specs=[ANY],
        out_specs=pl.BlockSpec(memory_space=pltpu.VMEM),
        out_shape=jax.ShapeDtypeStruct((4, rows, columns), jnp.float32),
        scratch_shapes=plane_sum_scratch(rows, columns)
        + [pltpu.SemaphoreType.DMA, dma_sems(PlaneSum.COPIES), dma_sems(PlaneSum.COPIES)],
        compiler_params=comm_params(3),
    )(values)


def close_kernel(
    shards, g_out, g_in, m_in, m_out, gain, out_all, in_all, m_in_all, m_out_all, gain_out,
    *scratch,
):
    sums = (scratch[:4], scratch[4:8])
    mine, arrived = (scratch[8], scratch[9]), (scratch[10], scratch[11])
    done = (scratch[12], scratch[13])
    gain_now, gain_in, gain_line = scratch[14:17]
    local_sems, send_sems, recv_sems = scratch[17:]
    wire = Wire(send_sems, recv_sems)
    ctx, shard = wire.ctx, wire.shard
    wire.meet(
        [wire.plane(mask) for mask in PLANE_PEERS] + [wire.line(s, shards) for s in range(1, shards)]
    )
    totals = [
        PlaneSum(wire, source, *sums[i], local_sems.at[i]) for i, source in enumerate((g_out, g_in))
    ]
    gain_now[...] = gain[...]

    def gain_start(at):
        return wire.send(gain_now, gain_in.at[at], wire.plane(PLANE_PEERS[at]))

    def gain_add(at, copy):
        copy.wait_recv()
        wire.sent(copy)
        gain_now[...] += gain_in[at]

    gain_copy = gain_start(0)
    for total in totals:
        total.step_one()
    gain_add(0, gain_copy)
    gain_copy = gain_start(1)
    for total in totals:
        total.step_two()
    gain_add(1, gain_copy)
    gain_copy = gain_start(2)
    gathers, locals_ = [], []
    for i, (source, target) in enumerate(((m_in, m_in_all), (m_out, m_out_all))):
        place = lambda who, target=target: target.at[who]
        rows = source.shape[0]
        gathers.append(PlaneGather(wire, source, place, rows, half_rows(rows, i)))
        copy = pltpu.make_async_copy(source, place(ctx), local_sems.at[2 + i])
        copy.start()
        locals_.append(copy)
    lines = []
    for i, total in enumerate(totals):

        def store(part, value, i=i):
            mine[i][part] = value.astype(jnp.bfloat16)

        total.result(store)
        lines.append(
            [
                wire.send(
                    mine[i].at[lax.rem(shard + step, shards)],
                    arrived[i].at[step - 1],
                    wire.line(step, shards),
                )
                for step in range(1, shards)
            ]
        )
    gain_add(2, gain_copy)
    gain_copies = [
        wire.send(
            gain_now.at[lax.rem(shard + step, shards)], gain_line.at[step - 1], wire.line(step, shards)
        )
        for step in range(1, shards)
    ]
    small = []
    for i, target in enumerate((out_all, in_all)):
        for copy in lines[i]:
            copy.wait_recv()
        value = mine[i][shard].astype(jnp.float32)
        for step in range(shards - 1):
            value += arrived[i][step].astype(jnp.float32)
        done[i][...] = value.astype(jnp.bfloat16)
        place = lambda who, target=target: target.at[who]
        rows = target.shape[1]
        small.append(PlaneGather(wire, done[i], place, rows, half_rows(rows, i)))
        copy = pltpu.make_async_copy(done[i], place(ctx), local_sems.at[4 + i])
        copy.start()
        locals_.append(copy)
    for copy in gain_copies:
        copy.wait_recv()
    value = gain_now[shard]
    for step in range(shards - 1):
        value += gain_line[step]
    gain_out[...] = value
    for gather in gathers + small:
        gather.forward()
    for gather in gathers + small:
        gather.corner()
    for gather in gathers + small:
        gather.settle()
    for copy in locals_:
        copy.wait()
    wire.finish()


def close(g_out, g_in, m_in, m_out, gain, ctx_size, shards):
    sums, mine, arrived, done = [], [], [], []
    for grad in (g_out, g_in):
        rows, columns = grad.shape[3:]
        sums += plane_sum_scratch(rows, columns)
        mine.append(pltpu.VMEM((shards, rows, columns), jnp.bfloat16))
        arrived.append(pltpu.VMEM((shards - 1, rows, columns), jnp.bfloat16))
        done.append(pltpu.VMEM((rows, columns), jnp.bfloat16))
    gains = [
        pltpu.VMEM(gain.shape, jnp.float32),
        pltpu.VMEM((3,) + gain.shape, jnp.float32),
        pltpu.VMEM((shards - 1,) + gain.shape[1:], jnp.float32),
    ]
    copies = 2 * (PlaneSum.COPIES + 2 * PlaneGather.COPIES + shards - 1) + 3 + shards - 1
    whole = lambda shape: jax.ShapeDtypeStruct((ctx_size,) + shape, jnp.bfloat16)
    return pl.pallas_call(
        functools.partial(close_kernel, shards),
        name="close",
        in_specs=[ANY] * 4 + [pl.BlockSpec(memory_space=pltpu.VMEM)],
        out_specs=[ANY] * 4 + [pl.BlockSpec(memory_space=pltpu.VMEM)],
        out_shape=[
            whole(g_out.shape[3:]),
            whole(g_in.shape[3:]),
            whole(m_in.shape),
            whole(m_out.shape),
            jax.ShapeDtypeStruct(gain.shape[1:], jnp.float32),
        ],
        scratch_shapes=sums + mine + arrived + done + gains + [dma_sems(6), dma_sems(copies), dma_sems(copies)],
        compiler_params=comm_params(4),
    )(g_out, g_in, m_in, m_out, gain)


def finish_in_kernel(shards, chips, main, rest, in_ref, out_ref):
    per_shard = chips * (main + rest)
    split = shards * main
    for core in range(2):
        for shard in range(shards):
            start = (core * shards + shard) * per_shard
            for chip in range(chips):
                block = in_ref[chip * 2 + core, :, shard * main : (shard + 1) * main]
                out_ref[:, start + chip * main : start + (chip + 1) * main] = block.astype(jnp.float32)
            tails = [
                in_ref[chip * 2 + core, :, split : split + shards * rest].astype(jnp.float32)[
                    :, shard * rest : (shard + 1) * rest
                ]
                for chip in range(chips)
            ]
            out_ref[:, start + chips * main : start + per_shard] = jnp.concatenate(tails, axis=1)


def finish_in(values, shards, main, rest):
    ctx_size, rows, units = values.shape
    tile = rows // 8
    return pl.pallas_call(
        functools.partial(finish_in_kernel, shards, ctx_size // 2, main, rest),
        name="finish_in",
        grid=(rows // tile,),
        in_specs=[pl.BlockSpec((ctx_size, tile, units), lambda i: (0, i, 0))],
        out_specs=pl.BlockSpec((tile, 2 * FF), lambda i: (i, 0)),
        out_shape=jax.ShapeDtypeStruct((rows, 2 * FF), jnp.float32),
        compiler_params=pltpu.CompilerParams(vmem_limit_bytes=VMEM_LIMIT),
    )(values)


def finish_out_kernel(chips, main, rest, in_ref, out_ref):
    chip = pl.program_id(1)
    out_ref[pl.ds(chip * main, main), :] = in_ref[0, :main, :].astype(jnp.float32)
    out_ref[pl.ds(chips * main + chip * rest, rest), :] = in_ref[0, main:, :].astype(jnp.float32)


def finish_out(values, main, rest):
    ctx_size, units, half = values.shape
    chips = ctx_size // 2
    return pl.pallas_call(
        functools.partial(finish_out_kernel, chips, main, rest),
        name="finish_out",
        grid=(2, chips),
        in_specs=[pl.BlockSpec((1, units, half), lambda k, q: (q * 2 + k, 0, 0))],
        out_specs=pl.BlockSpec((chips * units, half), lambda k, q: (0, k)),
        out_shape=jax.ShapeDtypeStruct((chips * units, 2 * half), jnp.float32),
        compiler_params=pltpu.CompilerParams(vmem_limit_bytes=VMEM_LIMIT),
    )(values)


class Layout:
    def __init__(self, ctx_size, fsdp_size):
        self.ctx_size = ctx_size
        self.shards = fsdp_size
        self.chips = ctx_size // 2
        self.index = lax.axis_index("ctx")
        self.chip = self.index // 2
        self.core = self.index % 2
        units = FF // (self.shards * self.chips)
        self.main = units // LANES * LANES
        self.rest = units - self.main
        self.per_shard = FF // self.shards
        self.rest_start = self.chips * self.main
        self.plane = ctx_size == 8 and fsdp_size == 4

    def xor(self, values, mask):
        pairs = [(i, i ^ mask) for i in range(self.ctx_size)]
        return lax.ppermute(values, "ctx", pairs)

    def same_core_groups(self):
        return [[chip * 2 + core for chip in range(self.chips)] for core in range(2)]

    def gather_chips(self, values):
        if self.chips != 4:
            return lax.all_gather(
                values, "ctx", axis=0, tiled=True, axis_index_groups=self.same_core_groups()
            )
        half = values.shape[1] // 2
        from_x = self.xor(values, 2)
        from_y = self.xor(values, 4)
        corner_left = self.xor(from_x[:, :half], 4)
        corner_right = self.xor(from_y[:, half:], 2)
        corner = jnp.concatenate([corner_left, corner_right], axis=1)
        return jnp.concatenate([values, from_x, from_y, corner], axis=0)

    def scatter_chips(self, partial):
        if self.chips != 4:
            return lax.psum_scatter(
                low(partial),
                "ctx",
                scatter_dimension=0,
                tiled=True,
                axis_index_groups=self.same_core_groups(),
            ).astype(jnp.float32)
        own, to_x, to_y, corner = jnp.split(partial, 4, axis=0)
        half = own.shape[1] // 2
        corner = low(corner)
        left = self.xor(corner[:, :half], 2).astype(jnp.float32)
        right = self.xor(corner[:, half:], 4).astype(jnp.float32)
        to_y = jnp.concatenate([to_y[:, :half] + left, to_y[:, half:]], axis=1)
        to_x = jnp.concatenate([to_x[:, :half], to_x[:, half:] + right], axis=1)
        from_y = self.xor(low(to_y), 4).astype(jnp.float32)
        from_x = self.xor(low(to_x), 2).astype(jnp.float32)
        return own + from_y + from_x

    def columns_of_chip(self, weights, start):
        parts = []
        if self.main:
            for shard in range(self.shards):
                at = start + shard * self.per_shard + self.chip * self.main
                parts.append(lax.dynamic_slice_in_dim(weights, at, self.main, 1))
        if self.rest:
            for shard in range(self.shards):
                at = start + shard * self.per_shard + self.rest_start + self.chip * self.rest
                parts.append(lax.dynamic_slice_in_dim(weights, at, self.rest, 1))
        return jnp.concatenate(parts, axis=1)

    def rows_of_chip(self, weights):
        parts = []
        if self.main:
            parts.append(lax.dynamic_slice_in_dim(weights, self.chip * self.main, self.main, 0))
        if self.rest:
            at = self.rest_start + self.chip * self.rest
            parts.append(lax.dynamic_slice_in_dim(weights, at, self.rest, 0))
        return jnp.concatenate(parts, axis=0)

    def by_core(self, mine, other):
        first = jnp.where(self.core == 0, mine, other)
        second = jnp.where(self.core == 0, other, mine)
        return first, second

    def gather_mlp_in(self, shard):
        mine = self.columns_of_chip(shard, self.core * FF)
        mine = lax.all_gather(mine, "fsdp", axis=0, tiled=True)
        return self.by_core(mine, self.xor(mine, 1))

    def gather_mlp_out(self, shard):
        width = shard.shape[1]
        half = lax.dynamic_slice_in_dim(shard, self.core * (width // 2), width // 2, 1)
        mine = lax.all_gather(self.rows_of_chip(half), "fsdp", axis=0)
        mine = jnp.concatenate(
            [
                mine[:, : self.main].reshape(self.shards * self.main, width // 2),
                mine[:, self.main :].reshape(self.shards * self.rest, width // 2),
            ],
            axis=0,
        )
        return jnp.concatenate(self.by_core(mine, self.xor(mine, 1)), axis=1)

    def sum_pair(self, first, second):
        keep = jnp.where(self.core == 0, first, second)
        send = jnp.where(self.core == 0, second, first)
        return keep + self.xor(low(send), 1).astype(jnp.float32)

    def reduce_mlp_in(self, gate, up):
        total = low(self.sum_pair(gate, up))
        return lax.psum_scatter(total, "fsdp", scatter_dimension=0, tiled=True)

    def order_mlp_in(self, every):
        rows = every.shape[1]
        if self.main:
            return finish_in(every, self.shards, self.main, self.rest)
        every = every.reshape(self.chips, 2, rows, every.shape[2])
        split = self.shards * self.main
        main = every[..., :split].reshape(self.chips, 2, rows, self.shards, self.main)
        rest = every[..., split:].reshape(self.chips, 2, rows, self.shards, self.rest)
        main = main.transpose(2, 1, 3, 0, 4).reshape(rows, 2, self.shards, -1)
        rest = rest.transpose(2, 1, 3, 0, 4).reshape(rows, 2, self.shards, -1)
        return jnp.concatenate([main, rest], axis=3).reshape(rows, 2 * FF).astype(jnp.float32)

    def reduce_mlp_out(self, grad):
        width = grad.shape[1]
        total = low(self.sum_pair(grad[:, : width // 2], grad[:, width // 2 :]))
        split = self.shards * self.main
        main = total[:split].reshape(self.shards, self.main, width // 2)
        rest = total[split:].reshape(self.shards, self.rest, width // 2)
        total = jnp.concatenate([main, rest], axis=1)
        return lax.psum_scatter(total, "fsdp", scatter_dimension=0, tiled=True)[0]

    def order_mlp_out(self, every):
        if self.main:
            return finish_out(every, self.main, self.rest)
        width = 2 * every.shape[2]
        every = every.reshape(self.chips, 2, self.main + self.rest, width // 2)
        main = every[:, :, : self.main].transpose(0, 2, 1, 3).reshape(-1, width)
        rest = every[:, :, self.main :].transpose(0, 2, 1, 3).reshape(-1, width)
        return jnp.concatenate([main, rest], axis=0).astype(jnp.float32)

    def gather_whole(self, shard):
        rows = shard.shape[0] // self.ctx_size
        piece = lax.dynamic_slice_in_dim(shard, self.index * rows, rows, 0)
        piece = lax.all_gather(piece, "fsdp", axis=0)
        piece = lax.all_gather(piece, "ctx", axis=1, tiled=True)
        return piece.reshape(-1, shard.shape[1])

    def reduce_whole(self, grad):
        rows = grad.shape[0] // self.shards
        total = grad.reshape(self.shards, rows, grad.shape[1])
        total = lax.psum_scatter(total, "ctx", scatter_dimension=1, tiled=True)
        total = lax.psum_scatter(total, "fsdp", scatter_dimension=0, tiled=True)[0]
        return lax.all_gather(total, "ctx", axis=0, tiled=True).astype(jnp.float32)

    def reduce_gain(self, grad):
        total = jnp.sum(lax.all_gather(grad, ("ctx", "fsdp"), axis=0), axis=0)
        rows = grad.shape[0] // self.shards
        return lax.dynamic_slice_in_dim(total, lax.axis_index("fsdp") * rows, rows)


def window_blocks(places_all, own_places, seq_ends, block):
    count = places_all.shape[0] // block
    blocks = places_all.reshape(count, block)
    held = blocks[:, 0] // block
    at = jnp.arange(count, dtype=jnp.int32)
    position = jnp.sum(jnp.where(held[None, :] == at[:, None], at[None, :], 0), axis=1)
    span = (WINDOW + block - 2) // block + 1
    first = own_places.reshape(-1, block)[:, 0] // block
    wanted = first[:, None] - (span - 1) + jnp.arange(span, dtype=jnp.int32)[None, :]
    where = position[jnp.maximum(wanted, 0)]
    key_place = jnp.where((wanted >= 0)[:, :, None], blocks[where], jnp.int32(1 << 30))
    key_place = key_place.reshape(where.shape[0], 1, span * block)
    starts = jnp.where(seq_ends[None, :] <= own_places[:, None], seq_ends[None, :], 0)
    least = jnp.maximum(jnp.max(starts, axis=1), own_places - (WINDOW - 1))
    return where, key_place, least


def per_device(
    ctx_size,
    fsdp_size,
    tokens,
    order,
    lengths,
    norm_attn,
    w_attn_in,
    w_attn_out,
    norm_mlp,
    w_mlp_in,
    w_mlp_out,
    cotangent,
):
    lay = Layout(ctx_size, fsdp_size)
    own_rows, width = tokens.shape[1:]
    query_dim = H * HD
    block = own_rows // ROUNDS
    places_all = order[0]
    own_places = lax.dynamic_slice_in_dim(places_all, lay.index * own_rows, own_rows)
    where, key_place, least = window_blocks(
        places_all, own_places, jnp.cumsum(lengths[0]), block
    )
    frequency = 10000.0 ** (-jnp.arange(HD // 2, dtype=jnp.float32) / (HD // 2))
    angles = own_places.astype(jnp.float32)[:, None] * frequency[None, :]
    cosine = jnp.cos(angles)
    sine_part = jnp.sin(angles)
    cosine = jnp.concatenate([cosine, cosine], axis=1)
    sine_part = jnp.concatenate([-sine_part, sine_part], axis=1)

    gains = jnp.stack([norm_attn, norm_mlp]).astype(jnp.float32)
    if lay.plane:
        gains = jnp.pad(gains, ((0, 6), (0, 0)))
        in_attn, out_attn, gains = gather_weights(
            w_attn_in, w_attn_out, gains, ctx_size, fsdp_size
        )
        gains = gains.transpose(1, 0, 2).reshape(8, width)
    else:
        in_attn = lay.gather_whole(w_attn_in)
        out_attn = lay.gather_whole(w_attn_out)
        gains = lax.all_gather(gains, "fsdp", axis=1, tiled=True)
    gate_in, up_in = lay.gather_mlp_in(w_mlp_in)
    out_mlp = lay.gather_mlp_out(w_mlp_out)
    upstream = cotangent[0]
    upstream_all = lay.gather_chips(upstream)

    normed_one, queries, key_value = project(tokens[0], gains[:1], in_attn, cosine, sine_part)
    if lay.plane:
        key_value = gather_plane(key_value, ctx_size)
    else:
        key_value = lax.all_gather(key_value, "ctx", axis=0)
    key_value = key_value.reshape(ctx_size * ROUNDS, block, 2 * HD)
    mixed = attend(where, queries, key_value, key_place, own_places[:, None], least[:, None])
    middle = tokens[0].astype(jnp.float32) + dot(mixed, out_attn)
    normed_two, norm_two_back = jax.vjp(rms_norm, middle, gains[1])
    normed_all = lay.gather_chips(low(normed_two))

    gate = dot(normed_all, gate_in)
    up = dot(normed_all, up_in)
    hidden, hidden_back = jax.vjp(geglu, gate, up)
    hidden = low(hidden)
    grad_hidden = dot_nt(upstream_all, out_mlp)
    grad_gate, grad_up = hidden_back(grad_hidden)
    grad_gate = low(grad_gate)
    grad_up = low(grad_up)
    grad_normed_two = lay.scatter_chips(dot_nt(grad_gate, gate_in) + dot_nt(grad_up, up_in))
    result = middle + lay.scatter_chips(dot(hidden, out_mlp))
    grad_out_mlp = lay.reduce_mlp_out(dot_tn(hidden, upstream_all))
    grad_in_mlp = lay.reduce_mlp_in(dot_tn(normed_all, grad_gate), dot_tn(normed_all, grad_up))

    grad_middle_norm, grad_gain_mlp = norm_two_back(grad_normed_two)
    grad_middle = upstream.astype(jnp.float32) + grad_middle_norm
    grad_branch = low(grad_middle)
    grad_out_attn = low(dot_tn(mixed, grad_branch))
    grad_mixed = low(dot_nt(grad_branch, out_attn))

    def repeated(values):
        values = values.reshape(ROUNDS, 1, block)
        return jnp.tile(values, (1, 1, HEADS_STEP))

    target = where % ROUNDS * ctx_size + where // ROUNDS
    grad_query, grad_kv = attend_back(
        jnp.concatenate([where, target], axis=1),
        queries,
        key_value,
        grad_mixed,
        key_place.reshape(ROUNDS, -1, 1),
        repeated(own_places),
        repeated(least),
        cosine,
        sine_part,
    )
    if lay.plane:
        grad_kv = sum_plane(grad_kv.reshape(ROUNDS, lay.chips, 2, block, 2 * HD))
        grad_kv = grad_kv.reshape(own_rows, 2 * HD)
    else:
        grad_kv = grad_kv.reshape(ROUNDS, ctx_size, block, 2 * HD)
        grad_kv = lax.psum_scatter(grad_kv, "ctx", scatter_dimension=1, tiled=True)
        grad_kv = grad_kv.reshape(own_rows, 2 * HD).astype(jnp.float32)
    grad_key = grad_kv[:, :HD] * cosine - jnp.roll(grad_kv[:, :HD], HD // 2, 1) * sine_part
    grad_projected = jnp.concatenate([grad_query, low(grad_key), low(grad_kv[:, HD:])], axis=1)
    grad_in_attn = low(dot_tn(normed_one, grad_projected))
    _, norm_one_back = jax.vjp(rms_norm, tokens[0].astype(jnp.float32), gains[0])
    grad_inputs_norm, grad_gain_attn = norm_one_back(dot_nt(grad_projected, in_attn))
    grad_inputs = grad_middle + grad_inputs_norm
    if lay.plane:
        split = lambda grad: grad.reshape(fsdp_size, lay.chips, 2, -1, grad.shape[1])
        grad_gains = jnp.stack([grad_gain_attn, grad_gain_mlp]).reshape(2, fsdp_size, -1)
        grad_gains = jnp.pad(grad_gains.transpose(1, 0, 2), ((0, 0), (0, 6), (0, 0)))
        grad_out_attn, grad_in_attn, grad_in_mlp, grad_out_mlp, grad_gains = close(
            split(grad_out_attn),
            split(grad_in_attn),
            grad_in_mlp,
            grad_out_mlp,
            grad_gains,
            ctx_size,
            fsdp_size,
        )
        whole = lambda grad: grad.reshape(-1, grad.shape[2]).astype(jnp.float32)
        grad_out_attn, grad_in_attn = whole(grad_out_attn), whole(grad_in_attn)
        grad_gain_attn, grad_gain_mlp = grad_gains[0], grad_gains[1]
    else:
        grad_out_attn = lay.reduce_whole(grad_out_attn)
        grad_in_attn = lay.reduce_whole(grad_in_attn)
        grad_in_mlp = lax.all_gather(grad_in_mlp, "ctx", axis=0)
        grad_out_mlp = lax.all_gather(grad_out_mlp, "ctx", axis=0)
        grad_gain_attn = lay.reduce_gain(grad_gain_attn)
        grad_gain_mlp = lay.reduce_gain(grad_gain_mlp)
    return (
        low(result)[None],
        grad_inputs[None],
        grad_gain_attn,
        grad_in_attn,
        grad_out_attn,
        grad_gain_mlp,
        lay.order_mlp_in(grad_in_mlp),
        lay.order_mlp_out(grad_out_mlp),
    )


def solution(mesh):
    in_specs = (
        P("fsdp", "ctx", None),
        P("fsdp", None),
        P("fsdp", None),
        P("fsdp"),
        P("fsdp", None),
        P("fsdp", None),
        P("fsdp"),
        P("fsdp", None),
        P("fsdp", None),
        P("fsdp", "ctx", None),
    )
    out_specs = (
        P("fsdp", "ctx", None),
        P("fsdp", "ctx", None),
        P("fsdp"),
        P("fsdp", None),
        P("fsdp", None),
        P("fsdp"),
        P("fsdp", None),
        P("fsdp", None),
    )

    def run(*arrays):
        return per_device(mesh.shape["ctx"], mesh.shape["fsdp"], *arrays)

    return jax.shard_map(run, mesh=mesh, in_specs=in_specs, out_specs=out_specs, check_vma=False)
```

```python
import functools

import jax
import jax.numpy as jnp
from jax import lax
from jax.experimental import pallas as pl
from jax.experimental.pallas import tpu as pltpu
from jax.sharding import PartitionSpec as P

H = 12
HD = 128
FF = 4608
WINDOW = 1024
ROUNDS = 4
LANES = 128


EPS = 1e-06


def rms_norm(values, gain):
    return values * lax.rsqrt(jnp.mean(values * values, axis=-1, keepdims=True) + EPS) * gain


def geglu(gate, up):
    return jax.nn.gelu(gate, approximate=True) * up


def dot(left, right):
    return jnp.dot(left, right, preferred_element_type=jnp.float32)


def dot_nt(left, right):
    return jnp.einsum("ab,cb->ac", left, right, preferred_element_type=jnp.float32)


def dot_tn(left, right):
    return jnp.einsum("ab,ac->bc", left, right, preferred_element_type=jnp.float32)


def nt_dot(left, right):
    return lax.dot_general(left, right, (((1,), (1,)), ((), ())), preferred_element_type=jnp.float32)


def tn_dot(left, right):
    return lax.dot_general(left, right, (((0,), (0,)), ((), ())), preferred_element_type=jnp.float32)


def low(values):
    return values.astype(jnp.bfloat16)


VMEM_LIMIT = 56 * 1024 * 1024
MLP_VMEM = 62 * 1024 * 1024

def gain_row(ref, which):
    parts = [ref[shard, which : which + 1, :] for shard in range(ref.shape[0])]
    return jnp.concatenate(parts, axis=1)


def norm_scale(values):
    return lax.rsqrt(jnp.mean(values * values, axis=-1, keepdims=True) + EPS)


def norm_back(values, gain, incoming):
    scale = norm_scale(values)
    weighted = incoming * gain
    inner = jnp.mean(weighted * values, axis=-1, keepdims=True)
    grad = scale * weighted - values * (scale * scale * scale * inner)
    return grad, jnp.sum(incoming * values * scale, axis=0, keepdims=True)


def project_kernel(heads, x_ref, gain_ref, w_ref, cos_ref, sin_ref, normed_ref, q_ref, kv_ref):
    step = pl.program_id(0)

    @pl.when(step == 0)
    def _():
        x = x_ref[...].astype(jnp.float32)
        normed_ref[...] = (x * norm_scale(x) * gain_row(gain_ref, 0)).astype(jnp.bfloat16)

    part = jnp.dot(normed_ref[...], w_ref[...], preferred_element_type=jnp.float32)
    cosine, sine_part = cos_ref[...], sin_ref[...]

    def turn(value):
        return value * cosine + pltpu.roll(value, HD // 2, 1) * sine_part

    @pl.when(step < heads // 2)
    def _():
        for j in range(2):
            q_ref[j] = (turn(part[:, j * HD : (j + 1) * HD]) * HD ** (-0.5)).astype(jnp.bfloat16)

    @pl.when(step == heads // 2)
    def _():
        kv_ref[:, :HD] = turn(part[:, :HD]).astype(jnp.bfloat16)
        kv_ref[:, HD:] = part[:, HD:].astype(jnp.bfloat16)


def project(x, gain, w, cosine, sine_part):
    rows, width = x.shape
    steps = H // 2 + 1
    whole = lambda *shape: pl.BlockSpec(shape, lambda i: (0,) * len(shape))
    return pl.pallas_call(
        functools.partial(project_kernel, H),
        grid=(steps,),
        name="project",
        in_specs=[
            whole(rows, width),
            whole(*gain.shape),
            pl.BlockSpec((width, 2 * HD), lambda i: (0, i)),
            whole(rows, HD),
            whole(rows, HD),
        ],
        out_specs=[
            whole(rows, width),
            pl.BlockSpec((2, rows, HD), lambda i: (jnp.minimum(i, H // 2 - 1), 0, 0)),
            whole(rows, 2 * HD),
        ],
        out_shape=[
            jax.ShapeDtypeStruct((rows, width), jnp.bfloat16),
            jax.ShapeDtypeStruct((H, rows, HD), jnp.bfloat16),
            jax.ShapeDtypeStruct((rows, 2 * HD), jnp.bfloat16),
        ],
        compiler_params=pltpu.CompilerParams(vmem_limit_bytes=VMEM_LIMIT),
    )(x, gain, w, cosine, sine_part)


HEADS_STEP = 4


def attend_kernel(blocks, block, where_ref, q_ref, kv_ref, key_place_ref, bounds_ref, out_ref, window, bias):
    r = pl.program_id(0)

    @pl.when(pl.program_id(1) == 0)
    def _():
        for j in range(blocks):
            window[j * block : (j + 1) * block, :] = kv_ref[where_ref[r, j]]
        key_place = key_place_ref[0]
        allowed = (key_place <= bounds_ref[:, :1]) & (key_place >= bounds_ref[:, 1:])
        bias[...] = jnp.where(allowed, 0.0, -1e30)

    queries = q_ref[...].reshape(HEADS_STEP * block, HD)
    scores = lax.dot_general(
        queries, window[:, :HD], (((1,), (1,)), ((), ())), preferred_element_type=jnp.float32
    )
    scores = scores.reshape(HEADS_STEP, block, blocks * block) + bias[...][None]
    peak = jnp.max(scores, axis=-1, keepdims=True)
    weights = jnp.exp(scores - peak)
    total = jnp.sum(weights, axis=-1, keepdims=True).reshape(HEADS_STEP * block, 1)
    weights = weights.astype(jnp.bfloat16).reshape(HEADS_STEP * block, blocks * block)
    mixed = jnp.dot(weights, window[:, HD:], preferred_element_type=jnp.float32) / total
    mixed = mixed.astype(jnp.bfloat16)
    for j in range(HEADS_STEP):
        out_ref[:, j * HD : (j + 1) * HD] = mixed[j * block : (j + 1) * block]


def attend(where, queries, kv_blocks, key_place, bounds):
    rounds, blocks = where.shape[0], where.shape[1] // 2
    heads, rows, _ = queries.shape
    block = rows // rounds
    span = blocks * block
    grid_spec = pltpu.PrefetchScalarGridSpec(
        num_scalar_prefetch=1,
        grid=(rounds, heads // HEADS_STEP),
        in_specs=[
            pl.BlockSpec((HEADS_STEP, block, HD), lambda r, h, *_: (h, r, 0)),
            pl.BlockSpec(kv_blocks.shape, lambda r, h, *_: (0, 0, 0)),
            pl.BlockSpec((1, 1, span), lambda r, h, *_: (r, 0, 0)),
            pl.BlockSpec((block, 2), lambda r, h, *_: (r, 0)),
        ],
        out_specs=pl.BlockSpec((block, HEADS_STEP * HD), lambda r, h, *_: (r, h)),
        scratch_shapes=[
            pltpu.VMEM((span, 2 * HD), jnp.bfloat16),
            pltpu.VMEM((block, span), jnp.float32),
        ],
    )
    return pl.pallas_call(
        functools.partial(attend_kernel, blocks, block),
        name="attend",
        grid_spec=grid_spec,
        out_shape=jax.ShapeDtypeStruct((rows, heads * HD), jnp.bfloat16),
        compiler_params=pltpu.CompilerParams(vmem_limit_bytes=VMEM_LIMIT),
    )(where, queries, kv_blocks, key_place, bounds)


def attend_back_kernel(
    blocks, block, where_ref, q_ref, kv_ref, grad_ref, key_place_ref, bounds_ref, cos_ref, sin_ref,
    grad_q_ref, grad_kv_ref, window, bias, window_grad, total_grad,
):
    r, h = pl.program_id(0), pl.program_id(1)
    last = pl.num_programs(1) - 1

    @pl.when((r == 0) & (h == 0))
    def _():
        total_grad[...] = jnp.zeros_like(total_grad)

    @pl.when(h == 0)
    def _():
        for j in range(blocks):
            window[j * block : (j + 1) * block, :] = kv_ref[where_ref[r, j]]
        key_place = jnp.broadcast_to(key_place_ref[0], (8, blocks * block)).T[:, :1]
        allowed = (key_place <= bounds_ref[0, :1, :]) & (key_place >= bounds_ref[0, 1:, :])
        bias[...] = jnp.where(allowed, 0.0, -1e30)
        window_grad[...] = jnp.zeros_like(window_grad)

    queries = q_ref[...].reshape(HEADS_STEP * block, HD)
    grads = jnp.concatenate([grad_ref[:, j * HD : (j + 1) * HD] for j in range(HEADS_STEP)], axis=0)
    keys, values = window[:, :HD], window[:, HD:]
    nt = (((1,), (1,)), ((), ()))
    tn = (((0,), (0,)), ((), ()))
    scores = lax.dot_general(keys, queries, nt, preferred_element_type=jnp.float32) + bias[...]
    peak = jnp.max(scores, axis=0, keepdims=True)
    weights = jnp.exp(scores - peak)
    probs = weights * (1.0 / jnp.sum(weights, axis=0, keepdims=True))
    grad_probs = lax.dot_general(values, grads, nt, preferred_element_type=jnp.float32)
    delta = jnp.sum(probs * grad_probs, axis=0, keepdims=True)
    grad_scores = (probs * (grad_probs - delta)).astype(jnp.bfloat16)
    window_grad[:, :HD] += jnp.dot(grad_scores, queries, preferred_element_type=jnp.float32)
    window_grad[:, HD:] += jnp.dot(
        probs.astype(jnp.bfloat16), grads, preferred_element_type=jnp.float32
    )
    grad_q = lax.dot_general(grad_scores, keys, tn, preferred_element_type=jnp.float32)
    cosine, sine_part = cos_ref[...], sin_ref[...]
    for j in range(HEADS_STEP):
        one = grad_q[j * block : (j + 1) * block]
        one = (one * cosine - pltpu.roll(one, HD // 2, 1) * sine_part) * HD ** (-0.5)
        grad_q_ref[:, j * HD : (j + 1) * HD] = one.astype(jnp.bfloat16)

    @pl.when(h == last)
    def _():
        for j in range(blocks):
            total_grad[where_ref[r, blocks + j]] += window_grad[j * block : (j + 1) * block, :]

    @pl.when((h == last) & (r == pl.num_programs(0) - 1))
    def _():
        grad_kv_ref[...] = total_grad[...].astype(jnp.bfloat16)


def attend_back(where, queries, kv_blocks, grads, key_place, bounds, cosine, sine_part):
    rounds, blocks = where.shape[0], where.shape[1] // 2
    heads, rows, _ = queries.shape
    block = rows // rounds
    span = blocks * block
    width = HEADS_STEP * block
    grid_spec = pltpu.PrefetchScalarGridSpec(
        num_scalar_prefetch=1,
        grid=(rounds, heads // HEADS_STEP),
        in_specs=[
            pl.BlockSpec((HEADS_STEP, block, HD), lambda r, h, *_: (h, r, 0)),
            pl.BlockSpec(kv_blocks.shape, lambda r, h, *_: (0, 0, 0)),
            pl.BlockSpec((block, HEADS_STEP * HD), lambda r, h, *_: (r, h)),
            pl.BlockSpec((1, 1, span), lambda r, h, *_: (r, 0, 0)),
            pl.BlockSpec((1, 2, width), lambda r, h, *_: (r, 0, 0)),
            pl.BlockSpec((block, HD), lambda r, h, *_: (r, 0)),
            pl.BlockSpec((block, HD), lambda r, h, *_: (r, 0)),
        ],
        out_specs=[
            pl.BlockSpec((block, HEADS_STEP * HD), lambda r, h, *_: (r, h)),
            pl.BlockSpec(kv_blocks.shape, lambda r, h, *_: (0, 0, 0)),
        ],
        scratch_shapes=[
            pltpu.VMEM((span, 2 * HD), jnp.bfloat16),
            pltpu.VMEM((span, width), jnp.float32),
            pltpu.VMEM((span, 2 * HD), jnp.float32),
            pltpu.VMEM(kv_blocks.shape, jnp.float32),
        ],
    )
    return pl.pallas_call(
        functools.partial(attend_back_kernel, blocks, block),
        name="attend_back",
        grid_spec=grid_spec,
        out_shape=[
            jax.ShapeDtypeStruct((rows, heads * HD), jnp.bfloat16),
            jax.ShapeDtypeStruct(kv_blocks.shape, jnp.bfloat16),
        ],
        compiler_params=pltpu.CompilerParams(vmem_limit_bytes=VMEM_LIMIT),
    )(where, queries, kv_blocks, grads, key_place, bounds, cosine, sine_part)


ANY = pl.BlockSpec(memory_space=pl.ANY)
MIDDLE_TILES = 3


def whole_block(shape):
    return pl.BlockSpec(shape, lambda i: (0,) * len(shape))


def middle_kernel(x_ref, mixed_ref, gain_ref, w_ref, middle_ref, normed_ref):
    step = pl.program_id(0)
    tile = w_ref.shape[1]
    columns = pl.ds(pl.multiple_of(step * tile, tile), tile)
    middle_ref[:, columns] = x_ref[:, columns].astype(jnp.float32) + dot(mixed_ref[...], w_ref[...])

    @pl.when(step == pl.num_programs(0) - 1)
    def _():
        values = middle_ref[...]
        normed_ref[...] = low(values * norm_scale(values) * gain_row(gain_ref, 1))


def middle_forward(x, mixed, gains, w):
    rows, width = x.shape
    inner = mixed.shape[1]
    return pl.pallas_call(
        middle_kernel,
        name="middle",
        grid=(MIDDLE_TILES,),
        in_specs=[
            whole_block((rows, width)),
            whole_block((rows, inner)),
            whole_block(gains.shape),
            pl.BlockSpec((inner, width // MIDDLE_TILES), lambda i: (0, i)),
        ],
        out_specs=[whole_block((rows, width))] * 2,
        out_shape=[
            jax.ShapeDtypeStruct((rows, width), jnp.float32),
            jax.ShapeDtypeStruct((rows, width), jnp.bfloat16),
        ],
        compiler_params=pltpu.CompilerParams(vmem_limit_bytes=VMEM_LIMIT),
    )(x, mixed, gains, w)


def middle_back_kernel(
    grad_ref, middle_ref, upstream_ref, mixed_ref, gain_ref, w_ref,
    grad_middle_ref, grad_mixed_ref, grad_w_ref, grad_gain_ref, token, branch,
):
    @pl.when(pl.program_id(0) == 0)
    def _():
        grad, grad_gain = norm_back(middle_ref[...], gain_row(gain_ref, 1), grad_ref[...])
        total = upstream_ref[...].astype(jnp.float32) + grad
        grad_middle_ref[...] = total
        branch[...] = low(total)
        grad_gain_ref[...] = grad_gain
        token[...] = jnp.zeros_like(token)

    grad_mixed_ref[...] = low(nt_dot(branch[...], w_ref[...]))
    grad_w_ref[...] = low(tn_dot(mixed_ref[...], branch[...]))


def middle_back(grad, middle, upstream, mixed, gains, w):
    rows, width = middle.shape
    inner = mixed.shape[1]
    tile = inner // MIDDLE_TILES
    return pl.pallas_call(
        middle_back_kernel,
        name="middle_back",
        grid=(MIDDLE_TILES,),
        in_specs=[
            whole_block((rows, width)),
            whole_block((rows, width)),
            whole_block((rows, width)),
            pl.BlockSpec((rows, tile), lambda i: (0, i)),
            whole_block(gains.shape),
            pl.BlockSpec((tile, width), lambda i: (i, 0)),
        ],
        out_specs=[
            whole_block((rows, width)),
            pl.BlockSpec((rows, tile), lambda i: (0, i)),
            pl.BlockSpec((tile, width), lambda i: (i, 0)),
            whole_block((1, width)),
            whole_block(TOKEN),
        ],
        out_shape=[
            jax.ShapeDtypeStruct((rows, width), jnp.float32),
            jax.ShapeDtypeStruct((rows, inner), jnp.bfloat16),
            jax.ShapeDtypeStruct((inner, width), jnp.bfloat16),
            jax.ShapeDtypeStruct((1, width), jnp.float32),
            token_shape(),
        ],
        scratch_shapes=[pltpu.VMEM((rows, width), jnp.bfloat16)],
        compiler_params=pltpu.CompilerParams(vmem_limit_bytes=VMEM_LIMIT),
    )(grad, middle, upstream, mixed, gains, w)


def project_back_kernel(
    grad_q_ref, grad_kv_ref, cos_ref, sin_ref, normed_ref, x_ref, grad_middle_ref, gain_ref, w_ref,
    grad_w_ref, grad_x_ref, grad_gain_ref, joined, grad_normed,
):
    step = pl.program_id(0)
    inner = grad_q_ref.shape[1]
    tile = w_ref.shape[0]

    @pl.when(step == 0)
    def _():
        joined[:, :inner] = grad_q_ref[...]
        keys = grad_kv_ref[:, :HD]
        keys = keys * cos_ref[...] - pltpu.roll(keys, HD // 2, 1) * sin_ref[...]
        joined[:, inner : inner + HD] = low(keys)
        joined[:, inner + HD :] = low(grad_kv_ref[:, HD:])

    columns = pl.ds(pl.multiple_of(step * tile, tile), tile)
    grad_normed[:, columns] = nt_dot(joined[...], w_ref[...])
    grad_w_ref[...] = low(tn_dot(normed_ref[...], joined[...]))

    @pl.when(step == pl.num_programs(0) - 1)
    def _():
        values = x_ref[...].astype(jnp.float32)
        grad, grad_gain = norm_back(values, gain_row(gain_ref, 0), grad_normed[...])
        grad_x_ref[...] = grad_middle_ref[...] + grad
        grad_gain_ref[...] = grad_gain


def project_back(grad_q, grad_kv, cosine, sine_part, normed, x, grad_middle, gains, w):
    rows, width = x.shape
    inner = w.shape[1]
    tile = width // MIDDLE_TILES
    return pl.pallas_call(
        project_back_kernel,
        name="project_back",
        grid=(MIDDLE_TILES,),
        in_specs=[
            whole_block(grad_q.shape),
            whole_block(grad_kv.shape),
            whole_block(cosine.shape),
            whole_block(cosine.shape),
            pl.BlockSpec((rows, tile), lambda i: (0, i)),
            whole_block((rows, width)),
            whole_block((rows, width)),
            whole_block(gains.shape),
            pl.BlockSpec((tile, inner), lambda i: (i, 0)),
        ],
        out_specs=[
            pl.BlockSpec((tile, inner), lambda i: (i, 0)),
            whole_block((rows, width)),
            whole_block((1, width)),
        ],
        out_shape=[
            jax.ShapeDtypeStruct((width, inner), jnp.bfloat16),
            jax.ShapeDtypeStruct((rows, width), jnp.float32),
            jax.ShapeDtypeStruct((1, width), jnp.float32),
        ],
        scratch_shapes=[
            pltpu.VMEM((rows, inner), jnp.bfloat16),
            pltpu.VMEM((rows, width), jnp.float32),
        ],
        compiler_params=pltpu.CompilerParams(vmem_limit_bytes=VMEM_LIMIT),
    )(grad_q, grad_kv, cosine, sine_part, normed, x, grad_middle, gains, w)


MESH_ID = pl.DeviceIdType.MESH


class Wire:
    def __init__(self, send_sems, recv_sems):
        self.send_sems = send_sems
        self.recv_sems = recv_sems
        self.count = 0
        self.open = []
        self.ctx = lax.axis_index("ctx")
        self.shard = lax.axis_index("fsdp")

    def other(self, mask):
        at = self.ctx
        for bit in (1, 2, 4):
            if mask & bit:
                at = at + bit - 2 * bit * lax.rem(at // bit, 2)
        return at

    def plane(self, mask):
        return (self.other(mask), self.shard)

    def line(self, step, shards):
        return (self.ctx, lax.rem(self.shard + step, shards))

    def meet(self, peers):
        barrier = pltpu.get_barrier_semaphore()
        for peer in peers:
            pl.semaphore_signal(barrier, inc=1, device_id=peer, device_id_type=MESH_ID)
        pl.semaphore_wait(barrier, len(peers))

    def send(self, source, target, peer):
        at = self.count
        self.count += 1
        copy = pltpu.make_async_remote_copy(
            src_ref=source,
            dst_ref=target,
            send_sem=self.send_sems.at[at],
            recv_sem=self.recv_sems.at[at],
            device_id=peer,
            device_id_type=MESH_ID,
        )
        copy.start()
        self.open.append(copy)
        return copy

    def sent(self, copy):
        copy.wait_send()
        self.open = [one for one in self.open if one is not copy]

    def finish(self):
        for copy in self.open:
            copy.wait_send()


class PlaneGather:
    COPIES = 9

    def __init__(self, wire, source, out_at, rows, split):
        self.wire, self.out_at, self.rows, self.split = wire, out_at, rows, split
        ctx = wire.ctx
        self.core = wire.send(source, out_at(ctx), wire.plane(1))
        self.x = wire.send(source, out_at(ctx), wire.plane(2))
        self.y = wire.send(source, out_at(ctx), wire.plane(4))

    def forward(self):
        wire, split = self.wire, self.split
        rest = self.rows - split
        self.x.wait_recv()
        block = self.out_at(wire.other(2))
        part = block.at[pl.ds(0, split)]
        self.corner_y = wire.send(part, part, wire.plane(4))
        self.core_x = wire.send(block, block, wire.plane(1))
        self.y.wait_recv()
        block = self.out_at(wire.other(4))
        part = block.at[pl.ds(split, rest)]
        self.corner_x = wire.send(part, part, wire.plane(2))
        self.core_y = wire.send(block, block, wire.plane(1))

    def corner(self):
        self.corner_y.wait_recv()
        self.corner_x.wait_recv()
        block = self.out_at(self.wire.other(6))
        self.core_corner = self.wire.send(block, block, self.wire.plane(1))

    def settle(self):
        self.core.wait_recv()
        self.core_x.wait_recv()
        self.core_y.wait_recv()
        self.core_corner.wait_recv()


def half_rows(rows, turn):
    low_half = rows // 32 * 16
    return low_half if turn % 2 else rows - low_half


def add_low(first, second):
    return (first.astype(jnp.float32) + second.astype(jnp.float32)).astype(jnp.bfloat16)


class PlaneSum:
    COPIES = 7

    def __init__(self, wire, source, own, pair, first, second, local_sem):
        self.wire, self.own, self.pair, self.first, self.second = wire, own, pair, first, second
        core = lax.rem(wire.ctx, 2)
        self.chips = {mask: wire.other(2 * mask) // 2 for mask in range(4)}
        self.swap = wire.send(source.at[:, :, 1 - core], pair, wire.plane(1))
        self.local = pltpu.make_async_copy(source.at[:, :, core], own, local_sem)
        self.local.start()

    def step_one(self):
        wire, own, pair, first, chips = self.wire, self.own, self.pair, self.first, self.chips
        self.local.wait()
        self.swap.wait_recv()

        def add_pair(index, carry):
            part, other = index // 4, lax.rem(index, 4)
            own[part, other] = add_low(own[part, other], pair[part, other])
            return carry

        lax.fori_loop(0, 16, add_pair, 0)
        low, high = pl.ds(0, 2), pl.ds(2, 2)
        self.one = [
            wire.send(own.at[low, chips[3]], first.at[0, 1], wire.plane(2)),
            wire.send(own.at[high, chips[3]], first.at[1, 1], wire.plane(4)),
            wire.send(own.at[low, chips[1]], first.at[0, 0], wire.plane(2)),
            wire.send(own.at[high, chips[2]], first.at[1, 0], wire.plane(4)),
        ]

    def step_two(self):
        wire, own, first, second, chips = self.wire, self.own, self.first, self.second, self.chips
        self.one[0].wait_recv()
        for part in range(2):
            own[part, chips[2]] = add_low(own[part, chips[2]], first[0, 1, part])
        self.two = [wire.send(own.at[pl.ds(0, 2), chips[2]], second.at[pl.ds(0, 2)], wire.plane(4))]
        self.one[1].wait_recv()
        for part in range(2):
            own[part + 2, chips[1]] = add_low(own[part + 2, chips[1]], first[1, 1, part])
        self.two.append(
            wire.send(own.at[pl.ds(2, 2), chips[1]], second.at[pl.ds(2, 2)], wire.plane(2))
        )

    def result(self, store):
        own, first, second, chips = self.own, self.first, self.second, self.chips
        for copy in self.one[2:] + self.two:
            copy.wait_recv()
        for part in range(4):
            total = own[part, chips[0]].astype(jnp.float32)
            total += first[part // 2, 0, part % 2].astype(jnp.float32)
            total += second[part].astype(jnp.float32)
            store(part, total)


def plane_sum_scratch(rows, columns):
    shape = lambda *lead: pltpu.VMEM(lead + (rows, columns), jnp.bfloat16)
    return [shape(4, 4), shape(4, 4), shape(2, 2, 2), shape(4)]


def dma_sems(count):
    return pltpu.SemaphoreType.DMA((count,))


PLANE_PEERS = (1, 2, 4)


def comm_params(number):
    return pltpu.CompilerParams(
        collective_id=number, has_side_effects=True, vmem_limit_bytes=VMEM_LIMIT
    )


class Relay:
    def __init__(self, source, stage, targets, sems):
        self.stage, self.targets, self.sems = stage, targets, sems
        self.load = pltpu.make_async_copy(source, stage, sems.at[0])
        self.load.start()

    def push(self):
        self.load.wait()
        self.stores = []
        for i, (part, target) in enumerate(self.targets):
            store = pltpu.make_async_copy(part, target, self.sems.at[1 + i])
            store.start()
            self.stores.append(store)

    def settle(self):
        for store in self.stores:
            store.wait()


TOKEN = (8, 128)


def token_shape():
    return jax.ShapeDtypeStruct(TOKEN, jnp.int32)


def after(token, values):
    return jnp.where(token[0, 0] != 0, jnp.zeros_like(values), values)


def share_line_kernel(
    shards, pack, in_ref, gain_a, gain_b, mlp_in, mlp_out, in_line, gain_all, mine, token,
    gain_now, in_stage, packed, tiles, local_sems, load_sems, send_sems, recv_sems,
):
    wire = Wire(send_sems, recv_sems)
    ctx, shard = wire.ctx, wire.shard
    chip, core = ctx // 2, lax.rem(ctx, 2)
    chips = pack.chips
    relay = Relay(in_ref.at[ctx], in_stage, [(in_stage, in_line.at[shard])], local_sems.at[0])
    gain_now[...] = jnp.zeros_like(gain_now)
    gain_now[:1] = gain_a[...].astype(jnp.float32)
    gain_now[1:2] = gain_b[...].astype(jnp.float32)
    token[...] = jnp.zeros_like(token)
    wire.meet([wire.line(step, shards) for step in range(1, shards)])
    copies = []
    for source, target in ((gain_now, gain_all), (in_ref.at[ctx], in_line)):
        for step in range(1, shards):
            copies.append(wire.send(source, target.at[shard], wire.line(step, shards)))
    gain_copy = pltpu.make_async_copy(gain_now, gain_all.at[shard], local_sems.at[1, 0])
    gain_copy.start()
    relay.push()

    loads = []

    def load(source, target):
        copy = pltpu.make_async_copy(source, target, load_sems.at[len(loads)])
        copy.start()
        loads.append(copy)

    def strip(start, count):
        return pl.ds(pl.multiple_of(start, LANES), count)

    main, rest, half, tail, split = pack.main, pack.rest, pack.half, pack.tail, pack.split
    per_shard = chips * (main + rest)
    base = core * (shards * per_shard)
    for part in range(shards):
        start = base + part * per_shard
        load(mlp_in.at[:, strip(start + chips * main, chips * rest)], tiles.at[part])
        column = part * main
        if column + main <= half:
            source = mlp_in.at[:, strip(start + chip * main, main)]
            load(source, packed.at[pl.ds(0, pack.rows), pl.ds(column, main)])
            continue
        for i, at in enumerate(range(0, pack.rows, split)):
            source = mlp_in.at[pl.ds(at, split), strip(start + chip * main, main)]
            load(source, packed.at[pl.ds(pack.rows, split), pl.ds(i * tail + column - half, main)])
    columns = strip(core * half, half)
    for start, count, row in (
        (chip * main, main, pack.out_start),
        (chips * main + chip * rest, rest, pack.out_start + main),
    ):
        source = mlp_out.at[pl.ds(pl.multiple_of(start, 16), count), columns]
        load(source, packed.at[pl.ds(row, count), :])
    for copy in loads:
        copy.wait()
    width = chips * rest
    ends = [
        pltpu.roll(tiles[part].astype(jnp.float32), lax.rem(width - chip * rest, width), 1)[:, :rest]
        for part in range(shards)
    ]
    ends = low(jnp.concatenate(ends, axis=1))
    for i, at in enumerate(range(0, pack.rows, split)):
        column = i * tail + shards * main - half
        packed[pack.rows : pack.rows + split, column : column + shards * rest] = ends[at : at + split]
    mine_copy = pltpu.make_async_copy(packed, mine, local_sems.at[1, 1])
    mine_copy.start()
    relay.settle()
    gain_copy.wait()
    mine_copy.wait()
    for copy in copies:
        copy.wait_recv()
    wire.finish()


def gather_shards(wire, line, target, rows, shards, count):
    gathers = []
    for step in range(1, shards):
        origin = lax.rem(wire.shard + shards - step, shards)
        place = lambda who, origin=origin: target.at[origin, who]
        gathers.append(PlaneGather(wire, line.at[origin], place, rows, half_rows(rows, step + count)))
    return gathers


def relay_shards(wire, whole, line, target, stage, piece, shards, sems):
    origins = [lax.rem(wire.shard + shards - step, shards) for step in range(1, shards)]
    places = [(piece.at[origin], target.at[origin, wire.ctx]) for origin in origins]
    return [
        Relay(whole, stage, [(stage, target.at[wire.shard])], sems.at[0]),
        Relay(line, piece, places, sems.at[1]),
    ]


def complete(gathers, relays):
    for relay in relays:
        relay.push()
    for gather in gathers:
        gather.forward()
    for gather in gathers:
        gather.corner()
    for gather in gathers:
        gather.settle()
    for relay in relays:
        relay.settle()


def share_plane_kernel(
    shards, in_ref, in_line, out_ref, in_all, out_line, token,
    in_stage, in_piece, out_stage, local_sems, send_sems, recv_sems,
):
    wire = Wire(send_sems, recv_sems)
    ctx, shard = wire.ctx, wire.shard
    relays = relay_shards(wire, in_ref, in_line, in_all, in_stage, in_piece, shards, local_sems)
    relays.append(
        Relay(out_ref.at[ctx], out_stage, [(out_stage, out_line.at[shard])], local_sems.at[2])
    )
    token[...] = jnp.zeros_like(token)
    wire.meet(
        [wire.plane(mask) for mask in PLANE_PEERS] + [wire.line(s, shards) for s in range(1, shards)]
    )
    gathers = gather_shards(wire, in_line, in_all, in_ref.shape[1], shards, 0)
    copies = [
        wire.send(out_ref.at[ctx], out_line.at[shard], wire.line(step, shards))
        for step in range(1, shards)
    ]
    complete(gathers, relays)
    for copy in copies:
        copy.wait_recv()
    wire.finish()


def gather_plane_kernel(
    shards, kv_ref, out_ref, out_line, kv_all, out_all, token,
    kv_stage, out_stage, out_piece, local_sems, send_sems, recv_sems,
):
    wire = Wire(send_sems, recv_sems)
    ctx = wire.ctx
    relays = relay_shards(wire, out_ref, out_line, out_all, out_stage, out_piece, shards, local_sems)
    relays.append(Relay(kv_ref, kv_stage, [(kv_stage, kv_all.at[ctx])], local_sems.at[2]))
    token[...] = jnp.zeros_like(token)
    wire.meet([wire.plane(mask) for mask in PLANE_PEERS])
    rows = kv_ref.shape[0]
    gathers = [PlaneGather(wire, kv_ref, lambda who: kv_all.at[who], rows, rows // 2)]
    gathers += gather_shards(wire, out_line, out_all, out_ref.shape[1], shards, 1)
    complete(gathers, relays)
    wire.finish()


def like(values, *lead):
    return jax.ShapeDtypeStruct(lead + values.shape[-2:], values.dtype)


def stage_like(values, *lead):
    return pltpu.VMEM(lead + values.shape[-2:], values.dtype)


def share_line(w_in, gain_a, gain_b, mlp_in, mlp_out, pack, shards):
    columns = gain_a.shape[1]
    copies = 2 * (shards - 1)
    loads = shards + shards + 1 + 2
    return pl.pallas_call(
        functools.partial(share_line_kernel, shards, pack),
        name="share_line",
        in_specs=[ANY] + [pl.BlockSpec(memory_space=pltpu.VMEM)] * 2 + [ANY] * 2,
        out_specs=[ANY] * 3 + [pl.BlockSpec(memory_space=pltpu.VMEM)],
        out_shape=[
            like(w_in, shards),
            jax.ShapeDtypeStruct((shards, 8, columns), jnp.float32),
            jax.ShapeDtypeStruct((pack.total, pack.half), mlp_in.dtype),
            token_shape(),
        ],
        scratch_shapes=[
            pltpu.VMEM((8, columns), jnp.float32),
            stage_like(w_in),
            pltpu.VMEM((pack.total, pack.half), mlp_in.dtype),
            pltpu.VMEM((shards, pack.rows, pack.chips * pack.rest), mlp_in.dtype),
            pltpu.SemaphoreType.DMA((2, 2)),
            dma_sems(loads),
            dma_sems(copies),
            dma_sems(copies),
        ],
        compiler_params=comm_params(1),
    )(w_in, gain_a, gain_b, mlp_in, mlp_out)


def share_plane(w_in, in_line, w_out, ctx_size, shards):
    copies = (shards - 1) * (PlaneGather.COPIES + 1)
    return pl.pallas_call(
        functools.partial(share_plane_kernel, shards),
        name="share_plane",
        in_specs=[ANY] * 3,
        out_specs=[ANY] * 2 + [pl.BlockSpec(memory_space=pltpu.VMEM)],
        out_shape=[like(w_in, shards, ctx_size), like(w_out, shards), token_shape()],
        scratch_shapes=[
            stage_like(w_in, ctx_size),
            stage_like(w_in, shards),
            stage_like(w_out),
            pltpu.SemaphoreType.DMA((3, shards)),
            dma_sems(copies),
            dma_sems(copies),
        ],
        compiler_params=comm_params(6),
    )(w_in, in_line, w_out)


def gather_plane(key_value, w_out, out_line, ctx_size, shards):
    copies = shards * PlaneGather.COPIES
    return pl.pallas_call(
        functools.partial(gather_plane_kernel, shards),
        name="gather_plane",
        in_specs=[ANY] * 3,
        out_specs=[ANY] * 2 + [pl.BlockSpec(memory_space=pltpu.VMEM)],
        out_shape=[like(key_value, ctx_size), like(w_out, shards, ctx_size), token_shape()],
        scratch_shapes=[
            stage_like(key_value),
            stage_like(w_out, ctx_size),
            stage_like(w_out, shards),
            pltpu.SemaphoreType.DMA((3, shards)),
            dma_sems(copies),
            dma_sems(copies),
        ],
        compiler_params=comm_params(2),
    )(key_value, w_out, out_line)


def sum_plane_kernel(in_ref, out_ref, own, pair, first, second, local_sem, send_sems, recv_sems):
    wire = Wire(send_sems, recv_sems)
    wire.meet([wire.plane(mask) for mask in PLANE_PEERS])
    total = PlaneSum(wire, in_ref, own, pair, first, second, local_sem)
    total.step_one()
    total.step_two()

    def store(part, value):
        out_ref[part] = value

    total.result(store)
    wire.finish()


def sum_plane(values):
    rows, columns = values.shape[3:]
    return pl.pallas_call(
        sum_plane_kernel,
        name="sum_plane",
        in_specs=[ANY],
        out_specs=pl.BlockSpec(memory_space=pltpu.VMEM),
        out_shape=jax.ShapeDtypeStruct((4, rows, columns), jnp.float32),
        scratch_shapes=plane_sum_scratch(rows, columns)
        + [pltpu.SemaphoreType.DMA, dma_sems(PlaneSum.COPIES), dma_sems(PlaneSum.COPIES)],
        compiler_params=comm_params(3),
    )(values)


def close_kernel(
    shards, g_out, g_in, m_ref, gain_a, gain_b, out_all, in_all, m_all, gain_out,
    *scratch,
):
    sums = (scratch[:4], scratch[4:8])
    mine, arrived = (scratch[8], scratch[9]), (scratch[10], scratch[11])
    done = (scratch[12], scratch[13])
    gain_now, gain_in, gain_line, stage = scratch[14:18]
    local_sems, relay_sems, send_sems, recv_sems = scratch[18:]
    wire = Wire(send_sems, recv_sems)
    ctx, shard = wire.ctx, wire.shard
    wire.meet(
        [wire.plane(mask) for mask in PLANE_PEERS] + [wire.line(s, shards) for s in range(1, shards)]
    )
    totals = [
        PlaneSum(wire, source, *sums[i], local_sems.at[i]) for i, source in enumerate((g_out, g_in))
    ]
    relay = Relay(m_ref, stage, [(stage, m_all.at[ctx])], relay_sems)
    gain_now[...] = jnp.zeros_like(gain_now)
    columns = gain_now.shape[2]
    for part in range(shards):
        span = slice(part * columns, (part + 1) * columns)
        gain_now[part, :1] = gain_a[:, span]
        gain_now[part, 1:2] = gain_b[:, span]

    def gain_start(at):
        return wire.send(gain_now, gain_in.at[at], wire.plane(PLANE_PEERS[at]))

    def gain_add(at, copy):
        copy.wait_recv()
        wire.sent(copy)
        gain_now[...] += gain_in[at]

    gain_copy = gain_start(0)
    for total in totals:
        total.step_one()
    gain_add(0, gain_copy)
    gain_copy = gain_start(1)
    for total in totals:
        total.step_two()
    gain_add(1, gain_copy)
    gain_copy = gain_start(2)
    place = lambda who: m_all.at[who]
    rows = m_ref.shape[0]
    gathers, locals_ = [PlaneGather(wire, m_ref, place, rows, rows // 2)], []
    relay.push()
    lines = []
    for i, total in enumerate(totals):

        def store(part, value, i=i):
            mine[i][part] = value.astype(jnp.bfloat16)

        total.result(store)
        lines.append(
            [
                wire.send(
                    mine[i].at[lax.rem(shard + step, shards)],
                    arrived[i].at[step - 1],
                    wire.line(step, shards),
                )
                for step in range(1, shards)
            ]
        )
    gain_add(2, gain_copy)
    gain_copies = [
        wire.send(
            gain_now.at[lax.rem(shard + step, shards)], gain_line.at[step - 1], wire.line(step, shards)
        )
        for step in range(1, shards)
    ]
    small = []
    for i, target in enumerate((out_all, in_all)):
        for copy in lines[i]:
            copy.wait_recv()
        value = mine[i][shard].astype(jnp.float32)
        for step in range(shards - 1):
            value += arrived[i][step].astype(jnp.float32)
        done[i][...] = value.astype(jnp.bfloat16)
        place = lambda who, target=target: target.at[who]
        rows = target.shape[1]
        small.append(PlaneGather(wire, done[i], place, rows, half_rows(rows, i)))
        copy = pltpu.make_async_copy(done[i], place(ctx), local_sems.at[2 + i])
        copy.start()
        locals_.append(copy)
    for copy in gain_copies:
        copy.wait_recv()
    value = gain_now[shard]
    for step in range(shards - 1):
        value += gain_line[step]
    gain_out[...] = value
    for gather in gathers + small:
        gather.forward()
    for gather in gathers + small:
        gather.corner()
    for gather in gathers + small:
        gather.settle()
    for copy in locals_:
        copy.wait()
    relay.settle()
    wire.finish()


def close(g_out, g_in, m_part, gain_a, gain_b, ctx_size, shards):
    sums, mine, arrived, done = [], [], [], []
    for grad in (g_out, g_in):
        rows, columns = grad.shape[3:]
        sums += plane_sum_scratch(rows, columns)
        mine.append(pltpu.VMEM((shards, rows, columns), jnp.bfloat16))
        arrived.append(pltpu.VMEM((shards - 1, rows, columns), jnp.bfloat16))
        done.append(pltpu.VMEM((rows, columns), jnp.bfloat16))
    gain_shape = (shards, 8, gain_a.shape[1] // shards)
    rest = [
        pltpu.VMEM(gain_shape, jnp.float32),
        pltpu.VMEM((3,) + gain_shape, jnp.float32),
        pltpu.VMEM((shards - 1,) + gain_shape[1:], jnp.float32),
        pltpu.VMEM(m_part.shape, m_part.dtype),
        dma_sems(4),
        dma_sems(2),
    ]
    copies = 2 * (PlaneSum.COPIES + PlaneGather.COPIES + shards - 1) + PlaneGather.COPIES + 3 + shards - 1
    whole = lambda shape: jax.ShapeDtypeStruct((ctx_size,) + shape, jnp.bfloat16)
    vmem = pl.BlockSpec(memory_space=pltpu.VMEM)
    return pl.pallas_call(
        functools.partial(close_kernel, shards),
        name="close",
        in_specs=[ANY] * 3 + [vmem] * 2,
        out_specs=[ANY] * 3 + [vmem],
        out_shape=[
            whole(g_out.shape[3:]),
            whole(g_in.shape[3:]),
            whole(m_part.shape),
            jax.ShapeDtypeStruct(gain_shape[1:], jnp.float32),
        ],
        scratch_shapes=sums + mine + arrived + done + rest + [dma_sems(copies), dma_sems(copies)],
        compiler_params=comm_params(4),
    )(g_out, g_in, m_part, gain_a, gain_b)


class Pack:
    def __init__(self, rows, half, chips, units, main, rest):
        self.rows, self.half, self.chips, self.main, self.rest = rows, half, chips, main, rest
        self.tail = units - half
        self.split = rows // (half // self.tail)
        self.out_start = rows + self.split
        self.total = self.out_start + main + rest

    def in_spans(self, shard):
        yield (0, self.rows), (0, self.half), (shard * self.rows, self.rows), (0, self.half)
        for i, at in enumerate(range(0, self.rows, self.split)):
            yield (
                (self.rows, self.split),
                (i * self.tail, self.tail),
                (shard * self.rows + at, self.split),
                (self.half, self.tail),
            )

    def out_spans(self, shard, shards):
        yield (self.out_start, self.main), (shard * self.main, self.main)
        yield (self.out_start + self.main, self.rest), (shards * self.main + shard * self.rest, self.rest)


def finish_kernel(shards, chips, pack, step_rows, main_ref, tail_ref, out_part_ref, in_ref, out_ref):
    step = pl.program_id(0)
    main, rest, half, tail = pack.main, pack.rest, pack.half, pack.tail
    per_shard = chips * (main + rest)

    def columns_of(who, start, count):
        if start + count <= half:
            return main_ref[who, :, start : start + count]
        at = start - half
        return tails[who][:, at : at + count]

    second = step >= pl.num_programs(0) // 2
    tails = [
        jnp.where(second, tail_ref[who, :, tail:], tail_ref[who, :, :tail])
        for who in range(2 * chips)
    ]
    for core in range(2):
        for shard in range(shards):
            start = (core * shards + shard) * per_shard
            for chip in range(chips):
                block = columns_of(chip * 2 + core, shard * main, main)
                in_ref[:, start + chip * main : start + (chip + 1) * main] = block.astype(jnp.float32)
            ends = [
                columns_of(chip * 2 + core, shards * main, shards * rest).astype(jnp.float32)[
                    :, shard * rest : (shard + 1) * rest
                ]
                for chip in range(chips)
            ]
            in_ref[:, start + chips * main : start + per_shard] = jnp.concatenate(ends, axis=1)

    for chip in range(chips):

        @pl.when(step == chip)
        def _(chip=chip):
            for core in range(2):
                columns = slice(core * half, (core + 1) * half)
                block = out_part_ref[core]
                out_ref[chip * main : (chip + 1) * main, columns] = block[:main].astype(jnp.float32)
                start = chips * main + chip * rest
                out_ref[start : start + rest, columns] = block[main:].astype(jnp.float32)


def finish(values, pack, shards):
    ctx_size = values.shape[0]
    chips = ctx_size // 2
    steps = 8
    tile = pack.rows // steps
    per_out = pack.main + pack.rest
    assert pack.rows // pack.split == 2 and pack.split % tile == 0 and pack.out_start % per_out == 0
    return pl.pallas_call(
        functools.partial(finish_kernel, shards, chips, pack, tile),
        name="finish",
        grid=(steps,),
        in_specs=[
            pl.BlockSpec((ctx_size, tile, pack.half), lambda i: (0, i, 0)),
            pl.BlockSpec(
                (ctx_size, tile, pack.half),
                lambda i: (0, pack.rows // tile + i % (pack.split // tile), 0),
            ),
            pl.BlockSpec(
                (2, per_out, pack.half),
                lambda i: (jnp.minimum(i, chips - 1), pack.out_start // per_out, 0),
            ),
        ],
        out_specs=[
            pl.BlockSpec((tile, 2 * FF), lambda i: (i, 0)),
            whole_block((FF // shards, 2 * pack.half)),
        ],
        out_shape=[
            jax.ShapeDtypeStruct((pack.rows, 2 * FF), jnp.float32),
            jax.ShapeDtypeStruct((FF // shards, 2 * pack.half), jnp.float32),
        ],
        compiler_params=pltpu.CompilerParams(vmem_limit_bytes=VMEM_LIMIT),
    )(values, values, values)


TANH_SCALE = 0.7978845608028654
TANH_CUBE = 0.044715
UNIT_TILE = 384


def mlp_kernel(
    shards, pack, mine, x_own, c_own, c_x, c_y,
    normed_grad, out_own, out_x, out_y, out_left, out_right, grad_part,
    w_in, w_out, xs, cs, hidden, grads, part, from_x, from_y, corner_left, corner_right,
    out_stage, pair_in, pair_out, local_sems, send_sems, recv_sems,
):
    wire = Wire(send_sems, recv_sems)
    core = lax.rem(wire.ctx, 2)
    other = 1 - core
    rows, width = x_own.shape
    half = width // 2
    units = w_in.shape[2]
    tiles = units // UNIT_TILE
    left, right = pl.ds(0, half), pl.ds(half, half)
    locals_ = []

    def copy_in(source, target):
        copy = pltpu.make_async_copy(source, target, local_sems.at[len(locals_)])
        copy.start()
        locals_.append(copy)
        return copy

    def spans():
        for shard in range(shards):
            for p_rows, p_columns, w_rows, w_columns in pack.in_spans(shard):
                yield (shard, pl.ds(*p_rows), pl.ds(*p_columns)), w_in, (pl.ds(*w_rows), pl.ds(*w_columns))
            for p_rows, w_rows in pack.out_spans(shard, shards):
                yield (shard, pl.ds(*p_rows)), w_out, (pl.ds(*w_rows),)

    loads = [copy_in(x_own, xs.at[0]), copy_in(c_own, cs.at[0])]
    for here, target, there in spans():
        loads.append(copy_in(mine.at[here], target.at[(core,) + there]))
    late = [
        copy_in(source, target)
        for source, target in (
            (c_x, cs.at[1]),
            (c_y, cs.at[2]),
        )
    ]
    wire.meet([wire.plane(mask) for mask in PLANE_PEERS])
    x_copies = [
        wire.send(x_own, xs.at[1], wire.plane(2)),
        wire.send(x_own, xs.at[2], wire.plane(4)),
    ]
    swaps = [
        wire.send(mine.at[here], target.at[(core,) + there], wire.plane(1))
        for here, target, there in spans()
    ]
    for copy in loads:
        copy.wait()
    for copy in swaps:
        copy.wait_recv()

    def one_chunk(at):
        def one_tile(tile, carry):
            columns = pl.ds(pl.multiple_of(tile * UNIT_TILE, UNIT_TILE), UNIT_TILE)
            gate = dot(xs[at], w_in[0, :, columns])
            up = dot(xs[at], w_in[1, :, columns])
            grad = nt_dot(cs[at, :, left], w_out[0, columns, :])
            grad += nt_dot(cs[at, :, right], w_out[1, columns, :])
            square = gate * gate
            bend = jnp.tanh(TANH_SCALE * gate * (1.0 + TANH_CUBE * square))
            lift = 0.5 + 0.5 * bend
            value = gate * lift
            slope = lift + (0.5 * TANH_SCALE) * gate * (1.0 - bend * bend) * (
                1.0 + (3.0 * TANH_CUBE) * square
            )
            hidden[at, :, columns] = low(value * up)
            grads[0, at, :, columns] = low(grad * up * slope)
            grads[1, at, :, columns] = low(grad * value)
            return carry

        lax.fori_loop(0, tiles, one_tile, 0)

        def one_half(span):
            total = nt_dot(grads[0, at], w_in[0, span, :])
            return total + nt_dot(grads[1, at], w_in[1, span, :])

        return one_half

    one_half = one_chunk(0)
    for span in (left, right):
        normed_grad[:, span] = one_half(span)
    for copy in x_copies:
        copy.wait_recv()
    corners = [
        wire.send(xs.at[1, :, left], xs.at[3, :, left], wire.plane(4)),
        wire.send(xs.at[2, :, right], xs.at[3, :, right], wire.plane(2)),
    ]
    for copy in late:
        copy.wait()
    corners += [
        wire.send(cs.at[1, :, left], cs.at[3, :, left], wire.plane(4)),
        wire.send(cs.at[2, :, right], cs.at[3, :, right], wire.plane(2)),
    ]
    one_half = one_chunk(1)
    part[0, :, left] = low(one_half(left))
    early = [wire.send(part.at[0, :, left], from_x.at[:, left], wire.plane(2))]
    part[0, :, right] = low(one_half(right))
    one_half = one_chunk(2)
    part[1, :, right] = low(one_half(right))
    early.append(wire.send(part.at[1, :, right], from_y.at[:, right], wire.plane(4)))
    part[1, :, left] = low(one_half(left))
    for copy in corners:
        copy.wait_recv()
    one_half = one_chunk(3)
    part[2, :, left] = low(one_half(left))
    corner = [wire.send(part.at[2, :, left], corner_left, wire.plane(2))]
    part[2, :, right] = low(one_half(right))
    corner.append(wire.send(part.at[2, :, right], corner_right, wire.plane(4)))

    for at, target in ((1, out_x), (2, out_y), (0, out_own), (3, None)):
        slot = at % 2
        if at in (0, 3):
            for copy in out_copies[slot]:
                copy.wait()
        else:
            out_copies = {} if at == 1 else out_copies
        for n, span in enumerate((left, right)):
            out_stage[slot, :, span] = low(dot(hidden[at], w_out[n]))
        if target is None:
            out_copies[slot] = [
                copy_in(out_stage.at[slot, :, left], out_left),
                copy_in(out_stage.at[slot, :, right], out_right),
            ]
        else:
            out_copies[slot] = [copy_in(out_stage.at[slot], target)]

    everything = lambda ref: ref[...].reshape(ref.shape[0] * rows, ref.shape[2])

    def in_tile(which, tile):
        columns = pl.ds(tile * UNIT_TILE, UNIT_TILE)
        picked = grads[which, :, :, columns].reshape(4 * rows, UNIT_TILE)
        return columns, tn_dot(everything(xs), picked)

    pairs_in = []
    for tile in range(tiles):
        columns, value = in_tile(other, tile)
        w_in[0, :, columns] = low(value)
        pairs_in.append(wire.send(w_in.at[0, :, columns], pair_in.at[:, columns], wire.plane(1)))
    merged = []
    corner[0].wait_recv()
    part[1, :, left] = add_low(part[1, :, left], corner_left[...])
    merged.append(wire.send(part.at[1, :, left], from_y.at[:, left], wire.plane(4)))
    corner[1].wait_recv()
    part[0, :, right] = add_low(part[0, :, right], corner_right[...])
    merged.append(wire.send(part.at[0, :, right], from_x.at[:, right], wire.plane(2)))

    def out_tile(which, tile):
        columns = pl.ds(tile * UNIT_TILE, UNIT_TILE)
        picked = hidden[:, :, columns].reshape(4 * rows, UNIT_TILE)
        span = pl.ds(pl.multiple_of(which * half, half), half)
        return columns, tn_dot(picked, cs[:, :, span].reshape(4 * rows, half))

    pairs_out = []
    for tile in range(tiles):
        span, value = out_tile(other, tile)
        w_out[0, span, :] = low(value)
        pairs_out.append(wire.send(w_out.at[0, span, :], pair_out.at[span, :], wire.plane(1)))
    final = []
    for tile in range(tiles):
        columns, value = in_tile(core, tile)
        pairs_in[tile].wait_recv()
        w_in[1, :, columns] = low(value + pair_in[:, columns].astype(jnp.float32))
    for tile in range(tiles):
        span, value = out_tile(core, tile)
        pairs_out[tile].wait_recv()
        w_out[1, span, :] = low(value + pair_out[span, :].astype(jnp.float32))
    for here, source, there in spans():
        final.append(copy_in(source.at[(1,) + there], grad_part.at[here]))
    for copy in early + merged:
        copy.wait_recv()
    normed_grad[...] += from_x[...].astype(jnp.float32) + from_y[...].astype(jnp.float32)
    for copies in out_copies.values():
        for copy in copies:
            copy.wait()
    for copy in final:
        copy.wait()
    wire.finish()


def mlp(mine, x, upstream, pack):
    rows, width = x.shape
    half = width // 2
    units = pack.half + pack.tail
    shards = mine.shape[0]
    low_shape = lambda *shape: jax.ShapeDtypeStruct(shape, jnp.bfloat16)
    low_scratch = lambda *shape: pltpu.VMEM(shape, jnp.bfloat16)
    parts = shards * (1 + pack.rows // pack.split + 2)
    copies = parts + 6 + 2 + 2 + 2 + 2 * (units // UNIT_TILE)
    locals_ = 2 + parts + 2 + 5 + parts
    return pl.pallas_call(
        functools.partial(mlp_kernel, shards, pack),
        name="mlp",
        in_specs=[ANY] * 5,
        out_specs=[pl.BlockSpec(memory_space=pltpu.VMEM)] + [ANY] * 6,
        out_shape=[
            jax.ShapeDtypeStruct((rows, width), jnp.float32),
            low_shape(rows, width),
            low_shape(rows, width),
            low_shape(rows, width),
            low_shape(rows, half),
            low_shape(rows, half),
            low_shape(*mine.shape),
        ],
        scratch_shapes=[
            low_scratch(2, width, units),
            low_scratch(2, units, half),
            low_scratch(4, rows, width),
            low_scratch(4, rows, width),
            low_scratch(4, rows, units),
            low_scratch(2, 4, rows, units),
            low_scratch(3, rows, width),
            low_scratch(rows, width),
            low_scratch(rows, width),
            low_scratch(rows, half),
            low_scratch(rows, half),
            low_scratch(2, rows, width),
            low_scratch(width, units),
            low_scratch(units, half),
            dma_sems(locals_),
            dma_sems(copies),
            dma_sems(copies),
        ],
        compiler_params=pltpu.CompilerParams(
            collective_id=5, has_side_effects=True, vmem_limit_bytes=MLP_VMEM
        ),
    )(mine, x, *upstream)


class Layout:
    def __init__(self, ctx_size, fsdp_size):
        self.ctx_size = ctx_size
        self.shards = fsdp_size
        self.chips = ctx_size // 2
        self.index = lax.axis_index("ctx")
        self.chip = self.index // 2
        self.core = self.index % 2
        units = FF // (self.shards * self.chips)
        self.main = units // LANES * LANES
        self.rest = units - self.main
        self.per_shard = FF // self.shards
        self.rest_start = self.chips * self.main
        self.plane = ctx_size == 8 and fsdp_size == 4

    def xor(self, values, mask):
        pairs = [(i, i ^ mask) for i in range(self.ctx_size)]
        return lax.ppermute(values, "ctx", pairs)

    def same_core_groups(self):
        return [[chip * 2 + core for chip in range(self.chips)] for core in range(2)]

    def from_neighbours(self, values):
        return self.xor(values, 2), self.xor(values, 4)

    def from_corner(self, from_x, from_y):
        half = from_x.shape[1] // 2
        return self.xor(from_x[:, :half], 4), self.xor(from_y[:, half:], 2)

    def scatter_chip_blocks(self, own, to_x, to_y, left, right, token):
        half = left.shape[1]
        left = after(token, self.xor(left, 2))
        right = after(token, self.xor(right, 4))
        to_y = jnp.concatenate([add_low(to_y[:, :half], left), to_y[:, half:]], axis=1)
        to_x = jnp.concatenate([to_x[:, :half], add_low(to_x[:, half:], right)], axis=1)
        wide = lambda part: part.astype(jnp.float32)
        return wide(own) + wide(self.xor(to_y, 4)) + wide(self.xor(to_x, 2))

    def gather_chips(self, values):
        if self.chips != 4:
            return lax.all_gather(
                values, "ctx", axis=0, tiled=True, axis_index_groups=self.same_core_groups()
            )
        from_x, from_y = self.from_neighbours(values)
        left, right = self.from_corner(from_x, from_y)
        own = values
        return jnp.concatenate([own, from_x, from_y, jnp.concatenate([left, right], axis=1)], axis=0)

    def scatter_chips(self, partial):
        if self.chips != 4:
            return lax.psum_scatter(
                low(partial),
                "ctx",
                scatter_dimension=0,
                tiled=True,
                axis_index_groups=self.same_core_groups(),
            ).astype(jnp.float32)
        own, to_x, to_y, corner = jnp.split(partial, 4, axis=0)
        half = own.shape[1] // 2
        corner = low(corner)
        left = self.xor(corner[:, :half], 2).astype(jnp.float32)
        right = self.xor(corner[:, half:], 4).astype(jnp.float32)
        to_y = jnp.concatenate([to_y[:, :half] + left, to_y[:, half:]], axis=1)
        to_x = jnp.concatenate([to_x[:, :half], to_x[:, half:] + right], axis=1)
        from_y = self.xor(low(to_y), 4).astype(jnp.float32)
        from_x = self.xor(low(to_x), 2).astype(jnp.float32)
        return own + from_y + from_x

    def columns_of_chip(self, weights, start):
        parts = []
        if self.main:
            for shard in range(self.shards):
                at = start + shard * self.per_shard + self.chip * self.main
                parts.append(lax.dynamic_slice_in_dim(weights, at, self.main, 1))
        if self.rest:
            for shard in range(self.shards):
                at = start + shard * self.per_shard + self.rest_start + self.chip * self.rest
                parts.append(lax.dynamic_slice_in_dim(weights, at, self.rest, 1))
        return jnp.concatenate(parts, axis=1)

    def rows_of_chip(self, weights):
        parts = []
        if self.main:
            parts.append(lax.dynamic_slice_in_dim(weights, self.chip * self.main, self.main, 0))
        if self.rest:
            at = self.rest_start + self.chip * self.rest
            parts.append(lax.dynamic_slice_in_dim(weights, at, self.rest, 0))
        return jnp.concatenate(parts, axis=0)

    def by_core(self, mine, other):
        first = jnp.where(self.core == 0, mine, other)
        second = jnp.where(self.core == 0, other, mine)
        return first, second

    def mine_in(self, shard, later=0):
        return self.columns_of_chip(shard, self.core * FF + later)

    def mine_out(self, shard, later=0):
        width = shard.shape[1]
        half = lax.dynamic_slice_in_dim(shard, self.core * (width // 2) + later, width // 2, 1)
        return self.rows_of_chip(half)

    def gather_mlp_in(self, shard):
        mine = lax.all_gather(self.mine_in(shard), "fsdp", axis=0, tiled=True)
        return self.by_core(mine, self.xor(mine, 1))

    def gather_mlp_out(self, shard):
        width = shard.shape[1]
        mine = lax.all_gather(self.mine_out(shard), "fsdp", axis=0)
        mine = jnp.concatenate(
            [
                mine[:, : self.main].reshape(self.shards * self.main, width // 2),
                mine[:, self.main :].reshape(self.shards * self.rest, width // 2),
            ],
            axis=0,
        )
        return jnp.concatenate(self.by_core(mine, self.xor(mine, 1)), axis=1)

    def sum_pair(self, first, second):
        keep = jnp.where(self.core == 0, first, second)
        send = jnp.where(self.core == 0, second, first)
        return keep + self.xor(low(send), 1).astype(jnp.float32)

    def reduce_mlp_in(self, gate, up):
        total = low(self.sum_pair(gate, up))
        return lax.psum_scatter(total, "fsdp", scatter_dimension=0, tiled=True)

    def order_mlp_in(self, every):
        rows = every.shape[1]
        every = every.reshape(self.chips, 2, rows, every.shape[2])
        split = self.shards * self.main
        main = every[..., :split].reshape(self.chips, 2, rows, self.shards, self.main)
        rest = every[..., split:].reshape(self.chips, 2, rows, self.shards, self.rest)
        main = main.transpose(2, 1, 3, 0, 4).reshape(rows, 2, self.shards, -1)
        rest = rest.transpose(2, 1, 3, 0, 4).reshape(rows, 2, self.shards, -1)
        return jnp.concatenate([main, rest], axis=3).reshape(rows, 2 * FF).astype(jnp.float32)

    def reduce_mlp_out(self, grad):
        width = grad.shape[1]
        total = low(self.sum_pair(grad[:, : width // 2], grad[:, width // 2 :]))
        split = self.shards * self.main
        main = total[:split].reshape(self.shards, self.main, width // 2)
        rest = total[split:].reshape(self.shards, self.rest, width // 2)
        total = jnp.concatenate([main, rest], axis=1)
        return lax.psum_scatter(total, "fsdp", scatter_dimension=0, tiled=True)[0]

    def order_mlp_out(self, every):
        width = 2 * every.shape[2]
        every = every.reshape(self.chips, 2, self.main + self.rest, width // 2)
        main = every[:, :, : self.main].transpose(0, 2, 1, 3).reshape(-1, width)
        rest = every[:, :, self.main :].transpose(0, 2, 1, 3).reshape(-1, width)
        return jnp.concatenate([main, rest], axis=0).astype(jnp.float32)

    def gather_whole(self, shard):
        rows = shard.shape[0] // self.ctx_size
        piece = lax.dynamic_slice_in_dim(shard, self.index * rows, rows, 0)
        piece = lax.all_gather(piece, "fsdp", axis=0)
        piece = lax.all_gather(piece, "ctx", axis=1, tiled=True)
        return piece.reshape(-1, shard.shape[1])

    def reduce_whole(self, grad):
        rows = grad.shape[0] // self.shards
        total = grad.reshape(self.shards, rows, grad.shape[1])
        total = lax.psum_scatter(total, "ctx", scatter_dimension=1, tiled=True)
        total = lax.psum_scatter(total, "fsdp", scatter_dimension=0, tiled=True)[0]
        return lax.all_gather(total, "ctx", axis=0, tiled=True).astype(jnp.float32)

    def reduce_gain(self, grad):
        total = jnp.sum(lax.all_gather(grad, ("ctx", "fsdp"), axis=0), axis=0)
        rows = grad.shape[0] // self.shards
        return lax.dynamic_slice_in_dim(total, lax.axis_index("fsdp") * rows, rows)


def window_blocks(places_all, own_places, seq_ends, block):
    count = places_all.shape[0] // block
    blocks = places_all.reshape(count, block)
    held = blocks[:, 0] // block
    at = jnp.arange(count, dtype=jnp.int32)
    position = jnp.sum(jnp.where(held[None, :] == at[:, None], at[None, :], 0), axis=1)
    span = (WINDOW + block - 2) // block + 1
    first = own_places.reshape(-1, block)[:, 0] // block
    wanted = first[:, None] - (span - 1) + jnp.arange(span, dtype=jnp.int32)[None, :]
    where = position[jnp.maximum(wanted, 0)]
    key_place = jnp.where((wanted >= 0)[:, :, None], blocks[where], jnp.int32(1 << 30))
    key_place = key_place.reshape(where.shape[0], 1, span * block)
    starts = jnp.where(seq_ends[None, :] <= own_places[:, None], seq_ends[None, :], 0)
    least = jnp.maximum(jnp.max(starts, axis=1), own_places - (WINDOW - 1))
    return where, key_place, least


def per_device(
    ctx_size,
    fsdp_size,
    tokens,
    order,
    lengths,
    norm_attn,
    w_attn_in,
    w_attn_out,
    norm_mlp,
    w_mlp_in,
    w_mlp_out,
    cotangent,
):
    lay = Layout(ctx_size, fsdp_size)
    x, upstream = tokens[0], cotangent[0]
    own_rows, width = x.shape
    block = own_rows // ROUNDS
    places_all = order[0]
    own_places = lax.dynamic_slice_in_dim(places_all, lay.index * own_rows, own_rows)
    where, key_place, least = window_blocks(
        places_all, own_places, jnp.cumsum(lengths[0]), block
    )
    target = where % ROUNDS * ctx_size + where // ROUNDS
    where = jnp.concatenate([where, target], axis=1)
    bounds = jnp.stack([own_places, least])
    bounds_wide = bounds.reshape(2, ROUNDS, block).transpose(1, 0, 2)
    bounds_wide = jnp.tile(bounds_wide, (1, 1, HEADS_STEP))
    frequency = 10000.0 ** (-jnp.arange(HD // 2, dtype=jnp.float32) / (HD // 2))
    angles = own_places.astype(jnp.float32)[:, None] * frequency[None, :]
    cosine = jnp.cos(angles)
    sine_part = jnp.sin(angles)
    cosine = jnp.concatenate([cosine, cosine], axis=1)
    sine_part = jnp.concatenate([-sine_part, sine_part], axis=1)

    if lay.plane:
        pack = Pack(w_mlp_in.shape[0], width // 2, lay.chips, FF // lay.chips, lay.main, lay.rest)
        pieces = lambda w: w.reshape(ctx_size, w.shape[0] // ctx_size, w.shape[1])
        in_line, gains, mine, _ = share_line(
            pieces(w_attn_in), norm_attn[None], norm_mlp[None], w_mlp_in, w_mlp_out, pack, fsdp_size
        )
        mine = lax.all_gather(mine, "fsdp", axis=0)
        in_attn, out_line, token = share_plane(
            pieces(w_attn_in), in_line, pieces(w_attn_out), ctx_size, fsdp_size
        )
        in_attn = in_attn.reshape(width, -1)
    else:
        in_attn = lay.gather_whole(w_attn_in)
        out_attn = lay.gather_whole(w_attn_out)
        gains = jnp.pad(jnp.stack([norm_attn, norm_mlp]).astype(jnp.float32), ((0, 6), (0, 0)))
        gains = lax.all_gather(gains, "fsdp", axis=0)
        gate_in, up_in = lay.gather_mlp_in(w_mlp_in)
        out_mlp = lay.gather_mlp_out(w_mlp_out)
        upstream_all = lay.gather_chips(upstream)

    normed_one, queries, key_value = project(x, gains, in_attn, cosine, sine_part)
    if lay.plane:
        key_value, out_attn, token = gather_plane(
            key_value, pieces(w_attn_out), out_line, ctx_size, fsdp_size
        )
        out_attn = out_attn.reshape(-1, width)
        upstream_all = (upstream,) + lay.from_neighbours(after(token, upstream))
    else:
        key_value = lax.all_gather(key_value, "ctx", axis=0)
    key_value = key_value.reshape(ctx_size * ROUNDS, block, 2 * HD)
    mixed = attend(where, queries, key_value, key_place, bounds.T)
    middle, normed_two = middle_forward(x, mixed, gains, out_attn)

    if lay.plane:
        grad_normed_two, *out_parts, grad_mlp = mlp(
            mine, normed_two, upstream_all, pack
        )
        grad_mlp = lax.psum_scatter(grad_mlp, "fsdp", scatter_dimension=0, tiled=True)[0]
    else:
        normed_all = lay.gather_chips(normed_two)
        gate = dot(normed_all, gate_in)
        up = dot(normed_all, up_in)
        hidden, hidden_back = jax.vjp(geglu, gate, up)
        hidden = low(hidden)
        grad_hidden = dot_nt(upstream_all, out_mlp)
        grad_gate, grad_up = hidden_back(grad_hidden)
        grad_gate = low(grad_gate)
        grad_up = low(grad_up)
        grad_normed_two = lay.scatter_chips(dot_nt(grad_gate, gate_in) + dot_nt(grad_up, up_in))
        mixed_out = lay.scatter_chips(dot(hidden, out_mlp))
        grad_out_mlp = lay.reduce_mlp_out(dot_tn(hidden, upstream_all))
        grad_in_mlp = lay.reduce_mlp_in(dot_tn(normed_all, grad_gate), dot_tn(normed_all, grad_up))

    grad_middle, grad_mixed, grad_out_attn, grad_gain_mlp, token = middle_back(
        grad_normed_two, middle, upstream, mixed, gains, out_attn
    )
    if lay.plane:
        mixed_out = lay.scatter_chip_blocks(*out_parts, token)
    result = middle + mixed_out
    grad_query, grad_kv = attend_back(
        where, queries, key_value, grad_mixed, key_place, bounds_wide, cosine, sine_part
    )
    if lay.plane:
        grad_kv = sum_plane(grad_kv.reshape(ROUNDS, lay.chips, 2, block, 2 * HD))
        grad_kv = grad_kv.reshape(own_rows, 2 * HD)
    else:
        grad_kv = grad_kv.reshape(ROUNDS, ctx_size, block, 2 * HD)
        grad_kv = lax.psum_scatter(grad_kv, "ctx", scatter_dimension=1, tiled=True)
        grad_kv = grad_kv.reshape(own_rows, 2 * HD).astype(jnp.float32)
    grad_in_attn, grad_inputs, grad_gain_attn = project_back(
        grad_query, grad_kv, cosine, sine_part, normed_one, x, grad_middle, gains, in_attn
    )
    if lay.plane:
        split = lambda grad: grad.reshape(fsdp_size, lay.chips, 2, -1, grad.shape[1])
        grad_out_attn, grad_in_attn, grad_mlp, grad_gains = close(
            split(grad_out_attn),
            split(grad_in_attn),
            grad_mlp,
            grad_gain_attn,
            grad_gain_mlp,
            ctx_size,
            fsdp_size,
        )
        whole = lambda grad: grad.reshape(-1, grad.shape[2]).astype(jnp.float32)
        grad_out_attn, grad_in_attn = whole(grad_out_attn), whole(grad_in_attn)
        grad_in_mlp, grad_out_mlp = finish(grad_mlp, pack, fsdp_size)
        grad_gain_attn, grad_gain_mlp = grad_gains[0], grad_gains[1]
    else:
        grad_out_attn = lay.reduce_whole(grad_out_attn)
        grad_in_attn = lay.reduce_whole(grad_in_attn)
        grad_in_mlp = lay.order_mlp_in(lax.all_gather(grad_in_mlp, "ctx", axis=0))
        grad_out_mlp = lay.order_mlp_out(lax.all_gather(grad_out_mlp, "ctx", axis=0))
        grad_gain_attn = lay.reduce_gain(grad_gain_attn[0])
        grad_gain_mlp = lay.reduce_gain(grad_gain_mlp[0])
    return (
        low(result)[None],
        grad_inputs[None],
        grad_gain_attn,
        grad_in_attn,
        grad_out_attn,
        grad_gain_mlp,
        grad_in_mlp,
        grad_out_mlp,
    )


def solution(mesh):
    in_specs = (
        P("fsdp", "ctx", None),
        P("fsdp", None),
        P("fsdp", None),
        P("fsdp"),
        P("fsdp", None),
        P("fsdp", None),
        P("fsdp"),
        P("fsdp", None),
        P("fsdp", None),
        P("fsdp", "ctx", None),
    )
    out_specs = (
        P("fsdp", "ctx", None),
        P("fsdp", "ctx", None),
        P("fsdp"),
        P("fsdp", None),
        P("fsdp", None),
        P("fsdp"),
        P("fsdp", None),
        P("fsdp", None),
    )

    def run(*arrays):
        return per_device(mesh.shape["ctx"], mesh.shape["fsdp"], *arrays)

    return jax.shard_map(run, mesh=mesh, in_specs=in_specs, out_specs=out_specs, check_vma=False)
```

```python
import functools

import jax
import jax.numpy as jnp
from jax import lax
from jax.experimental import pallas as pl
from jax.experimental.pallas import tpu as pltpu
from jax.sharding import PartitionSpec as P

H = 12
HD = 128
FF = 4608
WINDOW = 1024
ROUNDS = 4
LANES = 128


EPS = 1e-06


def rms_norm(values, gain):
    return values * lax.rsqrt(jnp.mean(values * values, axis=-1, keepdims=True) + EPS) * gain


def geglu(gate, up):
    return jax.nn.gelu(gate, approximate=True) * up


def dot(left, right):
    return jnp.dot(left, right, preferred_element_type=jnp.float32)


def dot_nt(left, right):
    return jnp.einsum("ab,cb->ac", left, right, preferred_element_type=jnp.float32)


def dot_tn(left, right):
    return jnp.einsum("ab,ac->bc", left, right, preferred_element_type=jnp.float32)


def nt_dot(left, right):
    return lax.dot_general(left, right, (((1,), (1,)), ((), ())), preferred_element_type=jnp.float32)


def tn_dot(left, right):
    return lax.dot_general(left, right, (((0,), (0,)), ((), ())), preferred_element_type=jnp.float32)


def low(values):
    return values.astype(jnp.bfloat16)


VMEM_LIMIT = 56 * 1024 * 1024
MLP_VMEM = 62 * 1024 * 1024

def gain_row(ref, which):
    parts = [ref[shard, which : which + 1, :] for shard in range(ref.shape[0])]
    return jnp.concatenate(parts, axis=1)


def norm_scale(values):
    return lax.rsqrt(jnp.mean(values * values, axis=-1, keepdims=True) + EPS)


def norm_back(values, gain, incoming):
    scale = norm_scale(values)
    weighted = incoming * gain
    inner = jnp.mean(weighted * values, axis=-1, keepdims=True)
    grad = scale * weighted - values * (scale * scale * scale * inner)
    return grad, jnp.sum(incoming * values * scale, axis=0, keepdims=True)


def project_kernel(heads, x_ref, gain_ref, w_ref, cos_ref, sin_ref, normed_ref, q_ref, kv_ref):
    step = pl.program_id(0)

    @pl.when(step == 0)
    def _():
        x = x_ref[...].astype(jnp.float32)
        normed_ref[...] = (x * norm_scale(x) * gain_row(gain_ref, 0)).astype(jnp.bfloat16)

    part = jnp.dot(normed_ref[...], w_ref[...], preferred_element_type=jnp.float32)
    cosine, sine_part = cos_ref[...], sin_ref[...]

    def turn(value):
        return value * cosine + pltpu.roll(value, HD // 2, 1) * sine_part

    @pl.when(step < heads // 2)
    def _():
        for j in range(2):
            q_ref[j] = (turn(part[:, j * HD : (j + 1) * HD]) * HD ** (-0.5)).astype(jnp.bfloat16)

    @pl.when(step == heads // 2)
    def _():
        kv_ref[:, :HD] = turn(part[:, :HD]).astype(jnp.bfloat16)
        kv_ref[:, HD:] = part[:, HD:].astype(jnp.bfloat16)


def project(x, gain, w, cosine, sine_part):
    rows, width = x.shape
    steps = H // 2 + 1
    whole = lambda *shape: pl.BlockSpec(shape, lambda i: (0,) * len(shape))
    return pl.pallas_call(
        functools.partial(project_kernel, H),
        grid=(steps,),
        name="project",
        in_specs=[
            whole(rows, width),
            whole(*gain.shape),
            pl.BlockSpec((width, 2 * HD), lambda i: (0, i)),
            whole(rows, HD),
            whole(rows, HD),
        ],
        out_specs=[
            whole(rows, width),
            pl.BlockSpec((2, rows, HD), lambda i: (jnp.minimum(i, H // 2 - 1), 0, 0)),
            whole(rows, 2 * HD),
        ],
        out_shape=[
            jax.ShapeDtypeStruct((rows, width), jnp.bfloat16),
            jax.ShapeDtypeStruct((H, rows, HD), jnp.bfloat16),
            jax.ShapeDtypeStruct((rows, 2 * HD), jnp.bfloat16),
        ],
        compiler_params=pltpu.CompilerParams(vmem_limit_bytes=VMEM_LIMIT),
    )(x, gain, w, cosine, sine_part)


HEADS_STEP = 4
ANY = pl.BlockSpec(memory_space=pl.ANY)


class Window:
    def __init__(self, rows):
        self.block = rows // ROUNDS
        self.blocks = (WINDOW + self.block - 2) // self.block + 1
        self.span = self.blocks * self.block


def place_tables(
    index, devices, order_ref, lengths_ref, frequency_ref,
    where_ref, key_place_ref, bounds_ref, wide_ref, cos_ref, sin_ref,
):
    count, block = order_ref.shape
    window = Window(block * ROUNDS)
    blocks = order_ref[...].astype(jnp.float32)
    block_of = lambda place: jnp.floor((place + 0.5) * (1.0 / block))
    held = block_of(blocks[:, :1])
    offsets = low(blocks - held * block)
    at = lax.broadcasted_iota(jnp.int32, (count, 1), 0).astype(jnp.float32)
    lane = lax.broadcasted_iota(jnp.int32, (1, LANES), 1).astype(jnp.float32)
    step = jnp.where(lane < window.blocks, lane, lane - window.blocks)
    lengths = lengths_ref[...].astype(jnp.float32)
    ends = [lengths[:, :1]]
    for j in range(1, lengths.shape[1]):
        ends.append(ends[-1] + lengths[:, j : j + 1])

    def least_of(place):
        start = jnp.zeros_like(place)
        for end in ends:
            start = jnp.where(end <= place, end, start)
        return jnp.maximum(start, place - (WINDOW - 1))

    where_ref[...] = jnp.zeros_like(where_ref)
    own = []
    for r in range(ROUNDS):
        mine = order_ref[pl.ds(index * ROUNDS + r, 1), :].astype(jnp.float32)
        own.append(mine)
        wanted = block_of(mine[:, :1]) - (window.blocks - 1) + step
        match = (held == jnp.maximum(wanted, 0.0)).astype(jnp.float32)
        where = jnp.sum(match * at, axis=0, keepdims=True)
        device = jnp.floor((where + 0.5) * (1.0 / ROUNDS))
        target = (where - ROUNDS * device) * devices + device
        where_ref[r : r + 1, :] = jnp.where(lane < window.blocks, where, target).astype(jnp.int32)
        inner = tn_dot(low(match), offsets)
        pieces = []
        for j in range(window.blocks):
            one = wanted[:, j : j + 1]
            pieces.append(inner[j : j + 1] + jnp.where(one >= 0.0, one * block, 1e9))
        key_place_ref[r] = jnp.concatenate(pieces, axis=1)
        wide_ref[r, :1, :] = jnp.concatenate([mine] * HEADS_STEP, axis=1)
        wide_ref[r, 1:, :] = jnp.concatenate([least_of(mine)] * HEADS_STEP, axis=1)
    own = jnp.concatenate(own, axis=1)
    own = jnp.broadcast_to(own, (8, own.shape[1])).T[:, :1]
    bounds_ref[:, :1] = own
    bounds_ref[:, 1:] = least_of(own)
    angles = own * frequency_ref[...]
    cos_ref[...] = jnp.cos(angles)
    sign = jnp.where(lane < HD // 2, -1.0, 1.0)
    sin_ref[...] = jnp.sin(angles) * sign


def place_arrays(order, lengths, rows):
    window = Window(rows)
    frequency = 10000.0 ** (-jnp.arange(HD // 2, dtype=jnp.float32) / (HD // 2))
    operands = (
        order.reshape(-1, window.block),
        lengths,
        jnp.concatenate([frequency, frequency])[None],
    )
    wide = jax.ShapeDtypeStruct((rows, HD), jnp.float32)
    shapes = (
        jax.ShapeDtypeStruct((8, LANES), jnp.int32),
        jax.ShapeDtypeStruct((ROUNDS, 1, window.span), jnp.float32),
        jax.ShapeDtypeStruct((rows, 2), jnp.float32),
        jax.ShapeDtypeStruct((ROUNDS, 2, HEADS_STEP * window.block), jnp.float32),
        wide,
        wide,
    )
    return operands, shapes


def place_tables_alone(devices, order, lengths, rows):
    operands, shapes = place_arrays(order, lengths, rows)

    def kernel(*refs):
        place_tables(lax.axis_index("ctx"), devices, *refs)

    vmem = pl.BlockSpec(memory_space=pltpu.VMEM)
    return pl.pallas_call(
        kernel,
        name="places",
        in_specs=[vmem] * len(operands),
        out_specs=[vmem] * len(shapes),
        out_shape=shapes,
    )(*operands)


def load_window(blocks, block, where_ref, kv_ref, window):
    r = pl.program_id(0)
    for j in range(blocks):
        window[j * block : (j + 1) * block, :] = kv_ref[where_ref[r, j]]


def attend_kernel(
    blocks, block, where_ref, q_ref, kv_ref, key_place_ref, bounds_ref, out_ref, log_ref, window, bias
):
    load_window(blocks, block, where_ref, kv_ref, window)
    key_place = key_place_ref[0]
    allowed = (key_place <= bounds_ref[:, :1]) & (key_place >= bounds_ref[:, 1:])
    bias[...] = jnp.where(allowed, 0.0, -1e30)
    for part in range(q_ref.shape[0] // HEADS_STEP):
        first = part * HEADS_STEP
        queries = q_ref[first : first + HEADS_STEP].reshape(HEADS_STEP * block, HD)
        scores = nt_dot(queries, window[:, :HD])
        scores = scores.reshape(HEADS_STEP, block, blocks * block) + bias[...][None]
        peak = jnp.max(scores, axis=-1, keepdims=True)
        weights = jnp.exp(scores - peak)
        total = jnp.sum(weights, axis=-1, keepdims=True).reshape(HEADS_STEP * block, 1)
        weights = low(weights).reshape(HEADS_STEP * block, blocks * block)
        mixed = low(dot(weights, window[:, HD:]) / total)
        for j in range(HEADS_STEP):
            columns = slice((first + j) * HD, (first + j + 1) * HD)
            out_ref[:, columns] = mixed[j * block : (j + 1) * block]
        log_total = peak.reshape(HEADS_STEP * block, 1) + jnp.log(total)
        log_ref[0, part] = jnp.broadcast_to(log_total, (HEADS_STEP * block, LANES)).T[:1, :]


def attend(where, queries, kv_blocks, key_place, bounds):
    heads, rows, _ = queries.shape
    window = Window(rows)
    block, span, parts = window.block, window.span, heads // HEADS_STEP
    grid_spec = pltpu.PrefetchScalarGridSpec(
        num_scalar_prefetch=1,
        grid=(ROUNDS,),
        in_specs=[
            pl.BlockSpec((heads, block, HD), lambda r, *_: (0, r, 0)),
            pl.BlockSpec(kv_blocks.shape, lambda r, *_: (0, 0, 0)),
            pl.BlockSpec((1, 1, span), lambda r, *_: (r, 0, 0)),
            pl.BlockSpec((block, 2), lambda r, *_: (r, 0)),
        ],
        out_specs=[
            pl.BlockSpec((block, heads * HD), lambda r, *_: (r, 0)),
            pl.BlockSpec((1, parts, 1, HEADS_STEP * block), lambda r, *_: (r, 0, 0, 0)),
        ],
        scratch_shapes=[
            pltpu.VMEM((span, 2 * HD), jnp.bfloat16),
            pltpu.VMEM((block, span), jnp.float32),
        ],
    )
    return pl.pallas_call(
        functools.partial(attend_kernel, window.blocks, block),
        name="attend",
        grid_spec=grid_spec,
        out_shape=[
            jax.ShapeDtypeStruct((rows, heads * HD), jnp.bfloat16),
            jax.ShapeDtypeStruct((ROUNDS, parts, 1, HEADS_STEP * block), jnp.float32),
        ],
        compiler_params=pltpu.CompilerParams(vmem_limit_bytes=VMEM_LIMIT),
    )(where, queries, kv_blocks, key_place, bounds)


def attend_back_kernel(
    blocks, block, where_ref, q_ref, kv_ref, grad_ref, mixed_ref, log_ref, key_place_ref, bounds_ref,
    cos_ref, sin_ref, *refs,
):
    grad_q_ref, grad_kv_ref, window, bias, window_grad, total_grad = refs[-6:]
    r = pl.program_id(0)

    @pl.when(r == 0)
    def _():
        total_grad[...] = jnp.zeros_like(total_grad)

    load_window(blocks, block, where_ref, kv_ref, window)
    key_place = jnp.broadcast_to(key_place_ref[0], (8, blocks * block)).T[:, :1]
    allowed = (key_place <= bounds_ref[0, :1, :]) & (key_place >= bounds_ref[0, 1:, :])
    bias[...] = jnp.where(allowed, 0.0, -1e30)
    keys, values = window[:, :HD], window[:, HD:]
    cosine, sine_part = cos_ref[...], sin_ref[...]
    for part in range(q_ref.shape[0] // HEADS_STEP):
        first = part * HEADS_STEP
        spans = [slice((first + j) * HD, (first + j + 1) * HD) for j in range(HEADS_STEP)]
        queries = q_ref[first : first + HEADS_STEP].reshape(HEADS_STEP * block, HD)
        grads = jnp.concatenate([grad_ref[:, span] for span in spans], axis=0)
        delta = jnp.concatenate(
            [
                jnp.sum(
                    (grad_ref[:, span].astype(jnp.float32) * mixed_ref[:, span].astype(jnp.float32)).T,
                    axis=0,
                    keepdims=True,
                )
                for span in spans
            ],
            axis=1,
        )
        probs = jnp.exp(nt_dot(keys, queries) + (bias[...] - log_ref[0, part]))
        grad_scores = low(probs * (nt_dot(values, grads) - delta))
        grad_keys = dot(grad_scores, queries)
        grad_values = dot(low(probs), grads)
        if part == 0:
            window_grad[:, :HD] = grad_keys
            window_grad[:, HD:] = grad_values
        else:
            window_grad[:, :HD] += grad_keys
            window_grad[:, HD:] += grad_values
        grad_q = tn_dot(grad_scores, keys)
        for j, span in enumerate(spans):
            one = grad_q[j * block : (j + 1) * block]
            one = (one * cosine - pltpu.roll(one, HD // 2, 1) * sine_part) * HD ** (-0.5)
            grad_q_ref[:, span] = low(one)
    for j in range(blocks):
        total_grad[where_ref[r, blocks + j]] += window_grad[j * block : (j + 1) * block, :]

    @pl.when(r == pl.num_programs(0) - 1)
    def _():
        grad_kv_ref[...] = low(total_grad[...])


def attend_back(
    where, queries, kv_blocks, grads, mixed, log_total, key_place, bounds, cosine, sine_part, earlier
):
    heads, rows, _ = queries.shape
    window = Window(rows)
    block, span, parts = window.block, window.span, heads // HEADS_STEP
    width = HEADS_STEP * block
    grid_spec = pltpu.PrefetchScalarGridSpec(
        num_scalar_prefetch=1,
        grid=(ROUNDS,),
        in_specs=[
            pl.BlockSpec((heads, block, HD), lambda r, *_: (0, r, 0)),
            pl.BlockSpec(kv_blocks.shape, lambda r, *_: (0, 0, 0)),
            pl.BlockSpec((block, heads * HD), lambda r, *_: (r, 0)),
            pl.BlockSpec((block, heads * HD), lambda r, *_: (r, 0)),
            pl.BlockSpec((1, parts, 1, width), lambda r, *_: (r, 0, 0, 0)),
            pl.BlockSpec((1, 1, span), lambda r, *_: (r, 0, 0)),
            pl.BlockSpec((1, 2, width), lambda r, *_: (r, 0, 0)),
            pl.BlockSpec((block, HD), lambda r, *_: (r, 0)),
            pl.BlockSpec((block, HD), lambda r, *_: (r, 0)),
        ]
        + [ANY] * len(earlier),
        out_specs=[
            pl.BlockSpec((block, heads * HD), lambda r, *_: (r, 0)),
            pl.BlockSpec(kv_blocks.shape, lambda r, *_: (0, 0, 0)),
        ],
        scratch_shapes=[
            pltpu.VMEM((span, 2 * HD), jnp.bfloat16),
            pltpu.VMEM((span, width), jnp.float32),
            pltpu.VMEM((span, 2 * HD), jnp.float32),
            pltpu.VMEM(kv_blocks.shape, jnp.float32),
        ],
    )
    return pl.pallas_call(
        functools.partial(attend_back_kernel, window.blocks, block),
        name="attend_back",
        grid_spec=grid_spec,
        out_shape=[
            jax.ShapeDtypeStruct((rows, heads * HD), jnp.bfloat16),
            jax.ShapeDtypeStruct(kv_blocks.shape, jnp.bfloat16),
        ],
        compiler_params=pltpu.CompilerParams(vmem_limit_bytes=VMEM_LIMIT),
    )(
        where,
        queries,
        kv_blocks,
        grads,
        mixed,
        log_total,
        key_place,
        bounds,
        cosine,
        sine_part,
        *earlier,
    )


MIDDLE_TILES = 3


def whole_block(shape):
    return pl.BlockSpec(shape, lambda i: (0,) * len(shape))


def middle_kernel(x_ref, mixed_ref, gain_ref, w_ref, middle_ref, normed_ref):
    step = pl.program_id(0)
    tile = w_ref.shape[1]
    columns = pl.ds(pl.multiple_of(step * tile, tile), tile)
    middle_ref[:, columns] = x_ref[:, columns].astype(jnp.float32) + dot(mixed_ref[...], w_ref[...])

    @pl.when(step == pl.num_programs(0) - 1)
    def _():
        values = middle_ref[...]
        normed_ref[...] = low(values * norm_scale(values) * gain_row(gain_ref, 1))


def middle_forward(x, mixed, gains, w):
    rows, width = x.shape
    inner = mixed.shape[1]
    return pl.pallas_call(
        middle_kernel,
        name="middle",
        grid=(MIDDLE_TILES,),
        in_specs=[
            whole_block((rows, width)),
            whole_block((rows, inner)),
            whole_block(gains.shape),
            pl.BlockSpec((inner, width // MIDDLE_TILES), lambda i: (0, i)),
        ],
        out_specs=[whole_block((rows, width))] * 2,
        out_shape=[
            jax.ShapeDtypeStruct((rows, width), jnp.float32),
            jax.ShapeDtypeStruct((rows, width), jnp.bfloat16),
        ],
        compiler_params=pltpu.CompilerParams(vmem_limit_bytes=VMEM_LIMIT),
    )(x, mixed, gains, w)


def middle_back_kernel(
    grad_ref, middle_ref, upstream_ref, mixed_ref, gain_ref, w_ref,
    grad_middle_ref, grad_mixed_ref, grad_w_ref, grad_gain_ref, token, branch,
):
    @pl.when(pl.program_id(0) == 0)
    def _():
        grad, grad_gain = norm_back(middle_ref[...], gain_row(gain_ref, 1), grad_ref[...])
        total = upstream_ref[...].astype(jnp.float32) + grad
        grad_middle_ref[...] = total
        branch[...] = low(total)
        grad_gain_ref[...] = grad_gain
        token[...] = jnp.zeros_like(token)

    grad_mixed_ref[...] = low(nt_dot(branch[...], w_ref[...]))
    grad_w_ref[...] = low(tn_dot(mixed_ref[...], branch[...]))


def middle_back(grad, middle, upstream, mixed, gains, w):
    rows, width = middle.shape
    inner = mixed.shape[1]
    tile = inner // MIDDLE_TILES
    return pl.pallas_call(
        middle_back_kernel,
        name="middle_back",
        grid=(MIDDLE_TILES,),
        in_specs=[
            whole_block((rows, width)),
            whole_block((rows, width)),
            whole_block((rows, width)),
            pl.BlockSpec((rows, tile), lambda i: (0, i)),
            whole_block(gains.shape),
            pl.BlockSpec((tile, width), lambda i: (i, 0)),
        ],
        out_specs=[
            whole_block((rows, width)),
            pl.BlockSpec((rows, tile), lambda i: (0, i)),
            pl.BlockSpec((tile, width), lambda i: (i, 0)),
            whole_block((1, width)),
            whole_block(TOKEN),
        ],
        out_shape=[
            jax.ShapeDtypeStruct((rows, width), jnp.float32),
            jax.ShapeDtypeStruct((rows, inner), jnp.bfloat16),
            jax.ShapeDtypeStruct((inner, width), jnp.bfloat16),
            jax.ShapeDtypeStruct((1, width), jnp.float32),
            token_shape(),
        ],
        scratch_shapes=[pltpu.VMEM((rows, width), jnp.bfloat16)],
        compiler_params=pltpu.CompilerParams(vmem_limit_bytes=VMEM_LIMIT),
    )(grad, middle, upstream, mixed, gains, w)


def project_back_queries_kernel(grad_ref, normed_ref, w_ref, grad_w_ref, grad_normed_ref):
    grad_normed_ref[...] = nt_dot(grad_ref[...], w_ref[...])
    grad_w_ref[...] = low(tn_dot(normed_ref[...], grad_ref[...]))


def project_back_queries(grad_q, normed, w):
    rows, width = normed.shape
    inner = grad_q.shape[1]
    tile = width // MIDDLE_TILES
    return pl.pallas_call(
        project_back_queries_kernel,
        name="project_back_queries",
        grid=(MIDDLE_TILES,),
        in_specs=[
            whole_block(grad_q.shape),
            pl.BlockSpec((rows, tile), lambda i: (0, i)),
            pl.BlockSpec((tile, inner), lambda i: (i, 0)),
        ],
        out_specs=[
            pl.BlockSpec((tile, inner), lambda i: (i, 0)),
            pl.BlockSpec((rows, tile), lambda i: (0, i)),
        ],
        out_shape=[
            jax.ShapeDtypeStruct((width, inner), jnp.bfloat16),
            jax.ShapeDtypeStruct((rows, width), jnp.float32),
        ],
        compiler_params=pltpu.CompilerParams(vmem_limit_bytes=VMEM_LIMIT),
    )(grad_q, normed, w)


def project_back_keys_kernel(
    grad_kv_ref, cos_ref, sin_ref, normed_ref, partial_ref, x_ref, grad_middle_ref, gain_ref, w_ref,
    grad_w_ref, grad_x_ref, grad_gain_ref,
):
    keys = grad_kv_ref[:, :HD]
    keys = low(keys * cos_ref[...] - pltpu.roll(keys, HD // 2, 1) * sin_ref[...])
    joined = jnp.concatenate([keys, low(grad_kv_ref[:, HD:])], axis=1)
    grad_w_ref[...] = low(tn_dot(normed_ref[...], joined))
    grad_normed = partial_ref[...] + nt_dot(joined, w_ref[...])
    grad, grad_gain = norm_back(x_ref[...].astype(jnp.float32), gain_row(gain_ref, 0), grad_normed)
    grad_x_ref[...] = grad_middle_ref[...] + grad
    grad_gain_ref[...] = grad_gain


def project_back_keys(grad_kv, cosine, sine_part, normed, partial, x, grad_middle, gains, w):
    rows, width = x.shape
    inner = grad_kv.shape[1]
    arrays = (grad_kv, cosine, sine_part, normed, partial, x, grad_middle, gains)
    last = w.shape[1] // inner - 1
    return pl.pallas_call(
        project_back_keys_kernel,
        name="project_back_keys",
        grid=(1,),
        in_specs=[whole_block(one.shape) for one in arrays]
        + [pl.BlockSpec((width, inner), lambda i: (0, last))],
        out_specs=[whole_block((width, inner)), whole_block((rows, width)), whole_block((1, width))],
        out_shape=[
            jax.ShapeDtypeStruct((width, inner), jnp.bfloat16),
            jax.ShapeDtypeStruct((rows, width), jnp.float32),
            jax.ShapeDtypeStruct((1, width), jnp.float32),
        ],
        compiler_params=pltpu.CompilerParams(vmem_limit_bytes=VMEM_LIMIT),
    )(*arrays, w)


MESH_ID =MESH_ID = pl.DeviceIdType.MESH


class Wire:
    def __init__(self, send_sems, recv_sems):
        self.send_sems = send_sems
        self.recv_sems = recv_sems
        self.count = 0
        self.open = []
        self.ctx = lax.axis_index("ctx")
        self.shard = lax.axis_index("fsdp")

    def other(self, mask):
        at = self.ctx
        for bit in (1, 2, 4):
            if mask & bit:
                at = at + bit - 2 * bit * lax.rem(at // bit, 2)
        return at

    def plane(self, mask):
        return (self.other(mask), self.shard)

    def line(self, step, shards):
        return (self.ctx, lax.rem(self.shard + step, shards))

    def meet(self, peers):
        barrier = pltpu.get_barrier_semaphore()
        for peer in peers:
            pl.semaphore_signal(barrier, inc=1, device_id=peer, device_id_type=MESH_ID)
        pl.semaphore_wait(barrier, len(peers))

    def send(self, source, target, peer):
        at = self.count
        self.count += 1
        copy = pltpu.make_async_remote_copy(
            src_ref=source,
            dst_ref=target,
            send_sem=self.send_sems.at[at],
            recv_sem=self.recv_sems.at[at],
            device_id=peer,
            device_id_type=MESH_ID,
        )
        copy.start()
        self.open.append(copy)
        return copy

    def sent(self, copy):
        copy.wait_send()
        self.open = [one for one in self.open if one is not copy]

    def finish(self):
        for copy in self.open:
            copy.wait_send()


class PlaneGather:
    COPIES = 9

    def __init__(self, wire, source, out_at, rows, split):
        self.wire, self.out_at, self.rows, self.split = wire, out_at, rows, split
        ctx = wire.ctx
        self.core = wire.send(source, out_at(ctx), wire.plane(1))
        self.x = wire.send(source, out_at(ctx), wire.plane(2))
        self.y = wire.send(source, out_at(ctx), wire.plane(4))

    def forward(self):
        wire, split = self.wire, self.split
        rest = self.rows - split
        self.x.wait_recv()
        block = self.out_at(wire.other(2))
        part = block.at[pl.ds(0, split)]
        self.corner_y = wire.send(part, part, wire.plane(4))
        self.core_x = wire.send(block, block, wire.plane(1))
        self.y.wait_recv()
        block = self.out_at(wire.other(4))
        part = block.at[pl.ds(split, rest)]
        self.corner_x = wire.send(part, part, wire.plane(2))
        self.core_y = wire.send(block, block, wire.plane(1))

    def corner(self):
        self.corner_y.wait_recv()
        self.corner_x.wait_recv()
        block = self.out_at(self.wire.other(6))
        self.core_corner = self.wire.send(block, block, self.wire.plane(1))

    def settle(self):
        self.core.wait_recv()
        self.core_x.wait_recv()
        self.core_y.wait_recv()
        self.core_corner.wait_recv()


def half_rows(rows, turn):
    low_half = rows // 32 * 16
    return low_half if turn % 2 else rows - low_half


def add_low(first, second):
    return (first.astype(jnp.float32) + second.astype(jnp.float32)).astype(jnp.bfloat16)


class PlaneSum:
    COPIES = 7

    def __init__(self, wire, source, own, pair, first, second, local_sem):
        self.wire, self.own, self.pair, self.first, self.second = wire, own, pair, first, second
        core = lax.rem(wire.ctx, 2)
        self.chips = {mask: wire.other(2 * mask) // 2 for mask in range(4)}
        self.swap = wire.send(source.at[:, :, 1 - core], pair, wire.plane(1))
        self.local = pltpu.make_async_copy(source.at[:, :, core], own, local_sem)
        self.local.start()

    def step_one(self):
        wire, own, pair, first, chips = self.wire, self.own, self.pair, self.first, self.chips
        self.local.wait()
        self.swap.wait_recv()

        def add_pair(index, carry):
            part, other = index // 4, lax.rem(index, 4)
            own[part, other] = add_low(own[part, other], pair[part, other])
            return carry

        lax.fori_loop(0, 16, add_pair, 0)
        low, high = pl.ds(0, 2), pl.ds(2, 2)
        self.one = [
            wire.send(own.at[low, chips[3]], first.at[0, 1], wire.plane(2)),
            wire.send(own.at[high, chips[3]], first.at[1, 1], wire.plane(4)),
            wire.send(own.at[low, chips[1]], first.at[0, 0], wire.plane(2)),
            wire.send(own.at[high, chips[2]], first.at[1, 0], wire.plane(4)),
        ]

    def step_two(self):
        wire, own, first, second, chips = self.wire, self.own, self.first, self.second, self.chips
        self.one[0].wait_recv()
        for part in range(2):
            own[part, chips[2]] = add_low(own[part, chips[2]], first[0, 1, part])
        self.two = [wire.send(own.at[pl.ds(0, 2), chips[2]], second.at[pl.ds(0, 2)], wire.plane(4))]
        self.one[1].wait_recv()
        for part in range(2):
            own[part + 2, chips[1]] = add_low(own[part + 2, chips[1]], first[1, 1, part])
        self.two.append(
            wire.send(own.at[pl.ds(2, 2), chips[1]], second.at[pl.ds(2, 2)], wire.plane(2))
        )

    def result(self, store):
        own, first, second, chips = self.own, self.first, self.second, self.chips
        for copy in self.one[2:] + self.two:
            copy.wait_recv()
        for part in range(4):
            total = own[part, chips[0]].astype(jnp.float32)
            total += first[part // 2, 0, part % 2].astype(jnp.float32)
            total += second[part].astype(jnp.float32)
            store(part, total)


def plane_sum_scratch(rows, columns):
    shape = lambda *lead: pltpu.VMEM(lead + (rows, columns), jnp.bfloat16)
    return [shape(4, 4), shape(4, 4), shape(2, 2, 2), shape(4)]


def dma_sems(count):
    return pltpu.SemaphoreType.DMA((count,))


PLANE_PEERS = (1, 2, 4)


def comm_params(number):
    return pltpu.CompilerParams(
        collective_id=number, has_side_effects=True, vmem_limit_bytes=VMEM_LIMIT
    )


def take(values, count):
    return values[:count], values[count:]


class Relay:
    def __init__(self, source, stage, targets, sems):
        self.stage, self.targets, self.sems = stage, targets, sems
        self.load = pltpu.make_async_copy(source, stage, sems.at[0])
        self.load.start()

    def push(self):
        self.load.wait()
        self.stores = []
        for i, (part, target) in enumerate(self.targets):
            store = pltpu.make_async_copy(part, target, self.sems.at[1 + i])
            store.start()
            self.stores.append(store)

    def settle(self):
        for store in self.stores:
            store.wait()


TOKEN = (8, 128)


def token_shape():
    return jax.ShapeDtypeStruct(TOKEN, jnp.int32)


def after(token, values):
    return jnp.where(token[0, 0] != 0, jnp.zeros_like(values), values)


def share_line_kernel(
    shards, pack, in_ref, gain_a, gain_b, mlp_in, mlp_out, up_ref, in_line, gain_all, mine, up_x, up_y,
    gain_now, in_stage, packed, tiles, local_sems, load_sems, send_sems, recv_sems,
):
    wire = Wire(send_sems, recv_sems)
    ctx, shard = wire.ctx, wire.shard
    chip, core = ctx // 2, lax.rem(ctx, 2)
    chips = pack.chips
    relay = Relay(in_ref.at[ctx], in_stage, [(in_stage, in_line.at[shard])], local_sems.at[0])
    gain_now[...] = jnp.zeros_like(gain_now)
    gain_now[:1] = gain_a[...].astype(jnp.float32)
    gain_now[1:2] = gain_b[...].astype(jnp.float32)
    wire.meet(
        [wire.line(step, shards) for step in range(1, shards)] + [wire.plane(2), wire.plane(4)]
    )
    half = pack.half
    copies = [
        wire.send(up_ref.at[:, pl.ds(0, half)], up_x, wire.plane(2)),
        wire.send(up_ref.at[:, pl.ds(half, half)], up_y, wire.plane(4)),
    ]
    for source, target in ((gain_now, gain_all), (in_ref.at[ctx], in_line)):
        for step in range(1, shards):
            copies.append(wire.send(source, target.at[shard], wire.line(step, shards)))
    gain_copy = pltpu.make_async_copy(gain_now, gain_all.at[shard], local_sems.at[1, 0])
    gain_copy.start()
    relay.push()

    loads = []

    def load(source, target):
        copy = pltpu.make_async_copy(source, target, load_sems.at[len(loads)])
        copy.start()
        loads.append(copy)

    def strip(start, count):
        return pl.ds(pl.multiple_of(start, LANES), count)

    main, rest, half, tail, split = pack.main, pack.rest, pack.half, pack.tail, pack.split
    per_shard = chips * (main + rest)
    base = core * (shards * per_shard)
    for part in range(shards):
        start = base + part * per_shard
        load(mlp_in.at[:, strip(start + chips * main, chips * rest)], tiles.at[part])
        column = part * main
        if column + main <= half:
            source = mlp_in.at[:, strip(start + chip * main, main)]
            load(source, packed.at[pl.ds(0, pack.rows), pl.ds(column, main)])
            continue
        for i, at in enumerate(range(0, pack.rows, split)):
            source = mlp_in.at[pl.ds(at, split), strip(start + chip * main, main)]
            load(source, packed.at[pl.ds(pack.tail_start, split), pl.ds(i * tail + column - half, main)])
    columns = strip(core * half, half)
    for start, count, row in (
        (chip * main, main, pack.out_start),
        (chips * main + chip * rest, rest, pack.out_start + main),
    ):
        source = mlp_out.at[pl.ds(pl.multiple_of(start, 16), count), columns]
        load(source, packed.at[pl.ds(row, count), :])
    for copy in loads:
        copy.wait()
    width = chips * rest
    ends = [
        pltpu.roll(tiles[part].astype(jnp.float32), lax.rem(width - chip * rest, width), 1)[:, :rest]
        for part in range(shards)
    ]
    ends = low(jnp.concatenate(ends, axis=1))
    for i, at in enumerate(range(0, pack.rows, split)):
        column = i * tail + shards * main - half
        packed[pack.tail_start : pack.tail_start + split, column : column + shards * rest] = ends[at : at + split]
    mine_copy = pltpu.make_async_copy(packed, mine, local_sems.at[1, 1])
    mine_copy.start()
    relay.settle()
    gain_copy.wait()
    mine_copy.wait()
    for copy in copies:
        copy.wait_recv()
    wire.finish()


def gather_shards(wire, line, target, rows, shards, count):
    gathers = []
    for step in range(1, shards):
        origin = lax.rem(wire.shard + shards - step, shards)
        place = lambda who, origin=origin: target.at[origin, who]
        gathers.append(PlaneGather(wire, line.at[origin], place, rows, half_rows(rows, step + count)))
    return gathers


def relay_shards(wire, whole, line, target, stage, piece, shards, sems):
    origins = [lax.rem(wire.shard + shards - step, shards) for step in range(1, shards)]
    places = [(piece.at[origin], target.at[origin, wire.ctx]) for origin in origins]
    return [
        Relay(whole, stage, [(stage, target.at[wire.shard])], sems.at[0]),
        Relay(line, piece, places, sems.at[1]),
    ]


def complete(gathers, relays):
    for gather in gathers:
        gather.forward()
    for gather in gathers:
        gather.corner()
    for gather in gathers:
        gather.settle()
    for relay in relays:
        relay.settle()


def share_plane_kernel(
    shards, devices, in_ref, in_line, out_ref, order, lengths, frequency, in_all, out_line, *refs
):
    tables, scratch = take(refs, len(refs) - 6)
    in_stage, in_piece, out_stage, local_sems, send_sems, recv_sems = scratch
    wire = Wire(send_sems, recv_sems)
    ctx, shard = wire.ctx, wire.shard
    relays = relay_shards(wire, in_ref, in_line, in_all, in_stage, in_piece, shards, local_sems)
    relays.append(
        Relay(out_ref.at[ctx], out_stage, [(out_stage, out_line.at[shard])], local_sems.at[2])
    )
    wire.meet(
        [wire.plane(mask) for mask in PLANE_PEERS] + [wire.line(s, shards) for s in range(1, shards)]
    )
    gathers = gather_shards(wire, in_line, in_all, in_ref.shape[1], shards, 0)
    copies = [
        wire.send(out_ref.at[ctx], out_line.at[shard], wire.line(step, shards))
        for step in range(1, shards)
    ]
    for relay in relays:
        relay.push()
    place_tables(ctx, devices, order, lengths, frequency, *tables)
    complete(gathers, relays)
    for copy in copies:
        copy.wait_recv()
    wire.finish()


def gather_plane_kernel(
    shards, kv_ref, out_ref, out_line, kv_all, out_all, token,
    kv_stage, out_stage, out_piece, local_sems, send_sems, recv_sems,
):
    wire = Wire(send_sems, recv_sems)
    ctx = wire.ctx
    relays = relay_shards(wire, out_ref, out_line, out_all, out_stage, out_piece, shards, local_sems)
    relays.append(Relay(kv_ref, kv_stage, [(kv_stage, kv_all.at[ctx])], local_sems.at[2]))
    token[...] = jnp.zeros_like(token)
    wire.meet([wire.plane(mask) for mask in PLANE_PEERS])
    rows = kv_ref.shape[0]
    gathers = [PlaneGather(wire, kv_ref, lambda who: kv_all.at[who], rows, rows // 2)]
    gathers += gather_shards(wire, out_line, out_all, out_ref.shape[1], shards, 1)
    for relay in relays:
        relay.push()
    complete(gathers, relays)
    wire.finish()


def like(values, *lead):
    return jax.ShapeDtypeStruct(lead + values.shape[-2:], values.dtype)


def stage_like(values, *lead):
    return pltpu.VMEM(lead + values.shape[-2:], values.dtype)


def share_line(w_in, gain_a, gain_b, mlp_in, mlp_out, upstream, pack, shards):
    columns = gain_a.shape[1]
    copies = 2 * (shards - 1) + 2
    loads = shards + shards + 1 + 2
    return pl.pallas_call(
        functools.partial(share_line_kernel, shards, pack),
        name="share_line",
        in_specs=[ANY] + [pl.BlockSpec(memory_space=pltpu.VMEM)] * 2 + [ANY] * 3,
        out_specs=[ANY] * 5,
        out_shape=[
            like(w_in, shards),
            jax.ShapeDtypeStruct((shards, 8, columns), jnp.float32),
            jax.ShapeDtypeStruct((pack.total, pack.half), mlp_in.dtype),
        ]
        + [jax.ShapeDtypeStruct((upstream.shape[0], pack.half), upstream.dtype)] * 2,
        scratch_shapes=[
            pltpu.VMEM((8, columns), jnp.float32),
            stage_like(w_in),
            pltpu.VMEM((pack.total, pack.half), mlp_in.dtype),
            pltpu.VMEM((shards, pack.rows, pack.chips * pack.rest), mlp_in.dtype),
            pltpu.SemaphoreType.DMA((2, 2)),
            dma_sems(loads),
            dma_sems(copies),
            dma_sems(copies),
        ],
        compiler_params=comm_params(1),
    )(w_in, gain_a, gain_b, mlp_in, mlp_out, upstream)


def share_plane(w_in, in_line, w_out, order, lengths, rows, ctx_size, shards):
    copies = (shards - 1) * (PlaneGather.COPIES + 1)
    operands, shapes = place_arrays(order, lengths, rows)
    vmem = pl.BlockSpec(memory_space=pltpu.VMEM)
    return pl.pallas_call(
        functools.partial(share_plane_kernel, shards, ctx_size),
        name="share_plane",
        in_specs=[ANY] * 3 + [vmem] * len(operands),
        out_specs=[ANY] * 2 + [vmem] * len(shapes),
        out_shape=[like(w_in, shards, ctx_size), like(w_out, shards), *shapes],
        scratch_shapes=[
            stage_like(w_in, ctx_size),
            stage_like(w_in, shards),
            stage_like(w_out),
            pltpu.SemaphoreType.DMA((3, shards)),
            dma_sems(copies),
            dma_sems(copies),
        ],
        compiler_params=comm_params(6),
    )(w_in, in_line, w_out, *operands)


def gather_plane(key_value, w_out, out_line, ctx_size, shards):
    copies = shards * PlaneGather.COPIES
    return pl.pallas_call(
        functools.partial(gather_plane_kernel, shards),
        name="gather_plane",
        in_specs=[ANY] * 3,
        out_specs=[ANY] * 2 + [pl.BlockSpec(memory_space=pltpu.VMEM)],
        out_shape=[like(key_value, ctx_size), like(w_out, shards, ctx_size), token_shape()],
        scratch_shapes=[
            stage_like(key_value),
            stage_like(w_out, ctx_size),
            stage_like(w_out, shards),
            pltpu.SemaphoreType.DMA((3, shards)),
            dma_sems(copies),
            dma_sems(copies),
        ],
        compiler_params=comm_params(2),
    )(key_value, w_out, out_line)


class GainSum:
    def __init__(self, wire, now, arrived, line, shards):
        self.wire, self.now, self.arrived, self.line, self.shards = wire, now, arrived, line, shards
        self.at = 0
        self.start()

    def start(self):
        peer = self.wire.plane(PLANE_PEERS[self.at])
        self.copy = self.wire.send(self.now, self.arrived.at[self.at], peer)

    def add(self):
        self.copy.wait_recv()
        self.wire.sent(self.copy)
        self.now[...] += self.arrived[self.at]
        self.at += 1

    def step(self):
        self.add()
        self.start()

    def step_line(self):
        self.add()
        wire, shards = self.wire, self.shards
        self.copies = [
            wire.send(
                self.now.at[lax.rem(wire.shard + step, shards)],
                self.line.at[step - 1],
                wire.line(step, shards),
            )
            for step in range(1, shards)
        ]

    def result(self):
        for copy in self.copies:
            copy.wait_recv()
        value = self.now[self.wire.shard]
        for step in range(self.shards - 1):
            value += self.line[step]
        return value


def reduce_kernel(shards, plane_count, half_count, line_count, full_count, part_count, gain_count, *refs):
    planes, refs = take(refs, plane_count)
    halves, refs = take(refs, half_count)
    line_ins, refs = take(refs, line_count)
    fulls, refs = take(refs, full_count)
    parts, refs = take(refs, part_count)
    gain_rows, refs = take(refs, gain_count)
    plane_outs, refs = take(refs, plane_count)
    half_outs, refs = take(refs, half_count)
    full_outs, refs = take(refs, line_count + full_count)
    part_outs, refs = take(refs, part_count)
    gain_out, refs = take(refs, min(gain_count, 1))
    sums, refs = take(refs, 4 * (plane_count + half_count + full_count))
    mine, refs = take(refs, full_count)
    arrived, refs = take(refs, line_count + full_count)
    done, refs = take(refs, line_count + full_count)
    stages, refs = take(refs, part_count)
    gain_scratch, refs = take(refs, 3 * min(gain_count, 1))
    sum_sems, done_sems, part_sems, send_sems, recv_sems = refs

    wire = Wire(send_sems, recv_sems)
    ctx, shard = wire.ctx, wire.shard
    relays = [
        Relay(source, stage, [(stage, target.at[ctx])], part_sems.at[i])
        for i, (source, stage, target) in enumerate(zip(parts, stages, part_outs))
    ]
    if gain_count:
        gain_now = gain_scratch[0]
        gain_now[...] = jnp.zeros_like(gain_now)
        columns = gain_now.shape[2]
        for part in range(shards):
            for row, values in enumerate(gain_rows):
                gain_now[part, row : row + 1] = values[:, part * columns : (part + 1) * columns]
    wire.meet(
        [wire.plane(mask) for mask in PLANE_PEERS] + [wire.line(s, shards) for s in range(1, shards)]
    )
    totals = [
        PlaneSum(wire, source, *sums[4 * i : 4 * i + 4], sum_sems.at[i])
        for i, source in enumerate(planes + halves + fulls)
    ]
    lines = []

    def send_line(source):
        target = arrived[len(lines)]
        lines.append(
            [
                wire.send(
                    source.at[lax.rem(shard + step, shards)], target.at[step - 1], wire.line(step, shards)
                )
                for step in range(1, shards)
            ]
        )

    for source in line_ins:
        send_line(source)
    gain = GainSum(wire, *gain_scratch, shards) if gain_count else None
    for total in totals:
        total.step_one()
    if gain:
        gain.step()
    for total in totals:
        total.step_two()
    if gain:
        gain.step()
    gathers = []
    for source, target in zip(parts, part_outs):
        rows = source.shape[0]
        place = lambda who, target=target: target.at[who]
        gathers.append(PlaneGather(wire, source, place, rows, half_rows(rows, len(gathers))))
    for total, target in zip(totals, plane_outs):

        def store_wide(part, value, target=target):
            target[part] = value

        total.result(store_wide)
    for total, target in zip(totals[plane_count:], half_outs + mine):

        def store(part, value, target=target):
            target[part] = low(value)

        total.result(store)
    for source in mine:
        send_line(source)
    if gain:
        gain.step_line()
    for relay in relays:
        relay.push()
    locals_ = []
    for i, (source, target) in enumerate(zip(line_ins + mine, full_outs)):
        for copy in lines[i]:
            copy.wait_recv()
        value = source[shard].astype(jnp.float32)
        for step in range(shards - 1):
            value += arrived[i][step].astype(jnp.float32)
        done[i][...] = low(value)
        place = lambda who, target=target: target.at[who]
        rows = target.shape[1]
        gathers.append(PlaneGather(wire, done[i], place, rows, half_rows(rows, i)))
        copy = pltpu.make_async_copy(done[i], place(ctx), done_sems.at[i])
        copy.start()
        locals_.append(copy)
    if gain:
        gain_out[0][...] = gain.result()
    for gather in gathers:
        gather.forward()
    for gather in gathers:
        gather.corner()
    for gather in gathers:
        gather.settle()
    for copy in locals_:
        copy.wait()
    for relay in relays:
        relay.settle()
    wire.finish()


def reduce(name, number, ctx_size, shards, planes=(), halves=(), lines=(), fulls=(), parts=(), gains=()):
    sums, mine, arrived, done = [], [], [], []
    for array in (*planes, *halves, *fulls):
        sums += plane_sum_scratch(*array.shape[3:])
    for array in fulls:
        mine.append(pltpu.VMEM((shards, *array.shape[3:]), jnp.bfloat16))
    for array in (*lines, *fulls):
        rows, columns = array.shape[-2:]
        arrived.append(pltpu.VMEM((shards - 1, rows, columns), jnp.bfloat16))
        done.append(pltpu.VMEM((rows, columns), jnp.bfloat16))
    stages = [pltpu.VMEM(part.shape, part.dtype) for part in parts]
    copies = PlaneSum.COPIES * (len(planes) + len(halves) + len(fulls))
    copies += (PlaneGather.COPIES + shards - 1) * (len(lines) + len(fulls))
    copies += PlaneGather.COPIES * len(parts)
    vmem = pl.BlockSpec(memory_space=pltpu.VMEM)
    outs = [(vmem, jax.ShapeDtypeStruct((4,) + array.shape[3:], jnp.float32)) for array in planes]
    outs += [(vmem, jax.ShapeDtypeStruct((4,) + array.shape[3:], array.dtype)) for array in halves]
    outs += [(ANY, like(array, ctx_size)) for array in (*lines, *fulls)]
    outs += [(ANY, like(part, ctx_size)) for part in parts]
    gain_scratch = []
    if gains:
        shape = (shards, 8, gains[0].shape[1] // shards)
        outs.append((vmem, jax.ShapeDtypeStruct(shape[1:], jnp.float32)))
        gain_scratch = [
            pltpu.VMEM(shape, jnp.float32),
            pltpu.VMEM((3,) + shape, jnp.float32),
            pltpu.VMEM((shards - 1,) + shape[1:], jnp.float32),
        ]
        copies += 3 + shards - 1
    return pl.pallas_call(
        functools.partial(
            reduce_kernel,
            shards,
            len(planes),
            len(halves),
            len(lines),
            len(fulls),
            len(parts),
            len(gains),
        ),
        name=name,
        in_specs=[ANY] * (len(planes) + len(halves))
        + [vmem] * len(lines)
        + [ANY] * (len(fulls) + len(parts))
        + [vmem] * len(gains),
        out_specs=[spec for spec, _ in outs],
        out_shape=[shape for _, shape in outs],
        scratch_shapes=sums + mine + arrived + done + stages + gain_scratch
        + [
            dma_sems(max(1, len(planes) + len(halves) + len(fulls))),
            dma_sems(max(1, len(lines) + len(fulls))),
            pltpu.SemaphoreType.DMA((max(1, len(parts)), 2)),
            dma_sems(copies),
            dma_sems(copies),
        ],
        compiler_params=comm_params(number),
    )(*planes, *halves, *lines, *fulls, *parts, *gains)


class Pack:
    def __init__(self, rows, half, chips, units, main, rest):
        self.rows, self.half, self.chips, self.main, self.rest = rows, half, chips, main, rest
        self.tail = units - half
        self.split = rows // (half // self.tail)
        self.out_start = rows
        self.tail_start = rows + main + rest
        self.total = self.tail_start + self.split

    def in_spans(self, shard):
        yield (0, self.rows), (0, self.half), (shard * self.rows, self.rows), (0, self.half)
        for i, at in enumerate(range(0, self.rows, self.split)):
            yield (
                (self.tail_start, self.split),
                (i * self.tail, self.tail),
                (shard * self.rows + at, self.split),
                (self.half, self.tail),
            )

    def out_spans(self, shard, shards):
        every = (0, self.half)
        yield (self.out_start, self.main), every, (shard * self.main, self.main), every
        yield (
            (self.out_start + self.main, self.rest),
            every,
            (shards * self.main + shard * self.rest, self.rest),
            every,
        )


def finish_kernel(shards, chips, pack, step_rows, main_ref, tail_ref, out_part_ref, in_ref, out_ref):
    step = pl.program_id(0)
    main, rest, half, tail = pack.main, pack.rest, pack.half, pack.tail
    per_shard = chips * (main + rest)

    def columns_of(who, start, count):
        if start + count <= half:
            return main_ref[who, :, start : start + count]
        at = start - half
        return tails[who][:, at : at + count]

    second = step >= pl.num_programs(0) // 2
    tails = [
        jnp.where(second, tail_ref[who, :, tail:], tail_ref[who, :, :tail])
        for who in range(2 * chips)
    ]
    for core in range(2):
        for shard in range(shards):
            start = (core * shards + shard) * per_shard
            for chip in range(chips):
                block = columns_of(chip * 2 + core, shard * main, main)
                in_ref[:, start + chip * main : start + (chip + 1) * main] = block.astype(jnp.float32)
            ends = [
                columns_of(chip * 2 + core, shards * main, shards * rest).astype(jnp.float32)[
                    :, shard * rest : (shard + 1) * rest
                ]
                for chip in range(chips)
            ]
            in_ref[:, start + chips * main : start + per_shard] = jnp.concatenate(ends, axis=1)

    for chip in range(chips):

        @pl.when(step == chip)
        def _(chip=chip):
            for core in range(2):
                columns = slice(core * half, (core + 1) * half)
                block = out_part_ref[core]
                out_ref[chip * main : (chip + 1) * main, columns] = block[:main].astype(jnp.float32)
                start = chips * main + chip * rest
                out_ref[start : start + rest, columns] = block[main:].astype(jnp.float32)


def finish(first, second, pack, shards):
    ctx_size = first.shape[0]
    chips = ctx_size // 2
    steps = 8
    tile = pack.rows // steps
    per_out = pack.main + pack.rest
    assert pack.rows // pack.split == 2 and pack.split % tile == 0 and per_out % tile == 0
    return pl.pallas_call(
        functools.partial(finish_kernel, shards, chips, pack, tile),
        name="finish",
        grid=(steps,),
        in_specs=[
            pl.BlockSpec((ctx_size, tile, pack.half), lambda i: (0, i, 0)),
            pl.BlockSpec(
                (ctx_size, tile, pack.half),
                lambda i: (0, per_out // tile + i % (pack.split // tile), 0),
            ),
            pl.BlockSpec((2, per_out, pack.half), lambda i: (jnp.minimum(i, chips - 1), 0, 0)),
        ],
        out_specs=[
            pl.BlockSpec((tile, 2 * FF), lambda i: (i, 0)),
            whole_block((FF // shards, 2 * pack.half)),
        ],
        out_shape=[
            jax.ShapeDtypeStruct((pack.rows, 2 * FF), jnp.float32),
            jax.ShapeDtypeStruct((FF // shards, 2 * pack.half), jnp.float32),
        ],
        compiler_params=pltpu.CompilerParams(vmem_limit_bytes=VMEM_LIMIT),
    )(first, second, second)


TANH_SCALE = 0.7978845608028654
TANH_CUBE = 0.044715
UNIT_TILE = 384


def mlp_kernel(
    shards, pack, mine, x_own, x_x, x_y, c_own, c_x_left, c_x_right, c_y_left, c_y_right, c_left, c_right,
    normed_grad, out_own, out_x, out_y, out_left, out_right, grad_main, grad_rest,
    w_in, w_out, xs, cs, hidden, grads, part, from_x, from_y, corner_left, corner_right,
    out_stage, pair_in, pair_out, local_sems, send_sems, recv_sems,
):
    wire = Wire(send_sems, recv_sems)
    core = lax.rem(wire.ctx, 2)
    other = 1 - core
    rows, width = x_own.shape
    half = width // 2
    units = w_in.shape[2]
    tiles = units // UNIT_TILE
    left, right = pl.ds(0, half), pl.ds(half, half)
    locals_ = []

    def copy_in(source, target):
        copy = pltpu.make_async_copy(source, target, local_sems.at[len(locals_)])
        copy.start()
        locals_.append(copy)
        return copy

    def spans():
        for shard in range(shards):
            for one in pack.in_spans(shard):
                yield shard, w_in, one
            for one in pack.out_spans(shard, shards):
                yield shard, w_out, one

    def packed(shard, one):
        return mine.at[shard, pl.ds(*one[0]), pl.ds(*one[1])]

    def placed(which, target, one):
        return target.at[which, pl.ds(*one[2]), pl.ds(*one[3])]

    loads = [copy_in(x_own, xs.at[0]), copy_in(c_own, cs.at[0])]
    for shard, target, one in spans():
        loads.append(copy_in(packed(shard, one), placed(core, target, one)))
    late = [
        copy_in(source, target)
        for source, target in (
            (x_x, xs.at[1, :, left]),
            (x_y, xs.at[2, :, right]),
            (c_x_left, cs.at[1, :, left]),
            (c_x_right, cs.at[1, :, right]),
            (c_y_left, cs.at[2, :, left]),
            (c_y_right, cs.at[2, :, right]),
            (c_left, cs.at[3, :, left]),
            (c_right, cs.at[3, :, right]),
        )
    ]
    wire.meet([wire.plane(mask) for mask in PLANE_PEERS])
    x_copies = [
        wire.send(x_own.at[:, right], xs.at[1, :, right], wire.plane(2)),
        wire.send(x_own.at[:, left], xs.at[2, :, left], wire.plane(4)),
    ]
    swaps = [
        wire.send(packed(shard, one), placed(core, target, one), wire.plane(1))
        for shard, target, one in spans()
    ]
    for copy in loads:
        copy.wait()
    for copy in swaps:
        copy.wait_recv()

    def one_chunk(at):
        gate = dot(xs[at], w_in[0])
        up = dot(xs[at], w_in[1])
        grad = nt_dot(cs[at, :, left], w_out[0]) + nt_dot(cs[at, :, right], w_out[1])
        square = gate * gate
        bend = jnp.tanh(TANH_SCALE * gate * (1.0 + TANH_CUBE * square))
        lift = 0.5 + 0.5 * bend
        value = gate * lift
        slope = lift + (0.5 * TANH_SCALE) * gate * (1.0 - bend * bend) * (
            1.0 + (3.0 * TANH_CUBE) * square
        )
        hidden[at] = low(value * up)
        grads[0, at] = low(grad * up * slope)
        grads[1, at] = low(grad * value)

        def one_half(span):
            total = nt_dot(grads[0, at], w_in[0, span, :])
            return total + nt_dot(grads[1, at], w_in[1, span, :])

        return one_half

    one_half = one_chunk(0)
    for span in (left, right):
        normed_grad[:, span] = one_half(span)
    for copy in x_copies:
        copy.wait_recv()
    corners = [
        wire.send(x_x, xs.at[3, :, left], wire.plane(4)),
        wire.send(x_y, xs.at[3, :, right], wire.plane(2)),
    ]
    for copy in late:
        copy.wait()
    one_half = one_chunk(1)
    part[0, :, left] = low(one_half(left))
    early = [wire.send(part.at[0, :, left], from_x.at[:, left], wire.plane(2))]
    part[0, :, right] = low(one_half(right))
    one_half = one_chunk(2)
    part[1, :, right] = low(one_half(right))
    early.append(wire.send(part.at[1, :, right], from_y.at[:, right], wire.plane(4)))
    part[1, :, left] = low(one_half(left))
    for copy in corners:
        copy.wait_recv()
    one_half = one_chunk(3)
    part[2, :, left] = low(one_half(left))
    corner = [wire.send(part.at[2, :, left], corner_left, wire.plane(2))]
    part[2, :, right] = low(one_half(right))
    corner.append(wire.send(part.at[2, :, right], corner_right, wire.plane(4)))

    out_copies = {}

    def out_part(at, targets):
        slot = at % 2
        for copy in out_copies.get(slot, ()):
            copy.wait()
        for n, span in enumerate((left, right)):
            out_stage[slot, :, span] = low(dot(hidden[at], w_out[n]))
        out_copies[slot] = [copy_in(out_stage.at[(slot,) + here], target) for here, target in targets]

    every = slice(None)
    out_part(3, [((every, left), out_left), ((every, right), out_right)])
    out_part(2, [((), out_y)])
    out_part(1, [((), out_x)])
    out_part(0, [((), out_own)])

    everything = lambda ref: ref[...].reshape(ref.shape[0] * rows, ref.shape[2])

    def in_tile(which, tile):
        columns = pl.ds(tile * UNIT_TILE, UNIT_TILE)
        picked = grads[which, :, :, columns].reshape(4 * rows, UNIT_TILE)
        return columns, tn_dot(everything(xs), picked)

    pairs_in = []
    for tile in range(tiles):
        columns, value = in_tile(other, tile)
        w_in[0, :, columns] = low(value)
        pairs_in.append(wire.send(w_in.at[0, :, columns], pair_in.at[:, columns], wire.plane(1)))
    merged = []
    corner[0].wait_recv()
    part[1, :, left] = add_low(part[1, :, left], corner_left[...])
    merged.append(wire.send(part.at[1, :, left], from_y.at[:, left], wire.plane(4)))
    corner[1].wait_recv()
    part[0, :, right] = add_low(part[0, :, right], corner_right[...])
    merged.append(wire.send(part.at[0, :, right], from_x.at[:, right], wire.plane(2)))

    def out_tile(which, tile):
        columns = pl.ds(tile * UNIT_TILE, UNIT_TILE)
        picked = hidden[:, :, columns].reshape(4 * rows, UNIT_TILE)
        span = pl.ds(pl.multiple_of(which * half, half), half)
        return columns, tn_dot(picked, cs[:, :, span].reshape(4 * rows, half))

    pairs_out = []
    for tile in range(tiles):
        span, value = out_tile(other, tile)
        w_out[0, span, :] = low(value)
        pairs_out.append(wire.send(w_out.at[0, span, :], pair_out.at[span, :], wire.plane(1)))
    final = []
    for tile in range(tiles):
        columns, value = in_tile(core, tile)
        pairs_in[tile].wait_recv()
        w_in[1, :, columns] = low(value + pair_in[:, columns].astype(jnp.float32))
    for tile in range(tiles):
        span, value = out_tile(core, tile)
        pairs_out[tile].wait_recv()
        w_out[1, span, :] = low(value + pair_out[span, :].astype(jnp.float32))
    for shard, source, one in spans():
        start, count = one[0]
        if start < pack.rows:
            target = grad_main.at[shard, pl.ds(start, count), pl.ds(*one[1])]
        else:
            target = grad_rest.at[shard, pl.ds(start - pack.rows, count), pl.ds(*one[1])]
        final.append(copy_in(placed(1, source, one), target))
    for copy in early + merged:
        copy.wait_recv()
    normed_grad[...] += from_x[...].astype(jnp.float32) + from_y[...].astype(jnp.float32)
    for copies in out_copies.values():
        for copy in copies:
            copy.wait()
    for copy in final:
        copy.wait()
    wire.finish()


def mlp(mine, x, upstream, pack):
    rows, width = x[0].shape
    half = width // 2
    units = pack.half + pack.tail
    shards = mine.shape[0]
    low_shape = lambda *shape: jax.ShapeDtypeStruct(shape, jnp.bfloat16)
    low_scratch = lambda *shape: pltpu.VMEM(shape, jnp.bfloat16)
    parts = shards * (1 + pack.rows // pack.split + 2)
    copies = parts + 4 + 2 + 2 + 2 + 2 * (units // UNIT_TILE)
    locals_ = 2 + parts + 8 + 5 + parts
    return pl.pallas_call(
        functools.partial(mlp_kernel, shards, pack),
        name="mlp",
        in_specs=[ANY] * 11,
        out_specs=[pl.BlockSpec(memory_space=pltpu.VMEM)] + [ANY] * 7,
        out_shape=[
            jax.ShapeDtypeStruct((rows, width), jnp.float32),
            low_shape(rows, width),
            low_shape(rows, width),
            low_shape(rows, width),
            low_shape(rows, half),
            low_shape(rows, half),
            low_shape(shards, pack.rows, half),
            low_shape(shards, pack.total - pack.rows, half),
        ],
        scratch_shapes=[
            low_scratch(2, width, units),
            low_scratch(2, units, half),
            low_scratch(4, rows, width),
            low_scratch(4, rows, width),
            low_scratch(4, rows, units),
            low_scratch(2, 4, rows, units),
            low_scratch(3, rows, width),
            low_scratch(rows, width),
            low_scratch(rows, width),
            low_scratch(rows, half),
            low_scratch(rows, half),
            low_scratch(2, rows, width),
            low_scratch(width, units),
            low_scratch(units, half),
            dma_sems(locals_),
            dma_sems(copies),
            dma_sems(copies),
        ],
        compiler_params=pltpu.CompilerParams(
            collective_id=5, has_side_effects=True, vmem_limit_bytes=MLP_VMEM
        ),
    )(mine, *x, *upstream)


class Layout:
    def __init__(self, ctx_size, fsdp_size):
        self.ctx_size = ctx_size
        self.shards = fsdp_size
        self.chips = ctx_size // 2
        self.index = lax.axis_index("ctx")
        self.chip = self.index // 2
        self.core = self.index % 2
        units = FF // (self.shards * self.chips)
        self.main = units // LANES * LANES
        self.rest = units - self.main
        self.per_shard = FF // self.shards
        self.rest_start = self.chips * self.main
        self.plane = ctx_size == 8 and fsdp_size == 4

    def xor(self, values, mask):
        pairs = [(i, i ^ mask) for i in range(self.ctx_size)]
        return lax.ppermute(values, "ctx", pairs)

    def same_core_groups(self):
        return [[chip * 2 + core for chip in range(self.chips)] for core in range(2)]

    def join_corner(self, to_x, to_y, left, right, token):
        half = left.shape[1]
        left = after(token, self.xor(left, 2))
        right = after(token, self.xor(right, 4))
        to_y = jnp.concatenate([add_low(to_y[:, :half], left), to_y[:, half:]], axis=1)
        to_x = jnp.concatenate([to_x[:, :half], add_low(to_x[:, half:], right)], axis=1)
        return to_x, to_y

    def sum_neighbours(self, own, to_x, to_y):
        wide = lambda part: part.astype(jnp.float32)
        return wide(own) + wide(self.xor(to_y, 4)) + wide(self.xor(to_x, 2))

    def gather_chips(self, values):
        groups = self.same_core_groups()
        return lax.all_gather(values, "ctx", axis=0, tiled=True, axis_index_groups=groups)

    def scatter_chips(self, partial):
        groups = self.same_core_groups()
        total = lax.psum_scatter(
            low(partial), "ctx", scatter_dimension=0, tiled=True, axis_index_groups=groups
        )
        return total.astype(jnp.float32)

    def columns_of_chip(self, weights, start):
        parts = []
        if self.main:
            for shard in range(self.shards):
                at = start + shard * self.per_shard + self.chip * self.main
                parts.append(lax.dynamic_slice_in_dim(weights, at, self.main, 1))
        if self.rest:
            for shard in range(self.shards):
                at = start + shard * self.per_shard + self.rest_start + self.chip * self.rest
                parts.append(lax.dynamic_slice_in_dim(weights, at, self.rest, 1))
        return jnp.concatenate(parts, axis=1)

    def rows_of_chip(self, weights):
        parts = []
        if self.main:
            parts.append(lax.dynamic_slice_in_dim(weights, self.chip * self.main, self.main, 0))
        if self.rest:
            at = self.rest_start + self.chip * self.rest
            parts.append(lax.dynamic_slice_in_dim(weights, at, self.rest, 0))
        return jnp.concatenate(parts, axis=0)

    def by_core(self, mine, other):
        first = jnp.where(self.core == 0, mine, other)
        second = jnp.where(self.core == 0, other, mine)
        return first, second

    def mine_in(self, shard, later=0):
        return self.columns_of_chip(shard, self.core * FF + later)

    def mine_out(self, shard, later=0):
        width = shard.shape[1]
        half = lax.dynamic_slice_in_dim(shard, self.core * (width // 2) + later, width // 2, 1)
        return self.rows_of_chip(half)

    def gather_mlp_in(self, shard):
        mine = lax.all_gather(self.mine_in(shard), "fsdp", axis=0, tiled=True)
        return self.by_core(mine, self.xor(mine, 1))

    def gather_mlp_out(self, shard):
        width = shard.shape[1]
        mine = lax.all_gather(self.mine_out(shard), "fsdp", axis=0)
        mine = jnp.concatenate(
            [
                mine[:, : self.main].reshape(self.shards * self.main, width // 2),
                mine[:, self.main :].reshape(self.shards * self.rest, width // 2),
            ],
            axis=0,
        )
        return jnp.concatenate(self.by_core(mine, self.xor(mine, 1)), axis=1)

    def sum_pair(self, first, second):
        keep = jnp.where(self.core == 0, first, second)
        send = jnp.where(self.core == 0, second, first)
        return keep + self.xor(low(send), 1).astype(jnp.float32)

    def reduce_mlp_in(self, gate, up):
        total = low(self.sum_pair(gate, up))
        return lax.psum_scatter(total, "fsdp", scatter_dimension=0, tiled=True)

    def order_mlp_in(self, every):
        rows = every.shape[1]
        every = every.reshape(self.chips, 2, rows, every.shape[2])
        split = self.shards * self.main
        main = every[..., :split].reshape(self.chips, 2, rows, self.shards, self.main)
        rest = every[..., split:].reshape(self.chips, 2, rows, self.shards, self.rest)
        main = main.transpose(2, 1, 3, 0, 4).reshape(rows, 2, self.shards, -1)
        rest = rest.transpose(2, 1, 3, 0, 4).reshape(rows, 2, self.shards, -1)
        return jnp.concatenate([main, rest], axis=3).reshape(rows, 2 * FF).astype(jnp.float32)

    def reduce_mlp_out(self, grad):
        width = grad.shape[1]
        total = low(self.sum_pair(grad[:, : width // 2], grad[:, width // 2 :]))
        split = self.shards * self.main
        main = total[:split].reshape(self.shards, self.main, width // 2)
        rest = total[split:].reshape(self.shards, self.rest, width // 2)
        total = jnp.concatenate([main, rest], axis=1)
        return lax.psum_scatter(total, "fsdp", scatter_dimension=0, tiled=True)[0]

    def order_mlp_out(self, every):
        width = 2 * every.shape[2]
        every = every.reshape(self.chips, 2, self.main + self.rest, width // 2)
        main = every[:, :, : self.main].transpose(0, 2, 1, 3).reshape(-1, width)
        rest = every[:, :, self.main :].transpose(0, 2, 1, 3).reshape(-1, width)
        return jnp.concatenate([main, rest], axis=0).astype(jnp.float32)

    def gather_whole(self, shard):
        rows = shard.shape[0] // self.ctx_size
        piece = lax.dynamic_slice_in_dim(shard, self.index * rows, rows, 0)
        piece = lax.all_gather(piece, "fsdp", axis=0)
        piece = lax.all_gather(piece, "ctx", axis=1, tiled=True)
        return piece.reshape(-1, shard.shape[1])

    def reduce_whole(self, grad):
        rows = grad.shape[0] // self.shards
        total = grad.reshape(self.shards, rows, grad.shape[1])
        total = lax.psum_scatter(total, "ctx", scatter_dimension=1, tiled=True)
        total = lax.psum_scatter(total, "fsdp", scatter_dimension=0, tiled=True)[0]
        return lax.all_gather(total, "ctx", axis=0, tiled=True).astype(jnp.float32)

    def reduce_gain(self, grad):
        total = jnp.sum(lax.all_gather(grad, ("ctx", "fsdp"), axis=0), axis=0)
        rows = grad.shape[0] // self.shards
        return lax.dynamic_slice_in_dim(total, lax.axis_index("fsdp") * rows, rows)


def per_device(
    ctx_size,
    fsdp_size,
    tokens,
    order,
    lengths,
    norm_attn,
    w_attn_in,
    w_attn_out,
    norm_mlp,
    w_mlp_in,
    w_mlp_out,
    cotangent,
):
    lay = Layout(ctx_size, fsdp_size)
    x, upstream = tokens[0], cotangent[0]
    own_rows, width = x.shape
    block = own_rows // ROUNDS
    if lay.plane:
        pack = Pack(w_mlp_in.shape[0], width // 2, lay.chips, FF // lay.chips, lay.main, lay.rest)
        pieces = lambda w: w.reshape(ctx_size, w.shape[0] // ctx_size, w.shape[1])
        in_line, gains, mine, upstream_x, upstream_y = share_line(
            pieces(w_attn_in),
            norm_attn[None],
            norm_mlp[None],
            w_mlp_in,
            w_mlp_out,
            upstream,
            pack,
            fsdp_size,
        )
        mine = lax.all_gather(mine, "fsdp", axis=0)
        in_attn, out_line, *tables = share_plane(
            pieces(w_attn_in),
            in_line,
            pieces(w_attn_out),
            order,
            lengths,
            own_rows,
            ctx_size,
            fsdp_size,
        )
        in_attn = in_attn.reshape(width, -1)
    else:
        tables = place_tables_alone(ctx_size, order, lengths, own_rows)
        in_attn = lay.gather_whole(w_attn_in)
        out_attn = lay.gather_whole(w_attn_out)
        gains = jnp.pad(jnp.stack([norm_attn, norm_mlp]).astype(jnp.float32), ((0, 6), (0, 0)))
        gains = lax.all_gather(gains, "fsdp", axis=0)
        gate_in, up_in = lay.gather_mlp_in(w_mlp_in)
        out_mlp = lay.gather_mlp_out(w_mlp_out)
        upstream_all = lay.gather_chips(upstream)

    where, key_place, bounds, bounds_wide, cosine, sine_part = tables
    normed_one, queries, key_value = project(x, gains, in_attn, cosine, sine_part)
    if lay.plane:
        key_value, out_attn, token = gather_plane(
            key_value, pieces(w_attn_out), out_line, ctx_size, fsdp_size
        )
        out_attn = out_attn.reshape(-1, width)
        half = width // 2
        upstream_all = (
            upstream,
            upstream_x,
            lay.xor(after(token, upstream[:, half:]), 2),
            lay.xor(after(token, upstream[:, :half]), 4),
            upstream_y,
            lay.xor(after(token, upstream_x), 4),
            lay.xor(after(token, upstream_y), 2),
        )
    else:
        key_value = lax.all_gather(key_value, "ctx", axis=0)
    key_value = key_value.reshape(ctx_size * ROUNDS, block, 2 * HD)
    mixed, log_total = attend(where, queries, key_value, key_place, bounds)
    middle, normed_two = middle_forward(x, mixed, gains, out_attn)

    if lay.plane:
        grad_normed_two, out_own, *out_parts, grad_main, grad_rest = mlp(
            mine,
            (normed_two, lay.xor(normed_two[:, :half], 2), lay.xor(normed_two[:, half:], 4)),
            upstream_all,
            pack,
        )
        grad_main = lax.psum_scatter(grad_main, "fsdp", scatter_dimension=0, tiled=True)[0]
        grad_rest = lax.psum_scatter(grad_rest, "fsdp", scatter_dimension=0, tiled=True)[0]
    else:
        normed_all = lay.gather_chips(normed_two)
        gate = dot(normed_all, gate_in)
        up = dot(normed_all, up_in)
        hidden, hidden_back = jax.vjp(geglu, gate, up)
        hidden = low(hidden)
        grad_hidden = dot_nt(upstream_all, out_mlp)
        grad_gate, grad_up = hidden_back(grad_hidden)
        grad_gate = low(grad_gate)
        grad_up = low(grad_up)
        grad_normed_two = lay.scatter_chips(dot_nt(grad_gate, gate_in) + dot_nt(grad_up, up_in))
        mixed_out = lay.scatter_chips(dot(hidden, out_mlp))
        grad_out_mlp = lay.reduce_mlp_out(dot_tn(hidden, upstream_all))
        grad_in_mlp = lay.reduce_mlp_in(dot_tn(normed_all, grad_gate), dot_tn(normed_all, grad_up))

    grad_middle, grad_mixed, grad_out_attn, grad_gain_mlp, token = middle_back(
        grad_normed_two, middle, upstream, mixed, gains, out_attn
    )
    out_parts = lay.join_corner(*out_parts, token) if lay.plane else ()
    grad_query, grad_kv = attend_back(
        where,
        queries,
        key_value,
        grad_mixed,
        mixed,
        log_total,
        key_place,
        bounds_wide,
        cosine,
        sine_part,
        out_parts,
    )
    if lay.plane:
        mixed_out = lay.sum_neighbours(out_own, *out_parts)
    result = middle + mixed_out
    grad_in_queries, grad_normed = project_back_queries(grad_query, normed_one, in_attn)
    split = lambda grad: grad.reshape(fsdp_size, lay.chips, 2, -1, grad.shape[1])
    if lay.plane:
        grad_kv = grad_kv.reshape(ROUNDS, lay.chips, 2, block, 2 * HD)
        grad_kv, grad_out_attn, grad_in_queries, grad_main = reduce(
            "reduce_early",
            3,
            ctx_size,
            fsdp_size,
            planes=[grad_kv],
            halves=[split(grad_out_attn), split(grad_in_queries)],
            parts=[grad_main],
        )
        grad_kv = grad_kv.reshape(own_rows, 2 * HD)
    else:
        grad_kv = grad_kv.reshape(ROUNDS, ctx_size, block, 2 * HD)
        grad_kv = lax.psum_scatter(grad_kv, "ctx", scatter_dimension=1, tiled=True)
        grad_kv = grad_kv.reshape(own_rows, 2 * HD).astype(jnp.float32)
    grad_in_keys, grad_inputs, grad_gain_attn = project_back_keys(
        grad_kv, cosine, sine_part, normed_one, grad_normed, x, grad_middle, gains, in_attn
    )
    if lay.plane:
        grad_out_attn, grad_in_queries, grad_in_keys, grad_rest, grad_gains = reduce(
            "reduce_late",
            4,
            ctx_size,
            fsdp_size,
            lines=[grad_out_attn, grad_in_queries],
            fulls=[split(grad_in_keys)],
            parts=[grad_rest],
            gains=[grad_gain_attn, grad_gain_mlp],
        )
        whole = lambda grad: grad.reshape(-1, grad.shape[2]).astype(jnp.float32)
        grad_out_attn = whole(grad_out_attn)
        grad_in_attn = jnp.concatenate([whole(grad_in_queries), whole(grad_in_keys)], axis=1)
        grad_in_mlp, grad_out_mlp = finish(grad_main, grad_rest, pack, fsdp_size)
        grad_gain_attn, grad_gain_mlp = grad_gains[0], grad_gains[1]
    else:
        grad_in_attn = jnp.concatenate([grad_in_queries, grad_in_keys], axis=1)
        grad_out_attn = lay.reduce_whole(grad_out_attn)
        grad_in_attn = lay.reduce_whole(grad_in_attn)
        grad_in_mlp = lay.order_mlp_in(lax.all_gather(grad_in_mlp, "ctx", axis=0))
        grad_out_mlp = lay.order_mlp_out(lax.all_gather(grad_out_mlp, "ctx", axis=0))
        grad_gain_attn = lay.reduce_gain(grad_gain_attn[0])
        grad_gain_mlp = lay.reduce_gain(grad_gain_mlp[0])
    return (
        low(result)[None],
        grad_inputs[None],
        grad_gain_attn,
        grad_in_attn,
        grad_out_attn,
        grad_gain_mlp,
        grad_in_mlp,
        grad_out_mlp,
    )


def solution(mesh):
    in_specs = (
        P("fsdp", "ctx", None),
        P("fsdp", None),
        P("fsdp", None),
        P("fsdp"),
        P("fsdp", None),
        P("fsdp", None),
        P("fsdp"),
        P("fsdp", None),
        P("fsdp", None),
        P("fsdp", "ctx", None),
    )
    out_specs = (
        P("fsdp", "ctx", None),
        P("fsdp", "ctx", None),
        P("fsdp"),
        P("fsdp", None),
        P("fsdp", None),
        P("fsdp"),
        P("fsdp", None),
        P("fsdp", None),
    )

    def run(*arrays):
        return per_device(mesh.shape["ctx"], mesh.shape["fsdp"], *arrays)

    return jax.shard_map(run, mesh=mesh, in_specs=in_specs, out_specs=out_specs, check_vma=False)
```

```python
import functools

import jax
import jax.numpy as jnp
from jax import lax
from jax.experimental import pallas as pl
from jax.experimental.pallas import tpu as pltpu
from jax.sharding import PartitionSpec as P

H = 12
HD = 128
FF = 4608
WINDOW = 1024
ROUNDS = 4
LANES = 128


EPS = 1e-06


def rms_norm(values, gain):
    return values * lax.rsqrt(jnp.mean(values * values, axis=-1, keepdims=True) + EPS) * gain


def geglu(gate, up):
    return jax.nn.gelu(gate, approximate=True) * up


def dot(left, right):
    return jnp.dot(left, right, preferred_element_type=jnp.float32)


def dot_nt(left, right):
    return jnp.einsum("ab,cb->ac", left, right, preferred_element_type=jnp.float32)


def dot_tn(left, right):
    return jnp.einsum("ab,ac->bc", left, right, preferred_element_type=jnp.float32)


def nt_dot(left, right):
    return lax.dot_general(left, right, (((1,), (1,)), ((), ())), preferred_element_type=jnp.float32)


def tn_dot(left, right):
    return lax.dot_general(left, right, (((0,), (0,)), ((), ())), preferred_element_type=jnp.float32)


def low(values):
    return values.astype(jnp.bfloat16)


VMEM_LIMIT = 56 * 1024 * 1024
MLP_VMEM = 62 * 1024 * 1024

def gain_row(ref, which):
    parts = [ref[shard, which : which + 1, :] for shard in range(ref.shape[0])]
    return jnp.concatenate(parts, axis=1)


def norm_scale(values):
    return lax.rsqrt(jnp.mean(values * values, axis=-1, keepdims=True) + EPS)


def norm_back(values, gain, incoming):
    scale = norm_scale(values)
    weighted = incoming * gain
    inner = jnp.mean(weighted * values, axis=-1, keepdims=True)
    grad = scale * weighted - values * (scale * scale * scale * inner)
    return grad, jnp.sum(incoming * values * scale, axis=0, keepdims=True)


def project_kernel(heads, x_ref, gain_ref, w_ref, cos_ref, sin_ref, normed_ref, heads_ref):
    step = pl.program_id(0)

    @pl.when(step == 0)
    def _():
        x = x_ref[...].astype(jnp.float32)
        normed_ref[...] = low(x * norm_scale(x) * gain_row(gain_ref, 0))

    part = dot(normed_ref[...], w_ref[...])
    cosine, sine_part = cos_ref[...], sin_ref[...]
    count = heads_ref.shape[0]
    for j in range(count):
        value = part[:, j * HD : (j + 1) * HD]
        turned = value * cosine + pltpu.roll(value, HD // 2, 1) * sine_part
        head = step * count + j
        value = jnp.where(head < heads, turned * HD ** (-0.5), jnp.where(head == heads, turned, value))
        heads_ref[j] = low(value)


def project(x, gain, w, cosine, sine_part):
    rows, width = x.shape
    count = (H + 2) // PROJECT_STEPS
    whole = lambda *shape: pl.BlockSpec(shape, lambda i: (0,) * len(shape))
    return pl.pallas_call(
        functools.partial(project_kernel, H),
        grid=(PROJECT_STEPS,),
        name="project",
        in_specs=[
            whole(rows, width),
            whole(*gain.shape),
            pl.BlockSpec((width, count * HD), lambda i: (0, i)),
            whole(rows, HD),
            whole(rows, HD),
        ],
        out_specs=[
            whole(rows, width),
            pl.BlockSpec((count, rows, HD), lambda i: (i, 0, 0)),
        ],
        out_shape=[
            jax.ShapeDtypeStruct((rows, width), jnp.bfloat16),
            jax.ShapeDtypeStruct((H + 2, rows, HD), jnp.bfloat16),
        ],
        compiler_params=pltpu.CompilerParams(vmem_limit_bytes=VMEM_LIMIT),
    )(x, gain, w, cosine, sine_part)


PROJECT_STEPS = 2
HEADS_STEP = 4
ANY = pl.BlockSpec(memory_space=pl.ANY)


class Window:
    def __init__(self, rows):
        self.block = rows // ROUNDS
        self.blocks = (WINDOW + self.block - 2) // self.block + 1
        self.span = self.blocks * self.block


def place_tables(
    index, devices, order_ref, lengths_ref, frequency_ref,
    where_ref, key_place_ref, bounds_ref, wide_ref, cos_ref, sin_ref, order_rows,
):
    block = bounds_ref.shape[0] // ROUNDS
    count = order_ref.shape[1] // block
    window = Window(block * ROUNDS)
    blocks = [order_ref[:, i * block : (i + 1) * block] for i in range(count)]
    order_rows[...] = jnp.concatenate(blocks, axis=0).astype(jnp.float32)
    blocks = order_rows[...]
    block_of = lambda place: jnp.floor((place + 0.5) * (1.0 / block))
    held = block_of(blocks[:, :1])
    offsets = low(blocks - held * block)
    at = lax.broadcasted_iota(jnp.int32, (count, 1), 0).astype(jnp.float32)
    lane = lax.broadcasted_iota(jnp.int32, (1, LANES), 1).astype(jnp.float32)
    step = jnp.where(lane < window.blocks, lane, lane - window.blocks)
    lengths = lengths_ref[...].astype(jnp.float32)
    ends = [lengths[:, :1]]
    for j in range(1, lengths.shape[1]):
        ends.append(ends[-1] + lengths[:, j : j + 1])

    def least_of(place):
        start = jnp.zeros_like(place)
        for end in ends:
            start = jnp.where(end <= place, end, start)
        return jnp.maximum(start, place - (WINDOW - 1))

    where_ref[...] = jnp.zeros_like(where_ref)
    own = []
    for r in range(ROUNDS):
        mine = order_rows[pl.ds(index * ROUNDS + r, 1), :]
        own.append(mine)
        wanted = block_of(mine[:, :1]) - (window.blocks - 1) + step
        match = (held == jnp.maximum(wanted, 0.0)).astype(jnp.float32)
        where = jnp.sum(match * at, axis=0, keepdims=True)
        device = jnp.floor((where + 0.5) * (1.0 / ROUNDS))
        target = (where - ROUNDS * device) * devices + device
        where_ref[r : r + 1, :] = jnp.where(lane < window.blocks, where, target).astype(jnp.int32)
        inner = tn_dot(low(match), offsets)
        pieces = []
        for j in range(window.blocks):
            one = wanted[:, j : j + 1]
            pieces.append(inner[j : j + 1] + jnp.where(one >= 0.0, one * block, 1e9))
        key_place_ref[r] = jnp.concatenate(pieces, axis=1)
        wide_ref[r, :1, :] = jnp.concatenate([mine] * HEADS_STEP, axis=1)
        wide_ref[r, 1:, :] = jnp.concatenate([least_of(mine)] * HEADS_STEP, axis=1)
    own = jnp.concatenate(own, axis=1)
    own = jnp.broadcast_to(own, (8, own.shape[1])).T[:, :1]
    bounds_ref[:, :1] = own
    bounds_ref[:, 1:] = least_of(own)
    angles = own * frequency_ref[...]
    cos_ref[...] = jnp.cos(angles)
    sign = jnp.where(lane < HD // 2, -1.0, 1.0)
    sin_ref[...] = jnp.sin(angles) * sign


def place_arrays(order, lengths, rows):
    window = Window(rows)
    frequency = 10000.0 ** (-jnp.arange(HD // 2, dtype=jnp.float32) / (HD // 2))
    operands = (
        order,
        lengths,
        jnp.concatenate([frequency, frequency])[None],
    )
    wide = jax.ShapeDtypeStruct((rows, HD), jnp.float32)
    shapes = (
        jax.ShapeDtypeStruct((8, LANES), jnp.int32),
        jax.ShapeDtypeStruct((ROUNDS, 1, window.span), jnp.float32),
        jax.ShapeDtypeStruct((rows, 2), jnp.float32),
        jax.ShapeDtypeStruct((ROUNDS, 2, HEADS_STEP * window.block), jnp.float32),
        wide,
        wide,
    )
    return operands, shapes


def place_tables_alone(devices, order, lengths, rows):
    operands, shapes = place_arrays(order, lengths, rows)

    def kernel(*refs):
        place_tables(lax.axis_index("ctx"), devices, *refs)

    block = Window(rows).block

    vmem = pl.BlockSpec(memory_space=pltpu.VMEM)
    return pl.pallas_call(
        kernel,
        name="places",
        in_specs=[vmem] * len(operands),
        out_specs=[vmem] * len(shapes),
        out_shape=shapes,
        scratch_shapes=[pltpu.VMEM((order.shape[1] // block, block), jnp.float32)],
    )(*operands)


def load_window(blocks, block, where_ref, kv_ref, window):
    r = pl.program_id(0)
    for j in range(blocks):
        rows = slice(j * block, (j + 1) * block)
        at = where_ref[r, j]
        device, round_ = at // ROUNDS, lax.rem(at, ROUNDS)
        span = pl.ds(pl.multiple_of(round_ * block, 16), block)
        window[rows, :HD] = kv_ref[device, 0, span, :]
        window[rows, HD:] = kv_ref[device, 1, span, :]


def attend_kernel(
    blocks, block, where_ref, q_ref, kv_ref, key_place_ref, bounds_ref, out_ref, log_ref, window, bias
):
    load_window(blocks, block, where_ref, kv_ref, window)
    key_place = key_place_ref[0]
    allowed = (key_place <= bounds_ref[:, :1]) & (key_place >= bounds_ref[:, 1:])
    bias[...] = jnp.where(allowed, 0.0, -1e30)
    for part in range(q_ref.shape[0] // HEADS_STEP):
        first = part * HEADS_STEP
        queries = q_ref[first : first + HEADS_STEP].reshape(HEADS_STEP * block, HD)
        scores = nt_dot(queries, window[:, :HD])
        scores = scores.reshape(HEADS_STEP, block, blocks * block) + bias[...][None]
        peak = jnp.max(scores, axis=-1, keepdims=True)
        weights = jnp.exp(scores - peak)
        total = jnp.sum(weights, axis=-1, keepdims=True).reshape(HEADS_STEP * block, 1)
        weights = low(weights).reshape(HEADS_STEP * block, blocks * block)
        mixed = low(dot(weights, window[:, HD:]) / total)
        for j in range(HEADS_STEP):
            columns = slice((first + j) * HD, (first + j + 1) * HD)
            out_ref[:, columns] = mixed[j * block : (j + 1) * block]
        log_total = peak.reshape(HEADS_STEP * block, 1) + jnp.log(total)
        log_ref[0, part] = jnp.broadcast_to(log_total, (HEADS_STEP * block, LANES)).T[:1, :]


def attend(where, queries, kv_blocks, key_place, bounds):
    heads, rows = H, queries.shape[1]
    window = Window(rows)
    block, span, parts = window.block, window.span, heads // HEADS_STEP
    grid_spec = pltpu.PrefetchScalarGridSpec(
        num_scalar_prefetch=1,
        grid=(ROUNDS,),
        in_specs=[
            pl.BlockSpec((heads, block, HD), lambda r, *_: (0, r, 0)),
            pl.BlockSpec(kv_blocks.shape, lambda r, *_: (0, 0, 0, 0)),
            pl.BlockSpec((1, 1, span), lambda r, *_: (r, 0, 0)),
            pl.BlockSpec((block, 2), lambda r, *_: (r, 0)),
        ],
        out_specs=[
            pl.BlockSpec((block, heads * HD), lambda r, *_: (r, 0)),
            pl.BlockSpec((1, parts, 1, HEADS_STEP * block), lambda r, *_: (r, 0, 0, 0)),
        ],
        scratch_shapes=[
            pltpu.VMEM((span, 2 * HD), jnp.bfloat16),
            pltpu.VMEM((block, span), jnp.float32),
        ],
    )
    return pl.pallas_call(
        functools.partial(attend_kernel, window.blocks, block),
        name="attend",
        grid_spec=grid_spec,
        out_shape=[
            jax.ShapeDtypeStruct((rows, heads * HD), jnp.bfloat16),
            jax.ShapeDtypeStruct((ROUNDS, parts, 1, HEADS_STEP * block), jnp.float32),
        ],
        compiler_params=pltpu.CompilerParams(vmem_limit_bytes=VMEM_LIMIT),
    )(where, queries, kv_blocks, key_place, bounds)


def attend_back_kernel(
    blocks, block, where_ref, q_ref, kv_ref, grad_ref, mixed_ref, log_ref, key_place_ref, bounds_ref,
    cos_ref, sin_ref, *refs,
):
    grad_q_ref, grad_kv_ref, window, bias, window_grad, total_grad = refs[-6:]
    r = pl.program_id(0)

    @pl.when(r == 0)
    def _():
        total_grad[...] = jnp.zeros_like(total_grad)

    load_window(blocks, block, where_ref, kv_ref, window)
    key_place = jnp.broadcast_to(key_place_ref[0], (8, blocks * block)).T[:, :1]
    allowed = (key_place <= bounds_ref[0, :1, :]) & (key_place >= bounds_ref[0, 1:, :])
    bias[...] = jnp.where(allowed, 0.0, -1e30)
    keys, values = window[:, :HD], window[:, HD:]
    cosine, sine_part = cos_ref[...], sin_ref[...]
    for part in range(q_ref.shape[0] // HEADS_STEP):
        first = part * HEADS_STEP
        spans = [slice((first + j) * HD, (first + j + 1) * HD) for j in range(HEADS_STEP)]
        queries = q_ref[first : first + HEADS_STEP].reshape(HEADS_STEP * block, HD)
        grads = jnp.concatenate([grad_ref[:, span] for span in spans], axis=0)
        delta = jnp.concatenate(
            [
                jnp.sum(
                    (grad_ref[:, span].astype(jnp.float32) * mixed_ref[:, span].astype(jnp.float32)).T,
                    axis=0,
                    keepdims=True,
                )
                for span in spans
            ],
            axis=1,
        )
        probs = jnp.exp(nt_dot(keys, queries) + (bias[...] - log_ref[0, part]))
        grad_scores = low(probs * (nt_dot(values, grads) - delta))
        grad_keys = dot(grad_scores, queries)
        grad_values = dot(low(probs), grads)
        if part == 0:
            window_grad[:, :HD] = grad_keys
            window_grad[:, HD:] = grad_values
        else:
            window_grad[:, :HD] += grad_keys
            window_grad[:, HD:] += grad_values
        grad_q = tn_dot(grad_scores, keys)
        for j, span in enumerate(spans):
            one = grad_q[j * block : (j + 1) * block]
            one = (one * cosine - pltpu.roll(one, HD // 2, 1) * sine_part) * HD ** (-0.5)
            grad_q_ref[:, span] = low(one)
    for j in range(blocks):
        total_grad[where_ref[r, blocks + j]] += window_grad[j * block : (j + 1) * block, :]

    @pl.when(r == pl.num_programs(0) - 1)
    def _():
        grad_kv_ref[...] = low(total_grad[...])


def attend_back(
    where, queries, kv_blocks, grads, mixed, log_total, key_place, bounds, cosine, sine_part, earlier
):
    heads, rows = H, queries.shape[1]
    kv_sums = (kv_blocks.shape[0] * ROUNDS, rows // ROUNDS, 2 * HD)
    window = Window(rows)
    block, span, parts = window.block, window.span, heads // HEADS_STEP
    width = HEADS_STEP * block
    grid_spec = pltpu.PrefetchScalarGridSpec(
        num_scalar_prefetch=1,
        grid=(ROUNDS,),
        in_specs=[
            pl.BlockSpec((heads, block, HD), lambda r, *_: (0, r, 0)),
            pl.BlockSpec(kv_blocks.shape, lambda r, *_: (0, 0, 0, 0)),
            pl.BlockSpec((block, heads * HD), lambda r, *_: (r, 0)),
            pl.BlockSpec((block, heads * HD), lambda r, *_: (r, 0)),
            pl.BlockSpec((1, parts, 1, width), lambda r, *_: (r, 0, 0, 0)),
            pl.BlockSpec((1, 1, span), lambda r, *_: (r, 0, 0)),
            pl.BlockSpec((1, 2, width), lambda r, *_: (r, 0, 0)),
            pl.BlockSpec((block, HD), lambda r, *_: (r, 0)),
            pl.BlockSpec((block, HD), lambda r, *_: (r, 0)),
        ]
        + [ANY] * len(earlier),
        out_specs=[
            pl.BlockSpec((block, heads * HD), lambda r, *_: (r, 0)),
            pl.BlockSpec(kv_sums, lambda r, *_: (0, 0, 0)),
        ],
        scratch_shapes=[
            pltpu.VMEM((span, 2 * HD), jnp.bfloat16),
            pltpu.VMEM((span, width), jnp.float32),
            pltpu.VMEM((span, 2 * HD), jnp.float32),
            pltpu.VMEM(kv_sums, jnp.float32),
        ],
    )
    return pl.pallas_call(
        functools.partial(attend_back_kernel, window.blocks, block),
        name="attend_back",
        grid_spec=grid_spec,
        out_shape=[
            jax.ShapeDtypeStruct((rows, heads * HD), jnp.bfloat16),
            jax.ShapeDtypeStruct(kv_sums, jnp.bfloat16),
        ],
        compiler_params=pltpu.CompilerParams(vmem_limit_bytes=VMEM_LIMIT),
    )(
        where,
        queries,
        kv_blocks,
        grads,
        mixed,
        log_total,
        key_place,
        bounds,
        cosine,
        sine_part,
        *earlier,
    )


MIDDLE_TILES = 3
FORWARD_TILES = 2


def whole_block(shape):
    return pl.BlockSpec(shape, lambda i: (0,) * len(shape))


def middle_kernel(x_ref, mixed_ref, gain_ref, w_ref, middle_ref, left_ref, right_ref):
    step = pl.program_id(0)
    tile = w_ref.shape[1]
    columns = pl.ds(pl.multiple_of(step * tile, tile), tile)
    middle_ref[:, columns] = x_ref[:, columns].astype(jnp.float32) + dot(mixed_ref[...], w_ref[...])

    @pl.when(step == pl.num_programs(0) - 1)
    def _():
        values = middle_ref[...]
        normed = low(values * norm_scale(values) * gain_row(gain_ref, 1))
        half = left_ref.shape[1]
        left_ref[...] = normed[:, :half]
        right_ref[...] = normed[:, half:]


def middle_forward(x, mixed, gains, w):
    rows, width = x.shape
    half = width // 2
    inner = mixed.shape[1]
    return pl.pallas_call(
        middle_kernel,
        name="middle",
        grid=(FORWARD_TILES,),
        in_specs=[
            whole_block((rows, width)),
            whole_block((rows, inner)),
            whole_block(gains.shape),
            pl.BlockSpec((inner, width // FORWARD_TILES), lambda i: (0, i)),
        ],
        out_specs=[whole_block((rows, width))] + [whole_block((rows, half))] * 2,
        out_shape=[
            jax.ShapeDtypeStruct((rows, width), jnp.float32),
            jax.ShapeDtypeStruct((rows, half), jnp.bfloat16),
            jax.ShapeDtypeStruct((rows, half), jnp.bfloat16),
        ],
        compiler_params=pltpu.CompilerParams(vmem_limit_bytes=VMEM_LIMIT),
    )(x, mixed, gains, w)


def middle_back_kernel(
    grad_ref, middle_ref, upstream_ref, mixed_ref, gain_ref, w_ref,
    grad_middle_ref, grad_mixed_ref, grad_w_ref, grad_gain_ref, token, branch,
):
    @pl.when(pl.program_id(0) == 0)
    def _():
        grad, grad_gain = norm_back(middle_ref[...], gain_row(gain_ref, 1), grad_ref[...])
        total = upstream_ref[...].astype(jnp.float32) + grad
        grad_middle_ref[...] = total
        branch[...] = low(total)
        grad_gain_ref[...] = grad_gain
        token[...] = jnp.zeros_like(token)

    grad_mixed_ref[...] = low(nt_dot(branch[...], w_ref[...]))
    grad_w_ref[...] = low(tn_dot(mixed_ref[...], branch[...]))


def middle_back(grad, middle, upstream, mixed, gains, w):
    rows, width = middle.shape
    inner = mixed.shape[1]
    tile = inner // MIDDLE_TILES
    return pl.pallas_call(
        middle_back_kernel,
        name="middle_back",
        grid=(MIDDLE_TILES,),
        in_specs=[
            whole_block((rows, width)),
            whole_block((rows, width)),
            whole_block((rows, width)),
            pl.BlockSpec((rows, tile), lambda i: (0, i)),
            whole_block(gains.shape),
            pl.BlockSpec((tile, width), lambda i: (i, 0)),
        ],
        out_specs=[
            whole_block((rows, width)),
            pl.BlockSpec((rows, tile), lambda i: (0, i)),
            pl.BlockSpec((tile, width), lambda i: (i, 0)),
            whole_block((1, width)),
            whole_block(TOKEN),
        ],
        out_shape=[
            jax.ShapeDtypeStruct((rows, width), jnp.float32),
            jax.ShapeDtypeStruct((rows, inner), jnp.bfloat16),
            jax.ShapeDtypeStruct((inner, width), jnp.bfloat16),
            jax.ShapeDtypeStruct((1, width), jnp.float32),
            token_shape(),
        ],
        scratch_shapes=[pltpu.VMEM((rows, width), jnp.bfloat16)],
        compiler_params=pltpu.CompilerParams(vmem_limit_bytes=VMEM_LIMIT),
    )(grad, middle, upstream, mixed, gains, w)


def project_back_queries_kernel(grad_ref, normed_ref, w_ref, grad_w_ref, grad_normed_ref):
    grad_normed_ref[...] = nt_dot(grad_ref[...], w_ref[...])
    grad_w_ref[...] = low(tn_dot(normed_ref[...], grad_ref[...]))


def project_back_queries(grad_q, normed, w):
    rows, width = normed.shape
    inner = grad_q.shape[1]
    tile = width // MIDDLE_TILES
    return pl.pallas_call(
        project_back_queries_kernel,
        name="project_back_queries",
        grid=(MIDDLE_TILES,),
        in_specs=[
            whole_block(grad_q.shape),
            pl.BlockSpec((rows, tile), lambda i: (0, i)),
            pl.BlockSpec((tile, inner), lambda i: (i, 0)),
        ],
        out_specs=[
            pl.BlockSpec((tile, inner), lambda i: (i, 0)),
            pl.BlockSpec((rows, tile), lambda i: (0, i)),
        ],
        out_shape=[
            jax.ShapeDtypeStruct((width, inner), jnp.bfloat16),
            jax.ShapeDtypeStruct((rows, width), jnp.float32),
        ],
        compiler_params=pltpu.CompilerParams(vmem_limit_bytes=VMEM_LIMIT),
    )(grad_q, normed, w)


def project_back_keys_kernel(
    grad_kv_ref, cos_ref, sin_ref, normed_ref, partial_ref, x_ref, grad_middle_ref, gain_ref, w_ref,
    grad_w_ref, grad_x_ref, grad_gain_ref,
):
    keys = grad_kv_ref[:, :HD]
    keys = low(keys * cos_ref[...] - pltpu.roll(keys, HD // 2, 1) * sin_ref[...])
    joined = jnp.concatenate([keys, low(grad_kv_ref[:, HD:])], axis=1)
    grad_w_ref[...] = low(tn_dot(normed_ref[...], joined))
    grad_normed = partial_ref[...] + nt_dot(joined, w_ref[...])
    grad, grad_gain = norm_back(x_ref[...].astype(jnp.float32), gain_row(gain_ref, 0), grad_normed)
    grad_x_ref[...] = grad_middle_ref[...] + grad
    grad_gain_ref[...] = grad_gain


def project_back_keys(grad_kv, cosine, sine_part, normed, partial, x, grad_middle, gains, w):
    rows, width = x.shape
    inner = grad_kv.shape[1]
    arrays = (grad_kv, cosine, sine_part, normed, partial, x, grad_middle, gains)
    last = w.shape[1] // inner - 1
    return pl.pallas_call(
        project_back_keys_kernel,
        name="project_back_keys",
        grid=(1,),
        in_specs=[whole_block(one.shape) for one in arrays]
        + [pl.BlockSpec((width, inner), lambda i: (0, last))],
        out_specs=[whole_block((width, inner)), whole_block((rows, width)), whole_block((1, width))],
        out_shape=[
            jax.ShapeDtypeStruct((width, inner), jnp.bfloat16),
            jax.ShapeDtypeStruct((rows, width), jnp.float32),
            jax.ShapeDtypeStruct((1, width), jnp.float32),
        ],
        compiler_params=pltpu.CompilerParams(vmem_limit_bytes=VMEM_LIMIT),
    )(*arrays, w)


MESH_ID =MESH_ID = pl.DeviceIdType.MESH


class Wire:
    def __init__(self, send_sems, recv_sems):
        self.send_sems = send_sems
        self.recv_sems = recv_sems
        self.count = 0
        self.open = []
        self.ctx = lax.axis_index("ctx")
        self.shard = lax.axis_index("fsdp")

    def other(self, mask):
        at = self.ctx
        for bit in (1, 2, 4):
            if mask & bit:
                at = at + bit - 2 * bit * lax.rem(at // bit, 2)
        return at

    def plane(self, mask):
        return (self.other(mask), self.shard)

    def line(self, step, shards):
        return (self.ctx, lax.rem(self.shard + step, shards))

    def meet(self, peers):
        barrier = pltpu.get_barrier_semaphore()
        for peer in peers:
            pl.semaphore_signal(barrier, inc=1, device_id=peer, device_id_type=MESH_ID)
        pl.semaphore_wait(barrier, len(peers))

    def send(self, source, target, peer):
        at = self.count
        self.count += 1
        copy = pltpu.make_async_remote_copy(
            src_ref=source,
            dst_ref=target,
            send_sem=self.send_sems.at[at],
            recv_sem=self.recv_sems.at[at],
            device_id=peer,
            device_id_type=MESH_ID,
        )
        copy.start()
        self.open.append(copy)
        return copy

    def sent(self, copy):
        copy.wait_send()
        self.open = [one for one in self.open if one is not copy]

    def finish(self):
        for copy in self.open:
            copy.wait_send()


class PlaneGather:
    COPIES = 9

    def __init__(self, wire, source, out_at, rows, split):
        self.wire, self.out_at, self.rows, self.split = wire, out_at, rows, split
        ctx = wire.ctx
        self.core = wire.send(source, out_at(ctx), wire.plane(1))
        self.x = wire.send(source, out_at(ctx), wire.plane(2))
        self.y = wire.send(source, out_at(ctx), wire.plane(4))

    def forward(self):
        wire, split = self.wire, self.split
        rest = self.rows - split
        self.x.wait_recv()
        block = self.out_at(wire.other(2))
        part = block.at[pl.ds(0, split)]
        self.corner_y = wire.send(part, part, wire.plane(4))
        self.core_x = wire.send(block, block, wire.plane(1))
        self.y.wait_recv()
        block = self.out_at(wire.other(4))
        part = block.at[pl.ds(split, rest)]
        self.corner_x = wire.send(part, part, wire.plane(2))
        self.core_y = wire.send(block, block, wire.plane(1))

    def corner(self):
        self.corner_y.wait_recv()
        self.corner_x.wait_recv()
        block = self.out_at(self.wire.other(6))
        self.core_corner = self.wire.send(block, block, self.wire.plane(1))

    def settle(self):
        self.core.wait_recv()
        self.core_x.wait_recv()
        self.core_y.wait_recv()
        self.core_corner.wait_recv()


def half_rows(rows, turn):
    low_half = rows // 32 * 16
    return low_half if turn % 2 else rows - low_half


def add_low(first, second):
    return (first.astype(jnp.float32) + second.astype(jnp.float32)).astype(jnp.bfloat16)


class PlaneSum:
    COPIES = 7

    def __init__(self, wire, source, own, pair, first, second, local_sem):
        self.wire, self.own, self.pair, self.first, self.second = wire, own, pair, first, second
        core = lax.rem(wire.ctx, 2)
        self.chips = {mask: wire.other(2 * mask) // 2 for mask in range(4)}
        self.swap = wire.send(source.at[:, :, 1 - core], pair, wire.plane(1))
        self.local = pltpu.make_async_copy(source.at[:, :, core], own, local_sem)
        self.local.start()

    def step_one(self):
        wire, own, pair, first, chips = self.wire, self.own, self.pair, self.first, self.chips
        self.local.wait()
        self.swap.wait_recv()

        def add_pair(index, carry):
            part, other = index // 4, lax.rem(index, 4)
            own[part, other] = add_low(own[part, other], pair[part, other])
            return carry

        lax.fori_loop(0, 16, add_pair, 0)
        low, high = pl.ds(0, 2), pl.ds(2, 2)
        self.one = [
            wire.send(own.at[low, chips[3]], first.at[0, 1], wire.plane(2)),
            wire.send(own.at[high, chips[3]], first.at[1, 1], wire.plane(4)),
            wire.send(own.at[low, chips[1]], first.at[0, 0], wire.plane(2)),
            wire.send(own.at[high, chips[2]], first.at[1, 0], wire.plane(4)),
        ]

    def step_two(self):
        wire, own, first, second, chips = self.wire, self.own, self.first, self.second, self.chips
        self.one[0].wait_recv()
        for part in range(2):
            own[part, chips[2]] = add_low(own[part, chips[2]], first[0, 1, part])
        self.two = [wire.send(own.at[pl.ds(0, 2), chips[2]], second.at[pl.ds(0, 2)], wire.plane(4))]
        self.one[1].wait_recv()
        for part in range(2):
            own[part + 2, chips[1]] = add_low(own[part + 2, chips[1]], first[1, 1, part])
        self.two.append(
            wire.send(own.at[pl.ds(2, 2), chips[1]], second.at[pl.ds(2, 2)], wire.plane(2))
        )

    def result(self, store):
        own, first, second, chips = self.own, self.first, self.second, self.chips
        for copy in self.one[2:] + self.two:
            copy.wait_recv()
        for part in range(4):
            total = own[part, chips[0]].astype(jnp.float32)
            total += first[part // 2, 0, part % 2].astype(jnp.float32)
            total += second[part].astype(jnp.float32)
            store(part, total)


def plane_sum_scratch(rows, columns):
    shape = lambda *lead: pltpu.VMEM(lead + (rows, columns), jnp.bfloat16)
    return [shape(4, 4), shape(4, 4), shape(2, 2, 2), shape(4)]


def dma_sems(count):
    return pltpu.SemaphoreType.DMA((count,))


PLANE_PEERS = (1, 2, 4)


def comm_params(number):
    return pltpu.CompilerParams(
        collective_id=number, has_side_effects=True, vmem_limit_bytes=VMEM_LIMIT
    )


def take(values, count):
    return values[:count], values[count:]


class Relay:
    def __init__(self, source, stage, targets, sems):
        self.stage, self.targets, self.sems = stage, targets, sems
        self.load = pltpu.make_async_copy(source, stage, sems.at[0])
        self.load.start()

    def push(self):
        self.load.wait()
        self.stores = []
        for i, (part, target) in enumerate(self.targets):
            store = pltpu.make_async_copy(part, target, self.sems.at[1 + i])
            store.start()
            self.stores.append(store)

    def settle(self):
        for store in self.stores:
            store.wait()


TOKEN = (8, 128)


def token_shape():
    return jax.ShapeDtypeStruct(TOKEN, jnp.int32)


def after(token, values):
    return jnp.where(token[0, 0] != 0, jnp.zeros_like(values), values)


def share_line_kernel(
    shards, pack, in_ref, gain_ref, mlp_in, mlp_out, up_ref, in_line, gain_all, mine, up_x, up_y,
    gain_now, in_stage, packed, tiles, local_sems, load_sems, send_sems, recv_sems,
):
    wire = Wire(send_sems, recv_sems)
    ctx, shard = wire.ctx, wire.shard
    chip, core = ctx // 2, lax.rem(ctx, 2)
    chips = pack.chips
    relay = Relay(in_ref.at[ctx], in_stage, [(in_stage, in_line.at[shard])], local_sems.at[0])
    gain_now[...] = jnp.zeros_like(gain_now)
    gain_now[:2] = gain_ref[...].astype(jnp.float32)
    wire.meet(
        [wire.line(step, shards) for step in range(1, shards)] + [wire.plane(2), wire.plane(4)]
    )
    half = pack.half
    copies = [
        wire.send(up_ref.at[:, pl.ds(0, half)], up_x, wire.plane(2)),
        wire.send(up_ref.at[:, pl.ds(half, half)], up_y, wire.plane(4)),
    ]
    for source, target in ((gain_now, gain_all), (in_ref.at[ctx], in_line)):
        for step in range(1, shards):
            copies.append(wire.send(source, target.at[shard], wire.line(step, shards)))
    gain_copy = pltpu.make_async_copy(gain_now, gain_all.at[shard], local_sems.at[1, 0])
    gain_copy.start()
    relay.push()

    loads = []

    def load(source, target):
        copy = pltpu.make_async_copy(source, target, load_sems.at[len(loads)])
        copy.start()
        loads.append(copy)

    def strip(start, count):
        return pl.ds(pl.multiple_of(start, LANES), count)

    main, rest, half, tail, split = pack.main, pack.rest, pack.half, pack.tail, pack.split
    per_shard = chips * (main + rest)
    base = core * (shards * per_shard)
    for part in range(shards):
        start = base + part * per_shard
        load(mlp_in.at[:, strip(start + chips * main, chips * rest)], tiles.at[part])
        column = part * main
        if column + main <= half:
            source = mlp_in.at[:, strip(start + chip * main, main)]
            load(source, packed.at[pl.ds(pack.main_start, pack.rows), pl.ds(column, main)])
            continue
        for i, at in enumerate(range(0, pack.rows, split)):
            source = mlp_in.at[pl.ds(at, split), strip(start + chip * main, main)]
            load(source, packed.at[pl.ds(pack.tail_start, split), pl.ds(i * tail + column - half, main)])
    columns = strip(core * half, half)
    for start, count, row in (
        (chip * main, main, 0),
        (chips * main + chip * rest, rest, main),
    ):
        source = mlp_out.at[pl.ds(pl.multiple_of(start, 16), count), columns]
        load(source, packed.at[pl.ds(row, count), :])
    for copy in loads:
        copy.wait()
    width = chips * rest
    ends = [
        pltpu.roll(tiles[part].astype(jnp.float32), lax.rem(width - chip * rest, width), 1)[:, :rest]
        for part in range(shards)
    ]
    ends = low(jnp.concatenate(ends, axis=1))
    for i, at in enumerate(range(0, pack.rows, split)):
        column = i * tail + shards * main - half
        packed[pack.tail_start : pack.tail_start + split, column : column + shards * rest] = ends[at : at + split]
    mine_copy = pltpu.make_async_copy(packed, mine, local_sems.at[1, 1])
    mine_copy.start()
    relay.settle()
    gain_copy.wait()
    mine_copy.wait()
    for copy in copies:
        copy.wait_recv()
    wire.finish()


def gather_shards(wire, line, target, rows, shards, count):
    gathers = []
    for step in range(1, shards):
        origin = lax.rem(wire.shard + shards - step, shards)
        place = lambda who, origin=origin: target.at[origin, who]
        gathers.append(PlaneGather(wire, line.at[origin], place, rows, half_rows(rows, step + count)))
    return gathers


def relay_shards(wire, whole, line, target, stage, piece, shards, sems):
    origins = [lax.rem(wire.shard + shards - step, shards) for step in range(1, shards)]
    places = [(piece.at[origin], target.at[origin, wire.ctx]) for origin in origins]
    return [
        Relay(whole, stage, [(stage, target.at[wire.shard])], sems.at[0]),
        Relay(line, piece, places, sems.at[1]),
    ]


def complete(gathers, relays):
    for gather in gathers:
        gather.forward()
    for gather in gathers:
        gather.corner()
    for gather in gathers:
        gather.settle()
    for relay in relays:
        relay.settle()


def share_plane_kernel(
    shards, devices, in_ref, in_line, out_ref, order, lengths, frequency, in_all, out_line, *refs
):
    tables, scratch = take(refs, len(refs) - 7)
    order_rows, in_stage, in_piece, out_stage, local_sems, send_sems, recv_sems = scratch
    wire = Wire(send_sems, recv_sems)
    ctx, shard = wire.ctx, wire.shard
    relays = relay_shards(wire, in_ref, in_line, in_all, in_stage, in_piece, shards, local_sems)
    relays.append(
        Relay(out_ref.at[ctx], out_stage, [(out_stage, out_line.at[shard])], local_sems.at[2])
    )
    wire.meet(
        [wire.plane(mask) for mask in PLANE_PEERS] + [wire.line(s, shards) for s in range(1, shards)]
    )
    gathers = gather_shards(wire, in_line, in_all, in_ref.shape[1], shards, 0)
    copies = [
        wire.send(out_ref.at[ctx], out_line.at[shard], wire.line(step, shards))
        for step in range(1, shards)
    ]
    for relay in relays:
        relay.push()
    place_tables(ctx, devices, order, lengths, frequency, *tables, order_rows)
    complete(gathers, relays)
    for copy in copies:
        copy.wait_recv()
    wire.finish()


def gather_plane_kernel(
    shards, heads_ref, out_ref, out_line, kv_all, out_all, token,
    kv_stage, out_stage, out_piece, local_sems, send_sems, recv_sems,
):
    wire = Wire(send_sems, recv_sems)
    ctx = wire.ctx
    kv_ref = heads_ref.at[pl.ds(H, 2)]
    relays = relay_shards(wire, out_ref, out_line, out_all, out_stage, out_piece, shards, local_sems)
    relays.append(Relay(kv_ref, kv_stage, [(kv_stage, kv_all.at[ctx])], local_sems.at[2]))
    token[...] = jnp.zeros_like(token)
    wire.meet([wire.plane(mask) for mask in PLANE_PEERS])
    gathers = [PlaneGather(wire, kv_ref, lambda who: kv_all.at[who], 2, 1)]
    gathers += gather_shards(wire, out_line, out_all, out_ref.shape[1], shards, 1)
    for relay in relays:
        relay.push()
    complete(gathers, relays)
    wire.finish()


def like(values, *lead):
    return jax.ShapeDtypeStruct(lead + values.shape[-2:], values.dtype)


def stage_like(values, *lead):
    return pltpu.VMEM(lead + values.shape[-2:], values.dtype)


def share_line(w_in, gains, mlp_in, mlp_out, upstream, pack, shards):
    columns = gains.shape[1]
    copies = 2 * (shards - 1) + 2
    loads = shards + shards + 1 + 2
    return pl.pallas_call(
        functools.partial(share_line_kernel, shards, pack),
        name="share_line",
        in_specs=[ANY] + [pl.BlockSpec(memory_space=pltpu.VMEM)] + [ANY] * 3,
        out_specs=[ANY] * 5,
        out_shape=[
            like(w_in, shards),
            jax.ShapeDtypeStruct((shards, 8, columns), jnp.float32),
            jax.ShapeDtypeStruct((pack.total, pack.half), mlp_in.dtype),
        ]
        + [jax.ShapeDtypeStruct((upstream.shape[0], pack.half), upstream.dtype)] * 2,
        scratch_shapes=[
            pltpu.VMEM((8, columns), jnp.float32),
            stage_like(w_in),
            pltpu.VMEM((pack.total, pack.half), mlp_in.dtype),
            pltpu.VMEM((shards, pack.rows, pack.chips * pack.rest), mlp_in.dtype),
            pltpu.SemaphoreType.DMA((2, 2)),
            dma_sems(loads),
            dma_sems(copies),
            dma_sems(copies),
        ],
        compiler_params=comm_params(1),
    )(w_in, gains, mlp_in, mlp_out, upstream)


def share_plane(w_in, in_line, w_out, order, lengths, rows, ctx_size, shards):
    copies = (shards - 1) * (PlaneGather.COPIES + 1)
    operands, shapes = place_arrays(order, lengths, rows)
    vmem = pl.BlockSpec(memory_space=pltpu.VMEM)
    return pl.pallas_call(
        functools.partial(share_plane_kernel, shards, ctx_size),
        name="share_plane",
        in_specs=[ANY] * 3 + [vmem] * len(operands),
        out_specs=[ANY] * 2 + [vmem] * len(shapes),
        out_shape=[like(w_in, shards, ctx_size), like(w_out, shards), *shapes],
        scratch_shapes=[
            pltpu.VMEM((ctx_size * ROUNDS, rows // ROUNDS), jnp.float32),
            stage_like(w_in, ctx_size),
            stage_like(w_in, shards),
            stage_like(w_out),
            pltpu.SemaphoreType.DMA((3, shards)),
            dma_sems(copies),
            dma_sems(copies),
        ],
        compiler_params=comm_params(6),
    )(w_in, in_line, w_out, *operands)


def gather_plane(heads, w_out, out_line, ctx_size, shards):
    copies = shards * PlaneGather.COPIES
    key_value = jax.ShapeDtypeStruct((2,) + heads.shape[1:], heads.dtype)
    return pl.pallas_call(
        functools.partial(gather_plane_kernel, shards),
        name="gather_plane",
        in_specs=[ANY] * 3,
        out_specs=[ANY] * 2 + [pl.BlockSpec(memory_space=pltpu.VMEM)],
        out_shape=[like(key_value, ctx_size, 2), like(w_out, shards, ctx_size), token_shape()],
        scratch_shapes=[
            stage_like(key_value, 2),
            stage_like(w_out, ctx_size),
            stage_like(w_out, shards),
            pltpu.SemaphoreType.DMA((3, shards)),
            dma_sems(copies),
            dma_sems(copies),
        ],
        compiler_params=comm_params(2),
    )(heads, w_out, out_line)


class GainSum:
    def __init__(self, wire, now, arrived, line, shards):
        self.wire, self.now, self.arrived, self.line, self.shards = wire, now, arrived, line, shards
        self.at = 0
        self.start()

    def start(self):
        peer = self.wire.plane(PLANE_PEERS[self.at])
        self.copy = self.wire.send(self.now, self.arrived.at[self.at], peer)

    def add(self):
        self.copy.wait_recv()
        self.wire.sent(self.copy)
        self.now[...] += self.arrived[self.at]
        self.at += 1

    def step(self):
        self.add()
        self.start()

    def step_line(self):
        self.add()
        wire, shards = self.wire, self.shards
        self.copies = [
            wire.send(
                self.now.at[lax.rem(wire.shard + step, shards)],
                self.line.at[step - 1],
                wire.line(step, shards),
            )
            for step in range(1, shards)
        ]

    def result(self):
        for copy in self.copies:
            copy.wait_recv()
        value = self.now[self.wire.shard]
        for step in range(self.shards - 1):
            value += self.line[step]
        return value


def project_back_plane_kernel(
    kv_ref, g_out_ref, part_ref, grad_ref, normed_ref, x_ref, cos_ref, sin_ref, gain_ref, w_ref,
    out_half, q_half, k_half, part_all, grad_x_ref, grad_gain_ref,
    grad, normed, x, cosine, sine_part, gains, w, g_q, g_k, grad_normed, kv_sum, stage, *scratch,
):
    sums, scratch = take(scratch, 16)
    load_sems, sum_sems, part_sems, send_sems, recv_sems = scratch
    wire = Wire(send_sems, recv_sems)
    loads = []
    for source, target in (
        (grad_ref, grad),
        (normed_ref, normed),
        (w_ref, w),
        (cos_ref, cosine),
        (sin_ref, sine_part),
        (x_ref, x),
        (gain_ref, gains),
    ):
        loads.append(pltpu.make_async_copy(source, target, load_sems.at[len(loads)]))
        loads[-1].start()
    relay = Relay(part_ref, stage, [(stage, part_all.at[wire.ctx])], part_sems)
    wire.meet([wire.plane(mask) for mask in PLANE_PEERS])

    def plane_sum(source, at):
        return PlaneSum(wire, source, *sums[4 * at : 4 * at + 4], sum_sems.at[at])

    rows = part_ref.shape[0]
    keys_sum = plane_sum(kv_ref, 0)
    out_sum = plane_sum(g_out_ref, 1)
    gather = PlaneGather(wire, part_ref, lambda who: part_all.at[who], rows, rows // 32 * 16)
    keys_sum.step_one()
    out_sum.step_one()
    relay.push()
    for copy in loads:
        copy.wait()
    inner = grad.shape[1]
    tile = normed.shape[1] // 4
    pieces = g_q.shape[1:4]

    def queries_part(part, carry):
        span = pl.ds(pl.multiple_of(part * tile, tile), tile)
        value = low(tn_dot(normed[:, span], grad[...]))
        g_q[part] = value.reshape(*pieces, inner)
        grad_normed[:, span] = nt_dot(grad[...], w[span, :inner])
        return carry

    lax.fori_loop(0, 4, queries_part, 0)
    queries_sum = plane_sum(g_q, 2)
    keys_sum.step_two()

    def store_keys(part, value):
        kv_sum[part] = value

    keys_sum.result(store_keys)
    kv = kv_sum[...].reshape(normed.shape[0], 2 * HD)
    keys = kv[:, :HD]
    keys = low(keys * cosine[...] - pltpu.roll(keys, HD // 2, 1) * sine_part[...])
    joined = jnp.concatenate([keys, low(kv[:, HD:])], axis=1)
    for part in range(4):
        span = slice(part * tile, (part + 1) * tile)
        g_k[part] = low(tn_dot(normed[:, span], joined)).reshape(*pieces, 2 * HD)
        grad_normed[:, span] += nt_dot(joined, w[span, inner:])
    pair_sum = plane_sum(g_k, 3)
    out_sum.step_two()
    queries_sum.step_one()
    pair_sum.step_one()
    gather.forward()
    change, grad_gain = norm_back(x[...].astype(jnp.float32), gain_row(gains, 0), grad_normed[...])
    grad_x_ref[...] = change
    grad_gain_ref[...] = grad_gain
    queries_sum.step_two()
    pair_sum.step_two()
    gather.corner()
    for total, target in ((out_sum, out_half), (queries_sum, q_half), (pair_sum, k_half)):

        def store(part, value, target=target):
            target[part] = low(value)

        total.result(store)
    gather.settle()
    relay.settle()
    wire.finish()


def project_back_plane(grad_kv, g_out, part, grad_q, normed, x, cosine, sine_part, gains, w, ctx_size):
    rows, width = x.shape
    inner = grad_q.shape[1]
    lead = g_out.shape[:4]
    vmem = pl.BlockSpec(memory_space=pltpu.VMEM)
    low_scratch = lambda *shape: pltpu.VMEM(shape, jnp.bfloat16)
    wide = lambda *shape: pltpu.VMEM(shape, jnp.float32)
    sums = []
    for piece in (grad_kv.shape[3:], g_out.shape[3:], (lead[3], inner), (lead[3], 2 * HD)):
        sums += plane_sum_scratch(*piece)
    copies = 4 * PlaneSum.COPIES + PlaneGather.COPIES
    half = lambda columns: jax.ShapeDtypeStruct((4, lead[3], columns), jnp.bfloat16)
    return pl.pallas_call(
        project_back_plane_kernel,
        name="project_back_plane",
        in_specs=[ANY] * 10,
        out_specs=[vmem] * 3 + [ANY] + [vmem] * 2,
        out_shape=[
            half(g_out.shape[4]),
            half(inner),
            half(2 * HD),
            like(part, ctx_size),
            jax.ShapeDtypeStruct((rows, width), jnp.float32),
            jax.ShapeDtypeStruct((1, width), jnp.float32),
        ],
        scratch_shapes=[
            low_scratch(*grad_q.shape),
            low_scratch(*normed.shape),
            low_scratch(*x.shape),
            wide(*cosine.shape),
            wide(*cosine.shape),
            wide(*gains.shape),
            low_scratch(*w.shape),
            low_scratch(*lead, inner),
            low_scratch(*lead, 2 * HD),
            wide(rows, width),
            wide(4, *grad_kv.shape[3:]),
            stage_like(part),
            *sums,
            dma_sems(7),
            dma_sems(4),
            dma_sems(2),
            dma_sems(copies),
            dma_sems(copies),
        ],
        compiler_params=comm_params(3),
    )(grad_kv, g_out, part, grad_q, normed, x, cosine, sine_part, gains, w)


def reduce_late_kernel(shards, line_count, *refs):
    line_ins, refs = take(refs, line_count)
    part_ref, gain_a, gain_b, *refs = refs
    line_outs, refs = take(refs, line_count)
    part_all, gain_out, *refs = refs
    arrived, refs = take(refs, line_count)
    done, refs = take(refs, line_count)
    stage, gain_now, gain_in, gain_line, done_sems, part_sems, send_sems, recv_sems = refs

    wire = Wire(send_sems, recv_sems)
    ctx, shard = wire.ctx, wire.shard
    relay = Relay(part_ref, stage, [(stage, part_all.at[ctx])], part_sems)
    gain_now[...] = jnp.zeros_like(gain_now)
    columns = gain_now.shape[2]
    for part in range(shards):
        for row, values in enumerate((gain_a, gain_b)):
            gain_now[part, row : row + 1] = values[:, part * columns : (part + 1) * columns]
    wire.meet(
        [wire.plane(mask) for mask in PLANE_PEERS] + [wire.line(s, shards) for s in range(1, shards)]
    )
    lines = [
        [
            wire.send(
                source.at[lax.rem(shard + step, shards)], target.at[step - 1], wire.line(step, shards)
            )
            for step in range(1, shards)
        ]
        for source, target in zip(line_ins, arrived)
    ]
    rows = part_ref.shape[0]
    gathers = [PlaneGather(wire, part_ref, lambda who: part_all.at[who], rows, rows // 32 * 16)]
    gain = GainSum(wire, gain_now, gain_in, gain_line, shards)
    gain.step()
    gain.step()
    gain.step_line()
    relay.push()
    gathers[0].forward()
    locals_ = []
    for i, (source, target) in enumerate(zip(line_ins, line_outs)):
        for copy in lines[i]:
            copy.wait_recv()
        value = source[shard].astype(jnp.float32)
        for step in range(shards - 1):
            value += arrived[i][step].astype(jnp.float32)
        done[i][...] = low(value)
        place = lambda who, target=target: target.at[who]
        gathers.append(PlaneGather(wire, done[i], place, target.shape[1], half_rows(target.shape[1], i)))
        copy = pltpu.make_async_copy(done[i], place(ctx), done_sems.at[i])
        copy.start()
        locals_.append(copy)
    gain_out[...] = gain.result()
    for gather in gathers[1:]:
        gather.forward()
    for gather in gathers:
        gather.corner()
    for gather in gathers:
        gather.settle()
    for copy in locals_:
        copy.wait()
    relay.settle()
    wire.finish()


def reduce_late(lines, part, gain_a, gain_b, ctx_size):
    shards = lines[0].shape[0]
    vmem = pl.BlockSpec(memory_space=pltpu.VMEM)
    gain_shape = (shards, 8, gain_a.shape[1] // shards)
    copies = (PlaneGather.COPIES + shards - 1) * len(lines) + PlaneGather.COPIES + 3 + shards - 1
    return pl.pallas_call(
        functools.partial(reduce_late_kernel, shards, len(lines)),
        name="reduce_late",
        in_specs=[vmem] * len(lines) + [ANY] + [vmem] * 2,
        out_specs=[ANY] * (len(lines) + 1) + [vmem],
        out_shape=[like(array, ctx_size) for array in (*lines, part)]
        + [jax.ShapeDtypeStruct(gain_shape[1:], jnp.float32)],
        scratch_shapes=[stage_like(array, shards - 1) for array in lines]
        + [stage_like(array) for array in (*lines, part)]
        + [
            pltpu.VMEM(gain_shape, jnp.float32),
            pltpu.VMEM((3,) + gain_shape, jnp.float32),
            pltpu.VMEM((shards - 1,) + gain_shape[1:], jnp.float32),
            dma_sems(len(lines)),
            dma_sems(2),
            dma_sems(copies),
            dma_sems(copies),
        ],
        compiler_params=comm_params(4),
    )(*lines, part, gain_a, gain_b)


class Pack:
    def __init__(self, rows, half, chips, units, main, rest):
        self.rows, self.half, self.chips, self.main, self.rest = rows, half, chips, main, rest
        self.tail = units - half
        self.split = rows // (half // self.tail)
        self.main_start = main + rest
        self.tail_start = self.main_start + rows
        self.total = self.tail_start + self.split

    def in_spans(self, shard):
        every = (0, self.half)
        yield (self.main_start, self.rows), every, (shard * self.rows, self.rows), every
        for i, at in enumerate(range(0, self.rows, self.split)):
            yield (
                (self.tail_start, self.split),
                (i * self.tail, self.tail),
                (shard * self.rows + at, self.split),
                (self.half, self.tail),
            )

    def out_spans(self, shard, shards):
        every = (0, self.half)
        yield (0, self.main), every, (shard * self.main, self.main), every
        yield (
            (self.main, self.rest),
            every,
            (shards * self.main + shard * self.rest, self.rest),
            every,
        )


def finish_kernel(
    shards, chips, pack, main_ref, tail_ref, out_main_ref, out_rest_ref, attn_out_ref, attn_q_ref, attn_kv_ref,
    in_ref, out_ref, grad_attn_out_ref, grad_attn_in_ref,
):
    step = pl.program_id(0)
    last = pl.num_programs(0) - 1
    main, rest, half, tail = pack.main, pack.rest, pack.half, pack.tail
    per_shard = chips * (main + rest)
    wide = lambda values: values.astype(jnp.float32)

    @pl.when(step < last)
    def _():
        second = step >= last // 2
        tails = [
            jnp.where(second, tail_ref[who, :, tail:], tail_ref[who, :, :tail])
            for who in range(2 * chips)
        ]

        def columns_of(who, start, count):
            if start + count <= half:
                return main_ref[who, :, start : start + count]
            return tails[who][:, start - half : start - half + count]

        for core in range(2):
            for shard in range(shards):
                start = (core * shards + shard) * per_shard
                for chip in range(chips):
                    block = wide(columns_of(chip * 2 + core, shard * main, main))
                    in_ref[:, start + chip * main : start + (chip + 1) * main] = block
                ends = [
                    wide(columns_of(chip * 2 + core, shards * main, shards * rest))[
                        :, shard * rest : (shard + 1) * rest
                    ]
                    for chip in range(chips)
                ]
                in_ref[:, start + chips * main : start + per_shard] = jnp.concatenate(ends, axis=1)
            out_ref[:, core * half : (core + 1) * half] = wide(out_main_ref[core])
        grad_attn_out_ref[...] = wide(attn_out_ref[0])
        inner = attn_q_ref.shape[2]
        grad_attn_in_ref[:, :inner] = wide(attn_q_ref[0])
        grad_attn_in_ref[:, inner:] = wide(attn_kv_ref[0])

    @pl.when(step == last)
    def _():
        for chip in range(chips):
            for core in range(2):
                block = wide(out_rest_ref[chip * 2 + core])
                out_ref[chip * rest : (chip + 1) * rest, core * half : (core + 1) * half] = block


def finish(first, second, attn_out, attn_q, attn_kv, pack, shards):
    ctx_size = first.shape[0]
    chips = ctx_size // 2
    steps = ctx_size
    tile = pack.rows // steps
    out_tile = pack.main // 2
    assert pack.rows // pack.split == 2 and pack.split % tile == 0
    assert out_tile == chips * pack.rest and pack.main % pack.rest == 0
    at = lambda i: jnp.minimum(i, steps - 1)
    rows = attn_out.shape[1]
    piece = lambda array: pl.BlockSpec((1,) + array.shape[1:], lambda i: (at(i), 0, 0))
    attn_in = attn_q.shape[2] + attn_kv.shape[2]
    return pl.pallas_call(
        functools.partial(finish_kernel, shards, chips, pack),
        name="finish",
        grid=(steps + 1,),
        in_specs=[
            pl.BlockSpec((ctx_size, tile, pack.half), lambda i: (0, at(i), 0)),
            pl.BlockSpec(
                (ctx_size, tile, pack.half),
                lambda i: (0, pack.rows // tile + at(i) % (pack.split // tile), 0),
            ),
            pl.BlockSpec((2, out_tile, pack.half), lambda i: (at(i) // 2, at(i) % 2, 0)),
            pl.BlockSpec((ctx_size, pack.rest, pack.half), lambda i: (0, pack.main // pack.rest, 0)),
            piece(attn_out),
            piece(attn_q),
            piece(attn_kv),
        ],
        out_specs=[
            pl.BlockSpec((tile, 2 * FF), lambda i: (at(i), 0)),
            pl.BlockSpec((out_tile, 2 * pack.half), lambda i: (i, 0)),
            pl.BlockSpec((rows, attn_out.shape[2]), lambda i: (at(i), 0)),
            pl.BlockSpec((rows, attn_in), lambda i: (at(i), 0)),
        ],
        out_shape=[
            jax.ShapeDtypeStruct((pack.rows, 2 * FF), jnp.float32),
            jax.ShapeDtypeStruct((FF // shards, 2 * pack.half), jnp.float32),
            jax.ShapeDtypeStruct((steps * rows, attn_out.shape[2]), jnp.float32),
            jax.ShapeDtypeStruct((steps * rows, attn_in), jnp.float32),
        ],
        compiler_params=pltpu.CompilerParams(vmem_limit_bytes=VMEM_LIMIT),
    )(second, second, first, first, attn_out, attn_q, attn_kv)


TANH_SCALE = 0.7978845608028654
TANH_CUBE = 0.044715
UNIT_TILE = 384


def mlp_kernel(
    shards, pack, mine, x_left, x_right, x_x, x_y, c_own, c_x_left, c_x_right, c_y_left, c_y_right, c_left, c_right,
    normed_grad, out_own, out_x, out_y, out_left, out_right, grad_first, grad_second,
    w_in, w_out, xs, cs, hidden, grads, part, from_x, from_y, corner_left, corner_right,
    out_stage, pair_in, pair_out, local_sems, send_sems, recv_sems,
):
    wire = Wire(send_sems, recv_sems)
    core = lax.rem(wire.ctx, 2)
    other = 1 - core
    rows, half = x_left.shape
    width = 2 * half
    units = w_in.shape[2]
    tiles = units // UNIT_TILE
    left, right = pl.ds(0, half), pl.ds(half, half)
    locals_ = []

    def copy_in(source, target):
        copy = pltpu.make_async_copy(source, target, local_sems.at[len(locals_)])
        copy.start()
        locals_.append(copy)
        return copy

    def spans():
        for shard in range(shards):
            for one in pack.in_spans(shard):
                yield shard, w_in, one
            for one in pack.out_spans(shard, shards):
                yield shard, w_out, one

    def packed(shard, one):
        return mine.at[shard, pl.ds(*one[0]), pl.ds(*one[1])]

    def placed(which, target, one):
        return target.at[which, pl.ds(*one[2]), pl.ds(*one[3])]

    loads = [
        copy_in(x_left, xs.at[0, :, left]),
        copy_in(x_right, xs.at[0, :, right]),
        copy_in(c_own, cs.at[0]),
    ]
    for shard, target, one in spans():
        loads.append(copy_in(packed(shard, one), placed(core, target, one)))
    late = [
        copy_in(source, target)
        for source, target in (
            (x_x, xs.at[1, :, left]),
            (x_y, xs.at[2, :, right]),
            (c_x_left, cs.at[1, :, left]),
            (c_x_right, cs.at[1, :, right]),
            (c_y_left, cs.at[2, :, left]),
            (c_y_right, cs.at[2, :, right]),
            (c_left, cs.at[3, :, left]),
            (c_right, cs.at[3, :, right]),
        )
    ]
    wire.meet([wire.plane(mask) for mask in PLANE_PEERS])
    x_copies = [
        wire.send(x_right, xs.at[1, :, right], wire.plane(2)),
        wire.send(x_left, xs.at[2, :, left], wire.plane(4)),
    ]
    swaps = [
        wire.send(packed(shard, one), placed(core, target, one), wire.plane(1))
        for shard, target, one in spans()
    ]
    for copy in loads:
        copy.wait()
    for copy in swaps:
        copy.wait_recv()

    def one_chunk(at):
        gate = dot(xs[at], w_in[0])
        up = dot(xs[at], w_in[1])
        grad = nt_dot(cs[at, :, left], w_out[0]) + nt_dot(cs[at, :, right], w_out[1])
        square = gate * gate
        bend = jnp.tanh(TANH_SCALE * gate * (1.0 + TANH_CUBE * square))
        lift = 0.5 + 0.5 * bend
        value = gate * lift
        slope = lift + (0.5 * TANH_SCALE) * gate * (1.0 - bend * bend) * (
            1.0 + (3.0 * TANH_CUBE) * square
        )
        hidden[at] = low(value * up)
        grads[0, at] = low(grad * up * slope)
        grads[1, at] = low(grad * value)

        def one_half(span):
            total = nt_dot(grads[0, at], w_in[0, span, :])
            return total + nt_dot(grads[1, at], w_in[1, span, :])

        return one_half

    one_half = one_chunk(0)
    for span in (left, right):
        normed_grad[:, span] = one_half(span)
    for copy in x_copies:
        copy.wait_recv()
    corners = [
        wire.send(x_x, xs.at[3, :, left], wire.plane(4)),
        wire.send(x_y, xs.at[3, :, right], wire.plane(2)),
    ]
    for copy in late:
        copy.wait()
    one_half = one_chunk(1)
    part[0, :, left] = low(one_half(left))
    early = [wire.send(part.at[0, :, left], from_x.at[:, left], wire.plane(2))]
    part[0, :, right] = low(one_half(right))
    one_half = one_chunk(2)
    part[1, :, right] = low(one_half(right))
    early.append(wire.send(part.at[1, :, right], from_y.at[:, right], wire.plane(4)))
    part[1, :, left] = low(one_half(left))
    for copy in corners:
        copy.wait_recv()
    one_half = one_chunk(3)
    part[2, :, left] = low(one_half(left))
    corner = [wire.send(part.at[2, :, left], corner_left, wire.plane(2))]
    part[2, :, right] = low(one_half(right))
    corner.append(wire.send(part.at[2, :, right], corner_right, wire.plane(4)))

    out_copies = {}

    def out_part(at, targets):
        slot = at % 2
        for copy in out_copies.get(slot, ()):
            copy.wait()
        for n, span in enumerate((left, right)):
            out_stage[slot, :, span] = low(dot(hidden[at], w_out[n]))
        out_copies[slot] = [copy_in(out_stage.at[(slot,) + here], target) for here, target in targets]

    every = slice(None)
    out_part(3, [((every, left), out_left), ((every, right), out_right)])
    out_part(2, [((), out_y)])
    out_part(1, [((), out_x)])
    out_part(0, [((), out_own)])

    everything = lambda ref: ref[...].reshape(ref.shape[0] * rows, ref.shape[2])

    def in_tile(which, tile):
        columns = pl.ds(tile * UNIT_TILE, UNIT_TILE)
        picked = grads[which, :, :, columns].reshape(4 * rows, UNIT_TILE)
        return columns, tn_dot(everything(xs), picked)

    pairs_in = []
    for tile in range(tiles):
        columns, value = in_tile(other, tile)
        w_in[0, :, columns] = low(value)
        pairs_in.append(wire.send(w_in.at[0, :, columns], pair_in.at[:, columns], wire.plane(1)))
    merged = []
    corner[0].wait_recv()
    part[1, :, left] = add_low(part[1, :, left], corner_left[...])
    merged.append(wire.send(part.at[1, :, left], from_y.at[:, left], wire.plane(4)))
    corner[1].wait_recv()
    part[0, :, right] = add_low(part[0, :, right], corner_right[...])
    merged.append(wire.send(part.at[0, :, right], from_x.at[:, right], wire.plane(2)))

    def out_tile(which, tile):
        columns = pl.ds(tile * UNIT_TILE, UNIT_TILE)
        picked = hidden[:, :, columns].reshape(4 * rows, UNIT_TILE)
        span = pl.ds(pl.multiple_of(which * half, half), half)
        return columns, tn_dot(picked, cs[:, :, span].reshape(4 * rows, half))

    pairs_out = []
    for tile in range(tiles):
        span, value = out_tile(other, tile)
        w_out[0, span, :] = low(value)
        pairs_out.append(wire.send(w_out.at[0, span, :], pair_out.at[span, :], wire.plane(1)))
    final = []
    for tile in range(tiles):
        columns, value = in_tile(core, tile)
        pairs_in[tile].wait_recv()
        w_in[1, :, columns] = low(value + pair_in[:, columns].astype(jnp.float32))
    for tile in range(tiles):
        span, value = out_tile(core, tile)
        pairs_out[tile].wait_recv()
        w_out[1, span, :] = low(value + pair_out[span, :].astype(jnp.float32))
    for shard, source, one in spans():
        start, count = one[0]
        if start < pack.main_start:
            target = grad_first.at[shard, pl.ds(start, count), pl.ds(*one[1])]
        else:
            target = grad_second.at[shard, pl.ds(start - pack.main_start, count), pl.ds(*one[1])]
        final.append(copy_in(placed(1, source, one), target))
    for copy in early + merged:
        copy.wait_recv()
    normed_grad[...] += from_x[...].astype(jnp.float32) + from_y[...].astype(jnp.float32)
    for copies in out_copies.values():
        for copy in copies:
            copy.wait()
    for copy in final:
        copy.wait()
    wire.finish()


def mlp(mine, x, upstream, pack):
    rows, half = x[0].shape
    width = 2 * half
    units = pack.half + pack.tail
    shards = mine.shape[0]
    low_shape = lambda *shape: jax.ShapeDtypeStruct(shape, jnp.bfloat16)
    low_scratch = lambda *shape: pltpu.VMEM(shape, jnp.bfloat16)
    parts = shards * (1 + pack.rows // pack.split + 2)
    copies = parts + 4 + 2 + 2 + 2 + 2 * (units // UNIT_TILE)
    locals_ = 3 + parts + 8 + 5 + parts
    return pl.pallas_call(
        functools.partial(mlp_kernel, shards, pack),
        name="mlp",
        in_specs=[ANY] * 12,
        out_specs=[pl.BlockSpec(memory_space=pltpu.VMEM)] + [ANY] * 7,
        out_shape=[
            jax.ShapeDtypeStruct((rows, width), jnp.float32),
            low_shape(rows, width),
            low_shape(rows, width),
            low_shape(rows, width),
            low_shape(rows, half),
            low_shape(rows, half),
            low_shape(shards, pack.main_start, half),
            low_shape(shards, pack.total - pack.main_start, half),
        ],
        scratch_shapes=[
            low_scratch(2, width, units),
            low_scratch(2, units, half),
            low_scratch(4, rows, width),
            low_scratch(4, rows, width),
            low_scratch(4, rows, units),
            low_scratch(2, 4, rows, units),
            low_scratch(3, rows, width),
            low_scratch(rows, width),
            low_scratch(rows, width),
            low_scratch(rows, half),
            low_scratch(rows, half),
            low_scratch(2, rows, width),
            low_scratch(width, units),
            low_scratch(units, half),
            dma_sems(locals_),
            dma_sems(copies),
            dma_sems(copies),
        ],
        compiler_params=pltpu.CompilerParams(
            collective_id=5, has_side_effects=True, vmem_limit_bytes=MLP_VMEM
        ),
    )(mine, *x, *upstream)


class Layout:
    def __init__(self, ctx_size, fsdp_size):
        self.ctx_size = ctx_size
        self.shards = fsdp_size
        self.chips = ctx_size // 2
        self.index = lax.axis_index("ctx")
        self.chip = self.index // 2
        self.core = self.index % 2
        units = FF // (self.shards * self.chips)
        self.main = units // LANES * LANES
        self.rest = units - self.main
        self.per_shard = FF // self.shards
        self.rest_start = self.chips * self.main
        self.plane = ctx_size == 8 and fsdp_size == 4

    def xor(self, values, mask):
        pairs = [(i, i ^ mask) for i in range(self.ctx_size)]
        return lax.ppermute(values, "ctx", pairs)

    def same_core_groups(self):
        return [[chip * 2 + core for chip in range(self.chips)] for core in range(2)]

    def join_corner(self, to_x, to_y, left, right, token):
        half = left.shape[1]
        left = after(token, self.xor(left, 2))
        right = after(token, self.xor(right, 4))
        to_y = jnp.concatenate([add_low(to_y[:, :half], left), to_y[:, half:]], axis=1)
        to_x = jnp.concatenate([to_x[:, :half], add_low(to_x[:, half:], right)], axis=1)
        return to_x, to_y

    def sum_neighbours(self, own, to_x, to_y):
        wide = lambda part: part.astype(jnp.float32)
        return wide(own) + wide(self.xor(to_y, 4)) + wide(self.xor(to_x, 2))

    def gather_chips(self, values):
        groups = self.same_core_groups()
        return lax.all_gather(values, "ctx", axis=0, tiled=True, axis_index_groups=groups)

    def scatter_chips(self, partial):
        groups = self.same_core_groups()
        total = lax.psum_scatter(
            low(partial), "ctx", scatter_dimension=0, tiled=True, axis_index_groups=groups
        )
        return total.astype(jnp.float32)

    def columns_of_chip(self, weights, start):
        parts = []
        if self.main:
            for shard in range(self.shards):
                at = start + shard * self.per_shard + self.chip * self.main
                parts.append(lax.dynamic_slice_in_dim(weights, at, self.main, 1))
        if self.rest:
            for shard in range(self.shards):
                at = start + shard * self.per_shard + self.rest_start + self.chip * self.rest
                parts.append(lax.dynamic_slice_in_dim(weights, at, self.rest, 1))
        return jnp.concatenate(parts, axis=1)

    def rows_of_chip(self, weights):
        parts = []
        if self.main:
            parts.append(lax.dynamic_slice_in_dim(weights, self.chip * self.main, self.main, 0))
        if self.rest:
            at = self.rest_start + self.chip * self.rest
            parts.append(lax.dynamic_slice_in_dim(weights, at, self.rest, 0))
        return jnp.concatenate(parts, axis=0)

    def by_core(self, mine, other):
        first = jnp.where(self.core == 0, mine, other)
        second = jnp.where(self.core == 0, other, mine)
        return first, second

    def mine_in(self, shard, later=0):
        return self.columns_of_chip(shard, self.core * FF + later)

    def mine_out(self, shard, later=0):
        width = shard.shape[1]
        half = lax.dynamic_slice_in_dim(shard, self.core * (width // 2) + later, width // 2, 1)
        return self.rows_of_chip(half)

    def gather_mlp_in(self, shard):
        mine = lax.all_gather(self.mine_in(shard), "fsdp", axis=0, tiled=True)
        return self.by_core(mine, self.xor(mine, 1))

    def gather_mlp_out(self, shard):
        width = shard.shape[1]
        mine = lax.all_gather(self.mine_out(shard), "fsdp", axis=0)
        mine = jnp.concatenate(
            [
                mine[:, : self.main].reshape(self.shards * self.main, width // 2),
                mine[:, self.main :].reshape(self.shards * self.rest, width // 2),
            ],
            axis=0,
        )
        return jnp.concatenate(self.by_core(mine, self.xor(mine, 1)), axis=1)

    def sum_pair(self, first, second):
        keep = jnp.where(self.core == 0, first, second)
        send = jnp.where(self.core == 0, second, first)
        return keep + self.xor(low(send), 1).astype(jnp.float32)

    def reduce_mlp_in(self, gate, up):
        total = low(self.sum_pair(gate, up))
        return lax.psum_scatter(total, "fsdp", scatter_dimension=0, tiled=True)

    def order_mlp_in(self, every):
        rows = every.shape[1]
        every = every.reshape(self.chips, 2, rows, every.shape[2])
        split = self.shards * self.main
        main = every[..., :split].reshape(self.chips, 2, rows, self.shards, self.main)
        rest = every[..., split:].reshape(self.chips, 2, rows, self.shards, self.rest)
        main = main.transpose(2, 1, 3, 0, 4).reshape(rows, 2, self.shards, -1)
        rest = rest.transpose(2, 1, 3, 0, 4).reshape(rows, 2, self.shards, -1)
        return jnp.concatenate([main, rest], axis=3).reshape(rows, 2 * FF).astype(jnp.float32)

    def reduce_mlp_out(self, grad):
        width = grad.shape[1]
        total = low(self.sum_pair(grad[:, : width // 2], grad[:, width // 2 :]))
        split = self.shards * self.main
        main = total[:split].reshape(self.shards, self.main, width // 2)
        rest = total[split:].reshape(self.shards, self.rest, width // 2)
        total = jnp.concatenate([main, rest], axis=1)
        return lax.psum_scatter(total, "fsdp", scatter_dimension=0, tiled=True)[0]

    def order_mlp_out(self, every):
        width = 2 * every.shape[2]
        every = every.reshape(self.chips, 2, self.main + self.rest, width // 2)
        main = every[:, :, : self.main].transpose(0, 2, 1, 3).reshape(-1, width)
        rest = every[:, :, self.main :].transpose(0, 2, 1, 3).reshape(-1, width)
        return jnp.concatenate([main, rest], axis=0).astype(jnp.float32)

    def gather_whole(self, shard):
        rows = shard.shape[0] // self.ctx_size
        piece = lax.dynamic_slice_in_dim(shard, self.index * rows, rows, 0)
        piece = lax.all_gather(piece, "fsdp", axis=0)
        piece = lax.all_gather(piece, "ctx", axis=1, tiled=True)
        return piece.reshape(-1, shard.shape[1])

    def reduce_whole(self, grad):
        rows = grad.shape[0] // self.shards
        total = grad.reshape(self.shards, rows, grad.shape[1])
        total = lax.psum_scatter(total, "ctx", scatter_dimension=1, tiled=True)
        total = lax.psum_scatter(total, "fsdp", scatter_dimension=0, tiled=True)[0]
        return lax.all_gather(total, "ctx", axis=0, tiled=True).astype(jnp.float32)

    def reduce_gain(self, grad):
        total = jnp.sum(lax.all_gather(grad, ("ctx", "fsdp"), axis=0), axis=0)
        rows = grad.shape[0] // self.shards
        return lax.dynamic_slice_in_dim(total, lax.axis_index("fsdp") * rows, rows)


def per_device(
    ctx_size,
    fsdp_size,
    tokens,
    order,
    lengths,
    norm_attn,
    w_attn_in,
    w_attn_out,
    norm_mlp,
    w_mlp_in,
    w_mlp_out,
    cotangent,
):
    lay = Layout(ctx_size, fsdp_size)
    x, upstream = tokens[0], cotangent[0]
    own_rows, width = x.shape
    block = own_rows // ROUNDS
    if lay.plane:
        pack = Pack(w_mlp_in.shape[0], width // 2, lay.chips, FF // lay.chips, lay.main, lay.rest)
        pieces = lambda w: w.reshape(ctx_size, w.shape[0] // ctx_size, w.shape[1])
        in_line, gains, mine, upstream_x, upstream_y = share_line(
            pieces(w_attn_in),
            jnp.stack([norm_attn, norm_mlp]),
            w_mlp_in,
            w_mlp_out,
            upstream,
            pack,
            fsdp_size,
        )
        mine = lax.all_gather(mine, "fsdp", axis=0)
        in_attn, out_line, *tables = share_plane(
            pieces(w_attn_in),
            in_line,
            pieces(w_attn_out),
            order,
            lengths,
            own_rows,
            ctx_size,
            fsdp_size,
        )
        in_attn = in_attn.reshape(width, -1)
    else:
        tables = place_tables_alone(ctx_size, order, lengths, own_rows)
        in_attn = lay.gather_whole(w_attn_in)
        out_attn = lay.gather_whole(w_attn_out)
        gains = jnp.pad(jnp.stack([norm_attn, norm_mlp]).astype(jnp.float32), ((0, 6), (0, 0)))
        gains = lax.all_gather(gains, "fsdp", axis=0)
        gate_in, up_in = lay.gather_mlp_in(w_mlp_in)
        out_mlp = lay.gather_mlp_out(w_mlp_out)
        upstream_all = lay.gather_chips(upstream)

    where, key_place, bounds, bounds_wide, cosine, sine_part = tables
    normed_one, queries = project(x, gains, in_attn, cosine, sine_part)
    if lay.plane:
        key_value, out_attn, token = gather_plane(
            queries, pieces(w_attn_out), out_line, ctx_size, fsdp_size
        )
        out_attn = out_attn.reshape(-1, width)
        half = width // 2
        upstream_all = (
            upstream,
            upstream_x,
            lay.xor(after(token, upstream[:, half:]), 2),
            lay.xor(after(token, upstream[:, :half]), 4),
            upstream_y,
            lay.xor(after(token, upstream_x), 4),
            lay.xor(after(token, upstream_y), 2),
        )
    else:
        key_value = lax.all_gather(queries[H:], "ctx", axis=0)
    mixed, log_total = attend(where, queries, key_value, key_place, bounds)
    middle, left, right = middle_forward(x, mixed, gains, out_attn)

    if lay.plane:
        grad_normed_two, out_own, *out_parts, grad_first, grad_second = mlp(
            mine,
            (left, right, lay.xor(left, 2), lay.xor(right, 4)),
            upstream_all,
            pack,
        )
        grad_first = lax.psum_scatter(grad_first, "fsdp", scatter_dimension=0, tiled=True)[0]
        grad_second = lax.psum_scatter(grad_second, "fsdp", scatter_dimension=0, tiled=True)[0]
    else:
        normed_all = lay.gather_chips(jnp.concatenate([left, right], axis=1))
        gate = dot(normed_all, gate_in)
        up = dot(normed_all, up_in)
        hidden, hidden_back = jax.vjp(geglu, gate, up)
        hidden = low(hidden)
        grad_hidden = dot_nt(upstream_all, out_mlp)
        grad_gate, grad_up = hidden_back(grad_hidden)
        grad_gate = low(grad_gate)
        grad_up = low(grad_up)
        grad_normed_two = lay.scatter_chips(dot_nt(grad_gate, gate_in) + dot_nt(grad_up, up_in))
        mixed_out = lay.scatter_chips(dot(hidden, out_mlp))
        grad_out_mlp = lay.reduce_mlp_out(dot_tn(hidden, upstream_all))
        grad_in_mlp = lay.reduce_mlp_in(dot_tn(normed_all, grad_gate), dot_tn(normed_all, grad_up))

    grad_middle, grad_mixed, grad_out_attn, grad_gain_mlp, token = middle_back(
        grad_normed_two, middle, upstream, mixed, gains, out_attn
    )
    out_parts = lay.join_corner(*out_parts, token) if lay.plane else ()
    grad_query, grad_kv = attend_back(
        where,
        queries,
        key_value,
        grad_mixed,
        mixed,
        log_total,
        key_place,
        bounds_wide,
        cosine,
        sine_part,
        out_parts,
    )
    if lay.plane:
        mixed_out = lay.sum_neighbours(out_own, *out_parts)
    result = middle + mixed_out
    if lay.plane:
        split = lambda grad: grad.reshape(fsdp_size, lay.chips, 2, -1, grad.shape[1])
        grad_kv = grad_kv.reshape(ROUNDS, lay.chips, 2, block, 2 * HD)
        *halves, grad_first, grad_inputs, grad_gain_attn = project_back_plane(
            grad_kv,
            split(grad_out_attn),
            grad_first,
            grad_query,
            normed_one,
            x,
            cosine,
            sine_part,
            gains,
            in_attn,
            ctx_size,
        )
        grad_inputs = grad_middle + grad_inputs
        grad_out_attn, grad_in_queries, grad_in_keys, grad_second, grad_gains = reduce_late(
            halves, grad_second, grad_gain_attn, grad_gain_mlp, ctx_size
        )
        grad_in_mlp, grad_out_mlp, grad_out_attn, grad_in_attn = finish(
            grad_first,
            grad_second,
            grad_out_attn,
            grad_in_queries,
            grad_in_keys,
            pack,
            fsdp_size,
        )
        grad_gain_attn, grad_gain_mlp = grad_gains[0], grad_gains[1]
    else:
        grad_kv = grad_kv.reshape(ROUNDS, ctx_size, block, 2 * HD)
        grad_kv = lax.psum_scatter(grad_kv, "ctx", scatter_dimension=1, tiled=True)
        grad_kv = grad_kv.reshape(own_rows, 2 * HD).astype(jnp.float32)
        grad_in_queries, grad_normed = project_back_queries(grad_query, normed_one, in_attn)
        grad_in_keys, grad_inputs, grad_gain_attn = project_back_keys(
            grad_kv, cosine, sine_part, normed_one, grad_normed, x, grad_middle, gains, in_attn
        )
        grad_in_attn = jnp.concatenate([grad_in_queries, grad_in_keys], axis=1)
        grad_out_attn = lay.reduce_whole(grad_out_attn)
        grad_in_attn = lay.reduce_whole(grad_in_attn)
        grad_in_mlp = lay.order_mlp_in(lax.all_gather(grad_in_mlp, "ctx", axis=0))
        grad_out_mlp = lay.order_mlp_out(lax.all_gather(grad_out_mlp, "ctx", axis=0))
        grad_gain_attn = lay.reduce_gain(grad_gain_attn[0])
        grad_gain_mlp = lay.reduce_gain(grad_gain_mlp[0])
    return (
        low(result)[None],
        grad_inputs[None],
        grad_gain_attn,
        grad_in_attn,
        grad_out_attn,
        grad_gain_mlp,
        grad_in_mlp,
        grad_out_mlp,
    )


def solution(mesh):
    in_specs = (
        P("fsdp", "ctx", None),
        P("fsdp", None),
        P("fsdp", None),
        P("fsdp"),
        P("fsdp", None),
        P("fsdp", None),
        P("fsdp"),
        P("fsdp", None),
        P("fsdp", None),
        P("fsdp", "ctx", None),
    )
    out_specs = (
        P("fsdp", "ctx", None),
        P("fsdp", "ctx", None),
        P("fsdp"),
        P("fsdp", None),
        P("fsdp", None),
        P("fsdp"),
        P("fsdp", None),
        P("fsdp", None),
    )

    def run(*arrays):
        return per_device(mesh.shape["ctx"], mesh.shape["fsdp"], *arrays)

    return jax.shard_map(run, mesh=mesh, in_specs=in_specs, out_specs=out_specs, check_vma=False)
```

```python
import functools

import jax
import jax.numpy as jnp
from jax import lax
from jax.experimental import pallas as pl
from jax.experimental.pallas import tpu as pltpu
from jax.sharding import PartitionSpec as P

H = 12
HD = 128
FF = 4608
WINDOW = 1024
ROUNDS = 4
LANES = 128


EPS = 1e-06


def rms_norm(values, gain):
    return values * lax.rsqrt(jnp.mean(values * values, axis=-1, keepdims=True) + EPS) * gain


def geglu(gate, up):
    return jax.nn.gelu(gate, approximate=True) * up


def dot(left, right):
    return jnp.dot(left, right, preferred_element_type=jnp.float32)


def dot_nt(left, right):
    return jnp.einsum("ab,cb->ac", left, right, preferred_element_type=jnp.float32)


def dot_tn(left, right):
    return jnp.einsum("ab,ac->bc", left, right, preferred_element_type=jnp.float32)


def nt_dot(left, right):
    return lax.dot_general(left, right, (((1,), (1,)), ((), ())), preferred_element_type=jnp.float32)


def tn_dot(left, right):
    return lax.dot_general(left, right, (((0,), (0,)), ((), ())), preferred_element_type=jnp.float32)


def low(values):
    return values.astype(jnp.bfloat16)


VMEM_LIMIT = 56 * 1024 * 1024
MLP_VMEM = 62 * 1024 * 1024

def gain_row(ref, which):
    parts = [ref[shard, which : which + 1, :] for shard in range(ref.shape[0])]
    return jnp.concatenate(parts, axis=1)


def norm_scale(values):
    return lax.rsqrt(jnp.mean(values * values, axis=-1, keepdims=True) + EPS)


def norm_back(values, gain, incoming):
    scale = norm_scale(values)
    weighted = incoming * gain
    inner = jnp.mean(weighted * values, axis=-1, keepdims=True)
    grad = scale * weighted - values * (scale * scale * scale * inner)
    return grad, jnp.sum(incoming * values * scale, axis=0, keepdims=True)


def project_kernel(heads, x_ref, gain_ref, w_ref, cos_ref, sin_ref, normed_ref, heads_ref):
    step = pl.program_id(0)

    @pl.when(step == 0)
    def _():
        x = x_ref[...].astype(jnp.float32)
        normed_ref[...] = low(x * norm_scale(x) * gain_row(gain_ref, 0))

    part = dot(normed_ref[...], w_ref[...])
    cosine, sine_part = cos_ref[...], sin_ref[...]
    count = heads_ref.shape[0]
    for j in range(count):
        value = part[:, j * HD : (j + 1) * HD]
        turned = value * cosine + pltpu.roll(value, HD // 2, 1) * sine_part
        head = step * count + j
        value = jnp.where(head < heads, turned * HD ** (-0.5), jnp.where(head == heads, turned, value))
        heads_ref[j] = low(value)


def project(x, gain, w, cosine, sine_part):
    rows, width = x.shape
    count = (H + 2) // PROJECT_STEPS
    whole = lambda *shape: pl.BlockSpec(shape, lambda i: (0,) * len(shape))
    return pl.pallas_call(
        functools.partial(project_kernel, H),
        grid=(PROJECT_STEPS,),
        name="project",
        in_specs=[
            whole(rows, width),
            whole(*gain.shape),
            pl.BlockSpec((width, count * HD), lambda i: (0, i)),
            whole(rows, HD),
            whole(rows, HD),
        ],
        out_specs=[
            whole(rows, width),
            pl.BlockSpec((count, rows, HD), lambda i: (i, 0, 0)),
        ],
        out_shape=[
            jax.ShapeDtypeStruct((rows, width), jnp.bfloat16),
            jax.ShapeDtypeStruct((H + 2, rows, HD), jnp.bfloat16),
        ],
        compiler_params=pltpu.CompilerParams(vmem_limit_bytes=VMEM_LIMIT),
    )(x, gain, w, cosine, sine_part)


PROJECT_STEPS = 2
HEADS_STEP = 4
ANY = pl.BlockSpec(memory_space=pl.ANY)


class Window:
    def __init__(self, rows):
        self.block = rows // ROUNDS
        self.blocks = (WINDOW + self.block - 2) // self.block + 1
        self.span = self.blocks * self.block


def place_tables(
    index, devices, order_ref, lengths_ref, frequency_ref,
    where_ref, key_place_ref, bounds_ref, wide_ref, cos_ref, sin_ref, order_rows,
):
    block = bounds_ref.shape[0] // ROUNDS
    count = order_ref.shape[1] // block
    window = Window(block * ROUNDS)
    blocks = [order_ref[:, i * block : (i + 1) * block] for i in range(count)]
    order_rows[...] = jnp.concatenate(blocks, axis=0).astype(jnp.float32)
    blocks = order_rows[...]
    block_of = lambda place: jnp.floor((place + 0.5) * (1.0 / block))
    held = block_of(blocks[:, :1])
    offsets = low(blocks - held * block)
    at = lax.broadcasted_iota(jnp.int32, (count, 1), 0).astype(jnp.float32)
    lane = lax.broadcasted_iota(jnp.int32, (1, LANES), 1).astype(jnp.float32)
    step = jnp.where(lane < window.blocks, lane, lane - window.blocks)
    lengths = lengths_ref[...].astype(jnp.float32)
    ends = [lengths[:, :1]]
    for j in range(1, lengths.shape[1]):
        ends.append(ends[-1] + lengths[:, j : j + 1])

    def least_of(place):
        start = jnp.zeros_like(place)
        for end in ends:
            start = jnp.where(end <= place, end, start)
        return jnp.maximum(start, place - (WINDOW - 1))

    where_ref[...] = jnp.zeros_like(where_ref)
    own = []
    for r in range(ROUNDS):
        mine = order_rows[pl.ds(index * ROUNDS + r, 1), :]
        own.append(mine)
        wanted = block_of(mine[:, :1]) - (window.blocks - 1) + step
        match = (held == jnp.maximum(wanted, 0.0)).astype(jnp.float32)
        where = jnp.sum(match * at, axis=0, keepdims=True)
        device = jnp.floor((where + 0.5) * (1.0 / ROUNDS))
        target = (where - ROUNDS * device) * devices + device
        where_ref[r : r + 1, :] = jnp.where(lane < window.blocks, where, target).astype(jnp.int32)
        inner = tn_dot(low(match), offsets)
        pieces = []
        for j in range(window.blocks):
            one = wanted[:, j : j + 1]
            pieces.append(inner[j : j + 1] + jnp.where(one >= 0.0, one * block, 1e9))
        key_place_ref[r] = jnp.concatenate(pieces, axis=1)
        wide_ref[r, :1, :] = jnp.concatenate([mine] * HEADS_STEP, axis=1)
        wide_ref[r, 1:, :] = jnp.concatenate([least_of(mine)] * HEADS_STEP, axis=1)
    own = jnp.concatenate(own, axis=1)
    own = jnp.broadcast_to(own, (8, own.shape[1])).T[:, :1]
    bounds_ref[:, :1] = own
    bounds_ref[:, 1:] = least_of(own)
    angles = own * frequency_ref[...]
    cos_ref[...] = jnp.cos(angles)
    sign = jnp.where(lane < HD // 2, -1.0, 1.0)
    sin_ref[...] = jnp.sin(angles) * sign


def place_arrays(order, lengths, rows):
    window = Window(rows)
    frequency = 10000.0 ** (-jnp.arange(HD // 2, dtype=jnp.float32) / (HD // 2))
    operands = (
        order,
        lengths,
        jnp.concatenate([frequency, frequency])[None],
    )
    wide = jax.ShapeDtypeStruct((rows, HD), jnp.float32)
    shapes = (
        jax.ShapeDtypeStruct((8, LANES), jnp.int32),
        jax.ShapeDtypeStruct((ROUNDS, 1, window.span), jnp.float32),
        jax.ShapeDtypeStruct((rows, 2), jnp.float32),
        jax.ShapeDtypeStruct((ROUNDS, 2, HEADS_STEP * window.block), jnp.float32),
        wide,
        wide,
    )
    return operands, shapes


def place_tables_alone(devices, order, lengths, rows):
    operands, shapes = place_arrays(order, lengths, rows)

    def kernel(*refs):
        place_tables(lax.axis_index("ctx"), devices, *refs)

    block = Window(rows).block

    vmem = pl.BlockSpec(memory_space=pltpu.VMEM)
    return pl.pallas_call(
        kernel,
        name="places",
        in_specs=[vmem] * len(operands),
        out_specs=[vmem] * len(shapes),
        out_shape=shapes,
        scratch_shapes=[pltpu.VMEM((order.shape[1] // block, block), jnp.float32)],
    )(*operands)


def load_window(blocks, block, where_ref, kv_ref, window):
    r = pl.program_id(0)
    for j in range(blocks):
        rows = slice(j * block, (j + 1) * block)
        at = where_ref[r, j]
        device, round_ = at // ROUNDS, lax.rem(at, ROUNDS)
        span = pl.ds(pl.multiple_of(round_ * block, 16), block)
        window[rows, :HD] = kv_ref[device, 0, span, :]
        window[rows, HD:] = kv_ref[device, 1, span, :]


def attend_kernel(
    blocks, block, where_ref, q_ref, kv_ref, key_place_ref, bounds_ref, out_ref, log_ref, window, bias
):
    load_window(blocks, block, where_ref, kv_ref, window)
    key_place = key_place_ref[0]
    allowed = (key_place <= bounds_ref[:, :1]) & (key_place >= bounds_ref[:, 1:])
    bias[...] = jnp.where(allowed, 0.0, -1e30)
    for part in range(q_ref.shape[0] // HEADS_STEP):
        first = part * HEADS_STEP
        queries = q_ref[first : first + HEADS_STEP].reshape(HEADS_STEP * block, HD)
        scores = nt_dot(queries, window[:, :HD])
        scores = scores.reshape(HEADS_STEP, block, blocks * block) + bias[...][None]
        peak = jnp.max(scores, axis=-1, keepdims=True)
        weights = jnp.exp(scores - peak)
        total = jnp.sum(weights, axis=-1, keepdims=True).reshape(HEADS_STEP * block, 1)
        weights = low(weights).reshape(HEADS_STEP * block, blocks * block)
        mixed = low(dot(weights, window[:, HD:]) / total)
        for j in range(HEADS_STEP):
            columns = slice((first + j) * HD, (first + j + 1) * HD)
            out_ref[:, columns] = mixed[j * block : (j + 1) * block]
        log_total = peak.reshape(HEADS_STEP * block, 1) + jnp.log(total)
        log_ref[0, part] = jnp.broadcast_to(log_total, (HEADS_STEP * block, LANES)).T[:1, :]


def attend(where, queries, kv_blocks, key_place, bounds):
    heads, rows = H, queries.shape[1]
    window = Window(rows)
    block, span, parts = window.block, window.span, heads // HEADS_STEP
    grid_spec = pltpu.PrefetchScalarGridSpec(
        num_scalar_prefetch=1,
        grid=(ROUNDS,),
        in_specs=[
            pl.BlockSpec((heads, block, HD), lambda r, *_: (0, r, 0)),
            pl.BlockSpec(kv_blocks.shape, lambda r, *_: (0, 0, 0, 0)),
            pl.BlockSpec((1, 1, span), lambda r, *_: (r, 0, 0)),
            pl.BlockSpec((block, 2), lambda r, *_: (r, 0)),
        ],
        out_specs=[
            pl.BlockSpec((block, heads * HD), lambda r, *_: (r, 0)),
            pl.BlockSpec((1, parts, 1, HEADS_STEP * block), lambda r, *_: (r, 0, 0, 0)),
        ],
        scratch_shapes=[
            pltpu.VMEM((span, 2 * HD), jnp.bfloat16),
            pltpu.VMEM((block, span), jnp.float32),
        ],
    )
    return pl.pallas_call(
        functools.partial(attend_kernel, window.blocks, block),
        name="attend",
        grid_spec=grid_spec,
        out_shape=[
            jax.ShapeDtypeStruct((rows, heads * HD), jnp.bfloat16),
            jax.ShapeDtypeStruct((ROUNDS, parts, 1, HEADS_STEP * block), jnp.float32),
        ],
        compiler_params=pltpu.CompilerParams(vmem_limit_bytes=VMEM_LIMIT),
    )(where, queries, kv_blocks, key_place, bounds)


def attend_back_kernel(
    blocks, block, where_ref, q_ref, kv_ref, grad_ref, mixed_ref, log_ref, key_place_ref, bounds_ref,
    cos_ref, sin_ref, *refs,
):
    grad_q_ref, grad_kv_ref, window, bias, window_grad, total_grad = refs[-6:]
    r = pl.program_id(0)

    @pl.when(r == 0)
    def _():
        total_grad[...] = jnp.zeros_like(total_grad)

    load_window(blocks, block, where_ref, kv_ref, window)
    key_place = jnp.broadcast_to(key_place_ref[0], (8, blocks * block)).T[:, :1]
    allowed = (key_place <= bounds_ref[0, :1, :]) & (key_place >= bounds_ref[0, 1:, :])
    bias[...] = jnp.where(allowed, 0.0, -1e30)
    keys, values = window[:, :HD], window[:, HD:]
    cosine, sine_part = cos_ref[...], sin_ref[...]
    for part in range(q_ref.shape[0] // HEADS_STEP):
        first = part * HEADS_STEP
        spans = [slice((first + j) * HD, (first + j + 1) * HD) for j in range(HEADS_STEP)]
        queries = q_ref[first : first + HEADS_STEP].reshape(HEADS_STEP * block, HD)
        grads = jnp.concatenate([grad_ref[:, span] for span in spans], axis=0)
        delta = jnp.concatenate(
            [
                jnp.sum(
                    (grad_ref[:, span].astype(jnp.float32) * mixed_ref[:, span].astype(jnp.float32)).T,
                    axis=0,
                    keepdims=True,
                )
                for span in spans
            ],
            axis=1,
        )
        probs = jnp.exp(nt_dot(keys, queries) + (bias[...] - log_ref[0, part]))
        grad_scores = low(probs * (nt_dot(values, grads) - delta))
        grad_keys = dot(grad_scores, queries)
        grad_values = dot(low(probs), grads)
        if part == 0:
            window_grad[:, :HD] = grad_keys
            window_grad[:, HD:] = grad_values
        else:
            window_grad[:, :HD] += grad_keys
            window_grad[:, HD:] += grad_values
        grad_q = tn_dot(grad_scores, keys)
        for j, span in enumerate(spans):
            one = grad_q[j * block : (j + 1) * block]
            one = (one * cosine - pltpu.roll(one, HD // 2, 1) * sine_part) * HD ** (-0.5)
            grad_q_ref[:, span] = low(one)
    for j in range(blocks):
        total_grad[where_ref[r, blocks + j]] += window_grad[j * block : (j + 1) * block, :]

    @pl.when(r == pl.num_programs(0) - 1)
    def _():
        grad_kv_ref[...] = low(total_grad[...])


def attend_back(
    where, queries, kv_blocks, grads, mixed, log_total, key_place, bounds, cosine, sine_part, earlier
):
    heads, rows = H, queries.shape[1]
    kv_sums = (kv_blocks.shape[0] * ROUNDS, rows // ROUNDS, 2 * HD)
    window = Window(rows)
    block, span, parts = window.block, window.span, heads // HEADS_STEP
    width = HEADS_STEP * block
    grid_spec = pltpu.PrefetchScalarGridSpec(
        num_scalar_prefetch=1,
        grid=(ROUNDS,),
        in_specs=[
            pl.BlockSpec((heads, block, HD), lambda r, *_: (0, r, 0)),
            pl.BlockSpec(kv_blocks.shape, lambda r, *_: (0, 0, 0, 0)),
            pl.BlockSpec((block, heads * HD), lambda r, *_: (r, 0)),
            pl.BlockSpec((block, heads * HD), lambda r, *_: (r, 0)),
            pl.BlockSpec((1, parts, 1, width), lambda r, *_: (r, 0, 0, 0)),
            pl.BlockSpec((1, 1, span), lambda r, *_: (r, 0, 0)),
            pl.BlockSpec((1, 2, width), lambda r, *_: (r, 0, 0)),
            pl.BlockSpec((block, HD), lambda r, *_: (r, 0)),
            pl.BlockSpec((block, HD), lambda r, *_: (r, 0)),
        ]
        + [ANY] * len(earlier),
        out_specs=[
            pl.BlockSpec((block, heads * HD), lambda r, *_: (r, 0)),
            pl.BlockSpec(kv_sums, lambda r, *_: (0, 0, 0)),
        ],
        scratch_shapes=[
            pltpu.VMEM((span, 2 * HD), jnp.bfloat16),
            pltpu.VMEM((span, width), jnp.float32),
            pltpu.VMEM((span, 2 * HD), jnp.float32),
            pltpu.VMEM(kv_sums, jnp.float32),
        ],
    )
    return pl.pallas_call(
        functools.partial(attend_back_kernel, window.blocks, block),
        name="attend_back",
        grid_spec=grid_spec,
        out_shape=[
            jax.ShapeDtypeStruct((rows, heads * HD), jnp.bfloat16),
            jax.ShapeDtypeStruct(kv_sums, jnp.bfloat16),
        ],
        compiler_params=pltpu.CompilerParams(vmem_limit_bytes=VMEM_LIMIT),
    )(
        where,
        queries,
        kv_blocks,
        grads,
        mixed,
        log_total,
        key_place,
        bounds,
        cosine,
        sine_part,
        *earlier,
    )


MIDDLE_TILES = 3
FORWARD_TILES = 2


def whole_block(shape):
    return pl.BlockSpec(shape, lambda i: (0,) * len(shape))


def middle_kernel(x_ref, mixed_ref, gain_ref, w_ref, middle_ref, left_ref, right_ref):
    step = pl.program_id(0)
    tile = w_ref.shape[1]
    columns = pl.ds(pl.multiple_of(step * tile, tile), tile)
    middle_ref[:, columns] = x_ref[:, columns].astype(jnp.float32) + dot(mixed_ref[...], w_ref[...])

    @pl.when(step == pl.num_programs(0) - 1)
    def _():
        values = middle_ref[...]
        normed = low(values * norm_scale(values) * gain_row(gain_ref, 1))
        half = left_ref.shape[1]
        left_ref[...] = normed[:, :half]
        right_ref[...] = normed[:, half:]


def middle_forward(x, mixed, gains, w):
    rows, width = x.shape
    half = width // 2
    inner = mixed.shape[1]
    return pl.pallas_call(
        middle_kernel,
        name="middle",
        grid=(FORWARD_TILES,),
        in_specs=[
            whole_block((rows, width)),
            whole_block((rows, inner)),
            whole_block(gains.shape),
            pl.BlockSpec((inner, width // FORWARD_TILES), lambda i: (0, i)),
        ],
        out_specs=[whole_block((rows, width))] + [whole_block((rows, half))] * 2,
        out_shape=[
            jax.ShapeDtypeStruct((rows, width), jnp.float32),
            jax.ShapeDtypeStruct((rows, half), jnp.bfloat16),
            jax.ShapeDtypeStruct((rows, half), jnp.bfloat16),
        ],
        compiler_params=pltpu.CompilerParams(vmem_limit_bytes=VMEM_LIMIT),
    )(x, mixed, gains, w)


def middle_back_kernel(
    grad_ref, middle_ref, upstream_ref, mixed_ref, gain_ref, w_ref,
    grad_middle_ref, grad_mixed_ref, grad_w_ref, grad_gain_ref, token, branch,
):
    @pl.when(pl.program_id(0) == 0)
    def _():
        grad, grad_gain = norm_back(middle_ref[...], gain_row(gain_ref, 1), grad_ref[...])
        total = upstream_ref[...].astype(jnp.float32) + grad
        grad_middle_ref[...] = total
        branch[...] = low(total)
        grad_gain_ref[...] = grad_gain
        token[...] = jnp.zeros_like(token)

    grad_mixed_ref[...] = low(nt_dot(branch[...], w_ref[...]))
    grad_w_ref[...] = low(tn_dot(mixed_ref[...], branch[...]))


def middle_back(grad, middle, upstream, mixed, gains, w):
    rows, width = middle.shape
    inner = mixed.shape[1]
    tile = inner // MIDDLE_TILES
    return pl.pallas_call(
        middle_back_kernel,
        name="middle_back",
        grid=(MIDDLE_TILES,),
        in_specs=[
            whole_block((rows, width)),
            whole_block((rows, width)),
            whole_block((rows, width)),
            pl.BlockSpec((rows, tile), lambda i: (0, i)),
            whole_block(gains.shape),
            pl.BlockSpec((tile, width), lambda i: (i, 0)),
        ],
        out_specs=[
            whole_block((rows, width)),
            pl.BlockSpec((rows, tile), lambda i: (0, i)),
            pl.BlockSpec((tile, width), lambda i: (i, 0)),
            whole_block((1, width)),
            whole_block(TOKEN),
        ],
        out_shape=[
            jax.ShapeDtypeStruct((rows, width), jnp.float32),
            jax.ShapeDtypeStruct((rows, inner), jnp.bfloat16),
            jax.ShapeDtypeStruct((inner, width), jnp.bfloat16),
            jax.ShapeDtypeStruct((1, width), jnp.float32),
            token_shape(),
        ],
        scratch_shapes=[pltpu.VMEM((rows, width), jnp.bfloat16)],
        compiler_params=pltpu.CompilerParams(vmem_limit_bytes=VMEM_LIMIT),
    )(grad, middle, upstream, mixed, gains, w)


def project_back_queries_kernel(grad_ref, normed_ref, w_ref, grad_w_ref, grad_normed_ref):
    grad_normed_ref[...] = nt_dot(grad_ref[...], w_ref[...])
    grad_w_ref[...] = low(tn_dot(normed_ref[...], grad_ref[...]))


def project_back_queries(grad_q, normed, w):
    rows, width = normed.shape
    inner = grad_q.shape[1]
    tile = width // MIDDLE_TILES
    return pl.pallas_call(
        project_back_queries_kernel,
        name="project_back_queries",
        grid=(MIDDLE_TILES,),
        in_specs=[
            whole_block(grad_q.shape),
            pl.BlockSpec((rows, tile), lambda i: (0, i)),
            pl.BlockSpec((tile, inner), lambda i: (i, 0)),
        ],
        out_specs=[
            pl.BlockSpec((tile, inner), lambda i: (i, 0)),
            pl.BlockSpec((rows, tile), lambda i: (0, i)),
        ],
        out_shape=[
            jax.ShapeDtypeStruct((width, inner), jnp.bfloat16),
            jax.ShapeDtypeStruct((rows, width), jnp.float32),
        ],
        compiler_params=pltpu.CompilerParams(vmem_limit_bytes=VMEM_LIMIT),
    )(grad_q, normed, w)


def project_back_keys_kernel(
    grad_kv_ref, cos_ref, sin_ref, normed_ref, partial_ref, x_ref, grad_middle_ref, gain_ref, w_ref,
    grad_w_ref, grad_x_ref, grad_gain_ref,
):
    keys = grad_kv_ref[:, :HD]
    keys = low(keys * cos_ref[...] - pltpu.roll(keys, HD // 2, 1) * sin_ref[...])
    joined = jnp.concatenate([keys, low(grad_kv_ref[:, HD:])], axis=1)
    grad_w_ref[...] = low(tn_dot(normed_ref[...], joined))
    grad_normed = partial_ref[...] + nt_dot(joined, w_ref[...])
    grad, grad_gain = norm_back(x_ref[...].astype(jnp.float32), gain_row(gain_ref, 0), grad_normed)
    grad_x_ref[...] = grad_middle_ref[...] + grad
    grad_gain_ref[...] = grad_gain


def project_back_keys(grad_kv, cosine, sine_part, normed, partial, x, grad_middle, gains, w):
    rows, width = x.shape
    inner = grad_kv.shape[1]
    arrays = (grad_kv, cosine, sine_part, normed, partial, x, grad_middle, gains)
    last = w.shape[1] // inner - 1
    return pl.pallas_call(
        project_back_keys_kernel,
        name="project_back_keys",
        grid=(1,),
        in_specs=[whole_block(one.shape) for one in arrays]
        + [pl.BlockSpec((width, inner), lambda i: (0, last))],
        out_specs=[whole_block((width, inner)), whole_block((rows, width)), whole_block((1, width))],
        out_shape=[
            jax.ShapeDtypeStruct((width, inner), jnp.bfloat16),
            jax.ShapeDtypeStruct((rows, width), jnp.float32),
            jax.ShapeDtypeStruct((1, width), jnp.float32),
        ],
        compiler_params=pltpu.CompilerParams(vmem_limit_bytes=VMEM_LIMIT),
    )(*arrays, w)


MESH_ID =MESH_ID = pl.DeviceIdType.MESH


class Wire:
    def __init__(self, send_sems, recv_sems):
        self.send_sems = send_sems
        self.recv_sems = recv_sems
        self.count = 0
        self.open = []
        self.ctx = lax.axis_index("ctx")
        self.shard = lax.axis_index("fsdp")

    def other(self, mask):
        at = self.ctx
        for bit in (1, 2, 4):
            if mask & bit:
                at = at + bit - 2 * bit * lax.rem(at // bit, 2)
        return at

    def plane(self, mask):
        return (self.other(mask), self.shard)

    def line(self, step, shards):
        return (self.ctx, lax.rem(self.shard + step, shards))

    def meet(self, peers):
        barrier = pltpu.get_barrier_semaphore()
        for peer in peers:
            pl.semaphore_signal(barrier, inc=1, device_id=peer, device_id_type=MESH_ID)
        pl.semaphore_wait(barrier, len(peers))

    def send(self, source, target, peer):
        at = self.count
        self.count += 1
        copy = pltpu.make_async_remote_copy(
            src_ref=source,
            dst_ref=target,
            send_sem=self.send_sems.at[at],
            recv_sem=self.recv_sems.at[at],
            device_id=peer,
            device_id_type=MESH_ID,
        )
        copy.start()
        self.open.append(copy)
        return copy

    def sent(self, copy):
        copy.wait_send()
        self.open = [one for one in self.open if one is not copy]

    def finish(self):
        for copy in self.open:
            copy.wait_send()


class PlaneGather:
    COPIES = 9

    def __init__(self, wire, source, out_at, rows, split):
        self.wire, self.out_at, self.rows, self.split = wire, out_at, rows, split
        ctx = wire.ctx
        self.core = wire.send(source, out_at(ctx), wire.plane(1))
        self.x = wire.send(source, out_at(ctx), wire.plane(2))
        self.y = wire.send(source, out_at(ctx), wire.plane(4))

    def forward(self):
        wire, split = self.wire, self.split
        rest = self.rows - split
        self.x.wait_recv()
        block = self.out_at(wire.other(2))
        part = block.at[pl.ds(0, split)]
        self.corner_y = wire.send(part, part, wire.plane(4))
        self.core_x = wire.send(block, block, wire.plane(1))
        self.y.wait_recv()
        block = self.out_at(wire.other(4))
        part = block.at[pl.ds(split, rest)]
        self.corner_x = wire.send(part, part, wire.plane(2))
        self.core_y = wire.send(block, block, wire.plane(1))

    def corner(self):
        self.corner_y.wait_recv()
        self.corner_x.wait_recv()
        block = self.out_at(self.wire.other(6))
        self.core_corner = self.wire.send(block, block, self.wire.plane(1))

    def settle(self):
        self.core.wait_recv()
        self.core_x.wait_recv()
        self.core_y.wait_recv()
        self.core_corner.wait_recv()


def half_rows(rows, turn):
    low_half = rows // 32 * 16
    return low_half if turn % 2 else rows - low_half


def add_low(first, second):
    return (first.astype(jnp.float32) + second.astype(jnp.float32)).astype(jnp.bfloat16)


class PlaneSum:
    COPIES = 7

    def __init__(self, wire, source, own, pair, first, second, local_sem):
        self.wire, self.own, self.pair, self.first, self.second = wire, own, pair, first, second
        core = lax.rem(wire.ctx, 2)
        self.chips = {mask: wire.other(2 * mask) // 2 for mask in range(4)}
        self.swap = wire.send(source.at[:, :, 1 - core], pair, wire.plane(1))
        self.local = pltpu.make_async_copy(source.at[:, :, core], own, local_sem)
        self.local.start()

    def step_one(self):
        wire, own, pair, first, chips = self.wire, self.own, self.pair, self.first, self.chips
        self.local.wait()
        self.swap.wait_recv()

        def add_pair(index, carry):
            part, other = index // 4, lax.rem(index, 4)
            own[part, other] = add_low(own[part, other], pair[part, other])
            return carry

        lax.fori_loop(0, 16, add_pair, 0)
        low, high = pl.ds(0, 2), pl.ds(2, 2)
        self.one = [
            wire.send(own.at[low, chips[3]], first.at[0, 1], wire.plane(2)),
            wire.send(own.at[high, chips[3]], first.at[1, 1], wire.plane(4)),
            wire.send(own.at[low, chips[1]], first.at[0, 0], wire.plane(2)),
            wire.send(own.at[high, chips[2]], first.at[1, 0], wire.plane(4)),
        ]

    def step_two(self):
        wire, own, first, second, chips = self.wire, self.own, self.first, self.second, self.chips
        self.one[0].wait_recv()
        for part in range(2):
            own[part, chips[2]] = add_low(own[part, chips[2]], first[0, 1, part])
        self.two = [wire.send(own.at[pl.ds(0, 2), chips[2]], second.at[pl.ds(0, 2)], wire.plane(4))]
        self.one[1].wait_recv()
        for part in range(2):
            own[part + 2, chips[1]] = add_low(own[part + 2, chips[1]], first[1, 1, part])
        self.two.append(
            wire.send(own.at[pl.ds(2, 2), chips[1]], second.at[pl.ds(2, 2)], wire.plane(2))
        )

    def result(self, store):
        own, first, second, chips = self.own, self.first, self.second, self.chips
        for copy in self.one[2:] + self.two:
            copy.wait_recv()
        for part in range(4):
            total = own[part, chips[0]].astype(jnp.float32)
            total += first[part // 2, 0, part % 2].astype(jnp.float32)
            total += second[part].astype(jnp.float32)
            store(part, total)


def plane_sum_scratch(rows, columns):
    shape = lambda *lead: pltpu.VMEM(lead + (rows, columns), jnp.bfloat16)
    return [shape(4, 4), shape(4, 4), shape(2, 2, 2), shape(4)]


def dma_sems(count):
    return pltpu.SemaphoreType.DMA((count,))


PLANE_PEERS = (1, 2, 4)


def comm_params(number):
    return pltpu.CompilerParams(
        collective_id=number, has_side_effects=True, vmem_limit_bytes=VMEM_LIMIT
    )


def take(values, count):
    return values[:count], values[count:]


class Relay:
    def __init__(self, source, stage, targets, sems):
        self.stage, self.targets, self.sems = stage, targets, sems
        self.load = pltpu.make_async_copy(source, stage, sems.at[0])
        self.load.start()

    def push(self):
        self.load.wait()
        self.stores = []
        for i, (part, target) in enumerate(self.targets):
            store = pltpu.make_async_copy(part, target, self.sems.at[1 + i])
            store.start()
            self.stores.append(store)

    def settle(self):
        for store in self.stores:
            store.wait()


TOKEN = (8, 128)


def token_shape():
    return jax.ShapeDtypeStruct(TOKEN, jnp.int32)


def after(token, values):
    return jnp.where(token[0, 0] != 0, jnp.zeros_like(values), values)


def share_line_kernel(
    shards, pack, in_ref, gain_ref, mlp_in, mlp_out, up_ref, in_line, gain_all, mine, up_x, up_y,
    gain_now, in_stage, packed, tiles, local_sems, load_sems, send_sems, recv_sems,
):
    wire = Wire(send_sems, recv_sems)
    ctx, shard = wire.ctx, wire.shard
    chip, core = ctx // 2, lax.rem(ctx, 2)
    chips = pack.chips
    relay = Relay(in_ref.at[ctx], in_stage, [(in_stage, in_line.at[shard])], local_sems.at[0])
    gain_now[...] = jnp.zeros_like(gain_now)
    gain_now[:2] = gain_ref[...].astype(jnp.float32)
    wire.meet(
        [wire.line(step, shards) for step in range(1, shards)] + [wire.plane(2), wire.plane(4)]
    )
    half = pack.half
    copies = [
        wire.send(up_ref.at[:, pl.ds(0, half)], up_x, wire.plane(2)),
        wire.send(up_ref.at[:, pl.ds(half, half)], up_y, wire.plane(4)),
    ]
    for source, target in ((gain_now, gain_all), (in_ref.at[ctx], in_line)):
        for step in range(1, shards):
            copies.append(wire.send(source, target.at[shard], wire.line(step, shards)))
    gain_copy = pltpu.make_async_copy(gain_now, gain_all.at[shard], local_sems.at[1, 0])
    gain_copy.start()
    relay.push()

    loads = []

    def load(source, target):
        copy = pltpu.make_async_copy(source, target, load_sems.at[len(loads)])
        copy.start()
        loads.append(copy)

    def strip(start, count):
        return pl.ds(pl.multiple_of(start, LANES), count)

    main, rest, half, tail, split = pack.main, pack.rest, pack.half, pack.tail, pack.split
    per_shard = chips * (main + rest)
    base = core * (shards * per_shard)
    for part in range(shards):
        start = base + part * per_shard
        load(mlp_in.at[:, strip(start + chips * main, chips * rest)], tiles.at[part])
        column = part * main
        if column + main <= half:
            source = mlp_in.at[:, strip(start + chip * main, main)]
            load(source, packed.at[pl.ds(pack.main_start, pack.rows), pl.ds(column, main)])
            continue
        for i, at in enumerate(range(0, pack.rows, split)):
            source = mlp_in.at[pl.ds(at, split), strip(start + chip * main, main)]
            load(source, packed.at[pl.ds(pack.tail_start, split), pl.ds(i * tail + column - half, main)])
    columns = strip(core * half, half)
    for start, count, row in (
        (chip * main, main, 0),
        (chips * main + chip * rest, rest, main),
    ):
        source = mlp_out.at[pl.ds(pl.multiple_of(start, 16), count), columns]
        load(source, packed.at[pl.ds(row, count), :])
    for copy in loads:
        copy.wait()
    width = chips * rest
    ends = [
        pltpu.roll(tiles[part].astype(jnp.float32), lax.rem(width - chip * rest, width), 1)[:, :rest]
        for part in range(shards)
    ]
    ends = low(jnp.concatenate(ends, axis=1))
    for i, at in enumerate(range(0, pack.rows, split)):
        column = i * tail + shards * main - half
        packed[pack.tail_start : pack.tail_start + split, column : column + shards * rest] = ends[at : at + split]
    mine_copy = pltpu.make_async_copy(packed, mine, local_sems.at[1, 1])
    mine_copy.start()
    relay.settle()
    gain_copy.wait()
    mine_copy.wait()
    for copy in copies:
        copy.wait_recv()
    wire.finish()


def gather_shards(wire, line, target, rows, shards, count):
    gathers = []
    for step in range(1, shards):
        origin = lax.rem(wire.shard + shards - step, shards)
        place = lambda who, origin=origin: target.at[origin, who]
        gathers.append(PlaneGather(wire, line.at[origin], place, rows, half_rows(rows, step + count)))
    return gathers


def relay_shards(wire, whole, line, target, stage, piece, shards, sems):
    origins = [lax.rem(wire.shard + shards - step, shards) for step in range(1, shards)]
    places = [(piece.at[origin], target.at[origin, wire.ctx]) for origin in origins]
    return [
        Relay(whole, stage, [(stage, target.at[wire.shard])], sems.at[0]),
        Relay(line, piece, places, sems.at[1]),
    ]


def complete(gathers, relays):
    for gather in gathers:
        gather.forward()
    for gather in gathers:
        gather.corner()
    for gather in gathers:
        gather.settle()
    for relay in relays:
        relay.settle()


def share_plane_kernel(
    shards, devices, in_ref, in_line, out_ref, order, lengths, frequency, in_all, out_line, *refs
):
    tables, scratch = take(refs, len(refs) - 7)
    order_rows, in_stage, in_piece, out_stage, local_sems, send_sems, recv_sems = scratch
    wire = Wire(send_sems, recv_sems)
    ctx, shard = wire.ctx, wire.shard
    relays = relay_shards(wire, in_ref, in_line, in_all, in_stage, in_piece, shards, local_sems)
    relays.append(
        Relay(out_ref.at[ctx], out_stage, [(out_stage, out_line.at[shard])], local_sems.at[2])
    )
    wire.meet(
        [wire.plane(mask) for mask in PLANE_PEERS] + [wire.line(s, shards) for s in range(1, shards)]
    )
    gathers = gather_shards(wire, in_line, in_all, in_ref.shape[1], shards, 0)
    copies = [
        wire.send(out_ref.at[ctx], out_line.at[shard], wire.line(step, shards))
        for step in range(1, shards)
    ]
    for relay in relays:
        relay.push()
    place_tables(ctx, devices, order, lengths, frequency, *tables, order_rows)
    complete(gathers, relays)
    for copy in copies:
        copy.wait_recv()
    wire.finish()


def gather_plane_kernel(
    shards, heads_ref, out_ref, out_line, kv_all, out_all, token,
    kv_stage, out_stage, out_piece, local_sems, send_sems, recv_sems,
):
    wire = Wire(send_sems, recv_sems)
    ctx = wire.ctx
    kv_ref = heads_ref.at[pl.ds(H, 2)]
    relays = relay_shards(wire, out_ref, out_line, out_all, out_stage, out_piece, shards, local_sems)
    relays.append(Relay(kv_ref, kv_stage, [(kv_stage, kv_all.at[ctx])], local_sems.at[2]))
    token[...] = jnp.zeros_like(token)
    wire.meet([wire.plane(mask) for mask in PLANE_PEERS])
    gathers = [PlaneGather(wire, kv_ref, lambda who: kv_all.at[who], 2, 1)]
    gathers += gather_shards(wire, out_line, out_all, out_ref.shape[1], shards, 1)
    for relay in relays:
        relay.push()
    complete(gathers, relays)
    wire.finish()


def like(values, *lead):
    return jax.ShapeDtypeStruct(lead + values.shape[-2:], values.dtype)


def stage_like(values, *lead):
    return pltpu.VMEM(lead + values.shape[-2:], values.dtype)


def share_line(w_in, gains, mlp_in, mlp_out, upstream, pack, shards):
    columns = gains.shape[1]
    copies = 2 * (shards - 1) + 2
    loads = shards + shards + 1 + 2
    return pl.pallas_call(
        functools.partial(share_line_kernel, shards, pack),
        name="share_line",
        in_specs=[ANY] + [pl.BlockSpec(memory_space=pltpu.VMEM)] + [ANY] * 3,
        out_specs=[ANY] * 5,
        out_shape=[
            like(w_in, shards),
            jax.ShapeDtypeStruct((shards, 8, columns), jnp.float32),
            jax.ShapeDtypeStruct((pack.total, pack.half), mlp_in.dtype),
        ]
        + [jax.ShapeDtypeStruct((upstream.shape[0], pack.half), upstream.dtype)] * 2,
        scratch_shapes=[
            pltpu.VMEM((8, columns), jnp.float32),
            stage_like(w_in),
            pltpu.VMEM((pack.total, pack.half), mlp_in.dtype),
            pltpu.VMEM((shards, pack.rows, pack.chips * pack.rest), mlp_in.dtype),
            pltpu.SemaphoreType.DMA((2, 2)),
            dma_sems(loads),
            dma_sems(copies),
            dma_sems(copies),
        ],
        compiler_params=comm_params(1),
    )(w_in, gains, mlp_in, mlp_out, upstream)


def share_plane(w_in, in_line, w_out, order, lengths, rows, ctx_size, shards):
    copies = (shards - 1) * (PlaneGather.COPIES + 1)
    operands, shapes = place_arrays(order, lengths, rows)
    vmem = pl.BlockSpec(memory_space=pltpu.VMEM)
    return pl.pallas_call(
        functools.partial(share_plane_kernel, shards, ctx_size),
        name="share_plane",
        in_specs=[ANY] * 3 + [vmem] * len(operands),
        out_specs=[ANY] * 2 + [vmem] * len(shapes),
        out_shape=[like(w_in, shards, ctx_size), like(w_out, shards), *shapes],
        scratch_shapes=[
            pltpu.VMEM((ctx_size * ROUNDS, rows // ROUNDS), jnp.float32),
            stage_like(w_in, ctx_size),
            stage_like(w_in, shards),
            stage_like(w_out),
            pltpu.SemaphoreType.DMA((3, shards)),
            dma_sems(copies),
            dma_sems(copies),
        ],
        compiler_params=comm_params(6),
    )(w_in, in_line, w_out, *operands)


def gather_plane(heads, w_out, out_line, ctx_size, shards):
    copies = shards * PlaneGather.COPIES
    key_value = jax.ShapeDtypeStruct((2,) + heads.shape[1:], heads.dtype)
    return pl.pallas_call(
        functools.partial(gather_plane_kernel, shards),
        name="gather_plane",
        in_specs=[ANY] * 3,
        out_specs=[ANY] * 2 + [pl.BlockSpec(memory_space=pltpu.VMEM)],
        out_shape=[like(key_value, ctx_size, 2), like(w_out, shards, ctx_size), token_shape()],
        scratch_shapes=[
            stage_like(key_value, 2),
            stage_like(w_out, ctx_size),
            stage_like(w_out, shards),
            pltpu.SemaphoreType.DMA((3, shards)),
            dma_sems(copies),
            dma_sems(copies),
        ],
        compiler_params=comm_params(2),
    )(heads, w_out, out_line)


class GainSum:
    def __init__(self, wire, now, arrived, line, shards):
        self.wire, self.now, self.arrived, self.line, self.shards = wire, now, arrived, line, shards
        self.at = 0
        self.start()

    def start(self):
        peer = self.wire.plane(PLANE_PEERS[self.at])
        self.copy = self.wire.send(self.now, self.arrived.at[self.at], peer)

    def add(self):
        self.copy.wait_recv()
        self.wire.sent(self.copy)
        self.now[...] += self.arrived[self.at]
        self.at += 1

    def step(self):
        self.add()
        self.start()

    def step_line(self):
        self.add()
        wire, shards = self.wire, self.shards
        self.copies = [
            wire.send(
                self.now.at[lax.rem(wire.shard + step, shards)],
                self.line.at[step - 1],
                wire.line(step, shards),
            )
            for step in range(1, shards)
        ]

    def result(self):
        for copy in self.copies:
            copy.wait_recv()
        value = self.now[self.wire.shard]
        for step in range(self.shards - 1):
            value += self.line[step]
        return value


def send_lines(wire, source, arrived, shards):
    return [
        wire.send(
            source.at[lax.rem(wire.shard + step, shards)], arrived.at[step - 1], wire.line(step, shards)
        )
        for step in range(1, shards)
    ]


def sum_lines(wire, copies, source, arrived):
    for copy in copies:
        copy.wait_recv()
    value = source[wire.shard].astype(jnp.float32)
    for step in range(len(copies)):
        value += arrived[step].astype(jnp.float32)
    return value


def project_back_plane_kernel(
    kv_ref, g_out_ref, part_ref, grad_ref, normed_ref, x_ref, cos_ref, sin_ref, gain_ref, w_ref,
    out_half, q_half, k_half, part_all, grad_x_ref, grad_gain_ref,
    grad, normed, x, cosine, sine_part, gains, w, g_q, g_k, grad_normed, kv_sum, stage, *scratch,
):
    sums, scratch = take(scratch, 16)
    load_sems, sum_sems, part_sems, send_sems, recv_sems = scratch
    wire = Wire(send_sems, recv_sems)
    loads = []
    for source, target in (
        (grad_ref, grad),
        (normed_ref, normed),
        (w_ref, w),
        (cos_ref, cosine),
        (sin_ref, sine_part),
        (x_ref, x),
        (gain_ref, gains),
    ):
        loads.append(pltpu.make_async_copy(source, target, load_sems.at[len(loads)]))
        loads[-1].start()
    relay = Relay(part_ref, stage, [(stage, part_all.at[wire.ctx])], part_sems)
    wire.meet([wire.plane(mask) for mask in PLANE_PEERS])

    def plane_sum(source, at):
        return PlaneSum(wire, source, *sums[4 * at : 4 * at + 4], sum_sems.at[at])

    rows = part_ref.shape[0]
    keys_sum = plane_sum(kv_ref, 0)
    out_sum = plane_sum(g_out_ref, 1)
    gather = PlaneGather(wire, part_ref, lambda who: part_all.at[who], rows, rows // 32 * 16)
    keys_sum.step_one()
    out_sum.step_one()
    relay.push()
    for copy in loads:
        copy.wait()
    inner = grad.shape[1]
    tile = normed.shape[1] // 4
    pieces = g_q.shape[1:4]

    def queries_part(part, carry):
        span = pl.ds(pl.multiple_of(part * tile, tile), tile)
        value = low(tn_dot(normed[:, span], grad[...]))
        g_q[part] = value.reshape(*pieces, inner)
        grad_normed[:, span] = nt_dot(grad[...], w[span, :inner])
        return carry

    lax.fori_loop(0, 4, queries_part, 0)
    queries_sum = plane_sum(g_q, 2)
    keys_sum.step_two()

    def store_keys(part, value):
        kv_sum[part] = value

    keys_sum.result(store_keys)
    kv = kv_sum[...].reshape(normed.shape[0], 2 * HD)
    keys = kv[:, :HD]
    keys = low(keys * cosine[...] - pltpu.roll(keys, HD // 2, 1) * sine_part[...])
    joined = jnp.concatenate([keys, low(kv[:, HD:])], axis=1)
    for part in range(4):
        span = slice(part * tile, (part + 1) * tile)
        g_k[part] = low(tn_dot(normed[:, span], joined)).reshape(*pieces, 2 * HD)
        grad_normed[:, span] += nt_dot(joined, w[span, inner:])
    pair_sum = plane_sum(g_k, 3)
    out_sum.step_two()
    queries_sum.step_one()
    pair_sum.step_one()
    gather.forward()

    def store_into(target):
        def store(part, value):
            target[part] = low(value)

        return store

    out_sum.result(store_into(out_half))
    change, grad_gain = norm_back(x[...].astype(jnp.float32), gain_row(gains, 0), grad_normed[...])
    grad_x_ref[...] = change
    grad_gain_ref[...] = grad_gain
    queries_sum.step_two()
    pair_sum.step_two()
    gather.corner()
    queries_sum.result(store_into(q_half))
    pair_sum.result(store_into(k_half))
    gather.settle()
    relay.settle()
    wire.finish()


def project_back_plane(
    grad_kv, g_out, part, grad_q, normed, x, cosine, sine_part, gains, w, ctx_size
):
    rows, width = x.shape
    inner = grad_q.shape[1]
    lead = g_out.shape[:4]
    vmem = pl.BlockSpec(memory_space=pltpu.VMEM)
    low_scratch = lambda *shape: pltpu.VMEM(shape, jnp.bfloat16)
    wide = lambda *shape: pltpu.VMEM(shape, jnp.float32)
    sums = []
    for piece in (grad_kv.shape[3:], g_out.shape[3:], (lead[3], inner), (lead[3], 2 * HD)):
        sums += plane_sum_scratch(*piece)
    copies = 4 * PlaneSum.COPIES + PlaneGather.COPIES
    half = lambda columns: jax.ShapeDtypeStruct((4, lead[3], columns), jnp.bfloat16)
    return pl.pallas_call(
        project_back_plane_kernel,
        name="project_back_plane",
        in_specs=[ANY] * 10,
        out_specs=[vmem] * 3 + [ANY] + [vmem] * 2,
        out_shape=[
            half(g_out.shape[4]),
            half(inner),
            half(2 * HD),
            like(part, ctx_size),
            jax.ShapeDtypeStruct((rows, width), jnp.float32),
            jax.ShapeDtypeStruct((1, width), jnp.float32),
        ],
        scratch_shapes=[
            low_scratch(*grad_q.shape),
            low_scratch(*normed.shape),
            low_scratch(*x.shape),
            wide(*cosine.shape),
            wide(*cosine.shape),
            wide(*gains.shape),
            low_scratch(*w.shape),
            low_scratch(*lead, inner),
            low_scratch(*lead, 2 * HD),
            wide(rows, width),
            wide(4, *grad_kv.shape[3:]),
            stage_like(part),
            *sums,
            dma_sems(7),
            dma_sems(4),
            dma_sems(2),
            dma_sems(copies),
            dma_sems(copies),
        ],
        compiler_params=comm_params(3),
    )(grad_kv, g_out, part, grad_q, normed, x, cosine, sine_part, gains, w)


TERMS = 4


def reduce_late_kernel(shards, line_count, part_count, *refs):
    line_ins, refs = take(refs, line_count)
    parts, refs = take(refs, part_count)
    gain_a, gain_b, *refs = refs
    terms, refs = take(refs, TERMS)
    line_outs, refs = take(refs, line_count)
    part_outs, refs = take(refs, part_count)
    gain_out, total_ref, *refs = refs
    arrived, refs = take(refs, line_count)
    done, refs = take(refs, line_count)
    stages, refs = take(refs, part_count)
    held, refs = take(refs, TERMS)
    gain_now, gain_in, gain_line, done_sems, part_sems, term_sems, send_sems, recv_sems = refs

    wire = Wire(send_sems, recv_sems)
    ctx, shard = wire.ctx, wire.shard
    relays = [
        Relay(source, stage, [(stage, target.at[ctx])], part_sems.at[i])
        for i, (source, stage, target) in enumerate(zip(parts, stages, part_outs))
    ]
    loads = [
        pltpu.make_async_copy(source, target, term_sems.at[i])
        for i, (source, target) in enumerate(zip(terms, held))
    ]
    for copy in loads:
        copy.start()
    gain_now[...] = jnp.zeros_like(gain_now)
    columns = gain_now.shape[2]
    for part in range(shards):
        for row, values in enumerate((gain_a, gain_b)):
            gain_now[part, row : row + 1] = values[:, part * columns : (part + 1) * columns]
    wire.meet(
        [wire.plane(mask) for mask in PLANE_PEERS] + [wire.line(s, shards) for s in range(1, shards)]
    )
    lines = [
        send_lines(wire, source, target, shards) for source, target in zip(line_ins, arrived)
    ]
    gathers = []
    for source, target in zip(parts, part_outs):
        rows = source.shape[0]
        place = lambda who, target=target: target.at[who]
        gathers.append(PlaneGather(wire, source, place, rows, rows // 32 * 16))
    gain = GainSum(wire, gain_now, gain_in, gain_line, shards)
    gain.step()
    gain.step()
    gain.step_line()
    for relay in relays:
        relay.push()
    for copy in loads:
        copy.wait()
    total = held[0][...]
    for one in held[1:]:
        total += one[...].astype(jnp.float32)
    total_ref[...] = low(total)
    for gather in gathers:
        gather.forward()
    locals_ = []
    for i, (source, target) in enumerate(zip(line_ins, line_outs)):
        done[i][...] = low(sum_lines(wire, lines[i], source, arrived[i]))
        place = lambda who, target=target: target.at[who]
        gathers.append(PlaneGather(wire, done[i], place, target.shape[1], half_rows(target.shape[1], i)))
        copy = pltpu.make_async_copy(done[i], place(ctx), done_sems.at[i])
        copy.start()
        locals_.append(copy)
    gain_out[...] = gain.result()
    for gather in gathers[part_count:]:
        gather.forward()
    for gather in gathers:
        gather.corner()
    for gather in gathers:
        gather.settle()
    for copy in locals_:
        copy.wait()
    for relay in relays:
        relay.settle()
    wire.finish()


def reduce_late(lines, parts, gain_a, gain_b, terms, ctx_size):
    shards = lines[0].shape[0]
    vmem = pl.BlockSpec(memory_space=pltpu.VMEM)
    gain_shape = (shards, 8, gain_a.shape[1] // shards)
    copies = (PlaneGather.COPIES + shards - 1) * len(lines) + PlaneGather.COPIES * len(parts)
    copies += 3 + shards - 1
    return pl.pallas_call(
        functools.partial(reduce_late_kernel, shards, len(lines), len(parts)),
        name="reduce_late",
        in_specs=[vmem] * len(lines) + [ANY] * len(parts) + [vmem] * 2 + [ANY] * TERMS,
        out_specs=[ANY] * (len(lines) + len(parts)) + [vmem] * 2,
        out_shape=[like(array, ctx_size) for array in (*lines, *parts)]
        + [
            jax.ShapeDtypeStruct(gain_shape[1:], jnp.float32),
            jax.ShapeDtypeStruct(terms[0].shape, jnp.bfloat16),
        ],
        scratch_shapes=[stage_like(array, shards - 1) for array in lines]
        + [stage_like(array) for array in (*lines, *parts, *terms)]
        + [
            pltpu.VMEM(gain_shape, jnp.float32),
            pltpu.VMEM((3,) + gain_shape, jnp.float32),
            pltpu.VMEM((shards - 1,) + gain_shape[1:], jnp.float32),
            dma_sems(len(lines)),
            pltpu.SemaphoreType.DMA((len(parts), 2)),
            dma_sems(TERMS),
            dma_sems(copies),
            dma_sems(copies),
        ],
        compiler_params=comm_params(4),
    )(*lines, *parts, gain_a, gain_b, *terms)


class Pack:
    def __init__(self, rows, half, chips, units, main, rest):
        self.rows, self.half, self.chips, self.main, self.rest = rows, half, chips, main, rest
        self.tail = units - half
        self.split = rows // (half // self.tail)
        self.main_start = main + rest
        self.tail_start = self.main_start + rows
        self.total = self.tail_start + self.split

    def in_spans(self, shard):
        every = (0, self.half)
        yield (self.main_start, self.rows), every, (shard * self.rows, self.rows), every
        for i, at in enumerate(range(0, self.rows, self.split)):
            yield (
                (self.tail_start, self.split),
                (i * self.tail, self.tail),
                (shard * self.rows + at, self.split),
                (self.half, self.tail),
            )

    def out_spans(self, shard, shards):
        every = (0, self.half)
        yield (0, self.main), every, (shard * self.main, self.main), every
        yield (
            (self.main, self.rest),
            every,
            (shards * self.main + shard * self.rest, self.rest),
            every,
        )


def finish_kernel(
    shards, chips, pack, main_ref, tail_ref, out_main_ref, out_rest_ref, attn_out_ref, attn_q_ref, attn_kv_ref,
    x_one_ref, x_two_ref, in_ref, out_ref, grad_attn_out_ref, grad_attn_in_ref, x_ref,
):
    step = pl.program_id(0)
    last = pl.num_programs(0) - 1
    main, rest, half, tail = pack.main, pack.rest, pack.half, pack.tail
    per_shard = chips * (main + rest)
    wide = lambda values: values.astype(jnp.float32)

    @pl.when(step < last)
    def _():
        second = step >= last // 2
        tails = [
            jnp.where(second, tail_ref[who, :, tail:], tail_ref[who, :, :tail])
            for who in range(2 * chips)
        ]

        def columns_of(who, start, count):
            if start + count <= half:
                return main_ref[who, :, start : start + count]
            return tails[who][:, start - half : start - half + count]

        for core in range(2):
            for shard in range(shards):
                start = (core * shards + shard) * per_shard
                for chip in range(chips):
                    block = wide(columns_of(chip * 2 + core, shard * main, main))
                    in_ref[:, start + chip * main : start + (chip + 1) * main] = block
                ends = [
                    wide(columns_of(chip * 2 + core, shards * main, shards * rest))[
                        :, shard * rest : (shard + 1) * rest
                    ]
                    for chip in range(chips)
                ]
                in_ref[:, start + chips * main : start + per_shard] = jnp.concatenate(ends, axis=1)
            out_ref[:, core * half : (core + 1) * half] = wide(out_main_ref[core])
        x_ref[...] = x_one_ref[...] + x_two_ref[...]
        grad_attn_out_ref[...] = wide(attn_out_ref[0])
        inner = attn_q_ref.shape[2]
        grad_attn_in_ref[:, :inner] = wide(attn_q_ref[0])
        grad_attn_in_ref[:, inner:] = wide(attn_kv_ref[0])

    @pl.when(step == last)
    def _():
        for chip in range(chips):
            for core in range(2):
                block = wide(out_rest_ref[chip * 2 + core])
                out_ref[chip * rest : (chip + 1) * rest, core * half : (core + 1) * half] = block


def finish(first, second, attn_out, attn_q, attn_kv, x_one, x_two, pack, shards):
    ctx_size = first.shape[0]
    chips = ctx_size // 2
    steps = ctx_size
    tile = pack.rows // steps
    out_tile = pack.main // 2
    assert pack.rows // pack.split == 2 and pack.split % tile == 0
    assert out_tile == chips * pack.rest and pack.main % pack.rest == 0
    at = lambda i: jnp.minimum(i, steps - 1)
    rows = attn_out.shape[1]
    x_rows = x_one.shape[0] // steps
    piece = lambda array: pl.BlockSpec((1,) + array.shape[1:], lambda i: (at(i), 0, 0))
    attn_in = attn_q.shape[2] + attn_kv.shape[2]
    return pl.pallas_call(
        functools.partial(finish_kernel, shards, chips, pack),
        name="finish",
        grid=(steps + 1,),
        in_specs=[
            pl.BlockSpec((ctx_size, tile, pack.half), lambda i: (0, at(i), 0)),
            pl.BlockSpec(
                (ctx_size, tile, pack.half),
                lambda i: (0, pack.rows // tile + at(i) % (pack.split // tile), 0),
            ),
            pl.BlockSpec((2, out_tile, pack.half), lambda i: (at(i) // 2, at(i) % 2, 0)),
            pl.BlockSpec((ctx_size, pack.rest, pack.half), lambda i: (0, pack.main // pack.rest, 0)),
            piece(attn_out),
            piece(attn_q),
            piece(attn_kv),
            pl.BlockSpec((x_rows, x_one.shape[1]), lambda i: (at(i), 0)),
            pl.BlockSpec((x_rows, x_one.shape[1]), lambda i: (at(i), 0)),
        ],
        out_specs=[
            pl.BlockSpec((tile, 2 * FF), lambda i: (at(i), 0)),
            pl.BlockSpec((out_tile, 2 * pack.half), lambda i: (i, 0)),
            pl.BlockSpec((rows, attn_out.shape[2]), lambda i: (at(i), 0)),
            pl.BlockSpec((rows, attn_in), lambda i: (at(i), 0)),
            pl.BlockSpec((x_rows, x_one.shape[1]), lambda i: (at(i), 0)),
        ],
        out_shape=[
            jax.ShapeDtypeStruct((pack.rows, 2 * FF), jnp.float32),
            jax.ShapeDtypeStruct((FF // shards, 2 * pack.half), jnp.float32),
            jax.ShapeDtypeStruct((steps * rows, attn_out.shape[2]), jnp.float32),
            jax.ShapeDtypeStruct((steps * rows, attn_in), jnp.float32),
            jax.ShapeDtypeStruct(x_one.shape, jnp.float32),
        ],
        compiler_params=pltpu.CompilerParams(vmem_limit_bytes=VMEM_LIMIT),
    )(second, second, first, first, attn_out, attn_q, attn_kv, x_one, x_two)


TANH_SCALE = 0.7978845608028654
TANH_CUBE = 0.044715
UNIT_TILE = 384


def mlp_kernel(
    shards, pack, mine, x_left, x_right, x_x, x_y, c_own, c_x_left, c_x_right, c_y_left, c_y_right, c_left, c_right,
    normed_grad, out_own, out_x, out_y, out_left, out_right, grad_first, grad_second,
    w_in, w_out, xs, cs, hidden, grads, part, from_x, from_y, corner_left, corner_right,
    out_stage, pair_in, pair_out, local_sems, send_sems, recv_sems,
):
    wire = Wire(send_sems, recv_sems)
    core = lax.rem(wire.ctx, 2)
    other = 1 - core
    rows, half = x_left.shape
    width = 2 * half
    units = w_in.shape[2]
    tiles = units // UNIT_TILE
    left, right = pl.ds(0, half), pl.ds(half, half)
    locals_ = []

    def copy_in(source, target):
        copy = pltpu.make_async_copy(source, target, local_sems.at[len(locals_)])
        copy.start()
        locals_.append(copy)
        return copy

    def spans():
        for shard in range(shards):
            for one in pack.in_spans(shard):
                yield shard, w_in, one
            for one in pack.out_spans(shard, shards):
                yield shard, w_out, one

    def packed(shard, one):
        return mine.at[shard, pl.ds(*one[0]), pl.ds(*one[1])]

    def placed(which, target, one):
        return target.at[which, pl.ds(*one[2]), pl.ds(*one[3])]

    loads = [
        copy_in(x_left, xs.at[0, :, left]),
        copy_in(x_right, xs.at[0, :, right]),
        copy_in(c_own, cs.at[0]),
    ]
    for shard, target, one in spans():
        loads.append(copy_in(packed(shard, one), placed(core, target, one)))
    late = [
        copy_in(source, target)
        for source, target in (
            (x_x, xs.at[1, :, left]),
            (x_y, xs.at[2, :, right]),
            (c_x_left, cs.at[1, :, left]),
            (c_x_right, cs.at[1, :, right]),
            (c_y_left, cs.at[2, :, left]),
            (c_y_right, cs.at[2, :, right]),
            (c_left, cs.at[3, :, left]),
            (c_right, cs.at[3, :, right]),
        )
    ]
    wire.meet([wire.plane(mask) for mask in PLANE_PEERS])
    x_copies = [
        wire.send(x_right, xs.at[1, :, right], wire.plane(2)),
        wire.send(x_left, xs.at[2, :, left], wire.plane(4)),
    ]
    swaps = [
        wire.send(packed(shard, one), placed(core, target, one), wire.plane(1))
        for shard, target, one in spans()
    ]
    for copy in loads:
        copy.wait()
    for copy in swaps:
        copy.wait_recv()

    def one_chunk(at):
        gate = dot(xs[at], w_in[0])
        up = dot(xs[at], w_in[1])
        grad = nt_dot(cs[at, :, left], w_out[0]) + nt_dot(cs[at, :, right], w_out[1])
        square = gate * gate
        bend = jnp.tanh(TANH_SCALE * gate * (1.0 + TANH_CUBE * square))
        lift = 0.5 + 0.5 * bend
        value = gate * lift
        slope = lift + (0.5 * TANH_SCALE) * gate * (1.0 - bend * bend) * (
            1.0 + (3.0 * TANH_CUBE) * square
        )
        hidden[at] = low(value * up)
        grads[0, at] = low(grad * up * slope)
        grads[1, at] = low(grad * value)

        def one_half(span):
            total = nt_dot(grads[0, at], w_in[0, span, :])
            return total + nt_dot(grads[1, at], w_in[1, span, :])

        return one_half

    own_half = one_chunk(0)
    for copy in x_copies:
        copy.wait_recv()
    corners = [
        wire.send(x_x, xs.at[3, :, left], wire.plane(4)),
        wire.send(x_y, xs.at[3, :, right], wire.plane(2)),
    ]
    for copy in late:
        copy.wait()
    one_half = one_chunk(1)
    part[0, :, left] = low(one_half(left))
    early = [wire.send(part.at[0, :, left], from_x.at[:, left], wire.plane(2))]
    part[0, :, right] = low(one_half(right))
    one_half = one_chunk(2)
    part[1, :, right] = low(one_half(right))
    early.append(wire.send(part.at[1, :, right], from_y.at[:, right], wire.plane(4)))
    part[1, :, left] = low(one_half(left))
    for copy in corners:
        copy.wait_recv()
    one_half = one_chunk(3)
    part[2, :, left] = low(one_half(left))
    corner = [wire.send(part.at[2, :, left], corner_left, wire.plane(2))]
    part[2, :, right] = low(one_half(right))
    corner.append(wire.send(part.at[2, :, right], corner_right, wire.plane(4)))

    for span in (left, right):
        normed_grad[:, span] = own_half(span)
    out_copies = {}

    def out_part(at, targets):
        slot = at % 2
        for copy in out_copies.get(slot, ()):
            copy.wait()
        for n, span in enumerate((left, right)):
            out_stage[slot, :, span] = low(dot(hidden[at], w_out[n]))
        out_copies[slot] = [copy_in(out_stage.at[(slot,) + here], target) for here, target in targets]

    every = slice(None)
    out_part(3, [((every, left), out_left), ((every, right), out_right)])
    out_part(2, [((), out_y)])
    out_part(1, [((), out_x)])
    out_part(0, [((), out_own)])

    everything = lambda ref: ref[...].reshape(ref.shape[0] * rows, ref.shape[2])

    def in_tile(which, tile):
        columns = pl.ds(tile * UNIT_TILE, UNIT_TILE)
        picked = grads[which, :, :, columns].reshape(4 * rows, UNIT_TILE)
        return columns, tn_dot(everything(xs), picked)

    pairs_in = []

    def send_in_tile(tile):
        columns, value = in_tile(other, tile)
        w_in[0, :, columns] = low(value)
        pairs_in.append(wire.send(w_in.at[0, :, columns], pair_in.at[:, columns], wire.plane(1)))

    for tile in range(tiles):
        send_in_tile(tile)
    merged = []
    corner[0].wait_recv()
    part[1, :, left] = add_low(part[1, :, left], corner_left[...])
    merged.append(wire.send(part.at[1, :, left], from_y.at[:, left], wire.plane(4)))
    corner[1].wait_recv()
    part[0, :, right] = add_low(part[0, :, right], corner_right[...])
    merged.append(wire.send(part.at[0, :, right], from_x.at[:, right], wire.plane(2)))

    def out_tile(which, tile):
        columns = pl.ds(tile * UNIT_TILE, UNIT_TILE)
        picked = hidden[:, :, columns].reshape(4 * rows, UNIT_TILE)
        span = pl.ds(pl.multiple_of(which * half, half), half)
        return columns, tn_dot(picked, cs[:, :, span].reshape(4 * rows, half))

    pairs_out = []
    for tile in range(tiles):
        span, value = out_tile(other, tile)
        w_out[0, span, :] = low(value)
        pairs_out.append(wire.send(w_out.at[0, span, :], pair_out.at[span, :], wire.plane(1)))
    final = []
    for tile in range(tiles):
        columns, value = in_tile(core, tile)
        pairs_in[tile].wait_recv()
        w_in[1, :, columns] = low(value + pair_in[:, columns].astype(jnp.float32))
    for tile in range(tiles):
        span, value = out_tile(core, tile)
        pairs_out[tile].wait_recv()
        w_out[1, span, :] = low(value + pair_out[span, :].astype(jnp.float32))
    for shard, source, one in spans():
        start, count = one[0]
        if start < pack.main_start:
            target = grad_first.at[shard, pl.ds(start, count), pl.ds(*one[1])]
        else:
            target = grad_second.at[shard, pl.ds(start - pack.main_start, count), pl.ds(*one[1])]
        final.append(copy_in(placed(1, source, one), target))
    for copy in early + merged:
        copy.wait_recv()
    normed_grad[...] += from_x[...].astype(jnp.float32) + from_y[...].astype(jnp.float32)
    for copies in out_copies.values():
        for copy in copies:
            copy.wait()
    for copy in final:
        copy.wait()
    wire.finish()


def mlp(mine, x, upstream, pack):
    rows, half = x[0].shape
    width = 2 * half
    units = pack.half + pack.tail
    shards = mine.shape[0]
    low_shape = lambda *shape: jax.ShapeDtypeStruct(shape, jnp.bfloat16)
    low_scratch = lambda *shape: pltpu.VMEM(shape, jnp.bfloat16)
    parts = shards * (1 + pack.rows // pack.split + 2)
    copies = parts + 4 + 2 + 2 + 2 + 2 * (units // UNIT_TILE)
    locals_ = 3 + parts + 8 + 5 + parts
    return pl.pallas_call(
        functools.partial(mlp_kernel, shards, pack),
        name="mlp",
        in_specs=[ANY] * 12,
        out_specs=[pl.BlockSpec(memory_space=pltpu.VMEM)] + [ANY] * 7,
        out_shape=[
            jax.ShapeDtypeStruct((rows, width), jnp.float32),
            low_shape(rows, width),
            low_shape(rows, width),
            low_shape(rows, width),
            low_shape(rows, half),
            low_shape(rows, half),
            low_shape(shards, pack.main_start, half),
            low_shape(shards, pack.total - pack.main_start, half),
        ],
        scratch_shapes=[
            low_scratch(2, width, units),
            low_scratch(2, units, half),
            low_scratch(4, rows, width),
            low_scratch(4, rows, width),
            low_scratch(4, rows, units),
            low_scratch(2, 4, rows, units),
            low_scratch(3, rows, width),
            low_scratch(rows, width),
            low_scratch(rows, width),
            low_scratch(rows, half),
            low_scratch(rows, half),
            low_scratch(2, rows, width),
            low_scratch(width, units),
            low_scratch(units, half),
            dma_sems(locals_),
            dma_sems(copies),
            dma_sems(copies),
        ],
        compiler_params=pltpu.CompilerParams(
            collective_id=5, has_side_effects=True, vmem_limit_bytes=MLP_VMEM
        ),
    )(mine, *x, *upstream)


class Layout:
    def __init__(self, ctx_size, fsdp_size):
        self.ctx_size = ctx_size
        self.shards = fsdp_size
        self.chips = ctx_size // 2
        self.index = lax.axis_index("ctx")
        self.chip = self.index // 2
        self.core = self.index % 2
        units = FF // (self.shards * self.chips)
        self.main = units // LANES * LANES
        self.rest = units - self.main
        self.per_shard = FF // self.shards
        self.rest_start = self.chips * self.main
        self.plane = ctx_size == 8 and fsdp_size == 4

    def xor(self, values, mask):
        pairs = [(i, i ^ mask) for i in range(self.ctx_size)]
        return lax.ppermute(values, "ctx", pairs)

    def same_core_groups(self):
        return [[chip * 2 + core for chip in range(self.chips)] for core in range(2)]

    def join_corner(self, to_x, to_y, left, right, token):
        half = left.shape[1]
        left = after(token, self.xor(left, 2))
        right = after(token, self.xor(right, 4))
        to_y = jnp.concatenate([add_low(to_y[:, :half], left), to_y[:, half:]], axis=1)
        to_x = jnp.concatenate([to_x[:, :half], add_low(to_x[:, half:], right)], axis=1)
        return to_x, to_y

    def gather_chips(self, values):
        groups = self.same_core_groups()
        return lax.all_gather(values, "ctx", axis=0, tiled=True, axis_index_groups=groups)

    def scatter_chips(self, partial):
        groups = self.same_core_groups()
        total = lax.psum_scatter(
            low(partial), "ctx", scatter_dimension=0, tiled=True, axis_index_groups=groups
        )
        return total.astype(jnp.float32)

    def columns_of_chip(self, weights, start):
        parts = []
        if self.main:
            for shard in range(self.shards):
                at = start + shard * self.per_shard + self.chip * self.main
                parts.append(lax.dynamic_slice_in_dim(weights, at, self.main, 1))
        if self.rest:
            for shard in range(self.shards):
                at = start + shard * self.per_shard + self.rest_start + self.chip * self.rest
                parts.append(lax.dynamic_slice_in_dim(weights, at, self.rest, 1))
        return jnp.concatenate(parts, axis=1)

    def rows_of_chip(self, weights):
        parts = []
        if self.main:
            parts.append(lax.dynamic_slice_in_dim(weights, self.chip * self.main, self.main, 0))
        if self.rest:
            at = self.rest_start + self.chip * self.rest
            parts.append(lax.dynamic_slice_in_dim(weights, at, self.rest, 0))
        return jnp.concatenate(parts, axis=0)

    def by_core(self, mine, other):
        first = jnp.where(self.core == 0, mine, other)
        second = jnp.where(self.core == 0, other, mine)
        return first, second

    def mine_in(self, shard, later=0):
        return self.columns_of_chip(shard, self.core * FF + later)

    def mine_out(self, shard, later=0):
        width = shard.shape[1]
        half = lax.dynamic_slice_in_dim(shard, self.core * (width // 2) + later, width // 2, 1)
        return self.rows_of_chip(half)

    def gather_mlp_in(self, shard):
        mine = lax.all_gather(self.mine_in(shard), "fsdp", axis=0, tiled=True)
        return self.by_core(mine, self.xor(mine, 1))

    def gather_mlp_out(self, shard):
        width = shard.shape[1]
        mine = lax.all_gather(self.mine_out(shard), "fsdp", axis=0)
        mine = jnp.concatenate(
            [
                mine[:, : self.main].reshape(self.shards * self.main, width // 2),
                mine[:, self.main :].reshape(self.shards * self.rest, width // 2),
            ],
            axis=0,
        )
        return jnp.concatenate(self.by_core(mine, self.xor(mine, 1)), axis=1)

    def sum_pair(self, first, second):
        keep = jnp.where(self.core == 0, first, second)
        send = jnp.where(self.core == 0, second, first)
        return keep + self.xor(low(send), 1).astype(jnp.float32)

    def reduce_mlp_in(self, gate, up):
        total = low(self.sum_pair(gate, up))
        return lax.psum_scatter(total, "fsdp", scatter_dimension=0, tiled=True)

    def order_mlp_in(self, every):
        rows = every.shape[1]
        every = every.reshape(self.chips, 2, rows, every.shape[2])
        split = self.shards * self.main
        main = every[..., :split].reshape(self.chips, 2, rows, self.shards, self.main)
        rest = every[..., split:].reshape(self.chips, 2, rows, self.shards, self.rest)
        main = main.transpose(2, 1, 3, 0, 4).reshape(rows, 2, self.shards, -1)
        rest = rest.transpose(2, 1, 3, 0, 4).reshape(rows, 2, self.shards, -1)
        return jnp.concatenate([main, rest], axis=3).reshape(rows, 2 * FF).astype(jnp.float32)

    def reduce_mlp_out(self, grad):
        width = grad.shape[1]
        total = low(self.sum_pair(grad[:, : width // 2], grad[:, width // 2 :]))
        split = self.shards * self.main
        main = total[:split].reshape(self.shards, self.main, width // 2)
        rest = total[split:].reshape(self.shards, self.rest, width // 2)
        total = jnp.concatenate([main, rest], axis=1)
        return lax.psum_scatter(total, "fsdp", scatter_dimension=0, tiled=True)[0]

    def order_mlp_out(self, every):
        width = 2 * every.shape[2]
        every = every.reshape(self.chips, 2, self.main + self.rest, width // 2)
        main = every[:, :, : self.main].transpose(0, 2, 1, 3).reshape(-1, width)
        rest = every[:, :, self.main :].transpose(0, 2, 1, 3).reshape(-1, width)
        return jnp.concatenate([main, rest], axis=0).astype(jnp.float32)

    def gather_whole(self, shard):
        rows = shard.shape[0] // self.ctx_size
        piece = lax.dynamic_slice_in_dim(shard, self.index * rows, rows, 0)
        piece = lax.all_gather(piece, "fsdp", axis=0)
        piece = lax.all_gather(piece, "ctx", axis=1, tiled=True)
        return piece.reshape(-1, shard.shape[1])

    def reduce_whole(self, grad):
        rows = grad.shape[0] // self.shards
        total = grad.reshape(self.shards, rows, grad.shape[1])
        total = lax.psum_scatter(total, "ctx", scatter_dimension=1, tiled=True)
        total = lax.psum_scatter(total, "fsdp", scatter_dimension=0, tiled=True)[0]
        return lax.all_gather(total, "ctx", axis=0, tiled=True).astype(jnp.float32)

    def reduce_gain(self, grad):
        total = jnp.sum(lax.all_gather(grad, ("ctx", "fsdp"), axis=0), axis=0)
        rows = grad.shape[0] // self.shards
        return lax.dynamic_slice_in_dim(total, lax.axis_index("fsdp") * rows, rows)


def per_device(
    ctx_size,
    fsdp_size,
    tokens,
    order,
    lengths,
    norm_attn,
    w_attn_in,
    w_attn_out,
    norm_mlp,
    w_mlp_in,
    w_mlp_out,
    cotangent,
):
    lay = Layout(ctx_size, fsdp_size)
    x, upstream = tokens[0], cotangent[0]
    own_rows, width = x.shape
    block = own_rows // ROUNDS
    if lay.plane:
        pack = Pack(w_mlp_in.shape[0], width // 2, lay.chips, FF // lay.chips, lay.main, lay.rest)
        pieces = lambda w: w.reshape(ctx_size, w.shape[0] // ctx_size, w.shape[1])
        in_line, gains, mine, upstream_x, upstream_y = share_line(
            pieces(w_attn_in),
            jnp.stack([norm_attn, norm_mlp]),
            w_mlp_in,
            w_mlp_out,
            upstream,
            pack,
            fsdp_size,
        )
        mine = lax.all_gather(mine, "fsdp", axis=0)
        in_attn, out_line, *tables = share_plane(
            pieces(w_attn_in),
            in_line,
            pieces(w_attn_out),
            order,
            lengths,
            own_rows,
            ctx_size,
            fsdp_size,
        )
        in_attn = in_attn.reshape(width, -1)
    else:
        tables = place_tables_alone(ctx_size, order, lengths, own_rows)
        in_attn = lay.gather_whole(w_attn_in)
        out_attn = lay.gather_whole(w_attn_out)
        gains = jnp.pad(jnp.stack([norm_attn, norm_mlp]).astype(jnp.float32), ((0, 6), (0, 0)))
        gains = lax.all_gather(gains, "fsdp", axis=0)
        gate_in, up_in = lay.gather_mlp_in(w_mlp_in)
        out_mlp = lay.gather_mlp_out(w_mlp_out)
        upstream_all = lay.gather_chips(upstream)

    where, key_place, bounds, bounds_wide, cosine, sine_part = tables
    normed_one, queries = project(x, gains, in_attn, cosine, sine_part)
    if lay.plane:
        key_value, out_attn, token = gather_plane(
            queries, pieces(w_attn_out), out_line, ctx_size, fsdp_size
        )
        out_attn = out_attn.reshape(-1, width)
        half = width // 2
        upstream_all = (
            upstream,
            upstream_x,
            lay.xor(after(token, upstream[:, half:]), 2),
            lay.xor(after(token, upstream[:, :half]), 4),
            upstream_y,
            lay.xor(after(token, upstream_x), 4),
            lay.xor(after(token, upstream_y), 2),
        )
    else:
        key_value = lax.all_gather(queries[H:], "ctx", axis=0)
    mixed, log_total = attend(where, queries, key_value, key_place, bounds)
    middle, left, right = middle_forward(x, mixed, gains, out_attn)

    if lay.plane:
        grad_normed_two, out_own, *out_parts, grad_first, grad_second = mlp(
            mine,
            (left, right, lay.xor(left, 2), lay.xor(right, 4)),
            upstream_all,
            pack,
        )
        grad_first = lax.psum_scatter(grad_first, "fsdp", scatter_dimension=0, tiled=True)[0]
        grad_second = lax.psum_scatter(grad_second, "fsdp", scatter_dimension=0, tiled=True)[0]
    else:
        normed_all = lay.gather_chips(jnp.concatenate([left, right], axis=1))
        gate = dot(normed_all, gate_in)
        up = dot(normed_all, up_in)
        hidden, hidden_back = jax.vjp(geglu, gate, up)
        hidden = low(hidden)
        grad_hidden = dot_nt(upstream_all, out_mlp)
        grad_gate, grad_up = hidden_back(grad_hidden)
        grad_gate = low(grad_gate)
        grad_up = low(grad_up)
        grad_normed_two = lay.scatter_chips(dot_nt(grad_gate, gate_in) + dot_nt(grad_up, up_in))
        result = low(middle + lay.scatter_chips(dot(hidden, out_mlp)))
        grad_out_mlp = lay.reduce_mlp_out(dot_tn(hidden, upstream_all))
        grad_in_mlp = lay.reduce_mlp_in(dot_tn(normed_all, grad_gate), dot_tn(normed_all, grad_up))

    grad_middle, grad_mixed, grad_out_attn, grad_gain_mlp, token = middle_back(
        grad_normed_two, middle, upstream, mixed, gains, out_attn
    )
    out_parts = lay.join_corner(*out_parts, token) if lay.plane else ()
    grad_query, grad_kv = attend_back(
        where,
        queries,
        key_value,
        grad_mixed,
        mixed,
        log_total,
        key_place,
        bounds_wide,
        cosine,
        sine_part,
        out_parts,
    )
    if lay.plane:
        split = lambda grad: grad.reshape(fsdp_size, lay.chips, 2, -1, grad.shape[1])
        grad_kv = grad_kv.reshape(ROUNDS, lay.chips, 2, block, 2 * HD)
        *halves, grad_first, grad_inputs, grad_gain_attn = project_back_plane(
            grad_kv,
            split(grad_out_attn),
            grad_first,
            grad_query,
            normed_one,
            x,
            cosine,
            sine_part,
            gains,
            in_attn,
            ctx_size,
        )
        to_x, to_y = out_parts
        terms = (middle, out_own, lay.xor(to_y, 4), lay.xor(to_x, 2))
        grad_out_attn, grad_in_queries, grad_in_keys, grad_second, grad_gains, result = reduce_late(
            halves, [grad_second], grad_gain_attn, grad_gain_mlp, terms, ctx_size
        )
        grad_in_mlp, grad_out_mlp, grad_out_attn, grad_in_attn, grad_inputs = finish(
            grad_first,
            grad_second,
            grad_out_attn,
            grad_in_queries,
            grad_in_keys,
            grad_middle,
            grad_inputs,
            pack,
            fsdp_size,
        )
        grad_gain_attn, grad_gain_mlp = grad_gains[0], grad_gains[1]
    else:
        grad_kv = grad_kv.reshape(ROUNDS, ctx_size, block, 2 * HD)
        grad_kv = lax.psum_scatter(grad_kv, "ctx", scatter_dimension=1, tiled=True)
        grad_kv = grad_kv.reshape(own_rows, 2 * HD).astype(jnp.float32)
        grad_in_queries, grad_normed = project_back_queries(grad_query, normed_one, in_attn)
        grad_in_keys, grad_inputs, grad_gain_attn = project_back_keys(
            grad_kv, cosine, sine_part, normed_one, grad_normed, x, grad_middle, gains, in_attn
        )
        grad_in_attn = jnp.concatenate([grad_in_queries, grad_in_keys], axis=1)
        grad_out_attn = lay.reduce_whole(grad_out_attn)
        grad_in_attn = lay.reduce_whole(grad_in_attn)
        grad_in_mlp = lay.order_mlp_in(lax.all_gather(grad_in_mlp, "ctx", axis=0))
        grad_out_mlp = lay.order_mlp_out(lax.all_gather(grad_out_mlp, "ctx", axis=0))
        grad_gain_attn = lay.reduce_gain(grad_gain_attn[0])
        grad_gain_mlp = lay.reduce_gain(grad_gain_mlp[0])
    return (
        result[None],
        grad_inputs[None],
        grad_gain_attn,
        grad_in_attn,
        grad_out_attn,
        grad_gain_mlp,
        grad_in_mlp,
        grad_out_mlp,
    )


def solution(mesh):
    in_specs = (
        P("fsdp", "ctx", None),
        P("fsdp", None),
        P("fsdp", None),
        P("fsdp"),
        P("fsdp", None),
        P("fsdp", None),
        P("fsdp"),
        P("fsdp", None),
        P("fsdp", None),
        P("fsdp", "ctx", None),
    )
    out_specs = (
        P("fsdp", "ctx", None),
        P("fsdp", "ctx", None),
        P("fsdp"),
        P("fsdp", None),
        P("fsdp", None),
        P("fsdp"),
        P("fsdp", None),
        P("fsdp", None),
    )

    def run(*arrays):
        return per_device(mesh.shape["ctx"], mesh.shape["fsdp"], *arrays)

    return jax.shard_map(run, mesh=mesh, in_specs=in_specs, out_specs=out_specs, check_vma=False)
```

```python
import functools

import jax
import jax.numpy as jnp
from jax import lax
from jax.experimental import pallas as pl
from jax.experimental.pallas import tpu as pltpu
from jax.sharding import PartitionSpec as P

H = 12
HD = 128
FF = 4608
WINDOW = 1024
ROUNDS = 4
LANES = 128


EPS = 1e-06


def rms_norm(values, gain):
    return values * lax.rsqrt(jnp.mean(values * values, axis=-1, keepdims=True) + EPS) * gain


def geglu(gate, up):
    return jax.nn.gelu(gate, approximate=True) * up


def dot(left, right):
    return jnp.dot(left, right, preferred_element_type=jnp.float32)


def dot_nt(left, right):
    return jnp.einsum("ab,cb->ac", left, right, preferred_element_type=jnp.float32)


def dot_tn(left, right):
    return jnp.einsum("ab,ac->bc", left, right, preferred_element_type=jnp.float32)


def nt_dot(left, right):
    return lax.dot_general(left, right, (((1,), (1,)), ((), ())), preferred_element_type=jnp.float32)


def tn_dot(left, right):
    return lax.dot_general(left, right, (((0,), (0,)), ((), ())), preferred_element_type=jnp.float32)


def low(values):
    return values.astype(jnp.bfloat16)


VMEM_LIMIT = 56 * 1024 * 1024
MLP_VMEM = 62 * 1024 * 1024

def gain_row(ref, which):
    parts = [ref[shard, which : which + 1, :] for shard in range(ref.shape[0])]
    return jnp.concatenate(parts, axis=1)


def norm_scale(values):
    return lax.rsqrt(jnp.mean(values * values, axis=-1, keepdims=True) + EPS)


def norm_back(values, gain, incoming):
    scale = norm_scale(values)
    weighted = incoming * gain
    inner = jnp.mean(weighted * values, axis=-1, keepdims=True)
    grad = scale * weighted - values * (scale * scale * scale * inner)
    return grad, jnp.sum(incoming * values * scale, axis=0, keepdims=True)


def project_kernel(heads, x_ref, gain_ref, w_ref, cos_ref, sin_ref, normed_ref, heads_ref):
    step = pl.program_id(0)

    @pl.when(step == 0)
    def _():
        x = x_ref[...].astype(jnp.float32)
        normed_ref[...] = low(x * norm_scale(x) * gain_row(gain_ref, 0))

    part = dot(normed_ref[...], w_ref[...])
    cosine, sine_part = cos_ref[...], sin_ref[...]
    count = heads_ref.shape[0]
    for j in range(count):
        value = part[:, j * HD : (j + 1) * HD]
        turned = value * cosine + pltpu.roll(value, HD // 2, 1) * sine_part
        head = step * count + j
        value = jnp.where(head < heads, turned * HD ** (-0.5), jnp.where(head == heads, turned, value))
        heads_ref[j] = low(value)


def project(x, gain, w, cosine, sine_part):
    rows, width = x.shape
    count = (H + 2) // PROJECT_STEPS
    whole = lambda *shape: pl.BlockSpec(shape, lambda i: (0,) * len(shape))
    return pl.pallas_call(
        functools.partial(project_kernel, H),
        grid=(PROJECT_STEPS,),
        name="project",
        in_specs=[
            whole(rows, width),
            whole(*gain.shape),
            pl.BlockSpec((width, count * HD), lambda i: (0, i)),
            whole(rows, HD),
            whole(rows, HD),
        ],
        out_specs=[
            whole(rows, width),
            pl.BlockSpec((count, rows, HD), lambda i: (i, 0, 0)),
        ],
        out_shape=[
            jax.ShapeDtypeStruct((rows, width), jnp.bfloat16),
            jax.ShapeDtypeStruct((H + 2, rows, HD), jnp.bfloat16),
        ],
        compiler_params=pltpu.CompilerParams(vmem_limit_bytes=VMEM_LIMIT),
    )(x, gain, w, cosine, sine_part)


PROJECT_STEPS = 2
HEADS_STEP = 4
ANY = pl.BlockSpec(memory_space=pl.ANY)


class Window:
    def __init__(self, rows):
        self.block = rows // ROUNDS
        self.blocks = (WINDOW + self.block - 2) // self.block + 1
        self.span = self.blocks * self.block


def place_tables(
    index, devices, order_ref, lengths_ref, frequency_ref,
    where_ref, key_place_ref, bounds_ref, wide_ref, cos_ref, sin_ref, order_rows,
):
    block = bounds_ref.shape[0] // ROUNDS
    count = order_ref.shape[1] // block
    window = Window(block * ROUNDS)
    blocks = [order_ref[:, i * block : (i + 1) * block] for i in range(count)]
    order_rows[...] = jnp.concatenate(blocks, axis=0).astype(jnp.float32)
    blocks = order_rows[...]
    block_of = lambda place: jnp.floor((place + 0.5) * (1.0 / block))
    held = block_of(blocks[:, :1])
    offsets = low(blocks - held * block)
    at = lax.broadcasted_iota(jnp.int32, (count, 1), 0).astype(jnp.float32)
    lane = lax.broadcasted_iota(jnp.int32, (1, LANES), 1).astype(jnp.float32)
    step = jnp.where(lane < window.blocks, lane, lane - window.blocks)
    lengths = lengths_ref[...].astype(jnp.float32)
    ends = [lengths[:, :1]]
    for j in range(1, lengths.shape[1]):
        ends.append(ends[-1] + lengths[:, j : j + 1])

    def least_of(place):
        start = jnp.zeros_like(place)
        for end in ends:
            start = jnp.where(end <= place, end, start)
        return jnp.maximum(start, place - (WINDOW - 1))

    where_ref[...] = jnp.zeros_like(where_ref)
    own = []
    for r in range(ROUNDS):
        mine = order_rows[pl.ds(index * ROUNDS + r, 1), :]
        own.append(mine)
        wanted = block_of(mine[:, :1]) - (window.blocks - 1) + step
        match = (held == jnp.maximum(wanted, 0.0)).astype(jnp.float32)
        where = jnp.sum(match * at, axis=0, keepdims=True)
        device = jnp.floor((where + 0.5) * (1.0 / ROUNDS))
        target = (where - ROUNDS * device) * devices + device
        where_ref[r : r + 1, :] = jnp.where(lane < window.blocks, where, target).astype(jnp.int32)
        inner = tn_dot(low(match), offsets)
        pieces = []
        for j in range(window.blocks):
            one = wanted[:, j : j + 1]
            pieces.append(inner[j : j + 1] + jnp.where(one >= 0.0, one * block, 1e9))
        key_place_ref[r] = jnp.concatenate(pieces, axis=1)
        wide_ref[r, :1, :] = jnp.concatenate([mine] * HEADS_STEP, axis=1)
        wide_ref[r, 1:, :] = jnp.concatenate([least_of(mine)] * HEADS_STEP, axis=1)
    own = jnp.concatenate(own, axis=1)
    own = jnp.broadcast_to(own, (8, own.shape[1])).T[:, :1]
    bounds_ref[:, :1] = own
    bounds_ref[:, 1:] = least_of(own)
    angles = own * frequency_ref[...]
    cos_ref[...] = jnp.cos(angles)
    sign = jnp.where(lane < HD // 2, -1.0, 1.0)
    sin_ref[...] = jnp.sin(angles) * sign


def place_arrays(order, lengths, rows):
    window = Window(rows)
    frequency = 10000.0 ** (-jnp.arange(HD // 2, dtype=jnp.float32) / (HD // 2))
    operands = (
        order,
        lengths,
        jnp.concatenate([frequency, frequency])[None],
    )
    wide = jax.ShapeDtypeStruct((rows, HD), jnp.float32)
    shapes = (
        jax.ShapeDtypeStruct((8, LANES), jnp.int32),
        jax.ShapeDtypeStruct((ROUNDS, 1, window.span), jnp.float32),
        jax.ShapeDtypeStruct((rows, 2), jnp.float32),
        jax.ShapeDtypeStruct((ROUNDS, 2, HEADS_STEP * window.block), jnp.float32),
        wide,
        wide,
    )
    return operands, shapes


def place_tables_alone(devices, order, lengths, rows):
    operands, shapes = place_arrays(order, lengths, rows)

    def kernel(*refs):
        place_tables(lax.axis_index("ctx"), devices, *refs)

    block = Window(rows).block

    vmem = pl.BlockSpec(memory_space=pltpu.VMEM)
    return pl.pallas_call(
        kernel,
        name="places",
        in_specs=[vmem] * len(operands),
        out_specs=[vmem] * len(shapes),
        out_shape=shapes,
        scratch_shapes=[pltpu.VMEM((order.shape[1] // block, block), jnp.float32)],
    )(*operands)


def load_window(blocks, block, where_ref, kv_ref, window):
    r = pl.program_id(0)
    for j in range(blocks):
        rows = slice(j * block, (j + 1) * block)
        at = where_ref[r, j]
        device, round_ = at // ROUNDS, lax.rem(at, ROUNDS)
        span = pl.ds(pl.multiple_of(round_ * block, 16), block)
        window[rows, :HD] = kv_ref[device, 0, span, :]
        window[rows, HD:] = kv_ref[device, 1, span, :]


def attend_kernel(
    blocks, block, where_ref, q_ref, kv_ref, key_place_ref, bounds_ref, out_ref, log_ref, window, bias
):
    load_window(blocks, block, where_ref, kv_ref, window)
    key_place = key_place_ref[0]
    allowed = (key_place <= bounds_ref[:, :1]) & (key_place >= bounds_ref[:, 1:])
    bias[...] = jnp.where(allowed, 0.0, -1e30)
    for part in range(q_ref.shape[0] // HEADS_STEP):
        first = part * HEADS_STEP
        queries = q_ref[first : first + HEADS_STEP].reshape(HEADS_STEP * block, HD)
        scores = nt_dot(queries, window[:, :HD])
        scores = scores.reshape(HEADS_STEP, block, blocks * block) + bias[...][None]
        peak = jnp.max(scores, axis=-1, keepdims=True)
        weights = jnp.exp(scores - peak)
        total = jnp.sum(weights, axis=-1, keepdims=True).reshape(HEADS_STEP * block, 1)
        weights = low(weights).reshape(HEADS_STEP * block, blocks * block)
        mixed = low(dot(weights, window[:, HD:]) / total)
        for j in range(HEADS_STEP):
            columns = slice((first + j) * HD, (first + j + 1) * HD)
            out_ref[:, columns] = mixed[j * block : (j + 1) * block]
        log_total = peak.reshape(HEADS_STEP * block, 1) + jnp.log(total)
        log_ref[0, part] = jnp.broadcast_to(log_total, (HEADS_STEP * block, LANES)).T[:1, :]


def attend(where, queries, kv_blocks, key_place, bounds):
    heads, rows = H, queries.shape[1]
    window = Window(rows)
    block, span, parts = window.block, window.span, heads // HEADS_STEP
    grid_spec = pltpu.PrefetchScalarGridSpec(
        num_scalar_prefetch=1,
        grid=(ROUNDS,),
        in_specs=[
            pl.BlockSpec((heads, block, HD), lambda r, *_: (0, r, 0)),
            pl.BlockSpec(kv_blocks.shape, lambda r, *_: (0, 0, 0, 0)),
            pl.BlockSpec((1, 1, span), lambda r, *_: (r, 0, 0)),
            pl.BlockSpec((block, 2), lambda r, *_: (r, 0)),
        ],
        out_specs=[
            pl.BlockSpec((block, heads * HD), lambda r, *_: (r, 0)),
            pl.BlockSpec((1, parts, 1, HEADS_STEP * block), lambda r, *_: (r, 0, 0, 0)),
        ],
        scratch_shapes=[
            pltpu.VMEM((span, 2 * HD), jnp.bfloat16),
            pltpu.VMEM((block, span), jnp.float32),
        ],
    )
    return pl.pallas_call(
        functools.partial(attend_kernel, window.blocks, block),
        name="attend",
        grid_spec=grid_spec,
        out_shape=[
            jax.ShapeDtypeStruct((rows, heads * HD), jnp.bfloat16),
            jax.ShapeDtypeStruct((ROUNDS, parts, 1, HEADS_STEP * block), jnp.float32),
        ],
        compiler_params=pltpu.CompilerParams(vmem_limit_bytes=VMEM_LIMIT),
    )(where, queries, kv_blocks, key_place, bounds)


def attend_back_kernel(
    blocks, block, where_ref, q_ref, kv_ref, grad_ref, mixed_ref, log_ref, key_place_ref, bounds_ref,
    cos_ref, sin_ref, *refs,
):
    grad_q_ref, grad_kv_ref, window, bias, window_grad, total_grad = refs[-6:]
    r = pl.program_id(0)

    @pl.when(r == 0)
    def _():
        total_grad[...] = jnp.zeros_like(total_grad)

    load_window(blocks, block, where_ref, kv_ref, window)
    key_place = jnp.broadcast_to(key_place_ref[0], (8, blocks * block)).T[:, :1]
    allowed = (key_place <= bounds_ref[0, :1, :]) & (key_place >= bounds_ref[0, 1:, :])
    bias[...] = jnp.where(allowed, 0.0, -1e30)
    keys, values = window[:, :HD], window[:, HD:]
    cosine, sine_part = cos_ref[...], sin_ref[...]
    for part in range(q_ref.shape[0] // HEADS_STEP):
        first = part * HEADS_STEP
        spans = [slice((first + j) * HD, (first + j + 1) * HD) for j in range(HEADS_STEP)]
        queries = q_ref[first : first + HEADS_STEP].reshape(HEADS_STEP * block, HD)
        grads = jnp.concatenate([grad_ref[:, span] for span in spans], axis=0)
        delta = jnp.concatenate(
            [
                jnp.sum(
                    (grad_ref[:, span].astype(jnp.float32) * mixed_ref[:, span].astype(jnp.float32)).T,
                    axis=0,
                    keepdims=True,
                )
                for span in spans
            ],
            axis=1,
        )
        probs = jnp.exp(nt_dot(keys, queries) + (bias[...] - log_ref[0, part]))
        grad_scores = low(probs * (nt_dot(values, grads) - delta))
        grad_keys = dot(grad_scores, queries)
        grad_values = dot(low(probs), grads)
        if part == 0:
            window_grad[:, :HD] = grad_keys
            window_grad[:, HD:] = grad_values
        else:
            window_grad[:, :HD] += grad_keys
            window_grad[:, HD:] += grad_values
        grad_q = tn_dot(grad_scores, keys)
        for j, span in enumerate(spans):
            one = grad_q[j * block : (j + 1) * block]
            one = (one * cosine - pltpu.roll(one, HD // 2, 1) * sine_part) * HD ** (-0.5)
            grad_q_ref[:, span] = low(one)
    for j in range(blocks):
        total_grad[where_ref[r, blocks + j]] += window_grad[j * block : (j + 1) * block, :]

    @pl.when(r == pl.num_programs(0) - 1)
    def _():
        grad_kv_ref[...] = low(total_grad[...])


def attend_back(
    where, queries, kv_blocks, grads, mixed, log_total, key_place, bounds, cosine, sine_part, earlier
):
    heads, rows = H, queries.shape[1]
    kv_sums = (kv_blocks.shape[0] * ROUNDS, rows // ROUNDS, 2 * HD)
    window = Window(rows)
    block, span, parts = window.block, window.span, heads // HEADS_STEP
    width = HEADS_STEP * block
    grid_spec = pltpu.PrefetchScalarGridSpec(
        num_scalar_prefetch=1,
        grid=(ROUNDS,),
        in_specs=[
            pl.BlockSpec((heads, block, HD), lambda r, *_: (0, r, 0)),
            pl.BlockSpec(kv_blocks.shape, lambda r, *_: (0, 0, 0, 0)),
            pl.BlockSpec((block, heads * HD), lambda r, *_: (r, 0)),
            pl.BlockSpec((block, heads * HD), lambda r, *_: (r, 0)),
            pl.BlockSpec((1, parts, 1, width), lambda r, *_: (r, 0, 0, 0)),
            pl.BlockSpec((1, 1, span), lambda r, *_: (r, 0, 0)),
            pl.BlockSpec((1, 2, width), lambda r, *_: (r, 0, 0)),
            pl.BlockSpec((block, HD), lambda r, *_: (r, 0)),
            pl.BlockSpec((block, HD), lambda r, *_: (r, 0)),
        ]
        + [ANY] * len(earlier),
        out_specs=[
            pl.BlockSpec((block, heads * HD), lambda r, *_: (r, 0)),
            pl.BlockSpec(kv_sums, lambda r, *_: (0, 0, 0)),
        ],
        scratch_shapes=[
            pltpu.VMEM((span, 2 * HD), jnp.bfloat16),
            pltpu.VMEM((span, width), jnp.float32),
            pltpu.VMEM((span, 2 * HD), jnp.float32),
            pltpu.VMEM(kv_sums, jnp.float32),
        ],
    )
    return pl.pallas_call(
        functools.partial(attend_back_kernel, window.blocks, block),
        name="attend_back",
        grid_spec=grid_spec,
        out_shape=[
            jax.ShapeDtypeStruct((rows, heads * HD), jnp.bfloat16),
            jax.ShapeDtypeStruct(kv_sums, jnp.bfloat16),
        ],
        compiler_params=pltpu.CompilerParams(vmem_limit_bytes=VMEM_LIMIT),
    )(
        where,
        queries,
        kv_blocks,
        grads,
        mixed,
        log_total,
        key_place,
        bounds,
        cosine,
        sine_part,
        *earlier,
    )


MIDDLE_TILES = 3
FORWARD_TILES = 2


def whole_block(shape):
    return pl.BlockSpec(shape, lambda i: (0,) * len(shape))


def middle_kernel(x_ref, mixed_ref, gain_ref, w_ref, middle_ref, left_ref, right_ref):
    step = pl.program_id(0)
    tile = w_ref.shape[1]
    columns = pl.ds(pl.multiple_of(step * tile, tile), tile)
    middle_ref[:, columns] = x_ref[:, columns].astype(jnp.float32) + dot(mixed_ref[...], w_ref[...])

    @pl.when(step == pl.num_programs(0) - 1)
    def _():
        values = middle_ref[...]
        normed = low(values * norm_scale(values) * gain_row(gain_ref, 1))
        half = left_ref.shape[1]
        left_ref[...] = normed[:, :half]
        right_ref[...] = normed[:, half:]


def middle_forward(x, mixed, gains, w):
    rows, width = x.shape
    half = width // 2
    inner = mixed.shape[1]
    return pl.pallas_call(
        middle_kernel,
        name="middle",
        grid=(FORWARD_TILES,),
        in_specs=[
            whole_block((rows, width)),
            whole_block((rows, inner)),
            whole_block(gains.shape),
            pl.BlockSpec((inner, width // FORWARD_TILES), lambda i: (0, i)),
        ],
        out_specs=[whole_block((rows, width))] + [whole_block((rows, half))] * 2,
        out_shape=[
            jax.ShapeDtypeStruct((rows, width), jnp.float32),
            jax.ShapeDtypeStruct((rows, half), jnp.bfloat16),
            jax.ShapeDtypeStruct((rows, half), jnp.bfloat16),
        ],
        compiler_params=pltpu.CompilerParams(vmem_limit_bytes=VMEM_LIMIT),
    )(x, mixed, gains, w)


def middle_back_kernel(
    grad_ref, middle_ref, upstream_ref, mixed_ref, gain_ref, w_ref,
    grad_middle_ref, grad_mixed_ref, grad_w_ref, grad_gain_ref, token, branch,
):
    @pl.when(pl.program_id(0) == 0)
    def _():
        grad, grad_gain = norm_back(middle_ref[...], gain_row(gain_ref, 1), grad_ref[...])
        total = upstream_ref[...].astype(jnp.float32) + grad
        grad_middle_ref[...] = total
        branch[...] = low(total)
        grad_gain_ref[...] = grad_gain
        token[...] = jnp.zeros_like(token)

    grad_mixed_ref[...] = low(nt_dot(branch[...], w_ref[...]))
    grad_w_ref[...] = low(tn_dot(mixed_ref[...], branch[...]))


def middle_back(grad, middle, upstream, mixed, gains, w):
    rows, width = middle.shape
    inner = mixed.shape[1]
    tile = inner // MIDDLE_TILES
    return pl.pallas_call(
        middle_back_kernel,
        name="middle_back",
        grid=(MIDDLE_TILES,),
        in_specs=[
            whole_block((rows, width)),
            whole_block((rows, width)),
            whole_block((rows, width)),
            pl.BlockSpec((rows, tile), lambda i: (0, i)),
            whole_block(gains.shape),
            pl.BlockSpec((tile, width), lambda i: (i, 0)),
        ],
        out_specs=[
            whole_block((rows, width)),
            pl.BlockSpec((rows, tile), lambda i: (0, i)),
            pl.BlockSpec((tile, width), lambda i: (i, 0)),
            whole_block((1, width)),
            whole_block(TOKEN),
        ],
        out_shape=[
            jax.ShapeDtypeStruct((rows, width), jnp.float32),
            jax.ShapeDtypeStruct((rows, inner), jnp.bfloat16),
            jax.ShapeDtypeStruct((inner, width), jnp.bfloat16),
            jax.ShapeDtypeStruct((1, width), jnp.float32),
            token_shape(),
        ],
        scratch_shapes=[pltpu.VMEM((rows, width), jnp.bfloat16)],
        compiler_params=pltpu.CompilerParams(vmem_limit_bytes=VMEM_LIMIT),
    )(grad, middle, upstream, mixed, gains, w)


def project_back_queries_kernel(grad_ref, normed_ref, w_ref, grad_w_ref, grad_normed_ref):
    grad_normed_ref[...] = nt_dot(grad_ref[...], w_ref[...])
    grad_w_ref[...] = low(tn_dot(normed_ref[...], grad_ref[...]))


def project_back_queries(grad_q, normed, w):
    rows, width = normed.shape
    inner = grad_q.shape[1]
    tile = width // MIDDLE_TILES
    return pl.pallas_call(
        project_back_queries_kernel,
        name="project_back_queries",
        grid=(MIDDLE_TILES,),
        in_specs=[
            whole_block(grad_q.shape),
            pl.BlockSpec((rows, tile), lambda i: (0, i)),
            pl.BlockSpec((tile, inner), lambda i: (i, 0)),
        ],
        out_specs=[
            pl.BlockSpec((tile, inner), lambda i: (i, 0)),
            pl.BlockSpec((rows, tile), lambda i: (0, i)),
        ],
        out_shape=[
            jax.ShapeDtypeStruct((width, inner), jnp.bfloat16),
            jax.ShapeDtypeStruct((rows, width), jnp.float32),
        ],
        compiler_params=pltpu.CompilerParams(vmem_limit_bytes=VMEM_LIMIT),
    )(grad_q, normed, w)


def project_back_keys_kernel(
    grad_kv_ref, cos_ref, sin_ref, normed_ref, partial_ref, x_ref, grad_middle_ref, gain_ref, w_ref,
    grad_w_ref, grad_x_ref, grad_gain_ref,
):
    keys = grad_kv_ref[:, :HD]
    keys = low(keys * cos_ref[...] - pltpu.roll(keys, HD // 2, 1) * sin_ref[...])
    joined = jnp.concatenate([keys, low(grad_kv_ref[:, HD:])], axis=1)
    grad_w_ref[...] = low(tn_dot(normed_ref[...], joined))
    grad_normed = partial_ref[...] + nt_dot(joined, w_ref[...])
    grad, grad_gain = norm_back(x_ref[...].astype(jnp.float32), gain_row(gain_ref, 0), grad_normed)
    grad_x_ref[...] = grad_middle_ref[...] + grad
    grad_gain_ref[...] = grad_gain


def project_back_keys(grad_kv, cosine, sine_part, normed, partial, x, grad_middle, gains, w):
    rows, width = x.shape
    inner = grad_kv.shape[1]
    arrays = (grad_kv, cosine, sine_part, normed, partial, x, grad_middle, gains)
    last = w.shape[1] // inner - 1
    return pl.pallas_call(
        project_back_keys_kernel,
        name="project_back_keys",
        grid=(1,),
        in_specs=[whole_block(one.shape) for one in arrays]
        + [pl.BlockSpec((width, inner), lambda i: (0, last))],
        out_specs=[whole_block((width, inner)), whole_block((rows, width)), whole_block((1, width))],
        out_shape=[
            jax.ShapeDtypeStruct((width, inner), jnp.bfloat16),
            jax.ShapeDtypeStruct((rows, width), jnp.float32),
            jax.ShapeDtypeStruct((1, width), jnp.float32),
        ],
        compiler_params=pltpu.CompilerParams(vmem_limit_bytes=VMEM_LIMIT),
    )(*arrays, w)


MESH_ID =MESH_ID = pl.DeviceIdType.MESH


class Wire:
    def __init__(self, send_sems, recv_sems):
        self.send_sems = send_sems
        self.recv_sems = recv_sems
        self.count = 0
        self.open = []
        self.ctx = lax.axis_index("ctx")
        self.shard = lax.axis_index("fsdp")

    def other(self, mask):
        at = self.ctx
        for bit in (1, 2, 4):
            if mask & bit:
                at = at + bit - 2 * bit * lax.rem(at // bit, 2)
        return at

    def plane(self, mask):
        return (self.other(mask), self.shard)

    def line(self, step, shards):
        return (self.ctx, lax.rem(self.shard + step, shards))

    def meet(self, peers):
        barrier = pltpu.get_barrier_semaphore()
        for peer in peers:
            pl.semaphore_signal(barrier, inc=1, device_id=peer, device_id_type=MESH_ID)
        pl.semaphore_wait(barrier, len(peers))

    def send(self, source, target, peer):
        at = self.count
        self.count += 1
        copy = pltpu.make_async_remote_copy(
            src_ref=source,
            dst_ref=target,
            send_sem=self.send_sems.at[at],
            recv_sem=self.recv_sems.at[at],
            device_id=peer,
            device_id_type=MESH_ID,
        )
        copy.start()
        self.open.append(copy)
        return copy

    def sent(self, copy):
        copy.wait_send()
        self.open = [one for one in self.open if one is not copy]

    def finish(self):
        for copy in self.open:
            copy.wait_send()


class PlaneGather:
    COPIES = 9

    def __init__(self, wire, source, out_at, rows, split):
        self.wire, self.out_at, self.rows, self.split = wire, out_at, rows, split
        ctx = wire.ctx
        self.core = wire.send(source, out_at(ctx), wire.plane(1))
        self.x = wire.send(source, out_at(ctx), wire.plane(2))
        self.y = wire.send(source, out_at(ctx), wire.plane(4))

    def forward(self):
        wire, split = self.wire, self.split
        rest = self.rows - split
        self.x.wait_recv()
        block = self.out_at(wire.other(2))
        part = block.at[pl.ds(0, split)]
        self.corner_y = wire.send(part, part, wire.plane(4))
        self.core_x = wire.send(block, block, wire.plane(1))
        self.y.wait_recv()
        block = self.out_at(wire.other(4))
        part = block.at[pl.ds(split, rest)]
        self.corner_x = wire.send(part, part, wire.plane(2))
        self.core_y = wire.send(block, block, wire.plane(1))

    def corner(self):
        self.corner_y.wait_recv()
        self.corner_x.wait_recv()
        block = self.out_at(self.wire.other(6))
        self.core_corner = self.wire.send(block, block, self.wire.plane(1))

    def settle(self):
        self.core.wait_recv()
        self.core_x.wait_recv()
        self.core_y.wait_recv()
        self.core_corner.wait_recv()


def half_rows(rows, turn):
    low_half = rows // 32 * 16
    return low_half if turn % 2 else rows - low_half


def add_low(first, second):
    return (first.astype(jnp.float32) + second.astype(jnp.float32)).astype(jnp.bfloat16)


class PlaneSum:
    COPIES = 7

    def __init__(self, wire, source, own, pair, first, second, local_sem):
        self.wire, self.own, self.pair, self.first, self.second = wire, own, pair, first, second
        core = lax.rem(wire.ctx, 2)
        self.chips = {mask: wire.other(2 * mask) // 2 for mask in range(4)}
        self.swap = wire.send(source.at[:, :, 1 - core], pair, wire.plane(1))
        self.local = pltpu.make_async_copy(source.at[:, :, core], own, local_sem)
        self.local.start()

    def step_one(self):
        wire, own, pair, first, chips = self.wire, self.own, self.pair, self.first, self.chips
        self.local.wait()
        self.swap.wait_recv()

        def add_pair(index, carry):
            part, other = index // 4, lax.rem(index, 4)
            own[part, other] = add_low(own[part, other], pair[part, other])
            return carry

        lax.fori_loop(0, 16, add_pair, 0)
        low, high = pl.ds(0, 2), pl.ds(2, 2)
        self.one = [
            wire.send(own.at[low, chips[3]], first.at[0, 1], wire.plane(2)),
            wire.send(own.at[high, chips[3]], first.at[1, 1], wire.plane(4)),
            wire.send(own.at[low, chips[1]], first.at[0, 0], wire.plane(2)),
            wire.send(own.at[high, chips[2]], first.at[1, 0], wire.plane(4)),
        ]

    def step_two(self):
        wire, own, first, second, chips = self.wire, self.own, self.first, self.second, self.chips
        self.one[0].wait_recv()
        for part in range(2):
            own[part, chips[2]] = add_low(own[part, chips[2]], first[0, 1, part])
        self.two = [wire.send(own.at[pl.ds(0, 2), chips[2]], second.at[pl.ds(0, 2)], wire.plane(4))]
        self.one[1].wait_recv()
        for part in range(2):
            own[part + 2, chips[1]] = add_low(own[part + 2, chips[1]], first[1, 1, part])
        self.two.append(
            wire.send(own.at[pl.ds(2, 2), chips[1]], second.at[pl.ds(2, 2)], wire.plane(2))
        )

    def result(self, store):
        own, first, second, chips = self.own, self.first, self.second, self.chips
        for copy in self.one[2:] + self.two:
            copy.wait_recv()
        for part in range(4):
            total = own[part, chips[0]].astype(jnp.float32)
            total += first[part // 2, 0, part % 2].astype(jnp.float32)
            total += second[part].astype(jnp.float32)
            store(part, total)


def plane_sum_scratch(rows, columns):
    shape = lambda *lead: pltpu.VMEM(lead + (rows, columns), jnp.bfloat16)
    return [shape(4, 4), shape(4, 4), shape(2, 2, 2), shape(4)]


def dma_sems(count):
    return pltpu.SemaphoreType.DMA((count,))


PLANE_PEERS = (1, 2, 4)


def comm_params(number):
    return pltpu.CompilerParams(
        collective_id=number, has_side_effects=True, vmem_limit_bytes=VMEM_LIMIT
    )


def take(values, count):
    return values[:count], values[count:]


class Relay:
    def __init__(self, source, stage, targets, sems):
        self.stage, self.targets, self.sems = stage, targets, sems
        self.load = pltpu.make_async_copy(source, stage, sems.at[0])
        self.load.start()

    def push(self):
        self.load.wait()
        self.stores = []
        for i, (part, target) in enumerate(self.targets):
            store = pltpu.make_async_copy(part, target, self.sems.at[1 + i])
            store.start()
            self.stores.append(store)

    def settle(self):
        for store in self.stores:
            store.wait()


TOKEN = (8, 128)


def token_shape():
    return jax.ShapeDtypeStruct(TOKEN, jnp.int32)


def after(token, values):
    return jnp.where(token[0, 0] != 0, jnp.zeros_like(values), values)


def share_line_kernel(
    shards, pack, in_ref, gain_ref, mlp_in, mlp_out, up_ref, in_line, gain_all, mine, up_x, up_y,
    gain_now, in_stage, packed, tiles, local_sems, load_sems, send_sems, recv_sems,
):
    wire = Wire(send_sems, recv_sems)
    ctx, shard = wire.ctx, wire.shard
    chip, core = ctx // 2, lax.rem(ctx, 2)
    chips = pack.chips
    relay = Relay(in_ref.at[ctx], in_stage, [(in_stage, in_line.at[shard])], local_sems.at[0])
    gain_now[...] = jnp.zeros_like(gain_now)
    gain_now[:2] = gain_ref[...].astype(jnp.float32)
    wire.meet(
        [wire.line(step, shards) for step in range(1, shards)] + [wire.plane(2), wire.plane(4)]
    )
    half = pack.half
    copies = [
        wire.send(up_ref.at[:, pl.ds(0, half)], up_x, wire.plane(2)),
        wire.send(up_ref.at[:, pl.ds(half, half)], up_y, wire.plane(4)),
    ]
    for source, target in ((gain_now, gain_all), (in_ref.at[ctx], in_line)):
        for step in range(1, shards):
            copies.append(wire.send(source, target.at[shard], wire.line(step, shards)))
    gain_copy = pltpu.make_async_copy(gain_now, gain_all.at[shard], local_sems.at[1, 0])
    gain_copy.start()
    relay.push()

    loads = []

    def load(source, target):
        copy = pltpu.make_async_copy(source, target, load_sems.at[len(loads)])
        copy.start()
        loads.append(copy)

    def strip(start, count):
        return pl.ds(pl.multiple_of(start, LANES), count)

    main, rest, half, tail, split = pack.main, pack.rest, pack.half, pack.tail, pack.split
    per_shard = chips * (main + rest)
    base = core * (shards * per_shard)
    for part in range(shards):
        start = base + part * per_shard
        load(mlp_in.at[:, strip(start + chips * main, chips * rest)], tiles.at[part])
        column = part * main
        if column + main <= half:
            source = mlp_in.at[:, strip(start + chip * main, main)]
            load(source, packed.at[pl.ds(pack.main_start, pack.rows), pl.ds(column, main)])
            continue
        for i, at in enumerate(range(0, pack.rows, split)):
            source = mlp_in.at[pl.ds(at, split), strip(start + chip * main, main)]
            load(source, packed.at[pl.ds(pack.tail_start, split), pl.ds(i * tail + column - half, main)])
    columns = strip(core * half, half)
    for start, count, row in (
        (chip * main, main, 0),
        (chips * main + chip * rest, rest, main),
    ):
        source = mlp_out.at[pl.ds(pl.multiple_of(start, 16), count), columns]
        load(source, packed.at[pl.ds(row, count), :])
    for copy in loads:
        copy.wait()
    width = chips * rest
    ends = [
        pltpu.roll(tiles[part].astype(jnp.float32), lax.rem(width - chip * rest, width), 1)[:, :rest]
        for part in range(shards)
    ]
    ends = low(jnp.concatenate(ends, axis=1))
    for i, at in enumerate(range(0, pack.rows, split)):
        column = i * tail + shards * main - half
        packed[pack.tail_start : pack.tail_start + split, column : column + shards * rest] = ends[at : at + split]
    mine_copy = pltpu.make_async_copy(packed, mine, local_sems.at[1, 1])
    mine_copy.start()
    relay.settle()
    gain_copy.wait()
    mine_copy.wait()
    for copy in copies:
        copy.wait_recv()
    wire.finish()


def gather_shards(wire, line, target, rows, shards, count):
    gathers = []
    for step in range(1, shards):
        origin = lax.rem(wire.shard + shards - step, shards)
        place = lambda who, origin=origin: target.at[origin, who]
        gathers.append(PlaneGather(wire, line.at[origin], place, rows, half_rows(rows, step + count)))
    return gathers


def relay_shards(wire, whole, line, target, stage, piece, shards, sems):
    origins = [lax.rem(wire.shard + shards - step, shards) for step in range(1, shards)]
    places = [(piece.at[origin], target.at[origin, wire.ctx]) for origin in origins]
    return [
        Relay(whole, stage, [(stage, target.at[wire.shard])], sems.at[0]),
        Relay(line, piece, places, sems.at[1]),
    ]


def complete(gathers, relays):
    for gather in gathers:
        gather.forward()
    for gather in gathers:
        gather.corner()
    for gather in gathers:
        gather.settle()
    for relay in relays:
        relay.settle()


def share_plane_kernel(
    shards, devices, in_ref, in_line, out_ref, order, lengths, frequency, in_all, out_line, *refs
):
    tables, scratch = take(refs, len(refs) - 7)
    order_rows, in_stage, in_piece, out_stage, local_sems, send_sems, recv_sems = scratch
    wire = Wire(send_sems, recv_sems)
    ctx, shard = wire.ctx, wire.shard
    relays = relay_shards(wire, in_ref, in_line, in_all, in_stage, in_piece, shards, local_sems)
    relays.append(
        Relay(out_ref.at[ctx], out_stage, [(out_stage, out_line.at[shard])], local_sems.at[2])
    )
    wire.meet(
        [wire.plane(mask) for mask in PLANE_PEERS] + [wire.line(s, shards) for s in range(1, shards)]
    )
    gathers = gather_shards(wire, in_line, in_all, in_ref.shape[1], shards, 0)
    copies = [
        wire.send(out_ref.at[ctx], out_line.at[shard], wire.line(step, shards))
        for step in range(1, shards)
    ]
    for relay in relays:
        relay.push()
    place_tables(ctx, devices, order, lengths, frequency, *tables, order_rows)
    complete(gathers, relays)
    for copy in copies:
        copy.wait_recv()
    wire.finish()


def gather_plane_kernel(
    shards, heads_ref, out_ref, out_line, kv_all, out_all, token,
    kv_stage, out_stage, out_piece, local_sems, send_sems, recv_sems,
):
    wire = Wire(send_sems, recv_sems)
    ctx = wire.ctx
    kv_ref = heads_ref.at[pl.ds(H, 2)]
    relays = relay_shards(wire, out_ref, out_line, out_all, out_stage, out_piece, shards, local_sems)
    relays.append(Relay(kv_ref, kv_stage, [(kv_stage, kv_all.at[ctx])], local_sems.at[2]))
    token[...] = jnp.zeros_like(token)
    wire.meet([wire.plane(mask) for mask in PLANE_PEERS])
    gathers = [PlaneGather(wire, kv_ref, lambda who: kv_all.at[who], 2, 1)]
    gathers += gather_shards(wire, out_line, out_all, out_ref.shape[1], shards, 1)
    for relay in relays:
        relay.push()
    complete(gathers, relays)
    wire.finish()


def like(values, *lead):
    return jax.ShapeDtypeStruct(lead + values.shape[-2:], values.dtype)


def stage_like(values, *lead):
    return pltpu.VMEM(lead + values.shape[-2:], values.dtype)


def share_line(w_in, gains, mlp_in, mlp_out, upstream, pack, shards):
    columns = gains.shape[1]
    copies = 2 * (shards - 1) + 2
    loads = shards + shards + 1 + 2
    return pl.pallas_call(
        functools.partial(share_line_kernel, shards, pack),
        name="share_line",
        in_specs=[ANY] + [pl.BlockSpec(memory_space=pltpu.VMEM)] + [ANY] * 3,
        out_specs=[ANY] * 5,
        out_shape=[
            like(w_in, shards),
            jax.ShapeDtypeStruct((shards, 8, columns), jnp.float32),
            jax.ShapeDtypeStruct((pack.total, pack.half), mlp_in.dtype),
        ]
        + [jax.ShapeDtypeStruct((upstream.shape[0], pack.half), upstream.dtype)] * 2,
        scratch_shapes=[
            pltpu.VMEM((8, columns), jnp.float32),
            stage_like(w_in),
            pltpu.VMEM((pack.total, pack.half), mlp_in.dtype),
            pltpu.VMEM((shards, pack.rows, pack.chips * pack.rest), mlp_in.dtype),
            pltpu.SemaphoreType.DMA((2, 2)),
            dma_sems(loads),
            dma_sems(copies),
            dma_sems(copies),
        ],
        compiler_params=comm_params(1),
    )(w_in, gains, mlp_in, mlp_out, upstream)


def share_plane(w_in, in_line, w_out, order, lengths, rows, ctx_size, shards):
    copies = (shards - 1) * (PlaneGather.COPIES + 1)
    operands, shapes = place_arrays(order, lengths, rows)
    vmem = pl.BlockSpec(memory_space=pltpu.VMEM)
    return pl.pallas_call(
        functools.partial(share_plane_kernel, shards, ctx_size),
        name="share_plane",
        in_specs=[ANY] * 3 + [vmem] * len(operands),
        out_specs=[ANY] * 2 + [vmem] * len(shapes),
        out_shape=[like(w_in, shards, ctx_size), like(w_out, shards), *shapes],
        scratch_shapes=[
            pltpu.VMEM((ctx_size * ROUNDS, rows // ROUNDS), jnp.float32),
            stage_like(w_in, ctx_size),
            stage_like(w_in, shards),
            stage_like(w_out),
            pltpu.SemaphoreType.DMA((3, shards)),
            dma_sems(copies),
            dma_sems(copies),
        ],
        compiler_params=comm_params(6),
    )(w_in, in_line, w_out, *operands)


def gather_plane(heads, w_out, out_line, ctx_size, shards):
    copies = shards * PlaneGather.COPIES
    key_value = jax.ShapeDtypeStruct((2,) + heads.shape[1:], heads.dtype)
    return pl.pallas_call(
        functools.partial(gather_plane_kernel, shards),
        name="gather_plane",
        in_specs=[ANY] * 3,
        out_specs=[ANY] * 2 + [pl.BlockSpec(memory_space=pltpu.VMEM)],
        out_shape=[like(key_value, ctx_size, 2), like(w_out, shards, ctx_size), token_shape()],
        scratch_shapes=[
            stage_like(key_value, 2),
            stage_like(w_out, ctx_size),
            stage_like(w_out, shards),
            pltpu.SemaphoreType.DMA((3, shards)),
            dma_sems(copies),
            dma_sems(copies),
        ],
        compiler_params=comm_params(2),
    )(heads, w_out, out_line)


class GainSum:
    def __init__(self, wire, now, arrived, line, shards):
        self.wire, self.now, self.arrived, self.line, self.shards = wire, now, arrived, line, shards
        self.at = 0
        self.start()

    def start(self):
        peer = self.wire.plane(PLANE_PEERS[self.at])
        self.copy = self.wire.send(self.now, self.arrived.at[self.at], peer)

    def add(self):
        self.copy.wait_recv()
        self.wire.sent(self.copy)
        self.now[...] += self.arrived[self.at]
        self.at += 1

    def step(self):
        self.add()
        self.start()

    def step_line(self):
        self.add()
        wire, shards = self.wire, self.shards
        self.copies = [
            wire.send(
                self.now.at[lax.rem(wire.shard + step, shards)],
                self.line.at[step - 1],
                wire.line(step, shards),
            )
            for step in range(1, shards)
        ]

    def result(self):
        for copy in self.copies:
            copy.wait_recv()
        value = self.now[self.wire.shard]
        for step in range(self.shards - 1):
            value += self.line[step]
        return value


def send_lines(wire, source, arrived, shards):
    return [
        wire.send(
            source.at[lax.rem(wire.shard + step, shards)], arrived.at[step - 1], wire.line(step, shards)
        )
        for step in range(1, shards)
    ]


def sum_lines(wire, copies, source, arrived):
    for copy in copies:
        copy.wait_recv()
    value = source[wire.shard].astype(jnp.float32)
    for step in range(len(copies)):
        value += arrived[step].astype(jnp.float32)
    return value


def project_back_plane_kernel(
    kv_ref, g_out_ref, part_ref, grad_ref, normed_ref, x_ref, cos_ref, sin_ref, gain_ref, w_ref,
    out_half, q_half, k_half, part_all, grad_x_ref, grad_gain_ref,
    grad, normed, x, cosine, sine_part, gains, w, g_q, g_k, grad_normed, kv_sum, stage, *scratch,
):
    sums, scratch = take(scratch, 16)
    load_sems, sum_sems, part_sems, send_sems, recv_sems = scratch
    wire = Wire(send_sems, recv_sems)
    loads = []
    for source, target in (
        (grad_ref, grad),
        (normed_ref, normed),
        (w_ref, w),
        (cos_ref, cosine),
        (sin_ref, sine_part),
        (x_ref, x),
        (gain_ref, gains),
    ):
        loads.append(pltpu.make_async_copy(source, target, load_sems.at[len(loads)]))
        loads[-1].start()
    relay = Relay(part_ref, stage, [(stage, part_all.at[wire.ctx])], part_sems)
    wire.meet([wire.plane(mask) for mask in PLANE_PEERS])

    def plane_sum(source, at):
        return PlaneSum(wire, source, *sums[4 * at : 4 * at + 4], sum_sems.at[at])

    rows = part_ref.shape[0]
    keys_sum = plane_sum(kv_ref, 0)
    out_sum = plane_sum(g_out_ref, 1)
    gather = PlaneGather(wire, part_ref, lambda who: part_all.at[who], rows, rows // 32 * 16)
    keys_sum.step_one()
    out_sum.step_one()
    relay.push()
    for copy in loads:
        copy.wait()
    inner = grad.shape[1]
    tile = normed.shape[1] // 4
    pieces = g_q.shape[1:4]

    def queries_part(part, carry):
        span = pl.ds(pl.multiple_of(part * tile, tile), tile)
        value = low(tn_dot(normed[:, span], grad[...]))
        g_q[part] = value.reshape(*pieces, inner)
        grad_normed[:, span] = nt_dot(grad[...], w[span, :inner])
        return carry

    lax.fori_loop(0, 4, queries_part, 0)
    queries_sum = plane_sum(g_q, 2)
    keys_sum.step_two()

    def store_keys(part, value):
        kv_sum[part] = value

    keys_sum.result(store_keys)
    kv = kv_sum[...].reshape(normed.shape[0], 2 * HD)
    keys = kv[:, :HD]
    keys = low(keys * cosine[...] - pltpu.roll(keys, HD // 2, 1) * sine_part[...])
    joined = jnp.concatenate([keys, low(kv[:, HD:])], axis=1)
    for part in range(4):
        span = slice(part * tile, (part + 1) * tile)
        g_k[part] = low(tn_dot(normed[:, span], joined)).reshape(*pieces, 2 * HD)
        grad_normed[:, span] += nt_dot(joined, w[span, inner:])
    pair_sum = plane_sum(g_k, 3)
    out_sum.step_two()
    queries_sum.step_one()
    pair_sum.step_one()
    gather.forward()

    def store_into(target):
        def store(part, value):
            target[part] = low(value)

        return store

    out_sum.result(store_into(out_half))
    change, grad_gain = norm_back(x[...].astype(jnp.float32), gain_row(gains, 0), grad_normed[...])
    grad_x_ref[...] = change
    grad_gain_ref[...] = grad_gain
    queries_sum.step_two()
    pair_sum.step_two()
    gather.corner()
    queries_sum.result(store_into(q_half))
    pair_sum.result(store_into(k_half))
    gather.settle()
    relay.settle()
    wire.finish()


def project_back_plane(
    grad_kv, g_out, part, grad_q, normed, x, cosine, sine_part, gains, w, ctx_size
):
    rows, width = x.shape
    inner = grad_q.shape[1]
    lead = g_out.shape[:4]
    vmem = pl.BlockSpec(memory_space=pltpu.VMEM)
    low_scratch = lambda *shape: pltpu.VMEM(shape, jnp.bfloat16)
    wide = lambda *shape: pltpu.VMEM(shape, jnp.float32)
    sums = []
    for piece in (grad_kv.shape[3:], g_out.shape[3:], (lead[3], inner), (lead[3], 2 * HD)):
        sums += plane_sum_scratch(*piece)
    copies = 4 * PlaneSum.COPIES + PlaneGather.COPIES
    half = lambda columns: jax.ShapeDtypeStruct((4, lead[3], columns), jnp.bfloat16)
    return pl.pallas_call(
        project_back_plane_kernel,
        name="project_back_plane",
        in_specs=[ANY] * 10,
        out_specs=[vmem] * 3 + [ANY] + [vmem] * 2,
        out_shape=[
            half(g_out.shape[4]),
            half(inner),
            half(2 * HD),
            like(part, ctx_size),
            jax.ShapeDtypeStruct((rows, width), jnp.float32),
            jax.ShapeDtypeStruct((1, width), jnp.float32),
        ],
        scratch_shapes=[
            low_scratch(*grad_q.shape),
            low_scratch(*normed.shape),
            low_scratch(*x.shape),
            wide(*cosine.shape),
            wide(*cosine.shape),
            wide(*gains.shape),
            low_scratch(*w.shape),
            low_scratch(*lead, inner),
            low_scratch(*lead, 2 * HD),
            wide(rows, width),
            wide(4, *grad_kv.shape[3:]),
            stage_like(part),
            *sums,
            dma_sems(7),
            dma_sems(4),
            dma_sems(2),
            dma_sems(copies),
            dma_sems(copies),
        ],
        compiler_params=comm_params(3),
    )(grad_kv, g_out, part, grad_q, normed, x, cosine, sine_part, gains, w)


TERMS = 4


def reduce_late_kernel(shards, line_count, part_count, *refs):
    line_ins, refs = take(refs, line_count)
    parts, refs = take(refs, part_count)
    gain_a, gain_b, *refs = refs
    terms, refs = take(refs, TERMS)
    line_outs, refs = take(refs, line_count)
    part_outs, refs = take(refs, part_count)
    gain_out, total_ref, *refs = refs
    arrived, refs = take(refs, line_count)
    done, refs = take(refs, line_count)
    stages, refs = take(refs, part_count)
    held, refs = take(refs, TERMS)
    gain_now, gain_in, gain_line, done_sems, part_sems, term_sems, send_sems, recv_sems = refs

    wire = Wire(send_sems, recv_sems)
    ctx, shard = wire.ctx, wire.shard
    relays = [
        Relay(source, stage, [(stage, target.at[ctx])], part_sems.at[i])
        for i, (source, stage, target) in enumerate(zip(parts, stages, part_outs))
    ]
    loads = [
        pltpu.make_async_copy(source, target, term_sems.at[i])
        for i, (source, target) in enumerate(zip(terms, held))
    ]
    for copy in loads:
        copy.start()
    gain_now[...] = jnp.zeros_like(gain_now)
    columns = gain_now.shape[2]
    for part in range(shards):
        for row, values in enumerate((gain_a, gain_b)):
            gain_now[part, row : row + 1] = values[:, part * columns : (part + 1) * columns]
    wire.meet(
        [wire.plane(mask) for mask in PLANE_PEERS] + [wire.line(s, shards) for s in range(1, shards)]
    )
    lines = [
        send_lines(wire, source, target, shards) for source, target in zip(line_ins, arrived)
    ]
    gathers = []
    for source, target in zip(parts, part_outs):
        rows = source.shape[0]
        place = lambda who, target=target: target.at[who]
        gathers.append(PlaneGather(wire, source, place, rows, rows // 32 * 16))
    gain = GainSum(wire, gain_now, gain_in, gain_line, shards)
    gain.step()
    gain.step()
    gain.step_line()
    for relay in relays:
        relay.push()
    for copy in loads:
        copy.wait()
    total = held[0][...]
    for one in held[1:]:
        total += one[...].astype(jnp.float32)
    total_ref[...] = low(total)
    for gather in gathers:
        gather.forward()
    locals_ = []
    for i, (source, target) in enumerate(zip(line_ins, line_outs)):
        done[i][...] = low(sum_lines(wire, lines[i], source, arrived[i]))
        place = lambda who, target=target: target.at[who]
        gathers.append(PlaneGather(wire, done[i], place, target.shape[1], half_rows(target.shape[1], i)))
        copy = pltpu.make_async_copy(done[i], place(ctx), done_sems.at[i])
        copy.start()
        locals_.append(copy)
    gain_out[...] = gain.result()
    for gather in gathers[part_count:]:
        gather.forward()
    for gather in gathers:
        gather.corner()
    for gather in gathers:
        gather.settle()
    for copy in locals_:
        copy.wait()
    for relay in relays:
        relay.settle()
    wire.finish()


def reduce_late(lines, parts, gain_a, gain_b, terms, ctx_size):
    shards = lines[0].shape[0]
    vmem = pl.BlockSpec(memory_space=pltpu.VMEM)
    gain_shape = (shards, 8, gain_a.shape[1] // shards)
    copies = (PlaneGather.COPIES + shards - 1) * len(lines) + PlaneGather.COPIES * len(parts)
    copies += 3 + shards - 1
    return pl.pallas_call(
        functools.partial(reduce_late_kernel, shards, len(lines), len(parts)),
        name="reduce_late",
        in_specs=[vmem] * len(lines) + [ANY] * len(parts) + [vmem] * 2 + [ANY] * TERMS,
        out_specs=[ANY] * (len(lines) + len(parts)) + [vmem] * 2,
        out_shape=[like(array, ctx_size) for array in (*lines, *parts)]
        + [
            jax.ShapeDtypeStruct(gain_shape[1:], jnp.float32),
            jax.ShapeDtypeStruct(terms[0].shape, jnp.bfloat16),
        ],
        scratch_shapes=[stage_like(array, shards - 1) for array in lines]
        + [stage_like(array) for array in (*lines, *parts, *terms)]
        + [
            pltpu.VMEM(gain_shape, jnp.float32),
            pltpu.VMEM((3,) + gain_shape, jnp.float32),
            pltpu.VMEM((shards - 1,) + gain_shape[1:], jnp.float32),
            dma_sems(len(lines)),
            pltpu.SemaphoreType.DMA((len(parts), 2)),
            dma_sems(TERMS),
            dma_sems(copies),
            dma_sems(copies),
        ],
        compiler_params=comm_params(4),
    )(*lines, *parts, gain_a, gain_b, *terms)


class Pack:
    def __init__(self, rows, half, chips, units, main, rest):
        self.rows, self.half, self.chips, self.main, self.rest = rows, half, chips, main, rest
        self.tail = units - half
        self.split = rows // (half // self.tail)
        self.main_start = main + rest
        self.tail_start = self.main_start + rows
        self.total = self.tail_start + self.split

    def in_spans(self, shard):
        every = (0, self.half)
        yield (self.main_start, self.rows), every, (shard * self.rows, self.rows), every
        for i, at in enumerate(range(0, self.rows, self.split)):
            yield (
                (self.tail_start, self.split),
                (i * self.tail, self.tail),
                (shard * self.rows + at, self.split),
                (self.half, self.tail),
            )

    def out_spans(self, shard, shards):
        every = (0, self.half)
        yield (0, self.main), every, (shard * self.main, self.main), every
        yield (
            (self.main, self.rest),
            every,
            (shards * self.main + shard * self.rest, self.rest),
            every,
        )


def finish_kernel(
    shards, chips, pack, main_ref, tail_ref, out_main_ref, out_rest_ref, attn_out_ref, attn_q_ref, attn_kv_ref,
    x_one_ref, x_two_ref, in_ref, out_ref, grad_attn_out_ref, grad_attn_in_ref, x_ref,
):
    step = pl.program_id(0)
    last = pl.num_programs(0) - 1
    main, rest, half, tail = pack.main, pack.rest, pack.half, pack.tail
    per_shard = chips * (main + rest)
    wide = lambda values: values.astype(jnp.float32)

    @pl.when(step < last)
    def _():
        second = step >= last // 2
        tails = [
            jnp.where(second, tail_ref[who, :, tail:], tail_ref[who, :, :tail])
            for who in range(2 * chips)
        ]

        def columns_of(who, start, count):
            if start + count <= half:
                return main_ref[who, :, start : start + count]
            return tails[who][:, start - half : start - half + count]

        for core in range(2):
            for shard in range(shards):
                start = (core * shards + shard) * per_shard
                for chip in range(chips):
                    block = wide(columns_of(chip * 2 + core, shard * main, main))
                    in_ref[:, start + chip * main : start + (chip + 1) * main] = block
                ends = [
                    wide(columns_of(chip * 2 + core, shards * main, shards * rest))[
                        :, shard * rest : (shard + 1) * rest
                    ]
                    for chip in range(chips)
                ]
                in_ref[:, start + chips * main : start + per_shard] = jnp.concatenate(ends, axis=1)
            out_ref[:, core * half : (core + 1) * half] = wide(out_main_ref[core])
        x_ref[...] = x_one_ref[...] + x_two_ref[...]
        grad_attn_out_ref[...] = wide(attn_out_ref[0])
        inner = attn_q_ref.shape[2]
        grad_attn_in_ref[:, :inner] = wide(attn_q_ref[0])
        grad_attn_in_ref[:, inner:] = wide(attn_kv_ref[0])

    @pl.when(step == last)
    def _():
        for chip in range(chips):
            for core in range(2):
                block = wide(out_rest_ref[chip * 2 + core])
                out_ref[chip * rest : (chip + 1) * rest, core * half : (core + 1) * half] = block


def finish(first, second, attn_out, attn_q, attn_kv, x_one, x_two, pack, shards):
    ctx_size = first.shape[0]
    chips = ctx_size // 2
    steps = ctx_size
    tile = pack.rows // steps
    out_tile = pack.main // 2
    assert pack.rows // pack.split == 2 and pack.split % tile == 0
    assert out_tile == chips * pack.rest and pack.main % pack.rest == 0
    at = lambda i: jnp.minimum(i, steps - 1)
    rows = attn_out.shape[1]
    x_rows = x_one.shape[0] // steps
    piece = lambda array: pl.BlockSpec((1,) + array.shape[1:], lambda i: (at(i), 0, 0))
    attn_in = attn_q.shape[2] + attn_kv.shape[2]
    return pl.pallas_call(
        functools.partial(finish_kernel, shards, chips, pack),
        name="finish",
        grid=(steps + 1,),
        in_specs=[
            pl.BlockSpec((ctx_size, tile, pack.half), lambda i: (0, at(i), 0)),
            pl.BlockSpec(
                (ctx_size, tile, pack.half),
                lambda i: (0, pack.rows // tile + at(i) % (pack.split // tile), 0),
            ),
            pl.BlockSpec((2, out_tile, pack.half), lambda i: (at(i) // 2, at(i) % 2, 0)),
            pl.BlockSpec((ctx_size, pack.rest, pack.half), lambda i: (0, pack.main // pack.rest, 0)),
            piece(attn_out),
            piece(attn_q),
            piece(attn_kv),
            pl.BlockSpec((x_rows, x_one.shape[1]), lambda i: (at(i), 0)),
            pl.BlockSpec((x_rows, x_one.shape[1]), lambda i: (at(i), 0)),
        ],
        out_specs=[
            pl.BlockSpec((tile, 2 * FF), lambda i: (at(i), 0)),
            pl.BlockSpec((out_tile, 2 * pack.half), lambda i: (i, 0)),
            pl.BlockSpec((rows, attn_out.shape[2]), lambda i: (at(i), 0)),
            pl.BlockSpec((rows, attn_in), lambda i: (at(i), 0)),
            pl.BlockSpec((x_rows, x_one.shape[1]), lambda i: (at(i), 0)),
        ],
        out_shape=[
            jax.ShapeDtypeStruct((pack.rows, 2 * FF), jnp.float32),
            jax.ShapeDtypeStruct((FF // shards, 2 * pack.half), jnp.float32),
            jax.ShapeDtypeStruct((steps * rows, attn_out.shape[2]), jnp.float32),
            jax.ShapeDtypeStruct((steps * rows, attn_in), jnp.float32),
            jax.ShapeDtypeStruct(x_one.shape, jnp.float32),
        ],
        compiler_params=pltpu.CompilerParams(vmem_limit_bytes=VMEM_LIMIT),
    )(second, second, first, first, attn_out, attn_q, attn_kv, x_one, x_two)


TANH_SCALE = 0.7978845608028654
TANH_CUBE = 0.044715
UNIT_TILE = 384


def mlp_kernel(
    shards, pack, mine, x_left, x_right, x_x, x_y, c_own, c_x_left, c_x_right, c_y_left, c_y_right, c_left, c_right,
    normed_grad, out_own, out_x, out_y, out_left, out_right, grad_first, grad_second,
    w_in, w_out, xs, cs, hidden, grads, part, from_x, from_y, corner_left, corner_right,
    out_stage, pair_in, pair_out, local_sems, send_sems, recv_sems,
):
    wire = Wire(send_sems, recv_sems)
    core = lax.rem(wire.ctx, 2)
    other = 1 - core
    rows, half = x_left.shape
    width = 2 * half
    units = w_in.shape[2]
    tiles = units // UNIT_TILE
    left, right = pl.ds(0, half), pl.ds(half, half)
    locals_ = []

    def copy_in(source, target):
        copy = pltpu.make_async_copy(source, target, local_sems.at[len(locals_)])
        copy.start()
        locals_.append(copy)
        return copy

    def spans():
        for shard in range(shards):
            for one in pack.in_spans(shard):
                yield shard, w_in, one
        for shard in range(shards):
            for one in pack.out_spans(shard, shards):
                yield shard, w_out, one

    def packed(shard, one):
        return mine.at[shard, pl.ds(*one[0]), pl.ds(*one[1])]

    def placed(which, target, one):
        return target.at[which, pl.ds(*one[2]), pl.ds(*one[3])]

    loads = [
        copy_in(x_left, xs.at[0, :, left]),
        copy_in(x_right, xs.at[0, :, right]),
    ]
    for shard, target, one in spans():
        loads.append(copy_in(packed(shard, one), placed(core, target, one)))
    loads.append(copy_in(c_own, cs.at[0]))
    late = [
        copy_in(source, target)
        for source, target in (
            (x_x, xs.at[1, :, left]),
            (x_y, xs.at[2, :, right]),
            (c_x_left, cs.at[1, :, left]),
            (c_x_right, cs.at[1, :, right]),
            (c_y_left, cs.at[2, :, left]),
            (c_y_right, cs.at[2, :, right]),
            (c_left, cs.at[3, :, left]),
            (c_right, cs.at[3, :, right]),
        )
    ]
    wire.meet([wire.plane(mask) for mask in PLANE_PEERS])
    x_copies = [
        wire.send(x_right, xs.at[1, :, right], wire.plane(2)),
        wire.send(x_left, xs.at[2, :, left], wire.plane(4)),
    ]
    swaps = [
        wire.send(packed(shard, one), placed(core, target, one), wire.plane(1))
        for shard, target, one in spans()
    ]
    first = sum(len(list(pack.in_spans(shard))) for shard in range(shards))
    for copy in loads[: 2 + first]:
        copy.wait()
    for copy in swaps[:first]:
        copy.wait_recv()

    def wait_rest():
        for copy in loads[2 + first :]:
            copy.wait()
        for copy in swaps[first:]:
            copy.wait_recv()

    def one_chunk(at, ready=None):
        gate = dot(xs[at], w_in[0])
        up = dot(xs[at], w_in[1])
        if ready is not None:
            ready()
        grad = nt_dot(cs[at, :, left], w_out[0]) + nt_dot(cs[at, :, right], w_out[1])
        square = gate * gate
        bend = jnp.tanh(TANH_SCALE * gate * (1.0 + TANH_CUBE * square))
        lift = 0.5 + 0.5 * bend
        value = gate * lift
        slope = lift + (0.5 * TANH_SCALE) * gate * (1.0 - bend * bend) * (
            1.0 + (3.0 * TANH_CUBE) * square
        )
        hidden[at] = low(value * up)
        grads[0, at] = low(grad * up * slope)
        grads[1, at] = low(grad * value)

        def one_half(span):
            total = nt_dot(grads[0, at], w_in[0, span, :])
            return total + nt_dot(grads[1, at], w_in[1, span, :])

        return one_half

    own_half = one_chunk(0, wait_rest)
    for copy in x_copies:
        copy.wait_recv()
    corners = [
        wire.send(x_x, xs.at[3, :, left], wire.plane(4)),
        wire.send(x_y, xs.at[3, :, right], wire.plane(2)),
    ]
    for copy in late:
        copy.wait()
    one_half = one_chunk(1)
    part[0, :, left] = low(one_half(left))
    early = [wire.send(part.at[0, :, left], from_x.at[:, left], wire.plane(2))]
    part[0, :, right] = low(one_half(right))
    one_half = one_chunk(2)
    part[1, :, right] = low(one_half(right))
    early.append(wire.send(part.at[1, :, right], from_y.at[:, right], wire.plane(4)))
    part[1, :, left] = low(one_half(left))
    for copy in corners:
        copy.wait_recv()
    one_half = one_chunk(3)
    part[2, :, left] = low(one_half(left))
    corner = [wire.send(part.at[2, :, left], corner_left, wire.plane(2))]
    part[2, :, right] = low(one_half(right))
    corner.append(wire.send(part.at[2, :, right], corner_right, wire.plane(4)))

    for span in (left, right):
        normed_grad[:, span] = own_half(span)
    out_copies = {}

    def out_part(at, targets):
        slot = at % 2
        for copy in out_copies.get(slot, ()):
            copy.wait()
        for n, span in enumerate((left, right)):
            out_stage[slot, :, span] = low(dot(hidden[at], w_out[n]))
        out_copies[slot] = [copy_in(out_stage.at[(slot,) + here], target) for here, target in targets]

    every = slice(None)
    out_part(3, [((every, left), out_left), ((every, right), out_right)])
    out_part(2, [((), out_y)])
    out_part(1, [((), out_x)])
    out_part(0, [((), out_own)])

    everything = lambda ref: ref[...].reshape(ref.shape[0] * rows, ref.shape[2])

    def in_tile(which, tile):
        columns = pl.ds(tile * UNIT_TILE, UNIT_TILE)
        picked = grads[which, :, :, columns].reshape(4 * rows, UNIT_TILE)
        return columns, tn_dot(everything(xs), picked)

    pairs_in = []

    def send_in_tile(tile):
        columns, value = in_tile(other, tile)
        w_in[0, :, columns] = low(value)
        pairs_in.append(wire.send(w_in.at[0, :, columns], pair_in.at[:, columns], wire.plane(1)))

    for tile in range(tiles):
        send_in_tile(tile)
    merged = []
    corner[0].wait_recv()
    part[1, :, left] = add_low(part[1, :, left], corner_left[...])
    merged.append(wire.send(part.at[1, :, left], from_y.at[:, left], wire.plane(4)))
    corner[1].wait_recv()
    part[0, :, right] = add_low(part[0, :, right], corner_right[...])
    merged.append(wire.send(part.at[0, :, right], from_x.at[:, right], wire.plane(2)))

    def out_tile(which, tile):
        columns = pl.ds(tile * UNIT_TILE, UNIT_TILE)
        picked = hidden[:, :, columns].reshape(4 * rows, UNIT_TILE)
        span = pl.ds(pl.multiple_of(which * half, half), half)
        return columns, tn_dot(picked, cs[:, :, span].reshape(4 * rows, half))

    pairs_out = []
    for tile in range(tiles):
        span, value = out_tile(other, tile)
        w_out[0, span, :] = low(value)
        pairs_out.append(wire.send(w_out.at[0, span, :], pair_out.at[span, :], wire.plane(1)))
    final = []
    for tile in range(tiles):
        columns, value = in_tile(core, tile)
        pairs_in[tile].wait_recv()
        w_in[1, :, columns] = low(value + pair_in[:, columns].astype(jnp.float32))
    for tile in range(tiles):
        span, value = out_tile(core, tile)
        pairs_out[tile].wait_recv()
        w_out[1, span, :] = low(value + pair_out[span, :].astype(jnp.float32))
    for shard, source, one in spans():
        start, count = one[0]
        if start < pack.main_start:
            target = grad_first.at[shard, pl.ds(start, count), pl.ds(*one[1])]
        else:
            target = grad_second.at[shard, pl.ds(start - pack.main_start, count), pl.ds(*one[1])]
        final.append(copy_in(placed(1, source, one), target))
    for copy in early + merged:
        copy.wait_recv()
    normed_grad[...] += from_x[...].astype(jnp.float32) + from_y[...].astype(jnp.float32)
    for copies in out_copies.values():
        for copy in copies:
            copy.wait()
    for copy in final:
        copy.wait()
    wire.finish()


def mlp(mine, x, upstream, pack):
    rows, half = x[0].shape
    width = 2 * half
    units = pack.half + pack.tail
    shards = mine.shape[0]
    low_shape = lambda *shape: jax.ShapeDtypeStruct(shape, jnp.bfloat16)
    low_scratch = lambda *shape: pltpu.VMEM(shape, jnp.bfloat16)
    parts = shards * (1 + pack.rows // pack.split + 2)
    copies = parts + 4 + 2 + 2 + 2 + 2 * (units // UNIT_TILE)
    locals_ = 3 + parts + 8 + 5 + parts
    return pl.pallas_call(
        functools.partial(mlp_kernel, shards, pack),
        name="mlp",
        in_specs=[ANY] * 12,
        out_specs=[pl.BlockSpec(memory_space=pltpu.VMEM)] + [ANY] * 7,
        out_shape=[
            jax.ShapeDtypeStruct((rows, width), jnp.float32),
            low_shape(rows, width),
            low_shape(rows, width),
            low_shape(rows, width),
            low_shape(rows, half),
            low_shape(rows, half),
            low_shape(shards, pack.main_start, half),
            low_shape(shards, pack.total - pack.main_start, half),
        ],
        scratch_shapes=[
            low_scratch(2, width, units),
            low_scratch(2, units, half),
            low_scratch(4, rows, width),
            low_scratch(4, rows, width),
            low_scratch(4, rows, units),
            low_scratch(2, 4, rows, units),
            low_scratch(3, rows, width),
            low_scratch(rows, width),
            low_scratch(rows, width),
            low_scratch(rows, half),
            low_scratch(rows, half),
            low_scratch(2, rows, width),
            low_scratch(width, units),
            low_scratch(units, half),
            dma_sems(locals_),
            dma_sems(copies),
            dma_sems(copies),
        ],
        compiler_params=pltpu.CompilerParams(
            collective_id=5, has_side_effects=True, vmem_limit_bytes=MLP_VMEM
        ),
    )(mine, *x, *upstream)


class Layout:
    def __init__(self, ctx_size, fsdp_size):
        self.ctx_size = ctx_size
        self.shards = fsdp_size
        self.chips = ctx_size // 2
        self.index = lax.axis_index("ctx")
        self.chip = self.index // 2
        self.core = self.index % 2
        units = FF // (self.shards * self.chips)
        self.main = units // LANES * LANES
        self.rest = units - self.main
        self.per_shard = FF // self.shards
        self.rest_start = self.chips * self.main
        self.plane = ctx_size == 8 and fsdp_size == 4

    def xor(self, values, mask):
        pairs = [(i, i ^ mask) for i in range(self.ctx_size)]
        return lax.ppermute(values, "ctx", pairs)

    def same_core_groups(self):
        return [[chip * 2 + core for chip in range(self.chips)] for core in range(2)]

    def join_corner(self, to_x, to_y, left, right, token):
        half = left.shape[1]
        left = after(token, self.xor(left, 2))
        right = after(token, self.xor(right, 4))
        to_y = jnp.concatenate([add_low(to_y[:, :half], left), to_y[:, half:]], axis=1)
        to_x = jnp.concatenate([to_x[:, :half], add_low(to_x[:, half:], right)], axis=1)
        return to_x, to_y

    def gather_chips(self, values):
        groups = self.same_core_groups()
        return lax.all_gather(values, "ctx", axis=0, tiled=True, axis_index_groups=groups)

    def scatter_chips(self, partial):
        groups = self.same_core_groups()
        total = lax.psum_scatter(
            low(partial), "ctx", scatter_dimension=0, tiled=True, axis_index_groups=groups
        )
        return total.astype(jnp.float32)

    def columns_of_chip(self, weights, start):
        parts = []
        if self.main:
            for shard in range(self.shards):
                at = start + shard * self.per_shard + self.chip * self.main
                parts.append(lax.dynamic_slice_in_dim(weights, at, self.main, 1))
        if self.rest:
            for shard in range(self.shards):
                at = start + shard * self.per_shard + self.rest_start + self.chip * self.rest
                parts.append(lax.dynamic_slice_in_dim(weights, at, self.rest, 1))
        return jnp.concatenate(parts, axis=1)

    def rows_of_chip(self, weights):
        parts = []
        if self.main:
            parts.append(lax.dynamic_slice_in_dim(weights, self.chip * self.main, self.main, 0))
        if self.rest:
            at = self.rest_start + self.chip * self.rest
            parts.append(lax.dynamic_slice_in_dim(weights, at, self.rest, 0))
        return jnp.concatenate(parts, axis=0)

    def by_core(self, mine, other):
        first = jnp.where(self.core == 0, mine, other)
        second = jnp.where(self.core == 0, other, mine)
        return first, second

    def mine_in(self, shard, later=0):
        return self.columns_of_chip(shard, self.core * FF + later)

    def mine_out(self, shard, later=0):
        width = shard.shape[1]
        half = lax.dynamic_slice_in_dim(shard, self.core * (width // 2) + later, width // 2, 1)
        return self.rows_of_chip(half)

    def gather_mlp_in(self, shard):
        mine = lax.all_gather(self.mine_in(shard), "fsdp", axis=0, tiled=True)
        return self.by_core(mine, self.xor(mine, 1))

    def gather_mlp_out(self, shard):
        width = shard.shape[1]
        mine = lax.all_gather(self.mine_out(shard), "fsdp", axis=0)
        mine = jnp.concatenate(
            [
                mine[:, : self.main].reshape(self.shards * self.main, width // 2),
                mine[:, self.main :].reshape(self.shards * self.rest, width // 2),
            ],
            axis=0,
        )
        return jnp.concatenate(self.by_core(mine, self.xor(mine, 1)), axis=1)

    def sum_pair(self, first, second):
        keep = jnp.where(self.core == 0, first, second)
        send = jnp.where(self.core == 0, second, first)
        return keep + self.xor(low(send), 1).astype(jnp.float32)

    def reduce_mlp_in(self, gate, up):
        total = low(self.sum_pair(gate, up))
        return lax.psum_scatter(total, "fsdp", scatter_dimension=0, tiled=True)

    def order_mlp_in(self, every):
        rows = every.shape[1]
        every = every.reshape(self.chips, 2, rows, every.shape[2])
        split = self.shards * self.main
        main = every[..., :split].reshape(self.chips, 2, rows, self.shards, self.main)
        rest = every[..., split:].reshape(self.chips, 2, rows, self.shards, self.rest)
        main = main.transpose(2, 1, 3, 0, 4).reshape(rows, 2, self.shards, -1)
        rest = rest.transpose(2, 1, 3, 0, 4).reshape(rows, 2, self.shards, -1)
        return jnp.concatenate([main, rest], axis=3).reshape(rows, 2 * FF).astype(jnp.float32)

    def reduce_mlp_out(self, grad):
        width = grad.shape[1]
        total = low(self.sum_pair(grad[:, : width // 2], grad[:, width // 2 :]))
        split = self.shards * self.main
        main = total[:split].reshape(self.shards, self.main, width // 2)
        rest = total[split:].reshape(self.shards, self.rest, width // 2)
        total = jnp.concatenate([main, rest], axis=1)
        return lax.psum_scatter(total, "fsdp", scatter_dimension=0, tiled=True)[0]

    def order_mlp_out(self, every):
        width = 2 * every.shape[2]
        every = every.reshape(self.chips, 2, self.main + self.rest, width // 2)
        main = every[:, :, : self.main].transpose(0, 2, 1, 3).reshape(-1, width)
        rest = every[:, :, self.main :].transpose(0, 2, 1, 3).reshape(-1, width)
        return jnp.concatenate([main, rest], axis=0).astype(jnp.float32)

    def gather_whole(self, shard):
        rows = shard.shape[0] // self.ctx_size
        piece = lax.dynamic_slice_in_dim(shard, self.index * rows, rows, 0)
        piece = lax.all_gather(piece, "fsdp", axis=0)
        piece = lax.all_gather(piece, "ctx", axis=1, tiled=True)
        return piece.reshape(-1, shard.shape[1])

    def reduce_whole(self, grad):
        rows = grad.shape[0] // self.shards
        total = grad.reshape(self.shards, rows, grad.shape[1])
        total = lax.psum_scatter(total, "ctx", scatter_dimension=1, tiled=True)
        total = lax.psum_scatter(total, "fsdp", scatter_dimension=0, tiled=True)[0]
        return lax.all_gather(total, "ctx", axis=0, tiled=True).astype(jnp.float32)

    def reduce_gain(self, grad):
        total = jnp.sum(lax.all_gather(grad, ("ctx", "fsdp"), axis=0), axis=0)
        rows = grad.shape[0] // self.shards
        return lax.dynamic_slice_in_dim(total, lax.axis_index("fsdp") * rows, rows)


def per_device(
    ctx_size,
    fsdp_size,
    tokens,
    order,
    lengths,
    norm_attn,
    w_attn_in,
    w_attn_out,
    norm_mlp,
    w_mlp_in,
    w_mlp_out,
    cotangent,
):
    lay = Layout(ctx_size, fsdp_size)
    x, upstream = tokens[0], cotangent[0]
    own_rows, width = x.shape
    block = own_rows // ROUNDS
    if lay.plane:
        pack = Pack(w_mlp_in.shape[0], width // 2, lay.chips, FF // lay.chips, lay.main, lay.rest)
        pieces = lambda w: w.reshape(ctx_size, w.shape[0] // ctx_size, w.shape[1])
        in_line, gains, mine, upstream_x, upstream_y = share_line(
            pieces(w_attn_in),
            jnp.stack([norm_attn, norm_mlp]),
            w_mlp_in,
            w_mlp_out,
            upstream,
            pack,
            fsdp_size,
        )
        mine = lax.all_gather(mine, "fsdp", axis=0)
        in_attn, out_line, *tables = share_plane(
            pieces(w_attn_in),
            in_line,
            pieces(w_attn_out),
            order,
            lengths,
            own_rows,
            ctx_size,
            fsdp_size,
        )
        in_attn = in_attn.reshape(width, -1)
    else:
        tables = place_tables_alone(ctx_size, order, lengths, own_rows)
        in_attn = lay.gather_whole(w_attn_in)
        out_attn = lay.gather_whole(w_attn_out)
        gains = jnp.pad(jnp.stack([norm_attn, norm_mlp]).astype(jnp.float32), ((0, 6), (0, 0)))
        gains = lax.all_gather(gains, "fsdp", axis=0)
        gate_in, up_in = lay.gather_mlp_in(w_mlp_in)
        out_mlp = lay.gather_mlp_out(w_mlp_out)
        upstream_all = lay.gather_chips(upstream)

    where, key_place, bounds, bounds_wide, cosine, sine_part = tables
    normed_one, queries = project(x, gains, in_attn, cosine, sine_part)
    if lay.plane:
        key_value, out_attn, token = gather_plane(
            queries, pieces(w_attn_out), out_line, ctx_size, fsdp_size
        )
        out_attn = out_attn.reshape(-1, width)
        half = width // 2
        upstream_all = (
            upstream,
            upstream_x,
            lay.xor(after(token, upstream[:, half:]), 2),
            lay.xor(after(token, upstream[:, :half]), 4),
            upstream_y,
            lay.xor(after(token, upstream_x), 4),
            lay.xor(after(token, upstream_y), 2),
        )
    else:
        key_value = lax.all_gather(queries[H:], "ctx", axis=0)
    mixed, log_total = attend(where, queries, key_value, key_place, bounds)
    middle, left, right = middle_forward(x, mixed, gains, out_attn)

    if lay.plane:
        grad_normed_two, out_own, *out_parts, grad_first, grad_second = mlp(
            mine,
            (left, right, lay.xor(left, 2), lay.xor(right, 4)),
            upstream_all,
            pack,
        )
        grad_first = lax.psum_scatter(grad_first, "fsdp", scatter_dimension=0, tiled=True)[0]
        grad_second = lax.psum_scatter(grad_second, "fsdp", scatter_dimension=0, tiled=True)[0]
    else:
        normed_all = lay.gather_chips(jnp.concatenate([left, right], axis=1))
        gate = dot(normed_all, gate_in)
        up = dot(normed_all, up_in)
        hidden, hidden_back = jax.vjp(geglu, gate, up)
        hidden = low(hidden)
        grad_hidden = dot_nt(upstream_all, out_mlp)
        grad_gate, grad_up = hidden_back(grad_hidden)
        grad_gate = low(grad_gate)
        grad_up = low(grad_up)
        grad_normed_two = lay.scatter_chips(dot_nt(grad_gate, gate_in) + dot_nt(grad_up, up_in))
        result = low(middle + lay.scatter_chips(dot(hidden, out_mlp)))
        grad_out_mlp = lay.reduce_mlp_out(dot_tn(hidden, upstream_all))
        grad_in_mlp = lay.reduce_mlp_in(dot_tn(normed_all, grad_gate), dot_tn(normed_all, grad_up))

    grad_middle, grad_mixed, grad_out_attn, grad_gain_mlp, token = middle_back(
        grad_normed_two, middle, upstream, mixed, gains, out_attn
    )
    out_parts = lay.join_corner(*out_parts, token) if lay.plane else ()
    grad_query, grad_kv = attend_back(
        where,
        queries,
        key_value,
        grad_mixed,
        mixed,
        log_total,
        key_place,
        bounds_wide,
        cosine,
        sine_part,
        out_parts,
    )
    if lay.plane:
        split = lambda grad: grad.reshape(fsdp_size, lay.chips, 2, -1, grad.shape[1])
        grad_kv = grad_kv.reshape(ROUNDS, lay.chips, 2, block, 2 * HD)
        *halves, grad_first, grad_inputs, grad_gain_attn = project_back_plane(
            grad_kv,
            split(grad_out_attn),
            grad_first,
            grad_query,
            normed_one,
            x,
            cosine,
            sine_part,
            gains,
            in_attn,
            ctx_size,
        )
        to_x, to_y = out_parts
        terms = (middle, out_own, lay.xor(to_y, 4), lay.xor(to_x, 2))
        grad_out_attn, grad_in_queries, grad_in_keys, grad_second, grad_gains, result = reduce_late(
            halves, [grad_second], grad_gain_attn, grad_gain_mlp, terms, ctx_size
        )
        grad_in_mlp, grad_out_mlp, grad_out_attn, grad_in_attn, grad_inputs = finish(
            grad_first,
            grad_second,
            grad_out_attn,
            grad_in_queries,
            grad_in_keys,
            grad_middle,
            grad_inputs,
            pack,
            fsdp_size,
        )
        grad_gain_attn, grad_gain_mlp = grad_gains[0], grad_gains[1]
    else:
        grad_kv = grad_kv.reshape(ROUNDS, ctx_size, block, 2 * HD)
        grad_kv = lax.psum_scatter(grad_kv, "ctx", scatter_dimension=1, tiled=True)
        grad_kv = grad_kv.reshape(own_rows, 2 * HD).astype(jnp.float32)
        grad_in_queries, grad_normed = project_back_queries(grad_query, normed_one, in_attn)
        grad_in_keys, grad_inputs, grad_gain_attn = project_back_keys(
            grad_kv, cosine, sine_part, normed_one, grad_normed, x, grad_middle, gains, in_attn
        )
        grad_in_attn = jnp.concatenate([grad_in_queries, grad_in_keys], axis=1)
        grad_out_attn = lay.reduce_whole(grad_out_attn)
        grad_in_attn = lay.reduce_whole(grad_in_attn)
        grad_in_mlp = lay.order_mlp_in(lax.all_gather(grad_in_mlp, "ctx", axis=0))
        grad_out_mlp = lay.order_mlp_out(lax.all_gather(grad_out_mlp, "ctx", axis=0))
        grad_gain_attn = lay.reduce_gain(grad_gain_attn[0])
        grad_gain_mlp = lay.reduce_gain(grad_gain_mlp[0])
    return (
        result[None],
        grad_inputs[None],
        grad_gain_attn,
        grad_in_attn,
        grad_out_attn,
        grad_gain_mlp,
        grad_in_mlp,
        grad_out_mlp,
    )


def solution(mesh):
    in_specs = (
        P("fsdp", "ctx", None),
        P("fsdp", None),
        P("fsdp", None),
        P("fsdp"),
        P("fsdp", None),
        P("fsdp", None),
        P("fsdp"),
        P("fsdp", None),
        P("fsdp", None),
        P("fsdp", "ctx", None),
    )
    out_specs = (
        P("fsdp", "ctx", None),
        P("fsdp", "ctx", None),
        P("fsdp"),
        P("fsdp", None),
        P("fsdp", None),
        P("fsdp"),
        P("fsdp", None),
        P("fsdp", None),
    )

    def run(*arrays):
        return per_device(mesh.shape["ctx"], mesh.shape["fsdp"], *arrays)

    return jax.shard_map(run, mesh=mesh, in_specs=in_specs, out_specs=out_specs, check_vma=False)
```
